128 devices in a mesh: fsdp: 4 (over x_lo, core), ctx: 32 (over y, z, x_hi).
Axes of the slice: x: 4 (x_hi: 2, x_lo: 2; x = x_hi * 2 + x_lo), y: 4, z: 4, core: 2. Of those that a mesh axis runs over, the one named last changes fastest.
Arguments:
- tokens: bfloat16 [4, 4096, 768], P('fsdp', 'ctx'), may hold values from -6 to 6
- cotangent: bfloat16 [4, 4096, 768], P('fsdp', 'ctx'), may hold values from -6 to 6
- ln1_gain: bfloat16 [2, 768], P(None, 'fsdp'), may hold values from 0.5 to 1.5
- ln1_bias: bfloat16 [2, 768], P(None, 'fsdp'), may hold values from -1.5 to 1.5
- ln2_gain: bfloat16 [2, 768], P(None, 'fsdp'), may hold values from 0.5 to 1.5
- ln2_bias: bfloat16 [2, 768], P(None, 'fsdp'), may hold values from -1.5 to 1.5
- qkv_weight: bfloat16 [2, 768, 2304], P(None, 'fsdp'), may hold values from -0.3125 to 0.3125
- qkv_bias: bfloat16 [2, 2304], P(None, 'fsdp'), may hold values from -2.5 to 2.5
- out_weight: bfloat16 [2, 768, 768], P(None, 'fsdp'), may hold values from -0.625 to 0.625
- out_bias: bfloat16 [2, 768], P(None, 'fsdp'), may hold values from -1.5 to 1.5
- up_weight: bfloat16 [2, 768, 3072], P(None, 'fsdp'), may hold values from -0.21875 to 0.21875
- up_bias: bfloat16 [2, 3072], P(None, 'fsdp'), may hold values from -2.5 to 2.5
- down_weight: bfloat16 [2, 3072, 768], P(None, 'fsdp'), may hold values from -0.109375 to 0.109375
- down_bias: bfloat16 [2, 768], P(None, 'fsdp'), may hold values from -1.5 to 1.5
Outputs:
- output: bfloat16 [4, 4096, 768], P('fsdp', 'ctx')
- input_grad: float32 [4, 4096, 768], P('fsdp', 'ctx')
- ln1_gain_grad: float32 [2, 768], P(None, 'fsdp')
- ln1_bias_grad: float32 [2, 768], P(None, 'fsdp')
- ln2_gain_grad: float32 [2, 768], P(None, 'fsdp')
- ln2_bias_grad: float32 [2, 768], P(None, 'fsdp')
- qkv_weight_grad: float32 [2, 768, 2304], P(None, 'fsdp')
- qkv_bias_grad: float32 [2, 2304], P(None, 'fsdp')
- out_weight_grad: float32 [2, 768, 768], P(None, 'fsdp')
- out_bias_grad: float32 [2, 768], P(None, 'fsdp')
- up_weight_grad: float32 [2, 768, 3072], P(None, 'fsdp')
- up_bias_grad: float32 [2, 3072], P(None, 'fsdp')
- down_weight_grad: float32 [2, 3072, 768], P(None, 'fsdp')
- down_bias_grad: float32 [2, 768], P(None, 'fsdp')
The draws below stay inside these ranges and needn't reach their ends.
All inputs are finite; a program needn't handle non-finite values.
Results may differ from the reference program's by a relative error of at most 0.04.
Values may be sent and summed in bfloat16 or wider, within the bound.
A program may use at most 256 MiB of HBM per device.

```python
import math
import jax
import jax.numpy as jnp
from jax import lax

D = 768
HEADS = 12
HEAD_DIM = 64
FF = 3072
ROTARY = 16
LAYERS = 2
LENGTH = 4096
SEQS = 4


def steps_of(own_key, extent, split, smallest, largest):
    gain, own = 1.0, jax.random.fold_in(own_key, 6)
    for axis_at, shards_of in split:
        heights = jnp.exp(jax.random.uniform(jax.random.fold_in(own, axis_at), (shards_of,), jnp.float32, smallest / len(split), largest / len(split)))
        gain = gain * jnp.repeat(heights, extent[axis_at] // shards_of).reshape([-1 if axis == axis_at else 1 for axis in range(len(extent))])
    return gain


def centred(own_key, extent, width, most, pieces=(), kind=jnp.bfloat16):
    level = steps_of(own_key, extent, pieces, -0.22, 0.18) if pieces else 1.0
    result = jax.random.normal(own_key, extent, jnp.float32) * width * level
    return jnp.minimum(jnp.maximum(result, -most), most).astype(kind)


def setup_inputs(seed: int = 0) -> dict:
    splits = jax.random.split(jax.random.key(seed), 15)
    tokens = centred(splits[0], (SEQS, LENGTH, D), 1.0, 6.0, ((0, 4), (1, 32)))
    cotangent = centred(splits[1], (SEQS, LENGTH, D), 1.0, 6.0, ((0, 4), (1, 32)))
    ln1_gain = jnp.clip(1.0 + 0.1 * jax.random.normal(splits[2], (LAYERS, D), jnp.float32), 0.5, 1.5).astype(jnp.bfloat16)
    ln1_bias = centred(splits[3], (LAYERS, D), 0.3, 1.5, ((1, 4),))
    ln2_gain = jnp.clip(1.0 + 0.1 * jax.random.normal(splits[4], (LAYERS, D), jnp.float32), 0.5, 1.5).astype(jnp.bfloat16)
    ln2_bias = centred(splits[5], (LAYERS, D), 0.3, 1.5, ((1, 4),))
    qkv_weight = centred(splits[6], (LAYERS, D, 3 * D), (D // 2) ** -0.5, 0.3125, ((1, 4),))
    qkv_bias = centred(splits[7], (LAYERS, 3 * D), 0.5, 2.5, ((1, 4),))
    out_weight = centred(splits[8], (LAYERS, D, D), (D // 8) ** -0.5, 0.625, ((1, 4),))
    out_bias = centred(splits[9], (LAYERS, D), 0.3, 1.5, ((1, 4),))
    up_weight = centred(splits[10], (LAYERS, D, FF), D ** -0.5, 0.21875, ((1, 4),))
    up_bias = centred(splits[11], (LAYERS, FF), 0.5, 2.5, ((1, 4),))
    down_weight = centred(splits[12], (LAYERS, FF, D), FF ** -0.5, 0.109375, ((1, 4),))
    down_bias = centred(splits[13], (LAYERS, D), 0.3, 1.5, ((1, 4),))
    return {"tokens": tokens, "cotangent": cotangent, "ln1_gain": ln1_gain, "ln1_bias": ln1_bias, "ln2_gain": ln2_gain, "ln2_bias": ln2_bias, "qkv_weight": qkv_weight, "qkv_bias": qkv_bias, "out_weight": out_weight, "out_bias": out_bias, "up_weight": up_weight, "up_bias": up_bias, "down_weight": down_weight, "down_bias": down_bias}


@jax.custom_vjp
def low(v):
    return lax.optimization_barrier(v.astype(jnp.bfloat16)).astype(jnp.float32)

@jax.custom_vjp
def low_back(v):
    return v

def low_keep(v):
    return (low(v), None)

def low_pass(kept, grad):
    return (grad,)

def back_keep(v):
    return (v, None)

def back_low(kept, grad):
    return (low(grad),)
low.defvjp(low_keep, low_pass)
low_back.defvjp(back_keep, back_low)
epsilon = 1e-05
masked_score = -1e+30
highest = lax.Precision.HIGHEST

def product(left, right):
    return jnp.dot(left, right, precision=highest, preferred_element_type=jnp.float32)

def layer_norm(values, norm_gain, norm_bias):
    centre = lax.optimization_barrier(jnp.mean(values, -1, keepdims=True))
    shifted = values - centre
    spread = lax.optimization_barrier(jnp.mean(shifted * shifted, -1, keepdims=True))
    return shifted * lax.rsqrt(spread + epsilon) * norm_gain + norm_bias

def rotate(values, positions):
    half_rot = ROTARY // 2
    exponent = jnp.arange(half_rot, dtype=jnp.float32) * (2.0 / ROTARY)
    frequency = jnp.power(10000.0, -exponent)
    angle = positions.astype(jnp.float32)[:, None] * frequency[None, :]
    cosine = jnp.cos(angle)[:, None, :]
    sine_part = jnp.sin(angle)[:, None, :]
    first_half = values[..., :half_rot]
    second_half = values[..., half_rot:ROTARY]
    return jnp.concatenate([first_half * cosine - second_half * sine_part, second_half * cosine + first_half * sine_part, values[..., ROTARY:]], -1)

def attend(queries, key_rows, value_rows):
    length = queries.shape[0]
    block_rows = math.gcd(length, 512)
    key_pos = jnp.arange(length, dtype=jnp.int32)

    def one_block(first_row):
        query_block = lax.dynamic_slice_in_dim(queries, first_row, block_rows, 0)
        scores = low_back(jnp.einsum('qhd,khd->hqk', query_block, key_rows, precision=highest) * 0.125)
        query_pos = first_row + jnp.arange(block_rows, dtype=jnp.int32)
        allowed = key_pos[None, :] <= query_pos[:, None]
        scores = jnp.where(allowed[None], scores, masked_score)
        row_top = lax.optimization_barrier(jnp.max(scores, -1, keepdims=True))
        weights = jnp.exp(scores - row_top)
        chances = low(weights / lax.optimization_barrier(jnp.sum(weights, -1, keepdims=True)))
        return jnp.einsum('hqk,khd->qhd', chances, value_rows, precision=highest)
    starts = jnp.arange(length // block_rows, dtype=jnp.int32) * block_rows
    blocks_out = lax.map(jax.checkpoint(one_block), starts)
    return blocks_out.reshape(length, queries.shape[1], queries.shape[2])

def layer(stream, weights, positions):
    gain_one, bias_one, gain_two, bias_two, w_qkv, b_qkv, w_out, b_out, w_up, b_up, w_down, b_down = weights
    row_count = stream.shape[0]
    head_shape = (row_count, HEADS, HEAD_DIM)
    norm_one = low(layer_norm(stream, gain_one, bias_one))
    norm_two = low(layer_norm(stream, gain_two, bias_two))
    joined = low_back(product(norm_one, w_qkv) + b_qkv)
    queries = low(rotate(joined[:, :D].reshape(head_shape), positions))
    key_rows = low(rotate(joined[:, D:2 * D].reshape(head_shape), positions))
    value_rows = low(joined[:, 2 * D:].reshape(head_shape))
    mixed = attend(queries, key_rows, value_rows).reshape(row_count, D)
    attn_branch = low_back(product(low(low_back(mixed)), w_out))
    hidden_pre = low_back(product(norm_two, w_up) + b_up)
    mlp_branch = low_back(product(low(jax.nn.gelu(hidden_pre, approximate=False)), w_down))
    return stream + attn_branch + b_out + mlp_branch + b_down

def reference(tokens, cotangent, ln1_gain, ln1_bias, ln2_gain, ln2_bias, qkv_weight, qkv_bias, out_weight, out_bias, up_weight, up_bias, down_weight, down_bias):
    params = (ln1_gain.astype(jnp.float32), ln1_bias.astype(jnp.float32), ln2_gain.astype(jnp.float32), ln2_bias.astype(jnp.float32), qkv_weight.astype(jnp.float32), qkv_bias.astype(jnp.float32), out_weight.astype(jnp.float32), out_bias.astype(jnp.float32), up_weight.astype(jnp.float32), up_bias.astype(jnp.float32), down_weight.astype(jnp.float32), down_bias.astype(jnp.float32))
    length = tokens.shape[1]
    positions = jnp.arange(length, dtype=jnp.int32)

    def forward(stream, weights):
        for layer_index in range(LAYERS):
            stream = layer(stream, tuple((member[layer_index] for member in weights)), positions)
        return stream

    def one_sequence(running, seq_pair):
        seq_tokens, seq_cotangent = seq_pair
        primal, pull_back = jax.vjp(forward, seq_tokens.astype(jnp.float32), params)
        seq_input_grad, weight_grads = pull_back(seq_cotangent.astype(jnp.float32))
        running = tuple((earlier + fresh for earlier, fresh in zip(running, weight_grads)))
        return (running, (primal.astype(jnp.bfloat16), seq_input_grad))
    start_grads = tuple((jnp.zeros_like(member) for member in params))
    totals, (output, input_grad) = lax.scan(one_sequence, start_grads, (tokens, cotangent))
    return (output, input_grad, totals[0], totals[1], totals[2], totals[3], totals[4], totals[5], totals[6], totals[7], totals[8], totals[9], totals[10], totals[11])
```

```python
import functools

import jax
import jax.numpy as jnp
from jax import lax
from jax.experimental import pallas as pl
from jax.experimental.pallas import tpu as pltpu
from jax.sharding import PartitionSpec as P

D = 768
HEADS = 12
HEAD_DIM = 64
FF = 3072
ROTARY = 16
LAYERS = 2
HALF = 384
BLOCK = 128
BLOCKS = 32
TILE = 512
PAIRS = 3

epsilon = 1e-05
masked_score = -1e30
MESH = pl.DeviceIdType.MESH
BF = jnp.bfloat16
F32 = jnp.float32


def mirrored(values):
    pairs = [(f * 32 + c, f * 32 + 31 - c) for f in range(4) for c in range(32)]
    return lax.ppermute(values, ("fsdp", "ctx"), pairs)


class Place:
    def __init__(self):
        self.fsdp = lax.axis_index("fsdp")
        self.ctx = lax.axis_index("ctx")
        self.y, self.z, self.h = self.ctx // 8, (self.ctx // 2) % 4, self.ctx % 2
        self.x_lo, self.core = self.fsdp // 2, self.fsdp % 2
        self.beside = (self.fsdp + 1 - 2 * self.core, self.ctx)
        self.mirror = (self.fsdp, BLOCKS - 1 - self.ctx)
        self.half = (self.fsdp, self.ctx + 1 - 2 * self.h)

    def along_x(self, step):
        x = (2 * self.h + self.x_lo + step) % 4
        return (2 * (x % 2) + self.core, self.y * 8 + self.z * 2 + x // 2)

    def ctx_at(self, dy, dz):
        return ((self.y + dy) % 4) * 8 + ((self.z + dz) % 4) * 2 + self.h

    def ring(self, t, da, db):
        return self.ctx_at(da, db) if t == 0 else self.ctx_at(db, da)

    def near(self, t, axis, sign):
        steps = (sign, 0) if axis == 0 else (0, sign)
        return (self.fsdp, self.ring(t, *steps))

    def around(self):
        return [self.near(0, axis, sign) for axis in (0, 1) for sign in (1, -1)]

    def greet(self, partners):
        barrier = pltpu.get_barrier_semaphore()
        for partner in partners:
            pl.semaphore_signal(barrier, inc=1, device_id=partner, device_id_type=MESH)
        pl.semaphore_wait(barrier, len(partners))


class Wire:
    def __init__(self, send_sem, recv_sem, local_sem=None):
        self.send_sem, self.recv_sem, self.local_sem = send_sem, recv_sem, local_sem
        self.sent, self.local = [], []

    def push(self, source, target, partner):
        number = len(self.sent)
        copy = pltpu.make_async_remote_copy(
            src_ref=source,
            dst_ref=target,
            send_sem=self.send_sem.at[number],
            recv_sem=self.recv_sem.at[number],
            device_id=partner,
            device_id_type=MESH,
        )
        copy.start()
        self.sent.append(copy)
        return copy

    def keep(self, source, target):
        copy = pltpu.make_async_copy(source, target, self.local_sem.at[len(self.local)])
        copy.start()
        self.local.append(copy)

    def drain(self):
        for copy in self.sent:
            copy.wait_send()
        for copy in self.local:
            copy.wait()


def share_param(place, wire, source, target):
    rows = source.shape[0]
    cut = rows // 2
    mine, far = place.fsdp * rows, ((place.fsdp + 2) % 4) * rows
    parts = (
        [(0, cut, 1), (cut, cut, 3)] if rows % 32 == 0 else [(0, rows, 1)]
    )
    across = [
        wire.push(
            source.at[pl.ds(start, count)],
            target.at[pl.ds(mine + start, count)],
            place.along_x(step),
        )
        for start, count, step in parts
    ]
    beside = wire.push(source, target.at[pl.ds(mine, rows)], place.beside)
    wire.keep(source, target.at[pl.ds(mine, rows)])
    last = [beside]

    def onward(copy, start, count):
        copy.wait_recv()
        spot = target.at[pl.ds(far + start, count)]
        last.append(wire.push(spot, spot, place.beside))

    steps = [
        functools.partial(onward, copy, start, count)
        for copy, (start, count, _) in zip(across, parts)
    ]
    return steps, last


def share_rows(place, wire, source, target):
    rows = source.shape[0]
    cut = rows // 2
    parts = [(0, cut, 1), (cut, cut, 3)] if rows % 32 == 0 else [(0, rows, 1)]
    across = [
        wire.push(
            source.at[pl.ds(start, count)],
            target.at[pl.ds(2 * rows + start, count)],
            place.along_x(step),
        )
        for start, count, step in parts
    ]
    last = [wire.push(source, target.at[pl.ds(rows, rows)], place.beside)]
    wire.keep(source, target.at[pl.ds(0, rows)])

    def onward(copy, start, count):
        copy.wait_recv()
        last.append(
            wire.push(
                target.at[pl.ds(2 * rows + start, count)],
                target.at[pl.ds(3 * rows + start, count)],
                place.beside,
            )
        )

    steps = [
        functools.partial(onward, copy, start, count)
        for copy, (start, count, _) in zip(across, parts)
    ]
    return steps, last


def share_slices(place, wire, source, target, stage):
    rows = source.shape[1]
    cut = rows // 2
    fsdp, core = place.fsdp, place.core
    parts = [(0, cut, 1), (cut, cut, 3)]
    passing, last = [], []
    for start, count, step in parts:
        partner = place.along_x(step)
        passing.append(
            wire.push(
                source.at[3 - fsdp, pl.ds(start, count)], stage.at[pl.ds(start, count)], partner
            )
        )
    for start, count, step in parts:
        last.append(
            wire.push(
                source.at[(fsdp + 2) % 4, pl.ds(start, count)],
                target.at[pl.ds(2 * rows + start, count)],
                place.along_x(step),
            )
        )
    last.append(
        wire.push(source.at[fsdp + 1 - 2 * core], target.at[pl.ds(rows, rows)], place.beside)
    )
    wire.keep(source.at[fsdp], target.at[pl.ds(0, rows)])

    def onward(copy, start, count):
        copy.wait_recv()
        last.append(
            wire.push(
                stage.at[pl.ds(start, count)],
                target.at[pl.ds(3 * rows + start, count)],
                place.beside,
            )
        )

    steps = [
        functools.partial(onward, copy, start, count)
        for copy, (start, count, _) in zip(passing, parts)
    ]
    return steps, last


def spread(place, wire, own, spot, ready, between=()):
    between = list(between)
    arrivals = {}

    def push(t, da, db, b, axis, sign):
        target = spot(t, place.ring(t, da, db), b)
        source = own(t, b) if da == 0 and db == 0 else target
        sa, sb = (sign, 0) if axis == 0 else (0, sign)
        arrivals[t, (da - sa) % 4, (db - sb) % 4, b] = wire.push(
            source, target, place.near(t, axis, sign)
        )

    def landed(t, da, db):
        for b in (0, 1):
            arrivals[t, da, db, b].wait_recv()

    def pause():
        if between:
            between.pop(0)()

    for b in (0, 1):
        for t in (0, 1):
            ready(t, b)
            for axis in (0, 1):
                for sign in (1, -1):
                    push(t, 0, 0, b, axis, sign)
    for da, keep, onward in ((1, 0, -1), (3, 1, 1)):
        for t in (0, 1):
            landed(t, da, 0)
            push(t, da, 0, keep, 0, onward)
            for sign in (1, -1):
                for b in (0, 1):
                    push(t, da, 0, b, 1, sign)
    for db, keep, onward in ((1, 0, -1), (3, 1, 1)):
        for t in (0, 1):
            landed(t, 0, db)
            push(t, 0, db, keep, 1, onward)
    for t in (0, 1):
        landed(t, 2, 0)
        for sign in (1, -1):
            for b in (0, 1):
                push(t, 2, 0, b, 1, sign)
    pause()
    for da in (1, 3, 2):
        for db, keep, onward in ((1, 0, -1), (3, 1, 1)):
            for t in (0, 1):
                landed(t, da, db)
                push(t, da, db, keep, 1, onward)
            pause()
    while between:
        pause()
    for da in (0, 1, 3, 2):
        for t in (0, 1):
            landed(t, da, 2)


ANY = pl.BlockSpec(memory_space=pl.ANY)
VM = pl.BlockSpec(memory_space=pltpu.VMEM)
SM = pl.BlockSpec(memory_space=pltpu.SMEM)


def room(*shape):
    return pltpu.VMEM(shape, BF)


def sems(count, local):
    return [
        pltpu.SemaphoreType.DMA((count,)),
        pltpu.SemaphoreType.DMA((count,)),
        pltpu.SemaphoreType.DMA((local,)),
    ]


def full_shape(shard):
    return jax.ShapeDtypeStruct((4 * shard.shape[-2], shard.shape[-1]), BF)


def first_kernel(weight_ref, vector_ref, weight_out, vector_out, *sem):
    place, wire = Place(), Wire(*sem)
    place.greet([place.beside, place.along_x(1), place.along_x(3)])
    steps, last = share_param(place, wire, vector_ref, vector_out)
    more, ends = share_param(place, wire, weight_ref.at[0], weight_out)
    for step in more + steps:
        step()
    for copy in last + ends:
        copy.wait_recv()
    wire.drain()


def gather_first(weight, vectors):
    return pl.pallas_call(
        first_kernel,
        out_shape=(full_shape(weight), full_shape(vectors)),
        in_specs=[ANY] * 2,
        out_specs=(ANY,) * 2,
        scratch_shapes=sems(16, 4),
        compiler_params=pltpu.CompilerParams(collective_id=0, has_side_effects=True),
        name="gather_first",
    )(weight, vectors)


def gather_kernel(jobs, q_ref, k_ref, v_ref, k_own, v_own, *refs):
    count = len(jobs)
    weights, refs = refs[:count], refs[count:]
    q_out, k_out, v_out = refs[:3]
    weights_out, refs = refs[3 : 3 + count], refs[3 + count :]
    place, wire = Place(), Wire(*refs)
    place.greet(
        place.around() + [place.mirror, place.beside, place.along_x(1), place.along_x(3)]
    )
    ins, outs = (k_own, v_own), (k_out, v_out)
    ctx = place.ctx
    swapped = [
        wire.push(source, out.at[ctx], place.mirror) for source, out in zip((k_ref, v_ref), outs)
    ]
    swapped.append(wire.push(q_ref, q_out, place.mirror))
    for t in (0, 1):
        wire.keep(ins[t], outs[t].at[ctx])
    work = []

    def ready(t, b):
        if b == 1:
            if t == 0:
                for layer, weight, target in zip(jobs, weights, weights_out):
                    work.append(share_param(place, wire, weight.at[layer], target))
            swapped[t].wait_recv()

    def spot(t, origin, b):
        return outs[t].at[origin if b == 0 else BLOCKS - 1 - origin]

    def own(t, b):
        return ins[t] if b == 0 else spot(t, ctx, 1)

    def onward(number):
        for steps, _ in work:
            for step in steps[number : number + 1]:
                step()

    spread(
        place,
        wire,
        own,
        spot,
        ready,
        [lambda: None] * 4 + [functools.partial(onward, 0), functools.partial(onward, 1)],
    )
    swapped[2].wait_recv()
    for _, last in work:
        for copy in last:
            copy.wait_recv()
    wire.drain()


def gather_pair(name, number, away, own, jobs):
    layers = [layer for layer, _ in jobs]
    weights = [weight for _, weight in jobs]
    whole = jax.ShapeDtypeStruct((BLOCKS, BLOCK, HALF), BF)
    return pl.pallas_call(
        functools.partial(gather_kernel, layers),
        out_shape=(jax.ShapeDtypeStruct((BLOCK, HALF), BF), whole, whole)
        + tuple(full_shape(weight) for weight in weights),
        in_specs=[ANY] * (5 + len(jobs)),
        out_specs=(ANY,) * (3 + len(jobs)),
        scratch_shapes=sems(96, 8),
        compiler_params=pltpu.CompilerParams(collective_id=number, has_side_effects=True),
        name=name,
    )(*away, *own, *weights)


def scatter_kernel(count, gk_ref, gv_ref, gq_ref, stack_ref, *refs):
    sources, refs = refs[:count], refs[count:]
    own_out, back_out, back_q, stack_out = refs[:4]
    targets, refs = refs[4 : 4 + count], refs[4 + count :]
    far, near, mix, total, last_far, last_near, last_mix, leave, stage = refs[:9]
    place, wire = Place(), Wire(*refs[9:])
    place.greet(
        place.around() + [place.mirror, place.beside, place.along_x(1), place.along_x(3)]
    )
    ins = (gk_ref, gv_ref)

    def block_at(t, da, db, b):
        origin = place.ring(t, da, db)
        return origin if b == 0 else BLOCKS - 1 - origin

    order = (2, 1, 3, 0)
    first, second = {}, {}
    for da in order:
        for t in (0, 1):
            first[t, da] = [
                wire.push(
                    ins[t].at[block_at(t, da, 2, b)], far.at[t, da, b], place.near(t, 1, sign)
                )
                for b, sign in ((0, 1), (1, -1))
            ]
    swapped = [wire.push(gq_ref, back_q, place.mirror)]
    work = [share_slices(place, wire, stack_ref, stack_out, stage)]
    for source, target in zip(sources, targets):
        work.append(share_rows(place, wire, source, target))
    for da in order:
        for t in (0, 1):
            copies = []
            for b, sign, db in ((0, 1, 1), (1, -1, 3)):
                copies.append(
                    wire.push(
                        ins[t].at[block_at(t, da, db, 1 - b)],
                        near.at[t, da, b, 1 - b],
                        place.near(t, 1, sign),
                    )
                )
                first[t, da][b].wait_recv()
                mix[t, da, b] = (
                    ins[t][block_at(t, da, db, b)].astype(F32) + far[t, da, b].astype(F32)
                ).astype(BF)
                copies.append(
                    wire.push(mix.at[t, da, b], near.at[t, da, b, b], place.near(t, 1, sign))
                )
            second[t, da] = copies

    def settle(t, da):
        for copy in second[t, da]:
            copy.wait_recv()
        for b in (0, 1):
            total[t, da, b] = (
                ins[t][block_at(t, da, 0, b)].astype(F32)
                + near[t, da, 0, b].astype(F32)
                + near[t, da, 1, b].astype(F32)
            ).astype(BF)

    third, fourth = {}, {}
    for t in (0, 1):
        settle(t, 2)
        third[t] = [
            wire.push(total.at[t, 2, b], last_far.at[t, b], place.near(t, 0, sign))
            for b, sign in ((0, 1), (1, -1))
        ]
    for t in (0, 1):
        fourth[t] = []
        for b, sign, da in ((0, 1, 1), (1, -1, 3)):
            settle(t, da)
            fourth[t].append(
                wire.push(
                    total.at[t, da, 1 - b], last_near.at[t, b, 1 - b], place.near(t, 0, sign)
                )
            )
    for t in (0, 1):
        for b, sign, da in ((0, 1, 1), (1, -1, 3)):
            third[t][b].wait_recv()
            last_mix[t, b] = (total[t, da, b].astype(F32) + last_far[t, b].astype(F32)).astype(BF)
            fourth[t].append(
                wire.push(last_mix.at[t, b], last_near.at[t, b, b], place.near(t, 0, sign))
            )
    for t in (0, 1):
        settle(t, 0)
    for steps, _ in work:
        for step in steps:
            step()
    for t in (0, 1):
        for copy in fourth[t]:
            copy.wait_recv()
        for b in (1, 0):
            done = (
                total[t, 0, b].astype(F32)
                + last_near[t, 0, b].astype(F32)
                + last_near[t, 1, b].astype(F32)
            )
            if b == 1:
                leave[t] = done.astype(BF)
                swapped.append(wire.push(leave.at[t], back_out.at[t], place.mirror))
            else:
                own_out[t] = done
    for _, last in work:
        for copy in last:
            copy.wait_recv()
    for copy in swapped:
        copy.wait_recv()
    wire.drain()


def rows_shape(source):
    return jax.ShapeDtypeStruct((4 * source.shape[0], source.shape[1]), BF)


def scatter_pair(name, number, grad_keys, grad_values, away, stacked, sources):
    return pl.pallas_call(
        functools.partial(scatter_kernel, len(sources)),
        out_shape=(
            jax.ShapeDtypeStruct((2, BLOCK, HALF), F32),
            jax.ShapeDtypeStruct((2, BLOCK, HALF), BF),
            jax.ShapeDtypeStruct((BLOCK, HALF), BF),
            rows_shape(stacked[0]),
        )
        + tuple(rows_shape(source) for source in sources),
        in_specs=[VM, VM] + [ANY] * (2 + len(sources)),
        out_specs=(VM,) + (ANY,) * (3 + len(sources)),
        scratch_shapes=[
            room(2, 4, 2, BLOCK, HALF),
            room(2, 4, 2, 2, BLOCK, HALF),
            room(2, 4, 2, BLOCK, HALF),
            room(2, 4, 2, BLOCK, HALF),
            room(2, 2, BLOCK, HALF),
            room(2, 2, 2, BLOCK, HALF),
            room(2, 2, BLOCK, HALF),
            room(2, BLOCK, HALF),
            room(*stacked.shape[1:]),
        ]
        + sems(112, 8),
        compiler_params=pltpu.CompilerParams(
            collective_id=number, has_side_effects=True, vmem_limit_bytes=40 * 2**20
        ),
        name=name,
    )(grad_keys, grad_values, away, stacked, *sources)


def late_kernel(one_ref, two_ref, one_out, two_out, *sem):
    place, wire = Place(), Wire(*sem)
    place.greet([place.beside, place.along_x(1), place.along_x(3)])
    work = [
        share_rows(place, wire, one_ref, one_out),
        share_rows(place, wire, two_ref, two_out),
    ]
    for steps, _ in work:
        for step in steps:
            step()
    for _, last in work:
        for copy in last:
            copy.wait_recv()
    wire.drain()


def gather_late(one, two):
    return pl.pallas_call(
        late_kernel,
        out_shape=(rows_shape(one), rows_shape(two)),
        in_specs=[ANY] * 2,
        out_specs=(ANY,) * 2,
        scratch_shapes=sems(16, 4),
        compiler_params=pltpu.CompilerParams(collective_id=5, has_side_effects=True),
        name="gather_late",
    )(one, two)


PIECE = 144
CUT = 80


def sum_kernel(
    one_ref, two_ref, small_ref, out_ref, small_out,
    far, mix, near, total, far_two, mix_two, near_two, part, other, final, small, heard, *sem,
):
    place, wire = Place(), Wire(*sem)
    y, z, h = place.y, place.z, place.h
    turns = [
        (place.fsdp, (y + 1 - 2 * (y % 2)) * 8 + z * 2 + h),
        (place.fsdp, ((y + 2) % 4) * 8 + z * 2 + h),
        (place.fsdp, y * 8 + (z + 1 - 2 * (z % 2)) * 2 + h),
        (place.fsdp, y * 8 + ((z + 2) % 4) * 2 + h),
        place.half,
    ]
    place.greet(place.around() + [turns[1], turns[3], place.half])
    ins = (one_ref, two_ref)
    parts = {0: pl.ds(0, CUT), 1: pl.ds(CUT, PIECE - CUT)}

    def chunk(t, da, db):
        origin = place.ring(t, da, db)
        return origin // 2

    def plus(*terms):
        result = terms[0].astype(F32)
        for term in terms[1:]:
            result = result + term.astype(F32)
        return result.astype(BF)

    small[...] = small_ref[...]
    passing = wire.push(small, heard.at[0], turns[0])
    order = (2, 1, 3, 0)
    way = {2: 1, 1: 1, 3: -1, 0: -1}
    first, second, loose = {}, {}, {}
    for db in order:
        for t in (0, 1):
            first[t, db] = wire.push(
                ins[t].at[chunk(t, 2, db)], far.at[t, db], place.near(t, 0, way[db])
            )
    for db in order:
        for t in (0, 1):
            loose[t, db] = wire.push(
                ins[t].at[chunk(t, -way[db], db)], near.at[t, db, 1], place.near(t, 0, -way[db])
            )
    for db in order:
        for t in (0, 1):
            first[t, db].wait_recv()
            mix[t, db] = plus(ins[t][chunk(t, way[db], db)], far[t, db])
            second[t, db] = wire.push(mix.at[t, db], near.at[t, db, 0], place.near(t, 0, way[db]))

    def hear(step):
        wire.sent[step_numbers[-1]].wait_send()
        wire.sent[step_numbers[-1]].wait_recv()
        small[...] += heard[step]
        waited.add(step_numbers[-1])
        if step < 4:
            step_numbers.append(len(wire.sent))
            wire.push(small, heard.at[step + 1], turns[step + 1])

    step_numbers, waited = [0], set()

    def settle(t, db):
        second[t, db].wait_recv()
        loose[t, db].wait_recv()
        total[t, db] = plus(ins[t][chunk(t, 0, db)], near[t, db, 0], near[t, db, 1])

    third, fourth = {}, {}
    for t in (0, 1):
        settle(t, 2)
        third[t] = [
            wire.push(
                total.at[t, 2, parts[b]], far_two.at[t, parts[b]], place.near(t, 1, sign)
            )
            for b, sign in ((0, 1), (1, -1))
        ]
    hear(0)
    for t in (0, 1):
        fourth[t] = []
        for b, sign, db in ((0, 1, 1), (1, -1, 3)):
            settle(t, db)
            fourth[t].append(
                wire.push(
                    total.at[t, db, parts[1 - b]],
                    near_two.at[t, b, parts[1 - b]],
                    place.near(t, 1, sign),
                )
            )
    hear(1)
    for t in (0, 1):
        for b, sign, db in ((0, 1, 1), (1, -1, 3)):
            third[t][b].wait_recv()
            mix_two[t, parts[b]] = plus(total[t, db, parts[b]], far_two[t, parts[b]])
            fourth[t].append(
                wire.push(
                    mix_two.at[t, parts[b]], near_two.at[t, b, parts[b]], place.near(t, 1, sign)
                )
            )
    hear(2)
    swapped = []
    for t in (0, 1):
        settle(t, 0)
        for copy in fourth[t]:
            copy.wait_recv()
        part[t] = plus(total[t, 0], near_two[t, 0], near_two[t, 1])
        swapped.append(wire.push(part.at[t], other.at[t], place.half))
    hear(3)

    def spot(t, origin, b):
        return out_ref.at[1 - t, origin // 2, parts[b]]

    def own(t, b):
        return final.at[1 - t, parts[b]]

    def ready(t, b):
        if b == 0:
            swapped[1 - t].wait_recv()
            final[1 - t] = plus(part[1 - t], other[1 - t])
            wire.keep(final.at[1 - t], out_ref.at[1 - t, place.ctx // 2])

    spread(place, wire, own, spot, ready)
    hear(4)
    small_out[...] = small[...]
    for number, copy in enumerate(wire.sent):
        if number not in waited:
            copy.wait_send()
    for copy in wire.local:
        copy.wait()


def sum_over_ctx(one, two, small):
    shape = (16, PIECE, D)
    return pl.pallas_call(
        sum_kernel,
        out_shape=(
            jax.ShapeDtypeStruct((2,) + shape, BF),
            jax.ShapeDtypeStruct(small.shape, F32),
        ),
        in_specs=[VM, VM, VM],
        out_specs=(ANY, VM),
        scratch_shapes=[
            room(2, 4, PIECE, D),
            room(2, 4, PIECE, D),
            room(2, 4, 2, PIECE, D),
            room(2, 4, PIECE, D),
            room(2, PIECE, D),
            room(2, PIECE, D),
            room(2, 2, PIECE, D),
            room(2, PIECE, D),
            room(2, PIECE, D),
            room(2, PIECE, D),
            pltpu.VMEM(small.shape, F32),
            pltpu.VMEM((5,) + small.shape, F32),
        ]
        + sems(128, 4),
        compiler_params=pltpu.CompilerParams(
            collective_id=6, has_side_effects=True, vmem_limit_bytes=48 * 2**20
        ),
        name="sum_over_ctx",
    )(one.reshape(shape), two.reshape(shape), small)


def weight_kernel(left_ref, joined_ref, low_ref, pre_ref, rows_ref, sums_ref, turned):
    turned[...] = jnp.transpose(left_ref[...])
    ones = jnp.ones((8, left_ref.shape[0]), BF)

    def panel(out, rows, right, at):
        rows_ref[out, :] = contract(turned[rows, :], right, ((1,), (0,))).astype(BF)
        if at is not None:
            sums_ref[:, at : at + D] = contract(ones, right, ((1,), (0,)))

    low = low_ref[...]
    panel(slice(1536, 2304), slice(0, 768), low, None)
    panel(slice(576, 768), slice(960, 1152), low, 0)
    for i in range(3):
        panel(
            slice(i * 192, (i + 1) * 192), slice(768, 960), joined_ref[:, i * D : (i + 1) * D], (1 + i) * D
        )
    for i in range(4):
        panel(
            slice(768 + i * 192, 960 + i * 192),
            slice(1152, 1344),
            pre_ref[:, i * D : (i + 1) * D],
            (4 + i) * D,
        )


def weight_grads(left, joined, low, pre):
    return pl.pallas_call(
        weight_kernel,
        out_shape=(
            jax.ShapeDtypeStruct((2304, D), BF),
            jax.ShapeDtypeStruct((8, 8 * D), F32),
        ),
        in_specs=[VM] * 4,
        out_specs=(VM, VM),
        scratch_shapes=[room(left.shape[1], left.shape[0])],
        compiler_params=pltpu.CompilerParams(vmem_limit_bytes=40 * 2**20),
        cost_estimate=pl.CostEstimate(
            flops=2 * 512 * 1769472, bytes_accessed=12 * 2**20, transcendentals=0
        ),
        name="weight_grads",
    )(left, joined, low, pre)


def pair_rows(values):
    lane = lax.broadcasted_iota(jnp.int32, values.shape, 1)
    zero = jnp.zeros_like(values)
    return jnp.concatenate(
        [jnp.where(lane < HEAD_DIM, values, zero), jnp.where(lane >= HEAD_DIM, values, zero)], 0
    )


def contract(left, right, dims):
    return lax.dot_general(left, right, (dims, ((), ())), preferred_element_type=F32)


def allowed_at(tile, block):
    key = tile * TILE + lax.broadcasted_iota(jnp.int32, (TILE, 2 * BLOCK), 0)
    query = block * BLOCK + lax.broadcasted_iota(jnp.int32, (TILE, 2 * BLOCK), 1) % BLOCK
    return key <= query


def forward_kernel(ctx_ref, q_ref, k_ref, v_ref, mixed_ref, turned_ref, log_ref, top, mass, acc):
    ctx = ctx_ref[0]
    for b in (0, 1):
        block = ctx if b == 0 else BLOCKS - 1 - ctx
        rows = slice(b * BLOCK, (b + 1) * BLOCK)
        queries = [
            pair_rows(q_ref[rows, p * 128 : (p + 1) * 128] * jnp.asarray(0.125, BF))
            for p in range(PAIRS)
        ]

        def step(tile, masked):
            start = pl.multiple_of(tile * TILE, TILE)
            for p in range(PAIRS):
                cols = slice(p * 128, (p + 1) * 128)
                scores = contract(k_ref[pl.ds(start, TILE), cols], queries[p], ((1,), (1,)))
                if masked:
                    scores = jnp.where(allowed_at(tile, block), scores, masked_score)
                    new_top = jnp.max(scores, 0, keepdims=True)
                else:
                    old_top = top[p : p + 1, :]
                    new_top = jnp.maximum(old_top, jnp.max(scores, 0, keepdims=True))
                weights = jnp.exp(scores - new_top)
                fresh_mass = jnp.sum(weights, 0, keepdims=True)
                fresh = contract(
                    v_ref[pl.ds(start, TILE), cols], weights.astype(BF), ((0,), (0,))
                )
                if not masked:
                    fade = jnp.exp(old_top - new_top)
                    fresh_mass = fresh_mass + mass[p : p + 1, :] * fade
                    fresh = fresh + acc[p] * fade
                top[p : p + 1, :] = new_top
                mass[p : p + 1, :] = fresh_mass
                acc[p] = fresh

        step(block // 4, True)

        @pl.loop(0, block // 4)
        def _(tile):
            step(tile, False)

        for p in range(PAIRS):
            cols = slice(p * 128, (p + 1) * 128)
            done = acc[p] / mass[p : p + 1, :]
            turned = jnp.concatenate([done[:HEAD_DIM, :BLOCK], done[HEAD_DIM:, BLOCK:]], 0)
            turned_ref[cols, rows] = turned
            mixed_ref[rows, cols] = jnp.transpose(turned).astype(BF)
            row = b * PAIRS + p
            log_ref[row : row + 1, :] = top[p : p + 1, :] + jnp.log(mass[p : p + 1, :])


def attend_forward(ctx, queries, keys, values):
    return pl.pallas_call(
        forward_kernel,
        out_shape=(
            jax.ShapeDtypeStruct((2 * BLOCK, HALF), BF),
            jax.ShapeDtypeStruct((HALF, 2 * BLOCK), F32),
            jax.ShapeDtypeStruct((8, 2 * BLOCK), F32),
        ),
        in_specs=[SM, VM, VM, VM],
        out_specs=(VM, VM, VM),
        scratch_shapes=[
            pltpu.VMEM((8, 2 * BLOCK), F32),
            pltpu.VMEM((8, 2 * BLOCK), F32),
            pltpu.VMEM((PAIRS, 128, 2 * BLOCK), F32),
        ],
        compiler_params=pltpu.CompilerParams(vmem_limit_bytes=40 * 2**20),
        cost_estimate=pl.CostEstimate(
            flops=4 * 33 * 128 * 128 * 6 * 128, bytes_accessed=8 * 2**20, transcendentals=33 * 128 * 128 * 6
        ),
        name="attend_forward",
    )(ctx, queries, keys, values)


def backward_kernel(
    ctx_ref, q_ref, k_ref, v_ref, g_ref, turned_ref, log_ref, gq_ref, gk_ref, gv_ref, gk_acc, gv_acc, gq_acc
):
    ctx = ctx_ref[0]
    gk_acc[...] = jnp.zeros_like(gk_acc)
    gv_acc[...] = jnp.zeros_like(gv_acc)
    for b in (0, 1):
        block = ctx if b == 0 else BLOCKS - 1 - ctx
        rows = slice(b * BLOCK, (b + 1) * BLOCK)
        queries, grads, deltas = [], [], []
        for p in range(PAIRS):
            cols = slice(p * 128, (p + 1) * 128)
            queries.append(pair_rows(q_ref[rows, cols] * jnp.asarray(0.125, BF)))
            grad = g_ref[rows, cols]
            grads.append(pair_rows(grad))
            both = jnp.transpose(grad.astype(F32)) * turned_ref[cols, rows]
            deltas.append(
                jnp.concatenate(
                    [
                        jnp.sum(both[:HEAD_DIM], 0, keepdims=True),
                        jnp.sum(both[HEAD_DIM:], 0, keepdims=True),
                    ],
                    1,
                )
            )
        gq_acc[...] = jnp.zeros_like(gq_acc)

        def step(tile, masked):
            start = pl.multiple_of(tile * TILE, TILE)
            here = pl.ds(start, TILE)
            for p in range(PAIRS):
                cols = slice(p * 128, (p + 1) * 128)
                row = b * PAIRS + p
                keys = k_ref[here, cols]
                scores = contract(keys, queries[p], ((1,), (1,)))
                chances = jnp.exp(scores - log_ref[row : row + 1, :])
                if masked:
                    chances = jnp.where(allowed_at(tile, block), chances, 0.0)
                grad_chance = contract(v_ref[here, cols], grads[p], ((1,), (1,)))
                grad_score = (chances * (grad_chance - deltas[p])).astype(BF)
                gv_acc[here, cols] += contract(chances.astype(BF), grads[p], ((1,), (0,)))
                gk_acc[here, cols] += contract(grad_score, queries[p], ((1,), (0,)))
                gq_acc[p] += contract(keys, grad_score, ((0,), (0,)))

        step(block // 4, True)

        @pl.loop(0, block // 4)
        def _(tile):
            step(tile, False)

        for p in range(PAIRS):
            cols = slice(p * 128, (p + 1) * 128)
            done = gq_acc[p] * 0.125
            turned = jnp.concatenate([done[:HEAD_DIM, :BLOCK], done[HEAD_DIM:, BLOCK:]], 0)
            gq_ref[rows, cols] = jnp.transpose(turned)
    gk_ref[...] = gk_acc[...].astype(BF)
    gv_ref[...] = gv_acc[...].astype(BF)


def attend_backward(ctx, queries, keys, values, grad_mixed, turned, log_total):
    whole = jax.ShapeDtypeStruct((BLOCKS * BLOCK, HALF), BF)
    return pl.pallas_call(
        backward_kernel,
        out_shape=(jax.ShapeDtypeStruct((2 * BLOCK, HALF), F32), whole, whole),
        in_specs=[SM] + [VM] * 6,
        out_specs=(VM, VM, VM),
        scratch_shapes=[
            pltpu.VMEM((BLOCKS * BLOCK, HALF), F32),
            pltpu.VMEM((BLOCKS * BLOCK, HALF), F32),
            pltpu.VMEM((PAIRS, 128, 2 * BLOCK), F32),
        ],
        compiler_params=pltpu.CompilerParams(vmem_limit_bytes=48 * 2**20),
        cost_estimate=pl.CostEstimate(
            flops=10 * 33 * 128 * 128 * 6 * 128, bytes_accessed=16 * 2**20, transcendentals=33 * 128 * 128 * 6
        ),
        name="attend_backward",
    )(ctx, queries, keys, values, grad_mixed, turned, log_total)


def norm_parts(values):
    centre = jnp.mean(values, -1, keepdims=True)
    shifted = values - centre
    spread = jnp.mean(shifted * shifted, -1, keepdims=True)
    scale = lax.rsqrt(spread + epsilon)
    return shifted * scale, scale


def norm_input_grad(grad_norm, gain, unit, scale):
    e = grad_norm * gain
    return scale * (
        e - jnp.mean(e, -1, keepdims=True) - unit * jnp.mean(e * unit, -1, keepdims=True)
    )


def turn_tables(first_row, row_count):
    half_rot = ROTARY // 2
    positions = first_row + jnp.arange(row_count, dtype=jnp.int32)
    exponent = jnp.arange(half_rot, dtype=F32) * (2.0 / ROTARY)
    frequency = jnp.power(10000.0, -exponent)
    angle = positions.astype(F32)[:, None] * frequency[None, :]
    cosine, sine = jnp.cos(angle), jnp.sin(angle)
    rest = jnp.zeros((row_count, HEAD_DIM - ROTARY), F32)
    none = jnp.zeros_like(sine)
    keep = jnp.tile(jnp.concatenate([cosine, cosine, rest + 1.0], 1), (1, HEADS))
    low = jnp.tile(jnp.concatenate([-sine, none, rest], 1), (1, HEADS))
    high = jnp.tile(jnp.concatenate([none, sine, rest], 1), (1, HEADS))
    return keep, low, high


def rotate(values, tables):
    keep, low, high = tables
    shift = ROTARY // 2
    return values * keep + jnp.roll(values, -shift, 1) * low + jnp.roll(values, shift, 1) * high


def rotate_back(values, tables):
    keep, low, high = tables
    shift = ROTARY // 2
    return (
        values * keep + jnp.roll(values * low, shift, 1) + jnp.roll(values * high, -shift, 1)
    )


def dot(left, right):
    return jnp.dot(left, right, preferred_element_type=F32)


def phi_parts(values):
    cumulative = 0.5 * (1.0 + lax.erf(values * (2.0**-0.5)))
    density = jnp.exp(-0.5 * values * values) * (0.5 / jnp.pi) ** 0.5
    return cumulative, density


def shards(
    tokens,
    cotangent,
    ln1_gain,
    ln1_bias,
    ln2_gain,
    ln2_bias,
    qkv_weight,
    qkv_bias,
    out_weight,
    out_bias,
    up_weight,
    up_bias,
    down_weight,
    down_bias,
):
    row_count = tokens.shape[1]
    fsdp = lax.axis_index("fsdp")
    ctx = lax.axis_index("ctx")
    upper = ctx % 2 == 1
    ctx_word = ctx.astype(jnp.int32).reshape(1)
    tables = turn_tables(ctx * row_count, row_count)

    def mine(values):
        return jnp.where(upper, values[:, HALF:], values[:, :HALF])

    def theirs(values):
        return jnp.where(upper, values[:, :HALF], values[:, HALF:])

    def join(own, other):
        return jnp.where(
            upper, jnp.concatenate([other, own], 1), jnp.concatenate([own, other], 1)
        )

    vectors = (ln1_gain, ln1_bias, ln2_gain, ln2_bias, out_bias, down_bias, qkv_bias, up_bias)
    packed = jnp.concatenate([vector.reshape(-1) for vector in vectors])
    packed = jnp.pad(packed, (0, 16 * HALF - packed.shape[0])).reshape(16, HALF)
    first_weight, table = gather_first(qkv_weight, packed)
    table = table.reshape(4, 16 * HALF).astype(F32)
    full_vectors, start = [], 0
    for vector in vectors:
        width = vector.shape[1]
        piece = table[:, start : start + LAYERS * width].reshape(4, LAYERS, width)
        full_vectors.append(jnp.transpose(piece, (1, 0, 2)).reshape(LAYERS, 4 * width))
        start += LAYERS * width
    gain_one, bias_one, gain_two, bias_two, b_out, b_down, b_qkv, b_up = full_vectors

    qkv_full = [first_weight, None]
    gathered = [None] * LAYERS
    stream = tokens[0].astype(F32)
    saved = []
    for layer_index in range(LAYERS):
        w_qkv = qkv_full[layer_index]
        unit, scale = norm_parts(stream)
        norm_one = (unit * gain_one[layer_index] + bias_one[layer_index]).astype(BF)
        norm_two = (unit * gain_two[layer_index] + bias_two[layer_index]).astype(BF)
        joined = dot(norm_one, w_qkv) + b_qkv[layer_index]
        queries = rotate(joined[:, :D], tables).astype(BF)
        key_rows = rotate(joined[:, D : 2 * D], tables).astype(BF)
        value_rows = joined[:, 2 * D :].astype(BF)
        jobs = [(layer_index, out_weight), (layer_index, up_weight), (layer_index, down_weight)]
        if layer_index + 1 < LAYERS:
            jobs.append((layer_index + 1, qkv_weight))
        other_queries, keys, values, w_out, w_up, w_down, *more = gather_pair(
            "gather_pair_%d" % layer_index,
            1 + layer_index,
            (theirs(queries), theirs(key_rows), theirs(value_rows)),
            (mine(key_rows), mine(value_rows)),
            jobs,
        )
        if more:
            qkv_full[layer_index + 1] = more[0]
        gathered[layer_index] = (w_qkv, w_out, w_up, w_down)
        queries = jnp.concatenate([mine(queries), other_queries], 0)
        keys = keys.reshape(BLOCKS * BLOCK, HALF)
        values = values.reshape(BLOCKS * BLOCK, HALF)
        mixed_two, turned, log_total = attend_forward(ctx_word, queries, keys, values)
        mixed_low = join(mixed_two[:BLOCK], mirrored(mixed_two[BLOCK:]))
        hidden_pre = dot(norm_two, w_up) + b_up[layer_index]
        hidden_low = (hidden_pre * phi_parts(hidden_pre)[0]).astype(BF)
        mlp_branch = dot(hidden_low, w_down)
        blank = jnp.zeros((row_count, 64), BF)
        stacked = jnp.stack(
            [
                jnp.concatenate(
                    [
                        hidden_low[:, d * D : (d + 1) * D],
                        norm_one[:, d * 192 : (d + 1) * 192],
                        mixed_low[:, d * 192 : (d + 1) * 192],
                        norm_two[:, d * 192 : (d + 1) * 192],
                        blank,
                    ],
                    1,
                )
                for d in range(4)
            ],
            0,
        )
        saved.append((unit, scale, queries, keys, values, turned, log_total, hidden_pre, stacked))
        stream = (
            stream + dot(mixed_low, w_out) + b_out[layer_index] + mlp_branch + b_down[layer_index]
        )

    gradient = cotangent[0].astype(F32)
    waiting, low_rows, pre_rows, left_rows = (), [None] * 2, [None] * 2, [None] * 2
    joined_rows, norm_rows = [None] * 2, [None] * 2
    for layer_index in range(LAYERS - 1, -1, -1):
        w_qkv, w_out, w_up, w_down = gathered[layer_index]
        unit, scale, queries, keys, values, turned, log_total, hidden_pre, stacked = saved[
            layer_index
        ]
        grad_low = gradient.astype(BF)
        grad_mixed = contract(grad_low, w_out, ((1,), (1,))).astype(BF)
        grad_mixed = jnp.concatenate([mine(grad_mixed), mirrored(theirs(grad_mixed))], 0)
        cumulative, density = phi_parts(hidden_pre)
        grad_hidden = contract(grad_low, w_down, ((1,), (1,)))
        grad_pre = (grad_hidden * (cumulative + hidden_pre * density)).astype(BF)
        grad_norm_two = contract(grad_pre, w_up, ((1,), (1,)))
        grad_query, grad_keys, grad_values = attend_backward(
            ctx_word, queries, keys, values, grad_mixed, turned, log_total
        )
        whole = (BLOCKS, BLOCK, HALF)
        own_pair, back_pair, back_query, left, low, pre, *more = scatter_pair(
            "scatter_pair_%d" % layer_index,
            3 + layer_index,
            grad_keys.reshape(whole),
            grad_values.reshape(whole),
            grad_query[BLOCK:].astype(BF),
            stacked,
            (grad_low, grad_pre) + waiting,
        )
        left_rows[layer_index], low_rows[layer_index], pre_rows[layer_index] = left, low, pre
        if more:
            joined_rows[layer_index + 1], norm_rows[layer_index + 1] = more
        grad_query = join(grad_query[:BLOCK], back_query.astype(F32))
        grad_key = join(own_pair[0], back_pair[0].astype(F32))
        grad_value = join(own_pair[1], back_pair[1].astype(F32))
        grad_joined = jnp.concatenate(
            [rotate_back(grad_query, tables), rotate_back(grad_key, tables), grad_value], 1
        ).astype(BF)
        grad_norm_one = contract(grad_joined, w_qkv, ((1,), (1,)))
        norm_sums = jnp.stack(
            [
                jnp.sum(grad_norm_one * unit, 0),
                jnp.sum(grad_norm_one, 0),
                jnp.sum(grad_norm_two * unit, 0),
                jnp.sum(grad_norm_two, 0),
            ],
            0,
        )
        waiting = (grad_joined, jnp.pad(norm_sums, ((0, 12), (0, 0))).astype(BF))
        gradient = (
            gradient
            + norm_input_grad(grad_norm_one, gain_one[layer_index], unit, scale)
            + norm_input_grad(grad_norm_two, gain_two[layer_index], unit, scale)
        )
    joined_rows[0], norm_rows[0] = gather_late(*waiting)

    def own_part(vector, width):
        return lax.dynamic_slice_in_dim(vector, fsdp * width, width, vector.ndim - 1)

    packs, lines = [], []
    for layer_index in range(LAYERS):
        rows, sums = weight_grads(
            left_rows[layer_index],
            joined_rows[layer_index],
            low_rows[layer_index],
            pre_rows[layer_index],
        )
        packs.append(rows)
        sums = sums[0]
        norms = own_part(jnp.sum(norm_rows[layer_index].reshape(4, 16, D)[:, :4].astype(F32), 0), 192)
        lines += [
            jnp.pad(own_part(sums[:D], 192), (0, D - 192)),
            jnp.pad(own_part(sums[D : 4 * D], 576), (0, D - 576)),
            own_part(sums[4 * D :], D),
            norms.reshape(D),
        ]
    summed, small = sum_over_ctx(packs[0], packs[1], jnp.stack(lines, 0))
    grads = []
    for layer_index in range(LAYERS):
        rows = summed[layer_index].reshape(2304, D)
        line = small[4 * layer_index : 4 * layer_index + 4]
        norms = line[3].reshape(4, 192)
        grads.append(
            (
                norms[0],
                norms[1],
                norms[2],
                norms[3],
                jnp.concatenate([rows[i * 192 : (i + 1) * 192] for i in range(3)], 1),
                line[1, :576],
                rows[576:768],
                line[0, :192],
                jnp.concatenate([rows[768 + i * 192 : 960 + i * 192] for i in range(4)], 1),
                line[2],
                rows[1536:],
                line[0, :192],
            )
        )
    stacked = [
        jnp.stack([grads[layer_index][member] for layer_index in range(LAYERS)], 0).astype(F32)
        for member in range(12)
    ]
    return (stream.astype(BF)[None], gradient[None], *stacked)


def solution(mesh):
    matrix, vector = P(None, "fsdp", None), P(None, "fsdp")
    rows = P("fsdp", "ctx", None)
    params = (
        vector,
        vector,
        vector,
        vector,
        matrix,
        vector,
        matrix,
        vector,
        matrix,
        vector,
        matrix,
        vector,
    )
    return jax.shard_map(
        shards,
        mesh=mesh,
        in_specs=(rows, rows) + params,
        out_specs=(rows, rows) + params,
        check_vma=False,
    )
```

```python
import functools

import jax
import jax.numpy as jnp
from jax import lax
from jax.experimental import pallas as pl
from jax.experimental.pallas import tpu as pltpu
from jax.sharding import PartitionSpec as P

D = 768
HEADS = 12
HEAD_DIM = 64
FF = 3072
ROTARY = 16
LAYERS = 2
HALF = 384
BLOCK = 128
BLOCKS = 32
TILE = 512
PAIRS = 3

epsilon = 1e-05
masked_score = -1e30
MESH = pl.DeviceIdType.MESH
BF = jnp.bfloat16
F32 = jnp.float32


def mirrored(values):
    pairs = [(f * 32 + c, f * 32 + 31 - c) for f in range(4) for c in range(32)]
    return lax.ppermute(values, ("fsdp", "ctx"), pairs)


class Place:
    def __init__(self):
        self.fsdp = lax.axis_index("fsdp")
        self.ctx = lax.axis_index("ctx")
        self.y, self.z, self.h = self.ctx // 8, (self.ctx // 2) % 4, self.ctx % 2
        self.x_lo, self.core = self.fsdp // 2, self.fsdp % 2
        self.beside = (self.fsdp + 1 - 2 * self.core, self.ctx)
        self.mirror = (self.fsdp, BLOCKS - 1 - self.ctx)
        self.half = (self.fsdp, self.ctx + 1 - 2 * self.h)

    def along_x(self, step):
        x = (2 * self.h + self.x_lo + step) % 4
        return (2 * (x % 2) + self.core, self.y * 8 + self.z * 2 + x // 2)

    def ctx_at(self, dy, dz):
        return ((self.y + dy) % 4) * 8 + ((self.z + dz) % 4) * 2 + self.h

    def ring(self, t, da, db):
        return self.ctx_at(da, db) if t == 0 else self.ctx_at(db, da)

    def near(self, t, axis, sign):
        steps = (sign, 0) if axis == 0 else (0, sign)
        return (self.fsdp, self.ring(t, *steps))

    def around(self):
        return [self.near(0, axis, sign) for axis in (0, 1) for sign in (1, -1)]

    def greet(self, partners):
        barrier = pltpu.get_barrier_semaphore()
        for partner in partners:
            pl.semaphore_signal(barrier, inc=1, device_id=partner, device_id_type=MESH)
        pl.semaphore_wait(barrier, len(partners))


class Wire:
    def __init__(self, send_sem, recv_sem, local_sem=None):
        self.send_sem, self.recv_sem, self.local_sem = send_sem, recv_sem, local_sem
        self.sent, self.local, self.bounced = [], [], []

    def push(self, source, target, partner):
        number = len(self.sent)
        copy = pltpu.make_async_remote_copy(
            src_ref=source,
            dst_ref=target,
            send_sem=self.send_sem.at[number],
            recv_sem=self.recv_sem.at[number],
            device_id=partner,
            device_id_type=MESH,
        )
        copy.start()
        self.sent.append(copy)
        return copy

    def keep(self, source, target, bounce=None):
        if bounce is None:
            copy = pltpu.make_async_copy(source, target, self.local_sem.at[len(self.local)])
        else:
            copy = pltpu.make_async_copy(source, bounce, self.local_sem.at[len(self.local)])
            self.bounced.append((len(self.local), bounce, target))
        copy.start()
        self.local.append(copy)

    def flush(self):
        for number, bounce, target in self.bounced:
            self.local[number].wait()
            copy = pltpu.make_async_copy(bounce, target, self.local_sem.at[number])
            copy.start()
            self.local[number] = copy
        self.bounced = []

    def drain(self):
        for copy in self.sent:
            copy.wait_send()
        for copy in self.local:
            copy.wait()


def share_param(place, wire, source, target, bounce):
    rows = source.shape[0]
    cut = rows // 2
    mine, far = place.fsdp * rows, ((place.fsdp + 2) % 4) * rows
    parts = [(0, cut, 1), (cut, cut, 3)]
    across = [
        wire.push(
            source.at[pl.ds(start, count)],
            target.at[pl.ds(mine + start, count)],
            place.along_x(step),
        )
        for start, count, step in parts
    ]
    beside = wire.push(source, target.at[pl.ds(mine, rows)], place.beside)
    wire.keep(source, target.at[pl.ds(mine, rows)], bounce)
    last = [beside]

    def onward(copy, start, count):
        copy.wait_recv()
        spot = target.at[pl.ds(far + start, count)]
        last.append(wire.push(spot, spot, place.beside))

    steps = [
        functools.partial(onward, copy, start, count)
        for copy, (start, count, _) in zip(across, parts)
    ]
    return steps, last


def share_rows(place, wire, source, target):
    rows = source.shape[0]
    cut = rows // 2
    parts = [(0, cut, 1), (cut, cut, 3)] if rows % 32 == 0 else [(0, rows, 1)]
    across = [
        wire.push(
            source.at[pl.ds(start, count)],
            target.at[pl.ds(2 * rows + start, count)],
            place.along_x(step),
        )
        for start, count, step in parts
    ]
    last = [wire.push(source, target.at[pl.ds(rows, rows)], place.beside)]
    wire.keep(source, target.at[pl.ds(0, rows)])

    def onward(copy, start, count):
        copy.wait_recv()
        last.append(
            wire.push(
                target.at[pl.ds(2 * rows + start, count)],
                target.at[pl.ds(3 * rows + start, count)],
                place.beside,
            )
        )

    steps = [
        functools.partial(onward, copy, start, count)
        for copy, (start, count, _) in zip(across, parts)
    ]
    return steps, last


def share_columns(place, wire, source, target, stage):
    rows = source.shape[0]
    cut = rows // 2
    fsdp, core = place.fsdp, place.core
    parts = [(0, cut, 1), (cut, cut, 3)]

    def panel(start, count, shard):
        return source.at[pl.ds(start, count), pl.ds(pl.multiple_of(shard * D, D), D)]

    passing, last = [], []
    for start, count, step in parts:
        passing.append(
            wire.push(
                panel(start, count, 3 - fsdp),
                stage.at[pl.ds(start, count)],
                place.along_x(step),
            )
        )
    for start, count, step in parts:
        last.append(
            wire.push(
                panel(start, count, (fsdp + 2) % 4),
                target.at[pl.ds(2 * rows + start, count)],
                place.along_x(step),
            )
        )
    last.append(
        wire.push(
            panel(0, rows, fsdp + 1 - 2 * core), target.at[pl.ds(rows, rows)], place.beside
        )
    )
    wire.keep(panel(0, rows, fsdp), target.at[pl.ds(0, rows)])

    def onward(copy, start, count):
        copy.wait_recv()
        last.append(
            wire.push(
                stage.at[pl.ds(start, count)],
                target.at[pl.ds(3 * rows + start, count)],
                place.beside,
            )
        )

    steps = [
        functools.partial(onward, copy, start, count)
        for copy, (start, count, _) in zip(passing, parts)
    ]
    return steps, last


def spread(place, wire, own, spot, ready, between=()):
    between = list(between)
    arrivals = {}

    def push(t, da, db, b, axis, sign):
        target = spot(t, place.ring(t, da, db), b)
        source = own(t, b) if da == 0 and db == 0 else target
        sa, sb = (sign, 0) if axis == 0 else (0, sign)
        arrivals[t, (da - sa) % 4, (db - sb) % 4, b] = wire.push(
            source, target, place.near(t, axis, sign)
        )

    def landed(t, da, db):
        for b in (0, 1):
            arrivals[t, da, db, b].wait_recv()

    def pause():
        if between:
            between.pop(0)()

    for b in (0, 1):
        for t in (0, 1):
            ready(t, b)
            for axis in (0, 1):
                for sign in (1, -1):
                    push(t, 0, 0, b, axis, sign)
    for da, keep, onward in ((1, 0, -1), (3, 1, 1)):
        for t in (0, 1):
            landed(t, da, 0)
            push(t, da, 0, keep, 0, onward)
            for sign in (1, -1):
                for b in (0, 1):
                    push(t, da, 0, b, 1, sign)
    for db, keep, onward in ((1, 0, -1), (3, 1, 1)):
        for t in (0, 1):
            landed(t, 0, db)
            push(t, 0, db, keep, 1, onward)
    for t in (0, 1):
        landed(t, 2, 0)
        for sign in (1, -1):
            for b in (0, 1):
                push(t, 2, 0, b, 1, sign)
    pause()
    for da in (1, 3, 2):
        for db, keep, onward in ((1, 0, -1), (3, 1, 1)):
            for t in (0, 1):
                landed(t, da, db)
                push(t, da, db, keep, 1, onward)
            pause()
    while between:
        pause()
    for da in (0, 1, 3, 2):
        for t in (0, 1):
            landed(t, da, 2)


ANY = pl.BlockSpec(memory_space=pl.ANY)
VM = pl.BlockSpec(memory_space=pltpu.VMEM)
SM = pl.BlockSpec(memory_space=pltpu.SMEM)


def room(*shape):
    return pltpu.VMEM(shape, BF)


def sems(count, local):
    return [
        pltpu.SemaphoreType.DMA((count,)),
        pltpu.SemaphoreType.DMA((count,)),
        pltpu.SemaphoreType.DMA((local,)),
    ]


def full_shape(shard):
    return jax.ShapeDtypeStruct((4 * shard.shape[-2], shard.shape[-1]), BF)


def first_kernel(weight_ref, vector_ref, weight_out, vector_out, bounce, *sem):
    place, wire = Place(), Wire(*sem)
    place.greet([place.beside, place.along_x(1), place.along_x(3)])
    far = vector_out.at[(place.fsdp + 2) % 4]
    across = wire.push(vector_ref, vector_out.at[place.fsdp], place.along_x(1))
    last = [wire.push(vector_ref, vector_out.at[place.fsdp], place.beside)]
    wire.keep(vector_ref, vector_out.at[place.fsdp])
    steps, ends = share_param(place, wire, weight_ref.at[0], weight_out, bounce)
    wire.flush()
    across.wait_recv()
    last.append(wire.push(far, far, place.beside))
    for step in steps:
        step()
    for copy in last + ends:
        copy.wait_recv()
    wire.drain()


def gather_first(weight, vectors):
    return pl.pallas_call(
        first_kernel,
        out_shape=(full_shape(weight), jax.ShapeDtypeStruct((4,) + vectors.shape, F32)),
        in_specs=[ANY, VM],
        out_specs=(ANY, ANY),
        scratch_shapes=[room(*weight.shape[1:])] + sems(16, 4),
        compiler_params=pltpu.CompilerParams(
            collective_id=0, has_side_effects=True, vmem_limit_bytes=16 * 2**20
        ),
        name="gather_first",
    )(weight, vectors)


def gather_kernel(jobs, q_ref, k_ref, v_ref, k_own, v_own, *refs):
    count = len(jobs)
    weights, refs = refs[:count], refs[count:]
    q_out, k_out, v_out = refs[:3]
    weights_out, refs = refs[3 : 3 + count], refs[3 + count :]
    bounces, refs = refs[:count], refs[count:]
    place, wire = Place(), Wire(*refs)
    place.greet(
        place.around() + [place.mirror, place.beside, place.along_x(1), place.along_x(3)]
    )
    ins, outs = (k_own, v_own), (k_out, v_out)
    ctx = place.ctx
    swapped = [
        wire.push(source, out.at[ctx], place.mirror) for source, out in zip((k_ref, v_ref), outs)
    ]
    swapped.append(wire.push(q_ref, q_out, place.mirror))
    for t in (0, 1):
        wire.keep(ins[t], outs[t].at[ctx])
    work = []

    def ready(t, b):
        if b == 1:
            if t == 0:
                for layer, weight, target, bounce in zip(jobs, weights, weights_out, bounces):
                    work.append(share_param(place, wire, weight.at[layer], target, bounce))
            swapped[t].wait_recv()

    def spot(t, origin, b):
        return outs[t].at[origin if b == 0 else BLOCKS - 1 - origin]

    def own(t, b):
        return ins[t] if b == 0 else spot(t, ctx, 1)

    def onward(number):
        for steps, _ in work:
            for step in steps[number : number + 1]:
                step()

    spread(
        place,
        wire,
        own,
        spot,
        ready,
        [wire.flush]
        + [lambda: None] * 3
        + [functools.partial(onward, 0), functools.partial(onward, 1)],
    )
    swapped[2].wait_recv()
    for _, last in work:
        for copy in last:
            copy.wait_recv()
    wire.drain()


def gather_pair(name, number, away, own, jobs):
    layers = [layer for layer, _ in jobs]
    weights = [weight for _, weight in jobs]
    whole = jax.ShapeDtypeStruct((BLOCKS, BLOCK, HALF), BF)
    return pl.pallas_call(
        functools.partial(gather_kernel, layers),
        out_shape=(jax.ShapeDtypeStruct((BLOCK, HALF), BF), whole, whole)
        + tuple(full_shape(weight) for weight in weights),
        in_specs=[VM] * 5 + [ANY] * len(jobs),
        out_specs=(ANY,) * (3 + len(jobs)),
        scratch_shapes=[room(*weight.shape[1:]) for weight in weights] + sems(96, 8),
        compiler_params=pltpu.CompilerParams(
            collective_id=number, has_side_effects=True, vmem_limit_bytes=24 * 2**20
        ),
        name=name,
    )(*away, *own, *weights)


def scatter_kernel(count, gk_ref, gv_ref, gq_ref, hidden_ref, *refs):
    sources, refs = refs[:count], refs[count:]
    own_out, back_out, back_q, hidden_out = refs[:4]
    targets, refs = refs[4 : 4 + count], refs[4 + count :]
    far, near, mix, total, last_far, last_near, last_mix, leave, stage = refs[:9]
    place, wire = Place(), Wire(*refs[9:])
    place.greet(
        place.around() + [place.mirror, place.beside, place.along_x(1), place.along_x(3)]
    )
    ins = (gk_ref, gv_ref)

    def block_at(t, da, db, b):
        origin = place.ring(t, da, db)
        return origin if b == 0 else BLOCKS - 1 - origin

    order = (2, 1, 3, 0)
    first, second = {}, {}
    for da in order:
        for t in (0, 1):
            first[t, da] = [
                wire.push(
                    ins[t].at[block_at(t, da, 2, b)], far.at[t, da, b], place.near(t, 1, sign)
                )
                for b, sign in ((0, 1), (1, -1))
            ]
    swapped = [wire.push(gq_ref, back_q, place.mirror)]
    work = [share_columns(place, wire, hidden_ref, hidden_out, stage)]
    for source, target in zip(sources, targets):
        work.append(share_rows(place, wire, source, target))
    for da in order:
        for t in (0, 1):
            copies = []
            for b, sign, db in ((0, 1, 1), (1, -1, 3)):
                copies.append(
                    wire.push(
                        ins[t].at[block_at(t, da, db, 1 - b)],
                        near.at[t, da, b, 1 - b],
                        place.near(t, 1, sign),
                    )
                )
                first[t, da][b].wait_recv()
                mix[t, da, b] = (
                    ins[t][block_at(t, da, db, b)].astype(F32) + far[t, da, b].astype(F32)
                ).astype(BF)
                copies.append(
                    wire.push(mix.at[t, da, b], near.at[t, da, b, b], place.near(t, 1, sign))
                )
            second[t, da] = copies

    def settle(t, da):
        for copy in second[t, da]:
            copy.wait_recv()
        for b in (0, 1):
            total[t, da, b] = (
                ins[t][block_at(t, da, 0, b)].astype(F32)
                + near[t, da, 0, b].astype(F32)
                + near[t, da, 1, b].astype(F32)
            ).astype(BF)

    third, fourth = {}, {}
    for t in (0, 1):
        settle(t, 2)
        third[t] = [
            wire.push(total.at[t, 2, b], last_far.at[t, b], place.near(t, 0, sign))
            for b, sign in ((0, 1), (1, -1))
        ]
    for t in (0, 1):
        fourth[t] = []
        for b, sign, da in ((0, 1, 1), (1, -1, 3)):
            settle(t, da)
            fourth[t].append(
                wire.push(
                    total.at[t, da, 1 - b], last_near.at[t, b, 1 - b], place.near(t, 0, sign)
                )
            )
    for t in (0, 1):
        for b, sign, da in ((0, 1, 1), (1, -1, 3)):
            third[t][b].wait_recv()
            last_mix[t, b] = (total[t, da, b].astype(F32) + last_far[t, b].astype(F32)).astype(BF)
            fourth[t].append(
                wire.push(last_mix.at[t, b], last_near.at[t, b, b], place.near(t, 0, sign))
            )
    for t in (0, 1):
        settle(t, 0)
    for steps, _ in work:
        for step in steps:
            step()
    for t in (0, 1):
        for copy in fourth[t]:
            copy.wait_recv()
        for b in (1, 0):
            done = (
                total[t, 0, b].astype(F32)
                + last_near[t, 0, b].astype(F32)
                + last_near[t, 1, b].astype(F32)
            )
            if b == 1:
                leave[t] = done.astype(BF)
                swapped.append(wire.push(leave.at[t], back_out.at[t], place.mirror))
            else:
                own_out[t] = done
    for _, last in work:
        for copy in last:
            copy.wait_recv()
    for copy in swapped:
        copy.wait_recv()
    wire.drain()


def rows_shape(source):
    return jax.ShapeDtypeStruct((4 * source.shape[0], source.shape[1]), BF)


def scatter_pair(name, number, grad_keys, grad_values, away, hidden, sources):
    return pl.pallas_call(
        functools.partial(scatter_kernel, len(sources)),
        out_shape=(
            jax.ShapeDtypeStruct((2, BLOCK, HALF), F32),
            jax.ShapeDtypeStruct((2, BLOCK, HALF), BF),
            jax.ShapeDtypeStruct((BLOCK, HALF), BF),
            jax.ShapeDtypeStruct((4 * BLOCK, D), BF),
        )
        + tuple(rows_shape(source) for source in sources),
        in_specs=[VM] * (4 + len(sources)),
        out_specs=(VM,) + (ANY,) * (3 + len(sources)),
        scratch_shapes=[
            room(2, 4, 2, BLOCK, HALF),
            room(2, 4, 2, 2, BLOCK, HALF),
            room(2, 4, 2, BLOCK, HALF),
            room(2, 4, 2, BLOCK, HALF),
            room(2, 2, BLOCK, HALF),
            room(2, 2, 2, BLOCK, HALF),
            room(2, 2, BLOCK, HALF),
            room(2, BLOCK, HALF),
            room(BLOCK, D),
        ]
        + sems(128, 12),
        compiler_params=pltpu.CompilerParams(
            collective_id=number, has_side_effects=True, vmem_limit_bytes=44 * 2**20
        ),
        name=name,
    )(grad_keys, grad_values, away, hidden, *sources)


def late_kernel(one_ref, two_ref, one_out, two_out, *sem):
    place, wire = Place(), Wire(*sem)
    place.greet([place.beside, place.along_x(1), place.along_x(3)])
    work = [
        share_rows(place, wire, one_ref, one_out),
        share_rows(place, wire, two_ref, two_out),
    ]
    for steps, _ in work:
        for step in steps:
            step()
    for _, last in work:
        for copy in last:
            copy.wait_recv()
    wire.drain()


def gather_late(one, two):
    return pl.pallas_call(
        late_kernel,
        out_shape=(rows_shape(one), rows_shape(two)),
        in_specs=[VM] * 2,
        out_specs=(ANY,) * 2,
        scratch_shapes=sems(16, 4),
        compiler_params=pltpu.CompilerParams(collective_id=5, has_side_effects=True),
        name="gather_late",
    )(one, two)


PIECE = 144
CUT = 80


def sum_kernel(
    one_ref, two_ref, small_one, small_two, out_ref, small_out,
    far, mix, near, total, far_two, mix_two, near_two, part, other, final, small, heard, *sem,
):
    place, wire = Place(), Wire(*sem)
    y, z, h = place.y, place.z, place.h
    turns = [
        (place.fsdp, (y + 1 - 2 * (y % 2)) * 8 + z * 2 + h),
        (place.fsdp, ((y + 2) % 4) * 8 + z * 2 + h),
        (place.fsdp, y * 8 + (z + 1 - 2 * (z % 2)) * 2 + h),
        (place.fsdp, y * 8 + ((z + 2) % 4) * 2 + h),
        place.half,
    ]
    place.greet(place.around() + [turns[1], turns[3], place.half])
    ins = (one_ref, two_ref)
    parts = {0: pl.ds(0, CUT), 1: pl.ds(CUT, PIECE - CUT)}

    def chunk(t, da, db):
        origin = place.ring(t, da, db)
        return origin // 2

    def plus(*terms):
        result = terms[0].astype(F32)
        for term in terms[1:]:
            result = result + term.astype(F32)
        return result.astype(BF)

    small[0] = small_one[...]
    small[1] = small_two[...]
    passing = wire.push(small, heard.at[0], turns[0])
    order = (2, 1, 3, 0)
    way = {2: 1, 1: 1, 3: -1, 0: -1}
    first, second, loose = {}, {}, {}
    for db in order:
        for t in (0, 1):
            first[t, db] = wire.push(
                ins[t].at[chunk(t, 2, db)], far.at[t, db], place.near(t, 0, way[db])
            )
    for db in order:
        for t in (0, 1):
            loose[t, db] = wire.push(
                ins[t].at[chunk(t, -way[db], db)], near.at[t, db, 1], place.near(t, 0, -way[db])
            )
    for db in order:
        for t in (0, 1):
            first[t, db].wait_recv()
            mix[t, db] = plus(ins[t][chunk(t, way[db], db)], far[t, db])
            second[t, db] = wire.push(mix.at[t, db], near.at[t, db, 0], place.near(t, 0, way[db]))

    def hear(step):
        wire.sent[step_numbers[-1]].wait_send()
        wire.sent[step_numbers[-1]].wait_recv()
        small[...] += heard[step]
        waited.add(step_numbers[-1])
        if step < 4:
            step_numbers.append(len(wire.sent))
            wire.push(small, heard.at[step + 1], turns[step + 1])

    step_numbers, waited = [0], set()

    def settle(t, db):
        second[t, db].wait_recv()
        loose[t, db].wait_recv()
        total[t, db] = plus(ins[t][chunk(t, 0, db)], near[t, db, 0], near[t, db, 1])

    third, fourth = {}, {}
    for t in (0, 1):
        settle(t, 2)
        third[t] = [
            wire.push(
                total.at[t, 2, parts[b]], far_two.at[t, parts[b]], place.near(t, 1, sign)
            )
            for b, sign in ((0, 1), (1, -1))
        ]
    hear(0)
    for t in (0, 1):
        fourth[t] = []
        for b, sign, db in ((0, 1, 1), (1, -1, 3)):
            settle(t, db)
            fourth[t].append(
                wire.push(
                    total.at[t, db, parts[1 - b]],
                    near_two.at[t, b, parts[1 - b]],
                    place.near(t, 1, sign),
                )
            )
    hear(1)
    for t in (0, 1):
        for b, sign, db in ((0, 1, 1), (1, -1, 3)):
            third[t][b].wait_recv()
            mix_two[t, parts[b]] = plus(total[t, db, parts[b]], far_two[t, parts[b]])
            fourth[t].append(
                wire.push(
                    mix_two.at[t, parts[b]], near_two.at[t, b, parts[b]], place.near(t, 1, sign)
                )
            )
    hear(2)
    swapped = []
    for t in (0, 1):
        settle(t, 0)
        for copy in fourth[t]:
            copy.wait_recv()
        part[t] = plus(total[t, 0], near_two[t, 0], near_two[t, 1])
        swapped.append(wire.push(part.at[t], other.at[t], place.half))
    hear(3)

    def spot(t, origin, b):
        return out_ref.at[1 - t, origin // 2, parts[b]]

    def own(t, b):
        return final.at[1 - t, parts[b]]

    def ready(t, b):
        if b == 0:
            swapped[1 - t].wait_recv()
            final[1 - t] = plus(part[1 - t], other[1 - t])
            wire.keep(final.at[1 - t], out_ref.at[1 - t, place.ctx // 2])

    spread(place, wire, own, spot, ready)
    hear(4)
    small_out[...] = small[...]
    for number, copy in enumerate(wire.sent):
        if number not in waited:
            copy.wait_send()
    for copy in wire.local:
        copy.wait()


def sum_over_ctx(one, two, small_one, small_two):
    shape = (16, PIECE, D)
    small_shape = (2,) + small_one.shape
    return pl.pallas_call(
        sum_kernel,
        out_shape=(
            jax.ShapeDtypeStruct((2,) + shape, BF),
            jax.ShapeDtypeStruct(small_shape, F32),
        ),
        in_specs=[VM] * 4,
        out_specs=(ANY, VM),
        scratch_shapes=[
            room(2, 4, PIECE, D),
            room(2, 4, PIECE, D),
            room(2, 4, 2, PIECE, D),
            room(2, 4, PIECE, D),
            room(2, PIECE, D),
            room(2, PIECE, D),
            room(2, 2, PIECE, D),
            room(2, PIECE, D),
            room(2, PIECE, D),
            room(2, PIECE, D),
            pltpu.VMEM(small_shape, F32),
            pltpu.VMEM((5,) + small_shape, F32),
        ]
        + sems(128, 4),
        compiler_params=pltpu.CompilerParams(
            collective_id=6, has_side_effects=True, vmem_limit_bytes=48 * 2**20
        ),
        name="sum_over_ctx",
    )(one.reshape(shape), two.reshape(shape), small_one, small_two)


def weight_kernel(
    fsdp_ref, one_ref, mixed_ref, two_ref, hidden_ref, joined_ref, low_ref, pre_ref, norm_ref,
    rows_ref, sums_ref, turned, turned_hidden,
):
    start = pl.multiple_of(fsdp_ref[0] * 192, 64)
    lefts = []
    for i, ref in enumerate((one_ref, mixed_ref, two_ref)):
        turned[i] = jnp.transpose(ref[...])
        lefts.append(turned[i, pl.ds(start, 192), :])
    turned_hidden[...] = jnp.transpose(hidden_ref[...])
    ones = jnp.ones((8, low_ref.shape[0]), BF)

    def panel(first, left, right, line):
        rows = left.shape[0]
        rows_ref[first : first + rows, :] = contract(left, right, ((1,), (0,))).astype(BF)
        if line is not None:
            sums_ref[line : line + 1, :] = contract(ones, right, ((1,), (0,)))[:1]

    low = low_ref[...]
    panel(1536, turned_hidden[...], low, None)
    panel(576, lefts[1], low, 0)
    for i in range(3):
        panel(i * 192, lefts[0], joined_ref[:, i * D : (i + 1) * D], 1 + i)
    for i in range(4):
        panel(768 + i * 192, lefts[2], pre_ref[:, i * D : (i + 1) * D], 4 + i)
    norms = norm_ref[0:16, :].astype(F32)
    for i in range(1, 4):
        norms = norms + norm_ref[i * 16 : (i + 1) * 16, :].astype(F32)
    sums_ref[8:16, :] = norms[:8]


def weight_grads(fsdp, one, mixed, two, hidden, joined, low, pre, norms):
    tokens = one.shape[0]
    return pl.pallas_call(
        weight_kernel,
        out_shape=(
            jax.ShapeDtypeStruct((2304, D), BF),
            jax.ShapeDtypeStruct((16, D), F32),
        ),
        in_specs=[SM] + [VM] * 8,
        out_specs=(VM, VM),
        scratch_shapes=[room(3, D, tokens), room(D, tokens)],
        compiler_params=pltpu.CompilerParams(vmem_limit_bytes=40 * 2**20),
        cost_estimate=pl.CostEstimate(
            flops=2 * 512 * 1769472, bytes_accessed=12 * 2**20, transcendentals=0
        ),
        name="weight_grads",
    )(fsdp, one, mixed, two, hidden, joined, low, pre, norms)


def pair_rows(values):
    lane = lax.broadcasted_iota(jnp.int32, values.shape, 1)
    zero = jnp.zeros_like(values)
    return jnp.concatenate(
        [jnp.where(lane < HEAD_DIM, values, zero), jnp.where(lane >= HEAD_DIM, values, zero)], 0
    )


def contract(left, right, dims):
    return lax.dot_general(left, right, (dims, ((), ())), preferred_element_type=F32)


def allowed_at(tile, block):
    key = tile * TILE + lax.broadcasted_iota(jnp.int32, (TILE, 2 * BLOCK), 0)
    query = block * BLOCK + lax.broadcasted_iota(jnp.int32, (TILE, 2 * BLOCK), 1) % BLOCK
    return key <= query


def forward_kernel(ctx_ref, q_ref, k_ref, v_ref, mixed_ref, turned_ref, log_ref, top, mass, acc):
    ctx = ctx_ref[0]
    for b in (0, 1):
        block = ctx if b == 0 else BLOCKS - 1 - ctx
        rows = slice(b * BLOCK, (b + 1) * BLOCK)
        queries = [
            pair_rows(q_ref[rows, p * 128 : (p + 1) * 128] * jnp.asarray(0.125, BF))
            for p in range(PAIRS)
        ]

        def step(tile, masked):
            start = pl.multiple_of(tile * TILE, TILE)
            for p in range(PAIRS):
                cols = slice(p * 128, (p + 1) * 128)
                scores = contract(k_ref[pl.ds(start, TILE), cols], queries[p], ((1,), (1,)))
                if masked:
                    scores = jnp.where(allowed_at(tile, block), scores, masked_score)
                    new_top = jnp.max(scores, 0, keepdims=True)
                else:
                    old_top = top[p : p + 1, :]
                    new_top = jnp.maximum(old_top, jnp.max(scores, 0, keepdims=True))
                weights = jnp.exp(scores - new_top)
                fresh_mass = jnp.sum(weights, 0, keepdims=True)
                fresh = contract(
                    v_ref[pl.ds(start, TILE), cols], weights.astype(BF), ((0,), (0,))
                )
                if not masked:
                    fade = jnp.exp(old_top - new_top)
                    fresh_mass = fresh_mass + mass[p : p + 1, :] * fade
                    fresh = fresh + acc[p] * fade
                top[p : p + 1, :] = new_top
                mass[p : p + 1, :] = fresh_mass
                acc[p] = fresh

        step(block // 4, True)

        @pl.loop(0, block // 4)
        def _(tile):
            step(tile, False)

        for p in range(PAIRS):
            cols = slice(p * 128, (p + 1) * 128)
            done = acc[p] / mass[p : p + 1, :]
            turned = jnp.concatenate([done[:HEAD_DIM, :BLOCK], done[HEAD_DIM:, BLOCK:]], 0)
            turned_ref[cols, rows] = turned
            mixed_ref[rows, cols] = jnp.transpose(turned).astype(BF)
            row = b * PAIRS + p
            log_ref[row : row + 1, :] = top[p : p + 1, :] + jnp.log(mass[p : p + 1, :])


def attend_forward(ctx, queries, keys, values):
    return pl.pallas_call(
        forward_kernel,
        out_shape=(
            jax.ShapeDtypeStruct((2 * BLOCK, HALF), BF),
            jax.ShapeDtypeStruct((HALF, 2 * BLOCK), F32),
            jax.ShapeDtypeStruct((8, 2 * BLOCK), F32),
        ),
        in_specs=[SM, VM, VM, VM],
        out_specs=(VM, VM, VM),
        scratch_shapes=[
            pltpu.VMEM((8, 2 * BLOCK), F32),
            pltpu.VMEM((8, 2 * BLOCK), F32),
            pltpu.VMEM((PAIRS, 128, 2 * BLOCK), F32),
        ],
        compiler_params=pltpu.CompilerParams(vmem_limit_bytes=40 * 2**20),
        cost_estimate=pl.CostEstimate(
            flops=4 * 33 * 128 * 128 * 6 * 128, bytes_accessed=8 * 2**20, transcendentals=33 * 128 * 128 * 6
        ),
        name="attend_forward",
    )(ctx, queries, keys, values)


def backward_kernel(
    ctx_ref, q_ref, k_ref, v_ref, g_ref, turned_ref, log_ref, gq_ref, gk_ref, gv_ref, gk_acc, gv_acc, gq_acc
):
    ctx = ctx_ref[0]
    gk_acc[...] = jnp.zeros_like(gk_acc)
    gv_acc[...] = jnp.zeros_like(gv_acc)
    for b in (0, 1):
        block = ctx if b == 0 else BLOCKS - 1 - ctx
        rows = slice(b * BLOCK, (b + 1) * BLOCK)
        queries, grads, deltas = [], [], []
        for p in range(PAIRS):
            cols = slice(p * 128, (p + 1) * 128)
            queries.append(pair_rows(q_ref[rows, cols] * jnp.asarray(0.125, BF)))
            grad = g_ref[rows, cols]
            grads.append(pair_rows(grad))
            both = jnp.transpose(grad.astype(F32)) * turned_ref[cols, rows]
            deltas.append(
                jnp.concatenate(
                    [
                        jnp.sum(both[:HEAD_DIM], 0, keepdims=True),
                        jnp.sum(both[HEAD_DIM:], 0, keepdims=True),
                    ],
                    1,
                )
            )
        gq_acc[...] = jnp.zeros_like(gq_acc)

        def step(tile, masked):
            start = pl.multiple_of(tile * TILE, TILE)
            here = pl.ds(start, TILE)
            for p in range(PAIRS):
                cols = slice(p * 128, (p + 1) * 128)
                row = b * PAIRS + p
                keys = k_ref[here, cols]
                scores = contract(keys, queries[p], ((1,), (1,)))
                chances = jnp.exp(scores - log_ref[row : row + 1, :])
                if masked:
                    chances = jnp.where(allowed_at(tile, block), chances, 0.0)
                grad_chance = contract(v_ref[here, cols], grads[p], ((1,), (1,)))
                grad_score = (chances * (grad_chance - deltas[p])).astype(BF)
                gv_acc[here, cols] += contract(chances.astype(BF), grads[p], ((1,), (0,)))
                gk_acc[here, cols] += contract(grad_score, queries[p], ((1,), (0,)))
                gq_acc[p] += contract(keys, grad_score, ((0,), (0,)))

        step(block // 4, True)

        @pl.loop(0, block // 4)
        def _(tile):
            step(tile, False)

        for p in range(PAIRS):
            cols = slice(p * 128, (p + 1) * 128)
            done = gq_acc[p] * 0.125
            turned = jnp.concatenate([done[:HEAD_DIM, :BLOCK], done[HEAD_DIM:, BLOCK:]], 0)
            gq_ref[rows, cols] = jnp.transpose(turned)
    gk_ref[...] = gk_acc[...].astype(BF)
    gv_ref[...] = gv_acc[...].astype(BF)


def attend_backward(ctx, queries, keys, values, grad_mixed, turned, log_total):
    whole = jax.ShapeDtypeStruct((BLOCKS * BLOCK, HALF), BF)
    return pl.pallas_call(
        backward_kernel,
        out_shape=(jax.ShapeDtypeStruct((2 * BLOCK, HALF), F32), whole, whole),
        in_specs=[SM] + [VM] * 6,
        out_specs=(VM, VM, VM),
        scratch_shapes=[
            pltpu.VMEM((BLOCKS * BLOCK, HALF), F32),
            pltpu.VMEM((BLOCKS * BLOCK, HALF), F32),
            pltpu.VMEM((PAIRS, 128, 2 * BLOCK), F32),
        ],
        compiler_params=pltpu.CompilerParams(vmem_limit_bytes=48 * 2**20),
        cost_estimate=pl.CostEstimate(
            flops=10 * 33 * 128 * 128 * 6 * 128, bytes_accessed=16 * 2**20, transcendentals=33 * 128 * 128 * 6
        ),
        name="attend_backward",
    )(ctx, queries, keys, values, grad_mixed, turned, log_total)


def norm_parts(values):
    centre = jnp.mean(values, -1, keepdims=True)
    shifted = values - centre
    spread = jnp.mean(shifted * shifted, -1, keepdims=True)
    scale = lax.rsqrt(spread + epsilon)
    return shifted * scale, scale


def norm_input_grad(grad_norm, gain, unit, scale):
    e = grad_norm * gain
    return scale * (
        e - jnp.mean(e, -1, keepdims=True) - unit * jnp.mean(e * unit, -1, keepdims=True)
    )


def turn_tables(first_row, row_count):
    half_rot = ROTARY // 2
    positions = first_row + jnp.arange(row_count, dtype=jnp.int32)
    exponent = jnp.arange(half_rot, dtype=F32) * (2.0 / ROTARY)
    frequency = jnp.power(10000.0, -exponent)
    angle = positions.astype(F32)[:, None] * frequency[None, :]
    cosine, sine = jnp.cos(angle), jnp.sin(angle)
    rest = jnp.zeros((row_count, HEAD_DIM - ROTARY), F32)
    none = jnp.zeros_like(sine)
    keep = jnp.tile(jnp.concatenate([cosine, cosine, rest + 1.0], 1), (1, HEADS))
    low = jnp.tile(jnp.concatenate([-sine, none, rest], 1), (1, HEADS))
    high = jnp.tile(jnp.concatenate([none, sine, rest], 1), (1, HEADS))
    return keep, low, high


def rotate(values, tables):
    keep, low, high = tables
    shift = ROTARY // 2
    return values * keep + jnp.roll(values, -shift, 1) * low + jnp.roll(values, shift, 1) * high


def rotate_back(values, tables):
    keep, low, high = tables
    shift = ROTARY // 2
    return (
        values * keep + jnp.roll(values * low, shift, 1) + jnp.roll(values * high, -shift, 1)
    )


def dot(left, right):
    return jnp.dot(left, right, preferred_element_type=F32)


def phi_parts(values):
    cumulative = 0.5 * (1.0 + lax.erf(values * (2.0**-0.5)))
    density = jnp.exp(-0.5 * values * values) * (0.5 / jnp.pi) ** 0.5
    return cumulative, density


def shards(
    tokens,
    cotangent,
    ln1_gain,
    ln1_bias,
    ln2_gain,
    ln2_bias,
    qkv_weight,
    qkv_bias,
    out_weight,
    out_bias,
    up_weight,
    up_bias,
    down_weight,
    down_bias,
):
    row_count = tokens.shape[1]
    fsdp = lax.axis_index("fsdp")
    ctx = lax.axis_index("ctx")
    upper = ctx % 2 == 1
    ctx_word = ctx.astype(jnp.int32).reshape(1)
    tables = turn_tables(ctx * row_count, row_count)

    def mine(values):
        return jnp.where(upper, values[:, HALF:], values[:, :HALF])

    def theirs(values):
        return jnp.where(upper, values[:, :HALF], values[:, HALF:])

    def join(own, other):
        return jnp.where(
            upper, jnp.concatenate([other, own], 1), jnp.concatenate([own, other], 1)
        )

    vectors = (ln1_gain, ln1_bias, ln2_gain, ln2_bias, out_bias, down_bias, qkv_bias, up_bias)
    packed = jnp.concatenate(vectors, 1).astype(F32)
    packed = jnp.pad(packed, ((0, 8 - LAYERS), (0, 2560 - packed.shape[1])))
    first_weight, table = gather_first(qkv_weight, packed)
    full_vectors, start = [], 0
    for vector in vectors:
        width = vector.shape[1]
        piece = table[:, :LAYERS, start : start + width]
        full_vectors.append(jnp.transpose(piece, (1, 0, 2)).reshape(LAYERS, 4 * width))
        start += width
    gain_one, bias_one, gain_two, bias_two, b_out, b_down, b_qkv, b_up = full_vectors

    qkv_full = [first_weight, None]
    gathered = [None] * LAYERS
    stream = tokens[0].astype(F32)
    saved = []
    for layer_index in range(LAYERS):
        w_qkv = qkv_full[layer_index]
        unit, scale = norm_parts(stream)
        norm_one = (unit * gain_one[layer_index] + bias_one[layer_index]).astype(BF)
        norm_two = (unit * gain_two[layer_index] + bias_two[layer_index]).astype(BF)
        joined = dot(norm_one, w_qkv) + b_qkv[layer_index]
        queries = rotate(joined[:, :D], tables).astype(BF)
        key_rows = rotate(joined[:, D : 2 * D], tables).astype(BF)
        value_rows = joined[:, 2 * D :].astype(BF)
        jobs = [(layer_index, out_weight), (layer_index, up_weight), (layer_index, down_weight)]
        if layer_index + 1 < LAYERS:
            jobs.append((layer_index + 1, qkv_weight))
        other_queries, keys, values, w_out, w_up, w_down, *more = gather_pair(
            "gather_pair_%d" % layer_index,
            1 + layer_index,
            (theirs(queries), theirs(key_rows), theirs(value_rows)),
            (mine(key_rows), mine(value_rows)),
            jobs,
        )
        if more:
            qkv_full[layer_index + 1] = more[0]
        gathered[layer_index] = (w_qkv, w_out, w_up, w_down)
        queries = jnp.concatenate([mine(queries), other_queries], 0)
        keys = keys.reshape(BLOCKS * BLOCK, HALF)
        values = values.reshape(BLOCKS * BLOCK, HALF)
        mixed_two, turned, log_total = attend_forward(ctx_word, queries, keys, values)
        mixed_low = join(mixed_two[:BLOCK], mirrored(mixed_two[BLOCK:]))
        hidden_pre = dot(norm_two, w_up) + b_up[layer_index]
        hidden_low = (hidden_pre * phi_parts(hidden_pre)[0]).astype(BF)
        mlp_branch = dot(hidden_low, w_down)
        lefts = (norm_one, mixed_low, norm_two)
        saved.append(
            (unit, scale, queries, keys, values, turned, log_total, hidden_pre, hidden_low, lefts)
        )
        stream = (
            stream + dot(mixed_low, w_out) + b_out[layer_index] + mlp_branch + b_down[layer_index]
        )

    gradient = cotangent[0].astype(F32)
    waiting, early_rows, late_rows = (), [None] * 2, [None] * 2
    for layer_index in range(LAYERS - 1, -1, -1):
        w_qkv, w_out, w_up, w_down = gathered[layer_index]
        unit, scale, queries, keys, values, turned, log_total, hidden_pre, hidden_low, lefts = saved[
            layer_index
        ]
        grad_low = gradient.astype(BF)
        grad_mixed = contract(grad_low, w_out, ((1,), (1,))).astype(BF)
        grad_mixed = jnp.concatenate([mine(grad_mixed), mirrored(theirs(grad_mixed))], 0)
        cumulative, density = phi_parts(hidden_pre)
        grad_hidden = contract(grad_low, w_down, ((1,), (1,)))
        grad_pre = (grad_hidden * (cumulative + hidden_pre * density)).astype(BF)
        grad_norm_two = contract(grad_pre, w_up, ((1,), (1,)))
        grad_query, grad_keys, grad_values = attend_backward(
            ctx_word, queries, keys, values, grad_mixed, turned, log_total
        )
        whole = (BLOCKS, BLOCK, HALF)
        own_pair, back_pair, back_query, *gathered_rows = scatter_pair(
            "scatter_pair_%d" % layer_index,
            3 + layer_index,
            grad_keys.reshape(whole),
            grad_values.reshape(whole),
            grad_query[BLOCK:].astype(BF),
            hidden_low,
            lefts + (grad_low, grad_pre) + waiting,
        )
        early_rows[layer_index] = gathered_rows[:6]
        if waiting:
            late_rows[layer_index + 1] = gathered_rows[6:]
        grad_query = join(grad_query[:BLOCK], back_query.astype(F32))
        grad_key = join(own_pair[0], back_pair[0].astype(F32))
        grad_value = join(own_pair[1], back_pair[1].astype(F32))
        grad_joined = jnp.concatenate(
            [rotate_back(grad_query, tables), rotate_back(grad_key, tables), grad_value], 1
        ).astype(BF)
        grad_norm_one = contract(grad_joined, w_qkv, ((1,), (1,)))
        norm_sums = jnp.stack(
            [
                jnp.sum(grad_norm_one * unit, 0),
                jnp.sum(grad_norm_one, 0),
                jnp.sum(grad_norm_two * unit, 0),
                jnp.sum(grad_norm_two, 0),
            ],
            0,
        )
        waiting = (grad_joined, jnp.pad(norm_sums, ((0, 12), (0, 0))).astype(BF))
        gradient = (
            gradient
            + norm_input_grad(grad_norm_one, gain_one[layer_index], unit, scale)
            + norm_input_grad(grad_norm_two, gain_two[layer_index], unit, scale)
        )
    late_rows[0] = gather_late(*waiting)
    fsdp_word = fsdp.astype(jnp.int32).reshape(1)
    packs, lines = [], []
    for layer_index in range(LAYERS):
        hidden, one, mixed, two, low, pre = early_rows[layer_index]
        joined, norms = late_rows[layer_index]
        rows, sums = weight_grads(fsdp_word, one, mixed, two, hidden, joined, low, pre, norms)
        packs.append(rows)
        lines.append(sums)
    summed, small = sum_over_ctx(*packs, *lines)

    def own_part(vectors, width):
        return lax.dynamic_slice_in_dim(vectors, fsdp * width, width, vectors.ndim - 1)

    bias_sum = own_part(small[:, 0], 192)
    joined_sum = own_part(small[:, 1:4].reshape(LAYERS, 3 * D), 576)
    up_sum = own_part(small[:, 4:8].reshape(LAYERS, 4 * D), D)
    norm_sums = own_part(small[:, 8:12], 192)
    rows = summed.reshape(LAYERS, 2304, D)

    def panels(first, count):
        pieces = [rows[:, first + i * 192 : first + (i + 1) * 192] for i in range(count)]
        return jnp.concatenate(pieces, 2).astype(F32)

    return (
        stream.astype(BF)[None],
        gradient[None],
        norm_sums[:, 0],
        norm_sums[:, 1],
        norm_sums[:, 2],
        norm_sums[:, 3],
        panels(0, 3),
        joined_sum,
        panels(576, 1),
        bias_sum,
        panels(768, 4),
        up_sum,
        rows[:, 1536:].astype(F32),
        bias_sum,
    )


def solution(mesh):
    matrix, vector = P(None, "fsdp", None), P(None, "fsdp")
    rows = P("fsdp", "ctx", None)
    params = (
        vector,
        vector,
        vector,
        vector,
        matrix,
        vector,
        matrix,
        vector,
        matrix,
        vector,
        matrix,
        vector,
    )
    return jax.shard_map(
        shards,
        mesh=mesh,
        in_specs=(rows, rows) + params,
        out_specs=(rows, rows) + params,
        check_vma=False,
    )
```

```python
import functools

import jax
import jax.numpy as jnp
from jax import lax
from jax.experimental import pallas as pl
from jax.experimental.pallas import tpu as pltpu
from jax.sharding import PartitionSpec as P

D = 768
HEADS = 12
HEAD_DIM = 64
FF = 3072
ROTARY = 16
LAYERS = 2
HALF = 384
BLOCK = 128
BLOCKS = 32
TILE = 512
PAIRS = 3

epsilon = 1e-05
masked_score = -1e30
MESH = pl.DeviceIdType.MESH
BF = jnp.bfloat16
F32 = jnp.float32


def mirrored(values):
    pairs = [(f * 32 + c, f * 32 + 31 - c) for f in range(4) for c in range(32)]
    return lax.ppermute(values, ("fsdp", "ctx"), pairs)


class Place:
    def __init__(self):
        self.fsdp = lax.axis_index("fsdp")
        self.ctx = lax.axis_index("ctx")
        self.y, self.z, self.h = self.ctx // 8, (self.ctx // 2) % 4, self.ctx % 2
        self.x_lo, self.core = self.fsdp // 2, self.fsdp % 2
        self.beside = (self.fsdp + 1 - 2 * self.core, self.ctx)
        self.mirror = (self.fsdp, BLOCKS - 1 - self.ctx)
        self.half = (self.fsdp, self.ctx + 1 - 2 * self.h)

    def along_x(self, step):
        x = (2 * self.h + self.x_lo + step) % 4
        return (2 * (x % 2) + self.core, self.y * 8 + self.z * 2 + x // 2)

    def ctx_at(self, dy, dz):
        return ((self.y + dy) % 4) * 8 + ((self.z + dz) % 4) * 2 + self.h

    def ring(self, t, da, db):
        return self.ctx_at(da, db) if t == 0 else self.ctx_at(db, da)

    def near(self, t, axis, sign):
        steps = (sign, 0) if axis == 0 else (0, sign)
        return (self.fsdp, self.ring(t, *steps))

    def around(self):
        return [self.near(0, axis, sign) for axis in (0, 1) for sign in (1, -1)]

    def greet(self, partners):
        barrier = pltpu.get_barrier_semaphore()
        for partner in partners:
            pl.semaphore_signal(barrier, inc=1, device_id=partner, device_id_type=MESH)
        pl.semaphore_wait(barrier, len(partners))


class Wire:
    def __init__(self, send_sem, recv_sem, local_sem=None):
        self.send_sem, self.recv_sem, self.local_sem = send_sem, recv_sem, local_sem
        self.sent, self.local, self.bounced = [], [], []

    def push(self, source, target, partner):
        number = len(self.sent)
        copy = pltpu.make_async_remote_copy(
            src_ref=source,
            dst_ref=target,
            send_sem=self.send_sem.at[number],
            recv_sem=self.recv_sem.at[number],
            device_id=partner,
            device_id_type=MESH,
        )
        copy.start()
        self.sent.append(copy)
        return copy

    def keep(self, source, target, bounce=None):
        if bounce is None:
            copy = pltpu.make_async_copy(source, target, self.local_sem.at[len(self.local)])
        else:
            copy = pltpu.make_async_copy(source, bounce, self.local_sem.at[len(self.local)])
            self.bounced.append((len(self.local), bounce, target))
        copy.start()
        self.local.append(copy)

    def flush(self):
        for number, bounce, target in self.bounced:
            self.local[number].wait()
            copy = pltpu.make_async_copy(bounce, target, self.local_sem.at[number])
            copy.start()
            self.local[number] = copy
        self.bounced = []

    def drain(self):
        for copy in self.sent:
            copy.wait_send()
        for copy in self.local:
            copy.wait()


def share_param(place, wire, source, target, bounce):
    rows = source.shape[0]
    cut = rows // 2
    mine, far = place.fsdp * rows, ((place.fsdp + 2) % 4) * rows
    parts = [(0, cut, 1), (cut, cut, 3)]
    across = [
        wire.push(
            source.at[pl.ds(start, count)],
            target.at[pl.ds(mine + start, count)],
            place.along_x(step),
        )
        for start, count, step in parts
    ]
    beside = wire.push(source, target.at[pl.ds(mine, rows)], place.beside)
    wire.keep(source, target.at[pl.ds(mine, rows)], bounce)
    last = [beside]

    def onward(copy, start, count):
        copy.wait_recv()
        spot = target.at[pl.ds(far + start, count)]
        last.append(wire.push(spot, spot, place.beside))

    steps = [
        functools.partial(onward, copy, start, count)
        for copy, (start, count, _) in zip(across, parts)
    ]
    return steps, last


def share_rows(place, wire, source, target):
    rows = source.shape[0]
    cut = rows // 2
    parts = [(0, cut, 1), (cut, cut, 3)] if rows % 32 == 0 else [(0, rows, 1)]
    across = [
        wire.push(
            source.at[pl.ds(start, count)],
            target.at[pl.ds(2 * rows + start, count)],
            place.along_x(step),
        )
        for start, count, step in parts
    ]
    last = [wire.push(source, target.at[pl.ds(rows, rows)], place.beside)]
    wire.keep(source, target.at[pl.ds(0, rows)])

    def onward(copy, start, count):
        copy.wait_recv()
        last.append(
            wire.push(
                target.at[pl.ds(2 * rows + start, count)],
                target.at[pl.ds(3 * rows + start, count)],
                place.beside,
            )
        )

    steps = [
        functools.partial(onward, copy, start, count)
        for copy, (start, count, _) in zip(across, parts)
    ]
    return steps, last


def share_columns(place, wire, source, target, stage):
    rows = source.shape[0]
    cut = rows // 2
    fsdp, core = place.fsdp, place.core
    parts = [(0, cut, 1), (cut, cut, 3)]

    def panel(start, count, shard):
        return source.at[pl.ds(start, count), pl.ds(pl.multiple_of(shard * D, D), D)]

    passing, last = [], []
    for start, count, step in parts:
        passing.append(
            wire.push(
                panel(start, count, 3 - fsdp),
                stage.at[pl.ds(start, count)],
                place.along_x(step),
            )
        )
    for start, count, step in parts:
        last.append(
            wire.push(
                panel(start, count, (fsdp + 2) % 4),
                target.at[pl.ds(2 * rows + start, count)],
                place.along_x(step),
            )
        )
    last.append(
        wire.push(
            panel(0, rows, fsdp + 1 - 2 * core), target.at[pl.ds(rows, rows)], place.beside
        )
    )
    wire.keep(panel(0, rows, fsdp), target.at[pl.ds(0, rows)])

    def onward(copy, start, count):
        copy.wait_recv()
        last.append(
            wire.push(
                stage.at[pl.ds(start, count)],
                target.at[pl.ds(3 * rows + start, count)],
                place.beside,
            )
        )

    steps = [
        functools.partial(onward, copy, start, count)
        for copy, (start, count, _) in zip(passing, parts)
    ]
    return steps, last


def spread(place, wire, own, spot, ready, between=()):
    between = list(between)
    arrivals = {}

    def push(t, da, db, b, axis, sign):
        target = spot(t, place.ring(t, da, db), b)
        source = own(t, b) if da == 0 and db == 0 else target
        sa, sb = (sign, 0) if axis == 0 else (0, sign)
        arrivals[t, (da - sa) % 4, (db - sb) % 4, b] = wire.push(
            source, target, place.near(t, axis, sign)
        )

    def landed(t, da, db):
        for b in (0, 1):
            arrivals[t, da, db, b].wait_recv()

    def pause():
        if between:
            between.pop(0)()

    for b in (0, 1):
        for t in (0, 1):
            ready(t, b)
            for axis in (0, 1):
                for sign in (1, -1):
                    push(t, 0, 0, b, axis, sign)
    for da, keep, onward in ((1, 0, -1), (3, 1, 1)):
        for t in (0, 1):
            landed(t, da, 0)
            push(t, da, 0, keep, 0, onward)
            for sign in (1, -1):
                for b in (0, 1):
                    push(t, da, 0, b, 1, sign)
    for db, keep, onward in ((1, 0, -1), (3, 1, 1)):
        for t in (0, 1):
            landed(t, 0, db)
            push(t, 0, db, keep, 1, onward)
    for t in (0, 1):
        landed(t, 2, 0)
        for sign in (1, -1):
            for b in (0, 1):
                push(t, 2, 0, b, 1, sign)
    pause()
    for da in (1, 3, 2):
        for db, keep, onward in ((1, 0, -1), (3, 1, 1)):
            for t in (0, 1):
                landed(t, da, db)
                push(t, da, db, keep, 1, onward)
            pause()
    while between:
        pause()
    for da in (0, 1, 3, 2):
        for t in (0, 1):
            landed(t, da, 2)


ANY = pl.BlockSpec(memory_space=pl.ANY)
VM = pl.BlockSpec(memory_space=pltpu.VMEM)
SM = pl.BlockSpec(memory_space=pltpu.SMEM)


def room(*shape):
    return pltpu.VMEM(shape, BF)


def sems(count, local):
    return [
        pltpu.SemaphoreType.DMA((count,)),
        pltpu.SemaphoreType.DMA((count,)),
        pltpu.SemaphoreType.DMA((local,)),
    ]


def full_shape(shard):
    return jax.ShapeDtypeStruct((4 * shard.shape[-2], shard.shape[-1]), BF)


def first_kernel(weight_ref, vector_ref, weight_out, vector_out, bounce, *sem):
    place, wire = Place(), Wire(*sem)
    place.greet([place.beside, place.along_x(1), place.along_x(3)])
    far = vector_out.at[(place.fsdp + 2) % 4]
    across = wire.push(vector_ref, vector_out.at[place.fsdp], place.along_x(1))
    last = [wire.push(vector_ref, vector_out.at[place.fsdp], place.beside)]
    wire.keep(vector_ref, vector_out.at[place.fsdp])
    steps, ends = share_param(place, wire, weight_ref.at[0], weight_out, bounce)
    wire.flush()
    across.wait_recv()
    last.append(wire.push(far, far, place.beside))
    for step in steps:
        step()
    for copy in last + ends:
        copy.wait_recv()
    wire.drain()


def gather_first(weight, vectors):
    return pl.pallas_call(
        first_kernel,
        out_shape=(full_shape(weight), jax.ShapeDtypeStruct((4,) + vectors.shape, F32)),
        in_specs=[ANY, VM],
        out_specs=(ANY, ANY),
        scratch_shapes=[room(*weight.shape[1:])] + sems(16, 4),
        compiler_params=pltpu.CompilerParams(
            collective_id=0, has_side_effects=True, vmem_limit_bytes=16 * 2**20
        ),
        name="gather_first",
    )(weight, vectors)


def gather_kernel(jobs, q_ref, k_ref, v_ref, k_own, v_own, *refs):
    count = len(jobs)
    weights, refs = refs[:count], refs[count:]
    q_out, k_out, v_out = refs[:3]
    weights_out, refs = refs[3 : 3 + count], refs[3 + count :]
    bounces, refs = refs[:count], refs[count:]
    place, wire = Place(), Wire(*refs)
    place.greet(
        place.around() + [place.mirror, place.beside, place.along_x(1), place.along_x(3)]
    )
    ins, outs = (k_own, v_own), (k_out, v_out)
    ctx = place.ctx
    swapped = [
        wire.push(source, out.at[ctx], place.mirror) for source, out in zip((k_ref, v_ref), outs)
    ]
    for t in (0, 1):
        wire.keep(ins[t], outs[t].at[ctx])
    work = []

    def ready(t, b):
        if b == 1:
            swapped[t].wait_recv()
            if t == 1:
                swapped.append(wire.push(q_ref, q_out, place.mirror))
                for layer, weight, target, bounce in zip(jobs, weights, weights_out, bounces):
                    work.append(share_param(place, wire, weight.at[layer], target, bounce))

    def spot(t, origin, b):
        return outs[t].at[origin if b == 0 else BLOCKS - 1 - origin]

    def own(t, b):
        return ins[t] if b == 0 else spot(t, ctx, 1)

    def onward(number):
        for steps, _ in work:
            for step in steps[number : number + 1]:
                step()

    spread(
        place,
        wire,
        own,
        spot,
        ready,
        [wire.flush]
        + [lambda: None] * 3
        + [functools.partial(onward, 0), functools.partial(onward, 1)],
    )
    swapped[2].wait_recv()
    for _, last in work:
        for copy in last:
            copy.wait_recv()
    wire.drain()


def gather_pair(name, number, away, own, jobs):
    layers = [layer for layer, _ in jobs]
    weights = [weight for _, weight in jobs]
    whole = jax.ShapeDtypeStruct((BLOCKS, BLOCK, HALF), BF)
    return pl.pallas_call(
        functools.partial(gather_kernel, layers),
        out_shape=(jax.ShapeDtypeStruct((BLOCK, HALF), BF), whole, whole)
        + tuple(full_shape(weight) for weight in weights),
        in_specs=[VM] * 5 + [ANY] * len(jobs),
        out_specs=(ANY,) * (3 + len(jobs)),
        scratch_shapes=[room(*weight.shape[1:]) for weight in weights] + sems(96, 8),
        compiler_params=pltpu.CompilerParams(
            collective_id=number, has_side_effects=True, vmem_limit_bytes=24 * 2**20
        ),
        name=name,
    )(*away, *own, *weights)


def scatter_kernel(count, gk_ref, gv_ref, gq_ref, hidden_ref, *refs):
    sources, refs = refs[:count], refs[count:]
    own_out, back_out, back_q, hidden_out = refs[:4]
    targets, refs = refs[4 : 4 + count], refs[4 + count :]
    far, near, mix, total, last_far, last_near, last_mix, leave, stage = refs[:9]
    place, wire = Place(), Wire(*refs[9:])
    place.greet(
        place.around() + [place.mirror, place.beside, place.along_x(1), place.along_x(3)]
    )
    ins = (gk_ref, gv_ref)

    def block_at(t, da, db, b):
        origin = place.ring(t, da, db)
        return origin if b == 0 else BLOCKS - 1 - origin

    order = [(da, t) for da in (2, 1, 3, 0) for t in (0, 1)]
    way = {0: 1, 1: -1}
    first, second, loose = {}, {}, {}
    for b in (1, 0):
        for da, t in order:
            first[t, da, b] = wire.push(
                ins[t].at[block_at(t, da, 2, b)], far.at[t, da, b], place.near(t, 1, way[b])
            )
    swapped = [wire.push(gq_ref, back_q, place.mirror)]
    for b in (1, 0):
        for da, t in order:
            loose[t, da, b] = wire.push(
                ins[t].at[block_at(t, da, -way[b], b)],
                near.at[t, da, 1, b],
                place.near(t, 1, -way[b]),
            )
    work = [share_columns(place, wire, hidden_ref, hidden_out, stage)]
    for source, target in zip(sources, targets):
        work.append(share_rows(place, wire, source, target))
    for b in (1, 0):
        for da, t in order:
            first[t, da, b].wait_recv()
            mix[t, da, b] = (
                ins[t][block_at(t, da, way[b], b)].astype(F32) + far[t, da, b].astype(F32)
            ).astype(BF)
            second[t, da, b] = wire.push(
                mix.at[t, da, b], near.at[t, da, 0, b], place.near(t, 1, way[b])
            )

    def settle(t, da, b):
        loose[t, da, b].wait_recv()
        second[t, da, b].wait_recv()
        total[t, da, b] = (
            ins[t][block_at(t, da, 0, b)].astype(F32)
            + near[t, da, 0, b].astype(F32)
            + near[t, da, 1, b].astype(F32)
        ).astype(BF)

    third, fourth = {}, {}
    for b in (1, 0):
        for t in (0, 1):
            settle(t, 2, b)
            third[t, b] = wire.push(
                total.at[t, 2, b], last_far.at[t, b], place.near(t, 0, way[b])
            )
        for t in (0, 1):
            settle(t, 1, b)
            settle(t, 3, b)
            fourth[t, b] = [
                wire.push(
                    total.at[t, -way[b] % 4, b], last_near.at[t, 1, b], place.near(t, 0, -way[b])
                )
            ]
        for t in (0, 1):
            third[t, b].wait_recv()
            last_mix[t, b] = (
                total[t, way[b] % 4, b].astype(F32) + last_far[t, b].astype(F32)
            ).astype(BF)
            fourth[t, b].append(
                wire.push(last_mix.at[t, b], last_near.at[t, 0, b], place.near(t, 0, way[b]))
            )
        for t in (0, 1):
            settle(t, 0, b)

    def final(t, b):
        for copy in fourth[t, b]:
            copy.wait_recv()
        return (
            total[t, 0, b].astype(F32)
            + last_near[t, 0, b].astype(F32)
            + last_near[t, 1, b].astype(F32)
        )

    for t in (0, 1):
        leave[t] = final(t, 1).astype(BF)
        swapped.append(wire.push(leave.at[t], back_out.at[t], place.mirror))
    for steps, _ in work:
        for step in steps:
            step()
    for t in (0, 1):
        own_out[t] = final(t, 0)
    for _, last in work:
        for copy in last:
            copy.wait_recv()
    for copy in swapped:
        copy.wait_recv()
    wire.drain()


def rows_shape(source):
    return jax.ShapeDtypeStruct((4 * source.shape[0], source.shape[1]), BF)


def scatter_pair(name, number, grad_keys, grad_values, away, hidden, sources):
    return pl.pallas_call(
        functools.partial(scatter_kernel, len(sources)),
        out_shape=(
            jax.ShapeDtypeStruct((2, BLOCK, HALF), F32),
            jax.ShapeDtypeStruct((2, BLOCK, HALF), BF),
            jax.ShapeDtypeStruct((BLOCK, HALF), BF),
            jax.ShapeDtypeStruct((4 * BLOCK, D), BF),
        )
        + tuple(rows_shape(source) for source in sources),
        in_specs=[VM] * (4 + len(sources)),
        out_specs=(VM,) + (ANY,) * (3 + len(sources)),
        scratch_shapes=[
            room(2, 4, 2, BLOCK, HALF),
            room(2, 4, 2, 2, BLOCK, HALF),
            room(2, 4, 2, BLOCK, HALF),
            room(2, 4, 2, BLOCK, HALF),
            room(2, 2, BLOCK, HALF),
            room(2, 2, 2, BLOCK, HALF),
            room(2, 2, BLOCK, HALF),
            room(2, BLOCK, HALF),
            room(BLOCK, D),
        ]
        + sems(128, 12),
        compiler_params=pltpu.CompilerParams(
            collective_id=number, has_side_effects=True, vmem_limit_bytes=44 * 2**20
        ),
        name=name,
    )(grad_keys, grad_values, away, hidden, *sources)


def late_kernel(one_ref, two_ref, one_out, two_out, *sem):
    place, wire = Place(), Wire(*sem)
    place.greet([place.beside, place.along_x(1), place.along_x(3)])
    work = [
        share_rows(place, wire, one_ref, one_out),
        share_rows(place, wire, two_ref, two_out),
    ]
    for steps, _ in work:
        for step in steps:
            step()
    for _, last in work:
        for copy in last:
            copy.wait_recv()
    wire.drain()


def gather_late(one, two):
    return pl.pallas_call(
        late_kernel,
        out_shape=(rows_shape(one), rows_shape(two)),
        in_specs=[VM] * 2,
        out_specs=(ANY,) * 2,
        scratch_shapes=sems(16, 4),
        compiler_params=pltpu.CompilerParams(collective_id=5, has_side_effects=True),
        name="gather_late",
    )(one, two)


PIECE = 144
CUT = 80


def sum_kernel(
    one_ref, two_ref, small_one, small_two, out_ref, small_out,
    far, mix, near, total, far_two, mix_two, near_two, part, other, final, small, heard, *sem,
):
    place, wire = Place(), Wire(*sem)
    y, z, h = place.y, place.z, place.h
    turns = [
        (place.fsdp, (y + 1 - 2 * (y % 2)) * 8 + z * 2 + h),
        (place.fsdp, ((y + 2) % 4) * 8 + z * 2 + h),
        (place.fsdp, y * 8 + (z + 1 - 2 * (z % 2)) * 2 + h),
        (place.fsdp, y * 8 + ((z + 2) % 4) * 2 + h),
        place.half,
    ]
    place.greet(place.around() + [turns[1], turns[3], place.half])
    ins = (one_ref, two_ref)
    parts = {0: pl.ds(0, CUT), 1: pl.ds(CUT, PIECE - CUT)}

    def chunk(t, da, db):
        origin = place.ring(t, da, db)
        return origin // 2

    def plus(*terms):
        result = terms[0].astype(F32)
        for term in terms[1:]:
            result = result + term.astype(F32)
        return result.astype(BF)

    small[0] = small_one[...]
    small[1] = small_two[...]
    passing = wire.push(small, heard.at[0], turns[0])
    order = (2, 1, 3, 0)
    way = {2: 1, 1: 1, 3: -1, 0: -1}
    first, second, loose = {}, {}, {}
    for db in order:
        for t in (0, 1):
            first[t, db] = wire.push(
                ins[t].at[chunk(t, 2, db)], far.at[t, db], place.near(t, 0, way[db])
            )
    for db in order:
        for t in (0, 1):
            loose[t, db] = wire.push(
                ins[t].at[chunk(t, -way[db], db)], near.at[t, db, 1], place.near(t, 0, -way[db])
            )
    for db in order:
        for t in (0, 1):
            first[t, db].wait_recv()
            mix[t, db] = plus(ins[t][chunk(t, way[db], db)], far[t, db])
            second[t, db] = wire.push(mix.at[t, db], near.at[t, db, 0], place.near(t, 0, way[db]))

    def hear(step):
        wire.sent[step_numbers[-1]].wait_send()
        wire.sent[step_numbers[-1]].wait_recv()
        small[...] += heard[step]
        waited.add(step_numbers[-1])
        if step < 4:
            step_numbers.append(len(wire.sent))
            wire.push(small, heard.at[step + 1], turns[step + 1])

    step_numbers, waited = [0], set()

    def settle(t, db):
        second[t, db].wait_recv()
        loose[t, db].wait_recv()
        total[t, db] = plus(ins[t][chunk(t, 0, db)], near[t, db, 0], near[t, db, 1])

    third, fourth = {}, {}
    for t in (0, 1):
        settle(t, 2)
        third[t] = [
            wire.push(
                total.at[t, 2, parts[b]], far_two.at[t, parts[b]], place.near(t, 1, sign)
            )
            for b, sign in ((0, 1), (1, -1))
        ]
    hear(0)
    for t in (0, 1):
        fourth[t] = []
        for b, sign, db in ((0, 1, 1), (1, -1, 3)):
            settle(t, db)
            fourth[t].append(
                wire.push(
                    total.at[t, db, parts[1 - b]],
                    near_two.at[t, b, parts[1 - b]],
                    place.near(t, 1, sign),
                )
            )
    hear(1)
    for t in (0, 1):
        for b, sign, db in ((0, 1, 1), (1, -1, 3)):
            third[t][b].wait_recv()
            mix_two[t, parts[b]] = plus(total[t, db, parts[b]], far_two[t, parts[b]])
            fourth[t].append(
                wire.push(
                    mix_two.at[t, parts[b]], near_two.at[t, b, parts[b]], place.near(t, 1, sign)
                )
            )
    hear(2)
    swapped = []
    for t in (0, 1):
        settle(t, 0)
        for copy in fourth[t]:
            copy.wait_recv()
        part[t] = plus(total[t, 0], near_two[t, 0], near_two[t, 1])
        swapped.append(wire.push(part.at[t], other.at[t], place.half))
    hear(3)

    def spot(t, origin, b):
        return out_ref.at[1 - t, origin // 2, parts[b]]

    def own(t, b):
        return final.at[1 - t, parts[b]]

    def ready(t, b):
        if b == 0:
            swapped[1 - t].wait_recv()
            final[1 - t] = plus(part[1 - t], other[1 - t])
            wire.keep(final.at[1 - t], out_ref.at[1 - t, place.ctx // 2])

    spread(place, wire, own, spot, ready)
    hear(4)
    small_out[...] = small[...]
    for number, copy in enumerate(wire.sent):
        if number not in waited:
            copy.wait_send()
    for copy in wire.local:
        copy.wait()


def sum_over_ctx(one, two, small_one, small_two):
    shape = (16, PIECE, D)
    small_shape = (2,) + small_one.shape
    return pl.pallas_call(
        sum_kernel,
        out_shape=(
            jax.ShapeDtypeStruct((2,) + shape, BF),
            jax.ShapeDtypeStruct(small_shape, F32),
        ),
        in_specs=[VM] * 4,
        out_specs=(ANY, VM),
        scratch_shapes=[
            room(2, 4, PIECE, D),
            room(2, 4, PIECE, D),
            room(2, 4, 2, PIECE, D),
            room(2, 4, PIECE, D),
            room(2, PIECE, D),
            room(2, PIECE, D),
            room(2, 2, PIECE, D),
            room(2, PIECE, D),
            room(2, PIECE, D),
            room(2, PIECE, D),
            pltpu.VMEM(small_shape, F32),
            pltpu.VMEM((5,) + small_shape, F32),
        ]
        + sems(128, 4),
        compiler_params=pltpu.CompilerParams(
            collective_id=6, has_side_effects=True, vmem_limit_bytes=48 * 2**20
        ),
        name="sum_over_ctx",
    )(one.reshape(shape), two.reshape(shape), small_one, small_two)


def weight_kernel(
    fsdp_ref, one_ref, mixed_ref, two_ref, hidden_ref, joined_ref, low_ref, pre_ref, norm_ref,
    rows_ref, sums_ref, turned, turned_hidden,
):
    start = pl.multiple_of(fsdp_ref[0] * 192, 64)
    lefts = []
    for i, ref in enumerate((one_ref, mixed_ref, two_ref)):
        turned[i] = jnp.transpose(ref[...])
        lefts.append(turned[i, pl.ds(start, 192), :])
    turned_hidden[...] = jnp.transpose(hidden_ref[...])
    ones = jnp.ones((8, low_ref.shape[0]), BF)

    def panel(first, left, right, line):
        rows = left.shape[0]
        rows_ref[first : first + rows, :] = contract(left, right, ((1,), (0,))).astype(BF)
        if line is not None:
            sums_ref[line : line + 1, :] = contract(ones, right, ((1,), (0,)))[:1]

    low = low_ref[...]
    panel(1536, turned_hidden[...], low, None)
    panel(576, lefts[1], low, 0)
    for i in range(3):
        panel(i * 192, lefts[0], joined_ref[:, i * D : (i + 1) * D], 1 + i)
    for i in range(4):
        panel(768 + i * 192, lefts[2], pre_ref[:, i * D : (i + 1) * D], 4 + i)
    norms = norm_ref[0:16, :].astype(F32)
    for i in range(1, 4):
        norms = norms + norm_ref[i * 16 : (i + 1) * 16, :].astype(F32)
    sums_ref[8:16, :] = norms[:8]


def weight_grads(fsdp, one, mixed, two, hidden, joined, low, pre, norms):
    tokens = one.shape[0]
    return pl.pallas_call(
        weight_kernel,
        out_shape=(
            jax.ShapeDtypeStruct((2304, D), BF),
            jax.ShapeDtypeStruct((16, D), F32),
        ),
        in_specs=[SM] + [VM] * 8,
        out_specs=(VM, VM),
        scratch_shapes=[room(3, D, tokens), room(D, tokens)],
        compiler_params=pltpu.CompilerParams(vmem_limit_bytes=40 * 2**20),
        cost_estimate=pl.CostEstimate(
            flops=2 * 512 * 1769472, bytes_accessed=12 * 2**20, transcendentals=0
        ),
        name="weight_grads",
    )(fsdp, one, mixed, two, hidden, joined, low, pre, norms)


def pair_rows(values):
    lane = lax.broadcasted_iota(jnp.int32, values.shape, 1)
    zero = jnp.zeros_like(values)
    return jnp.concatenate(
        [jnp.where(lane < HEAD_DIM, values, zero), jnp.where(lane >= HEAD_DIM, values, zero)], 0
    )


def contract(left, right, dims):
    return lax.dot_general(left, right, (dims, ((), ())), preferred_element_type=F32)


def allowed_at(tile, block):
    key = tile * TILE + lax.broadcasted_iota(jnp.int32, (TILE, 2 * BLOCK), 0)
    query = block * BLOCK + lax.broadcasted_iota(jnp.int32, (TILE, 2 * BLOCK), 1) % BLOCK
    return key <= query


def forward_kernel(
    ctx_ref, q_own, q_away, k_ref, v_ref, mixed_own, mixed_away, turned_ref, log_ref, top, mass, acc
):
    ctx = ctx_ref[0]
    for b in (0, 1):
        block = ctx if b == 0 else BLOCKS - 1 - ctx
        rows = slice(b * BLOCK, (b + 1) * BLOCK)
        q_ref, mixed_ref = (q_own, mixed_own) if b == 0 else (q_away, mixed_away)
        queries = [
            pair_rows(q_ref[:, p * 128 : (p + 1) * 128] * jnp.asarray(0.125, BF))
            for p in range(PAIRS)
        ]

        def step(tile, masked):
            start = pl.multiple_of(tile * TILE, TILE)
            for p in range(PAIRS):
                cols = slice(p * 128, (p + 1) * 128)
                scores = contract(k_ref[pl.ds(start, TILE), cols], queries[p], ((1,), (1,)))
                if masked:
                    scores = jnp.where(allowed_at(tile, block), scores, masked_score)
                    new_top = jnp.max(scores, 0, keepdims=True)
                else:
                    old_top = top[p : p + 1, :]
                    new_top = jnp.maximum(old_top, jnp.max(scores, 0, keepdims=True))
                weights = jnp.exp(scores - new_top)
                fresh_mass = jnp.sum(weights, 0, keepdims=True)
                fresh = contract(
                    v_ref[pl.ds(start, TILE), cols], weights.astype(BF), ((0,), (0,))
                )
                if not masked:
                    fade = jnp.exp(old_top - new_top)
                    fresh_mass = fresh_mass + mass[p : p + 1, :] * fade
                    fresh = fresh + acc[p] * fade
                top[p : p + 1, :] = new_top
                mass[p : p + 1, :] = fresh_mass
                acc[p] = fresh

        step(block // 4, True)

        @pl.loop(0, block // 4)
        def _(tile):
            step(tile, False)

        for p in range(PAIRS):
            cols = slice(p * 128, (p + 1) * 128)
            done = acc[p] / mass[p : p + 1, :]
            turned = jnp.concatenate([done[:HEAD_DIM, :BLOCK], done[HEAD_DIM:, BLOCK:]], 0)
            turned_ref[cols, rows] = turned
            mixed_ref[:, cols] = jnp.transpose(turned).astype(BF)
            row = b * PAIRS + p
            log_ref[row : row + 1, :] = top[p : p + 1, :] + jnp.log(mass[p : p + 1, :])


def attend_forward(ctx, own, away, keys, values):
    return pl.pallas_call(
        forward_kernel,
        out_shape=(
            jax.ShapeDtypeStruct((BLOCK, HALF), BF),
            jax.ShapeDtypeStruct((BLOCK, HALF), BF),
            jax.ShapeDtypeStruct((HALF, 2 * BLOCK), F32),
            jax.ShapeDtypeStruct((8, 2 * BLOCK), F32),
        ),
        in_specs=[SM, VM, VM, VM, VM],
        out_specs=(VM, VM, VM, VM),
        scratch_shapes=[
            pltpu.VMEM((8, 2 * BLOCK), F32),
            pltpu.VMEM((8, 2 * BLOCK), F32),
            pltpu.VMEM((PAIRS, 128, 2 * BLOCK), F32),
        ],
        compiler_params=pltpu.CompilerParams(vmem_limit_bytes=40 * 2**20),
        cost_estimate=pl.CostEstimate(
            flops=4 * 33 * 128 * 128 * 6 * 128, bytes_accessed=8 * 2**20, transcendentals=33 * 128 * 128 * 6
        ),
        name="attend_forward",
    )(ctx, own, away, keys, values)


def backward_kernel(
    ctx_ref, q_own, q_away, k_ref, v_ref, g_own, g_away, turned_ref, log_ref,
    gq_own, gq_away, gk_ref, gv_ref, gk_acc, gv_acc, gq_acc,
):
    ctx = ctx_ref[0]
    gk_acc[...] = jnp.zeros_like(gk_acc)
    gv_acc[...] = jnp.zeros_like(gv_acc)
    for b in (0, 1):
        block = ctx if b == 0 else BLOCKS - 1 - ctx
        rows = slice(b * BLOCK, (b + 1) * BLOCK)
        queries, grads, deltas = [], [], []
        q_ref, g_ref, gq_ref = (q_own, g_own, gq_own) if b == 0 else (q_away, g_away, gq_away)
        for p in range(PAIRS):
            cols = slice(p * 128, (p + 1) * 128)
            queries.append(pair_rows(q_ref[:, cols] * jnp.asarray(0.125, BF)))
            grad = g_ref[:, cols]
            grads.append(pair_rows(grad))
            both = jnp.transpose(grad.astype(F32)) * turned_ref[cols, rows]
            deltas.append(
                jnp.concatenate(
                    [
                        jnp.sum(both[:HEAD_DIM], 0, keepdims=True),
                        jnp.sum(both[HEAD_DIM:], 0, keepdims=True),
                    ],
                    1,
                )
            )
        gq_acc[...] = jnp.zeros_like(gq_acc)

        def step(tile, masked):
            start = pl.multiple_of(tile * TILE, TILE)
            here = pl.ds(start, TILE)
            for p in range(PAIRS):
                cols = slice(p * 128, (p + 1) * 128)
                row = b * PAIRS + p
                keys = k_ref[here, cols]
                scores = contract(keys, queries[p], ((1,), (1,)))
                chances = jnp.exp(scores - log_ref[row : row + 1, :])
                if masked:
                    chances = jnp.where(allowed_at(tile, block), chances, 0.0)
                grad_chance = contract(v_ref[here, cols], grads[p], ((1,), (1,)))
                grad_score = (chances * (grad_chance - deltas[p])).astype(BF)
                gv_acc[here, cols] += contract(chances.astype(BF), grads[p], ((1,), (0,)))
                gk_acc[here, cols] += contract(grad_score, queries[p], ((1,), (0,)))
                gq_acc[p] += contract(keys, grad_score, ((0,), (0,)))

        step(block // 4, True)

        @pl.loop(0, block // 4)
        def _(tile):
            step(tile, False)

        for p in range(PAIRS):
            cols = slice(p * 128, (p + 1) * 128)
            done = gq_acc[p] * 0.125
            turned = jnp.concatenate([done[:HEAD_DIM, :BLOCK], done[HEAD_DIM:, BLOCK:]], 0)
            gq_ref[:, cols] = jnp.transpose(turned).astype(gq_ref.dtype)
    gk_ref[...] = gk_acc[...].astype(BF)
    gv_ref[...] = gv_acc[...].astype(BF)


def attend_backward(ctx, own, away, keys, values, grad_own, grad_away, turned, log_total):
    whole = jax.ShapeDtypeStruct((BLOCKS * BLOCK, HALF), BF)
    return pl.pallas_call(
        backward_kernel,
        out_shape=(
            jax.ShapeDtypeStruct((BLOCK, HALF), F32),
            jax.ShapeDtypeStruct((BLOCK, HALF), BF),
            whole,
            whole,
        ),
        in_specs=[SM] + [VM] * 8,
        out_specs=(VM,) * 4,
        scratch_shapes=[
            pltpu.VMEM((BLOCKS * BLOCK, HALF), F32),
            pltpu.VMEM((BLOCKS * BLOCK, HALF), F32),
            pltpu.VMEM((PAIRS, 128, 2 * BLOCK), F32),
        ],
        compiler_params=pltpu.CompilerParams(vmem_limit_bytes=48 * 2**20),
        cost_estimate=pl.CostEstimate(
            flops=10 * 33 * 128 * 128 * 6 * 128, bytes_accessed=16 * 2**20, transcendentals=33 * 128 * 128 * 6
        ),
        name="attend_backward",
    )(ctx, own, away, keys, values, grad_own, grad_away, turned, log_total)


GAIN_ONE, BIAS_ONE, GAIN_TWO, BIAS_TWO, BIAS_OUT, BIAS_DOWN, BIAS_QKV, BIAS_UP = (
    0, 1, 2, 3, 4, 5, 6, 9,
)


def norm_parts(values):
    centre = jnp.mean(values, -1, keepdims=True)
    shifted = values - centre
    spread = jnp.mean(shifted * shifted, -1, keepdims=True)
    scale = lax.rsqrt(spread + epsilon)
    return shifted * scale, scale


def norm_input_grad(grad_norm, gain, unit, scale):
    e = grad_norm * gain
    return scale * (
        e - jnp.mean(e, -1, keepdims=True) - unit * jnp.mean(e * unit, -1, keepdims=True)
    )


def turn_tables(first_row, row_count):
    half_rot = ROTARY // 2
    positions = first_row + jnp.arange(row_count, dtype=jnp.int32)
    exponent = jnp.arange(half_rot, dtype=F32) * (2.0 / ROTARY)
    frequency = jnp.power(10000.0, -exponent)
    angle = positions.astype(F32)[:, None] * frequency[None, :]
    cosine, sine = jnp.cos(angle), jnp.sin(angle)
    rest = jnp.zeros((row_count, HEAD_DIM - ROTARY), F32)
    none = jnp.zeros_like(sine)
    keep = jnp.concatenate([cosine, cosine, rest + 1.0] * 2, 1)
    low = jnp.concatenate([-sine, none, rest] * 2, 1)
    high = jnp.concatenate([none, sine, rest] * 2, 1)
    return jnp.stack([keep, low, high], 0)


def rotate(values, table_ref):
    shift = ROTARY // 2
    return (
        values * table_ref[0]
        + pltpu.roll(values, 128 - shift, 1) * table_ref[1]
        + pltpu.roll(values, shift, 1) * table_ref[2]
    )


def rotate_back(values, table_ref):
    shift = ROTARY // 2
    return (
        values * table_ref[0]
        + pltpu.roll(values * table_ref[1], shift, 1)
        + pltpu.roll(values * table_ref[2], 128 - shift, 1)
    )


def phi_parts(values):
    cumulative = 0.5 * (1.0 + lax.erf(values * (2.0**-0.5)))
    density = jnp.exp(-0.5 * values * values) * (0.5 / jnp.pi) ** 0.5
    return cumulative, density


def line(vec_ref, row):
    return vec_ref[row : row + 1, :]


def put_halves(upper_ref, low, high, mine_ref, theirs_ref):
    upper = upper_ref[0] == 1

    @pl.when(upper)
    def _():
        mine_ref[...] = high
        theirs_ref[...] = low

    @pl.when(jnp.logical_not(upper))
    def _():
        mine_ref[...] = low
        theirs_ref[...] = high


def put_joined(upper_ref, mine, theirs, out_ref, first):
    upper = upper_ref[0] == 1
    low, high = slice(first, first + HALF), slice(first + HALF, first + D)

    @pl.when(upper)
    def _():
        out_ref[:, low] = theirs
        out_ref[:, high] = mine

    @pl.when(jnp.logical_not(upper))
    def _():
        out_ref[:, low] = mine
        out_ref[:, high] = theirs


def enter(upper_ref, stream, vec_ref, weight_ref, table_ref, one_ref, two_ref, *parts):
    unit, _ = norm_parts(stream)
    one = (unit * line(vec_ref, GAIN_ONE) + line(vec_ref, BIAS_ONE)).astype(BF)
    one_ref[...] = one
    two_ref[...] = (unit * line(vec_ref, GAIN_TWO) + line(vec_ref, BIAS_TWO)).astype(BF)
    for i in range(3):
        joined = contract(one, weight_ref[:, i * D : (i + 1) * D], ((1,), (0,)))
        joined = joined + line(vec_ref, BIAS_QKV + i)
        groups = [joined[:, g * 128 : (g + 1) * 128] for g in range(6)]
        if i < 2:
            groups = [rotate(group, table_ref) for group in groups]
        groups = [group.astype(BF) for group in groups]
        put_halves(
            upper_ref,
            jnp.concatenate(groups[:3], 1),
            jnp.concatenate(groups[3:], 1),
            parts[2 * i],
            parts[2 * i + 1],
        )


def enter_kernel(upper_ref, tokens_ref, vec_ref, weight_ref, table_ref, *outs):
    enter(upper_ref, tokens_ref[...].astype(F32), vec_ref, weight_ref, table_ref, *outs)


def leave(upper_ref, stream_ref, own_ref, away_ref, weight_ref, mlp_ref, vec_ref, mixed_ref):
    put_joined(upper_ref, own_ref[...], away_ref[...], mixed_ref, 0)
    return (
        stream_ref[...].astype(F32)
        + contract(mixed_ref[...], weight_ref[...], ((1,), (0,)))
        + line(vec_ref, BIAS_OUT)
        + mlp_ref[...]
        + line(vec_ref, BIAS_DOWN)
    )


def pass_kernel(
    upper_ref, stream_ref, own_ref, away_ref, out_ref, mlp_ref, vec_ref,
    next_vec_ref, weight_ref, table_ref, mixed_ref, next_ref, *outs,
):
    stream = leave(upper_ref, stream_ref, own_ref, away_ref, out_ref, mlp_ref, vec_ref, mixed_ref)
    next_ref[...] = stream
    enter(upper_ref, stream, next_vec_ref, weight_ref, table_ref, *outs)


def last_kernel(
    upper_ref, stream_ref, own_ref, away_ref, out_ref, mlp_ref, vec_ref, mixed_ref, next_ref
):
    next_ref[...] = leave(
        upper_ref, stream_ref, own_ref, away_ref, out_ref, mlp_ref, vec_ref, mixed_ref
    ).astype(BF)


def mlp_kernel(two_ref, up_ref, down_ref, vec_ref, pre_ref, hidden_ref, mlp_ref):
    two = two_ref[...]
    for i in range(FF // D):
        cols = slice(i * D, (i + 1) * D)
        pre = contract(two, up_ref[:, cols], ((1,), (0,))) + line(vec_ref, BIAS_UP + i)
        pre_ref[:, cols] = pre
        hidden = (pre * phi_parts(pre)[0]).astype(BF)
        hidden_ref[:, cols] = hidden
        fresh = contract(hidden, down_ref[cols, :], ((1,), (0,)))
        mlp_ref[...] = fresh if i == 0 else mlp_ref[...] + fresh


def back(upper_ref, gradient, weight_ref, low_ref, mine_ref, theirs_ref):
    low = gradient.astype(BF)
    low_ref[...] = low
    mixed = contract(low, weight_ref[...], ((1,), (1,))).astype(BF)
    put_halves(upper_ref, mixed[:, :HALF], mixed[:, HALF:], mine_ref, theirs_ref)


def back_kernel(upper_ref, cotangent_ref, weight_ref, *outs):
    back(upper_ref, cotangent_ref[...].astype(F32), weight_ref, *outs)


def mlp_back_kernel(low_ref, pre_ref, up_ref, down_ref, grad_pre_ref, norm_ref):
    low = low_ref[...]
    for i in range(FF // D):
        cols = slice(i * D, (i + 1) * D)
        pre = pre_ref[:, cols]
        cumulative, density = phi_parts(pre)
        hidden = contract(low, down_ref[cols, :], ((1,), (1,)))
        grad_pre = (hidden * (cumulative + pre * density)).astype(BF)
        grad_pre_ref[:, cols] = grad_pre
        fresh = contract(grad_pre, up_ref[:, cols], ((1,), (1,)))
        norm_ref[...] = fresh if i == 0 else norm_ref[...] + fresh


def join_kernel(
    more, upper_ref, own_ref, back_ref, own_q, back_q, table_ref, weight_ref, stream_ref, vec_ref,
    two_ref, gradient_ref, *refs,
):
    next_weight, refs = (refs[:1], refs[1:]) if more else ((), refs)
    joined_ref, sums_ref, next_ref, *outs = refs

    def turned(values):
        groups = [rotate_back(values[:, g * 128 : (g + 1) * 128], table_ref) for g in range(3)]
        return jnp.concatenate(groups, 1).astype(BF)

    put_joined(upper_ref, turned(own_q[...]), turned(back_q[...].astype(F32)), joined_ref, 0)
    put_joined(upper_ref, turned(own_ref[0]), turned(back_ref[0].astype(F32)), joined_ref, D)
    put_joined(upper_ref, own_ref[1].astype(BF), back_ref[1], joined_ref, 2 * D)
    one = contract(joined_ref[...], weight_ref[...], ((1,), (1,)))
    two = two_ref[...]
    unit, scale = norm_parts(stream_ref[...].astype(F32))
    sums = [jnp.sum(values, 0, keepdims=True) for values in (one * unit, one, two * unit, two)]
    sums_ref[...] = jnp.concatenate(sums + [jnp.zeros((12, D), F32)], 0).astype(BF)
    gradient = (
        gradient_ref[...].astype(F32)
        + norm_input_grad(one, line(vec_ref, GAIN_ONE), unit, scale)
        + norm_input_grad(two, line(vec_ref, GAIN_TWO), unit, scale)
    )
    next_ref[...] = gradient
    if more:
        back(upper_ref, gradient, next_weight[0], *outs)


def unpack_kernel(rows_ref, qkv_ref, out_ref, up_ref, down_ref):
    for i in range(3):
        qkv_ref[0, :, i * D : (i + 1) * D] = rows_ref[0, i * 192 : (i + 1) * 192, :].astype(F32)
    out_ref[0] = rows_ref[0, 576:768, :].astype(F32)
    for i in range(4):
        up_ref[0, :, i * D : (i + 1) * D] = rows_ref[
            0, 768 + i * 192 : 960 + i * 192, :
        ].astype(F32)
    down_ref[0] = rows_ref[0, 1536:, :].astype(F32)


def unpack(rows):
    shapes = [(192, 3 * D), (192, D), (192, FF), (D, D)]
    return pl.pallas_call(
        unpack_kernel,
        grid=(LAYERS,),
        out_shape=tuple(jax.ShapeDtypeStruct((LAYERS,) + shape, F32) for shape in shapes),
        in_specs=[pl.BlockSpec((1, 2304, D), lambda i: (i, 0, 0))],
        out_specs=tuple(pl.BlockSpec((1,) + shape, lambda i: (i, 0, 0)) for shape in shapes),
        compiler_params=pltpu.CompilerParams(vmem_limit_bytes=40 * 2**20),
        name="unpack",
    )(rows)


def dense(name, kernel, specs, outs, args, flops):
    shapes = tuple(
        jax.ShapeDtypeStruct((BLOCK, size) if isinstance(size, int) else size, kind)
        for size, kind in outs
    )
    return pl.pallas_call(
        kernel,
        out_shape=shapes,
        in_specs=specs,
        out_specs=(VM,) * len(shapes),
        compiler_params=pltpu.CompilerParams(vmem_limit_bytes=32 * 2**20),
        cost_estimate=pl.CostEstimate(
            flops=2 * BLOCK * flops, bytes_accessed=2 * flops, transcendentals=0
        ),
        name=name,
    )(*args)


ENTER_OUTS = ((D, BF),) * 2 + ((HALF, BF),) * 6


def shards(
    tokens,
    cotangent,
    ln1_gain,
    ln1_bias,
    ln2_gain,
    ln2_bias,
    qkv_weight,
    qkv_bias,
    out_weight,
    out_bias,
    up_weight,
    up_bias,
    down_weight,
    down_bias,
):
    row_count = tokens.shape[1]
    fsdp = lax.axis_index("fsdp")
    ctx = lax.axis_index("ctx")
    ctx_word = ctx.astype(jnp.int32).reshape(1)
    upper = (ctx % 2).astype(jnp.int32).reshape(1)
    tables = turn_tables(ctx * row_count, row_count)

    vectors = (ln1_gain, ln1_bias, ln2_gain, ln2_bias, out_bias, down_bias, qkv_bias, up_bias)
    packed = jnp.concatenate(vectors, 1).astype(F32)
    packed = jnp.pad(packed, ((0, 8 - LAYERS), (0, 2560 - packed.shape[1])))
    first_weight, table = gather_first(qkv_weight, packed)
    table = table[:, :LAYERS]
    six = table[:, :, :1152].reshape(4, LAYERS, 6, 192)
    vecs = jnp.concatenate(
        [
            jnp.transpose(six, (1, 2, 0, 3)).reshape(LAYERS, 6, D),
            jnp.transpose(table[:, :, 1152:1728], (1, 0, 2)).reshape(LAYERS, 3, D),
            jnp.transpose(table[:, :, 1728:2496], (1, 0, 2)).reshape(LAYERS, 4, D),
        ],
        1,
    )
    vecs = [vecs[layer_index] for layer_index in range(LAYERS)]

    qkv_full = [first_weight, None]
    gathered = [None] * LAYERS
    stream = tokens[0]
    entered = dense(
        "enter",
        enter_kernel,
        [SM] + [VM] * 4,
        ENTER_OUTS,
        (upper, stream, vecs[0], first_weight, tables),
        D * 3 * D,
    )
    saved = []
    for layer_index in range(LAYERS):
        norm_one, norm_two, q_own, q_away, k_own, k_away, v_own, v_away = entered
        jobs = [(layer_index, out_weight), (layer_index, up_weight), (layer_index, down_weight)]
        if layer_index + 1 < LAYERS:
            jobs.append((layer_index + 1, qkv_weight))
        q_other, keys, values, w_out, w_up, w_down, *more = gather_pair(
            "gather_pair_%d" % layer_index,
            1 + layer_index,
            (q_away, k_away, v_away),
            (k_own, v_own),
            jobs,
        )
        if more:
            qkv_full[layer_index + 1] = more[0]
        gathered[layer_index] = (qkv_full[layer_index], w_out, w_up, w_down)
        keys = keys.reshape(BLOCKS * BLOCK, HALF)
        values = values.reshape(BLOCKS * BLOCK, HALF)
        mixed_own, mixed_away, turned, log_total = attend_forward(
            ctx_word, q_own, q_other, keys, values
        )
        mixed_back = mirrored(mixed_away)
        hidden_pre, hidden_low, mlp_branch = dense(
            "mlp",
            mlp_kernel,
            [VM] * 4,
            ((FF, F32), (FF, BF), (D, F32)),
            (norm_two, w_up, w_down, vecs[layer_index]),
            2 * D * FF,
        )
        before = stream
        common = (upper, stream, mixed_own, mixed_back, w_out, mlp_branch, vecs[layer_index])
        if more:
            mixed_low, stream, *entered = dense(
                "pass_on",
                pass_kernel,
                [SM] + [VM] * 9,
                ((D, BF), (D, F32)) + ENTER_OUTS,
                common + (vecs[layer_index + 1], more[0], tables),
                D * 4 * D,
            )
        else:
            mixed_low, output = dense(
                "last", last_kernel, [SM] + [VM] * 6, ((D, BF), (D, BF)), common, D * D
            )
        lefts = (norm_one, mixed_low, norm_two)
        saved.append(
            (before, q_own, q_other, keys, values, turned, log_total, hidden_pre, hidden_low, lefts)
        )

    gradient = cotangent[0]
    waiting, early_rows, late_rows = (), [None] * 2, [None] * 2
    grad_low, grad_own, grad_away = dense(
        "back",
        back_kernel,
        [SM, VM, VM],
        ((D, BF), (HALF, BF), (HALF, BF)),
        (upper, gradient, gathered[LAYERS - 1][1]),
        D * D,
    )
    for layer_index in range(LAYERS - 1, -1, -1):
        w_qkv, w_out, w_up, w_down = gathered[layer_index]
        before, q_own, q_other, keys, values, turned, log_total, hidden_pre, hidden_low, lefts = (
            saved[layer_index]
        )
        grad_back = mirrored(grad_away)
        grad_pre, grad_norm_two = dense(
            "mlp_back",
            mlp_back_kernel,
            [VM] * 4,
            ((FF, BF), (D, F32)),
            (grad_low, hidden_pre, w_up, w_down),
            2 * D * FF,
        )
        gq_own, gq_away, grad_keys, grad_values = attend_backward(
            ctx_word, q_own, q_other, keys, values, grad_own, grad_back, turned, log_total
        )
        whole = (BLOCKS, BLOCK, HALF)
        own_pair, back_pair, back_query, *gathered_rows = scatter_pair(
            "scatter_pair_%d" % layer_index,
            3 + layer_index,
            grad_keys.reshape(whole),
            grad_values.reshape(whole),
            gq_away,
            hidden_low,
            lefts + (grad_low, grad_pre) + waiting,
        )
        early_rows[layer_index] = gathered_rows[:6]
        if waiting:
            late_rows[layer_index + 1] = gathered_rows[6:]
        going_on = layer_index > 0
        grad_joined, norm_sums, gradient, *outs = dense(
            "join_%d" % layer_index,
            functools.partial(join_kernel, going_on),
            [SM] + [VM] * (11 if going_on else 10),
            ((3 * D, BF), ((16, D), BF), (D, F32))
            + (((D, BF), (HALF, BF), (HALF, BF)) if going_on else ()),
            (
                upper,
                own_pair,
                back_pair,
                gq_own,
                back_query,
                tables,
                w_qkv,
                before,
                vecs[layer_index],
                grad_norm_two,
                gradient,
            )
            + ((gathered[layer_index - 1][1],) if going_on else ()),
            D * 3 * D,
        )
        waiting = (grad_joined, norm_sums)
        if going_on:
            grad_low, grad_own, grad_away = outs
    late_rows[0] = gather_late(*waiting)
    fsdp_word = fsdp.astype(jnp.int32).reshape(1)
    packs, lines = [], []
    for layer_index in range(LAYERS):
        hidden, one, mixed, two, low, pre = early_rows[layer_index]
        joined, norms = late_rows[layer_index]
        rows, sums = weight_grads(fsdp_word, one, mixed, two, hidden, joined, low, pre, norms)
        packs.append(rows)
        lines.append(sums)
    summed, small = sum_over_ctx(*packs, *lines)

    def own_part(vectors, width):
        return lax.dynamic_slice_in_dim(vectors, fsdp * width, width, vectors.ndim - 1)

    bias_sum = own_part(small[:, 0], 192)
    joined_sum = own_part(small[:, 1:4].reshape(LAYERS, 3 * D), 576)
    up_sum = own_part(small[:, 4:8].reshape(LAYERS, 4 * D), D)
    norm_sums = own_part(small[:, 8:12], 192)
    qkv_grad, out_grad, up_grad, down_grad = unpack(summed.reshape(LAYERS, 2304, D))
    return (
        output[None],
        gradient[None],
        norm_sums[:, 0],
        norm_sums[:, 1],
        norm_sums[:, 2],
        norm_sums[:, 3],
        qkv_grad,
        joined_sum,
        out_grad,
        bias_sum,
        up_grad,
        up_sum,
        down_grad,
        bias_sum,
    )


def solution(mesh):
    matrix, vector = P(None, "fsdp", None), P(None, "fsdp")
    rows = P("fsdp", "ctx", None)
    params = (
        vector,
        vector,
        vector,
        vector,
        matrix,
        vector,
        matrix,
        vector,
        matrix,
        vector,
        matrix,
        vector,
    )
    return jax.shard_map(
        shards,
        mesh=mesh,
        in_specs=(rows, rows) + params,
        out_specs=(rows, rows) + params,
        check_vma=False,
    )
```

```python
import functools

import jax
import jax.numpy as jnp
from jax import lax
from jax.experimental import pallas as pl
from jax.experimental.pallas import tpu as pltpu
from jax.sharding import PartitionSpec as P

D = 768
HEADS = 12
HEAD_DIM = 64
FF = 3072
ROTARY = 16
LAYERS = 2
HALF = 384
BLOCK = 128
BLOCKS = 32
TILE = 512
PAIRS = 3

epsilon = 1e-05
masked_score = -1e30
MESH = pl.DeviceIdType.MESH
BF = jnp.bfloat16
F32 = jnp.float32


def mirrored(values):
    pairs = [(f * 32 + c, f * 32 + 31 - c) for f in range(4) for c in range(32)]
    return lax.ppermute(values, ("fsdp", "ctx"), pairs)


class Place:
    def __init__(self):
        self.fsdp = lax.axis_index("fsdp")
        self.ctx = lax.axis_index("ctx")
        self.y, self.z, self.h = self.ctx // 8, (self.ctx // 2) % 4, self.ctx % 2
        self.x_lo, self.core = self.fsdp // 2, self.fsdp % 2
        self.beside = (self.fsdp + 1 - 2 * self.core, self.ctx)
        self.mirror = (self.fsdp, BLOCKS - 1 - self.ctx)
        self.half = (self.fsdp, self.ctx + 1 - 2 * self.h)

    def along_x(self, step):
        x = (2 * self.h + self.x_lo + step) % 4
        return (2 * (x % 2) + self.core, self.y * 8 + self.z * 2 + x // 2)

    def ctx_at(self, dy, dz):
        return ((self.y + dy) % 4) * 8 + ((self.z + dz) % 4) * 2 + self.h

    def ring(self, t, da, db):
        return self.ctx_at(da, db) if t == 0 else self.ctx_at(db, da)

    def near(self, t, axis, sign):
        steps = (sign, 0) if axis == 0 else (0, sign)
        return (self.fsdp, self.ring(t, *steps))

    def around(self):
        return [self.near(0, axis, sign) for axis in (0, 1) for sign in (1, -1)]

    def greet(self, partners):
        barrier = pltpu.get_barrier_semaphore()
        for partner in partners:
            pl.semaphore_signal(barrier, inc=1, device_id=partner, device_id_type=MESH)
        pl.semaphore_wait(barrier, len(partners))


class Wire:
    def __init__(self, send_sem, recv_sem, local_sem=None):
        self.send_sem, self.recv_sem, self.local_sem = send_sem, recv_sem, local_sem
        self.sent, self.local, self.bounced = [], [], []

    def push(self, source, target, partner):
        number = len(self.sent)
        copy = pltpu.make_async_remote_copy(
            src_ref=source,
            dst_ref=target,
            send_sem=self.send_sem.at[number],
            recv_sem=self.recv_sem.at[number],
            device_id=partner,
            device_id_type=MESH,
        )
        copy.start()
        self.sent.append(copy)
        return copy

    def keep(self, source, target, bounce=None):
        if bounce is None:
            copy = pltpu.make_async_copy(source, target, self.local_sem.at[len(self.local)])
        else:
            copy = pltpu.make_async_copy(source, bounce, self.local_sem.at[len(self.local)])
            self.bounced.append((len(self.local), bounce, target))
        copy.start()
        self.local.append(copy)

    def flush(self):
        for number, bounce, target in self.bounced:
            self.local[number].wait()
            copy = pltpu.make_async_copy(bounce, target, self.local_sem.at[number])
            copy.start()
            self.local[number] = copy
        self.bounced = []

    def drain(self):
        for copy in self.sent:
            copy.wait_send()
        for copy in self.local:
            copy.wait()


def share_param(place, wire, source, target, bounce):
    rows = source.shape[0]
    cut = rows // 2
    mine, far = place.fsdp * rows, ((place.fsdp + 2) % 4) * rows
    parts = [(0, cut, 1), (cut, cut, 3)]
    across = [
        wire.push(
            source.at[pl.ds(start, count)],
            target.at[pl.ds(mine + start, count)],
            place.along_x(step),
        )
        for start, count, step in parts
    ]
    beside = wire.push(source, target.at[pl.ds(mine, rows)], place.beside)
    wire.keep(source, target.at[pl.ds(mine, rows)], bounce)
    last = [beside]

    def onward(copy, start, count):
        copy.wait_recv()
        spot = target.at[pl.ds(far + start, count)]
        last.append(wire.push(spot, spot, place.beside))

    steps = [
        functools.partial(onward, copy, start, count)
        for copy, (start, count, _) in zip(across, parts)
    ]
    return steps, last


def share_rows(place, wire, source, target):
    rows = source.shape[0]
    cut = rows // 2
    parts = [(0, cut, 1), (cut, cut, 3)] if rows % 32 == 0 else [(0, rows, 1)]
    across = [
        wire.push(
            source.at[pl.ds(start, count)],
            target.at[pl.ds(2 * rows + start, count)],
            place.along_x(step),
        )
        for start, count, step in parts
    ]
    last = [wire.push(source, target.at[pl.ds(rows, rows)], place.beside)]
    wire.keep(source, target.at[pl.ds(0, rows)])

    def onward(copy, start, count):
        copy.wait_recv()
        last.append(
            wire.push(
                target.at[pl.ds(2 * rows + start, count)],
                target.at[pl.ds(3 * rows + start, count)],
                place.beside,
            )
        )

    steps = [
        functools.partial(onward, copy, start, count)
        for copy, (start, count, _) in zip(across, parts)
    ]
    return steps, last


def share_columns(place, wire, source, target, stage):
    rows = source.shape[0]
    cut = rows // 2
    fsdp, core = place.fsdp, place.core
    parts = [(0, cut, 1), (cut, cut, 3)]

    def panel(start, count, shard):
        return source.at[pl.ds(start, count), pl.ds(pl.multiple_of(shard * D, D), D)]

    passing, last = [], []
    for start, count, step in parts:
        passing.append(
            wire.push(
                panel(start, count, 3 - fsdp),
                stage.at[pl.ds(start, count)],
                place.along_x(step),
            )
        )
    for start, count, step in parts:
        last.append(
            wire.push(
                panel(start, count, (fsdp + 2) % 4),
                target.at[pl.ds(2 * rows + start, count)],
                place.along_x(step),
            )
        )
    last.append(
        wire.push(
            panel(0, rows, fsdp + 1 - 2 * core), target.at[pl.ds(rows, rows)], place.beside
        )
    )
    wire.keep(panel(0, rows, fsdp), target.at[pl.ds(0, rows)])

    def onward(copy, start, count):
        copy.wait_recv()
        last.append(
            wire.push(
                stage.at[pl.ds(start, count)],
                target.at[pl.ds(3 * rows + start, count)],
                place.beside,
            )
        )

    steps = [
        functools.partial(onward, copy, start, count)
        for copy, (start, count, _) in zip(passing, parts)
    ]
    return steps, last


def spread(place, wire, own, spot, ready, between=()):
    between = list(between)
    arrivals = {}

    def push(t, da, db, b, axis, sign):
        target = spot(t, place.ring(t, da, db), b)
        source = own(t, b) if da == 0 and db == 0 else target
        sa, sb = (sign, 0) if axis == 0 else (0, sign)
        arrivals[t, (da - sa) % 4, (db - sb) % 4, b] = wire.push(
            source, target, place.near(t, axis, sign)
        )

    def landed(t, da, db):
        for b in (0, 1):
            arrivals[t, da, db, b].wait_recv()

    def pause():
        if between:
            between.pop(0)()

    for b in (0, 1):
        for t in (0, 1):
            ready(t, b)
            for axis in (0, 1):
                for sign in (1, -1):
                    push(t, 0, 0, b, axis, sign)
    for da, keep, onward in ((1, 0, -1), (3, 1, 1)):
        for t in (0, 1):
            landed(t, da, 0)
            push(t, da, 0, keep, 0, onward)
            for sign in (1, -1):
                for b in (0, 1):
                    push(t, da, 0, b, 1, sign)
    for db, keep, onward in ((1, 0, -1), (3, 1, 1)):
        for t in (0, 1):
            landed(t, 0, db)
            push(t, 0, db, keep, 1, onward)
    for t in (0, 1):
        landed(t, 2, 0)
        for sign in (1, -1):
            for b in (0, 1):
                push(t, 2, 0, b, 1, sign)
    pause()
    for da in (1, 3, 2):
        for db, keep, onward in ((1, 0, -1), (3, 1, 1)):
            for t in (0, 1):
                landed(t, da, db)
                push(t, da, db, keep, 1, onward)
    while between:
        pause()
    for da in (0, 1, 3, 2):
        for t in (0, 1):
            landed(t, da, 2)


ANY = pl.BlockSpec(memory_space=pl.ANY)
VM = pl.BlockSpec(memory_space=pltpu.VMEM)
SM = pl.BlockSpec(memory_space=pltpu.SMEM)


def room(*shape):
    return pltpu.VMEM(shape, BF)


def sems(count, local):
    return [
        pltpu.SemaphoreType.DMA((count,)),
        pltpu.SemaphoreType.DMA((count,)),
        pltpu.SemaphoreType.DMA((local,)),
    ]


def full_shape(shard):
    return jax.ShapeDtypeStruct((4 * shard.shape[-2], shard.shape[-1]), BF)


def first_kernel(weight_ref, vector_ref, weight_out, vector_out, bounce, *sem):
    place, wire = Place(), Wire(*sem)
    place.greet([place.beside, place.along_x(1), place.along_x(3)])
    far = vector_out.at[(place.fsdp + 2) % 4]
    across = wire.push(vector_ref, vector_out.at[place.fsdp], place.along_x(1))
    last = [wire.push(vector_ref, vector_out.at[place.fsdp], place.beside)]
    wire.keep(vector_ref, vector_out.at[place.fsdp])
    steps, ends = share_param(place, wire, weight_ref.at[0], weight_out, bounce)
    wire.flush()
    across.wait_recv()
    last.append(wire.push(far, far, place.beside))
    for step in steps:
        step()
    for copy in last + ends:
        copy.wait_recv()
    wire.drain()


def gather_first(weight, vectors):
    return pl.pallas_call(
        first_kernel,
        out_shape=(full_shape(weight), jax.ShapeDtypeStruct((4,) + vectors.shape, F32)),
        in_specs=[ANY, VM],
        out_specs=(ANY, ANY),
        scratch_shapes=[room(*weight.shape[1:])] + sems(16, 4),
        compiler_params=pltpu.CompilerParams(
            collective_id=0, has_side_effects=True, vmem_limit_bytes=60 * 2**20
        ),
        name="gather_first",
    )(weight, vectors)


def gather_kernel(jobs, q_ref, k_ref, v_ref, k_own, v_own, *refs):
    count = len(jobs)
    weights, refs = refs[:count], refs[count:]
    q_out, k_out, v_out = refs[:3]
    weights_out, refs = refs[3 : 3 + count], refs[3 + count :]
    bounces, refs = refs[:count], refs[count:]
    place, wire = Place(), Wire(*refs)
    place.greet(
        place.around() + [place.mirror, place.beside, place.along_x(1), place.along_x(3)]
    )
    ins, outs = (k_own, v_own), (k_out, v_out)
    ctx = place.ctx
    swapped = [
        wire.push(source, out.at[ctx], place.mirror) for source, out in zip((k_ref, v_ref), outs)
    ]
    for t in (0, 1):
        wire.keep(ins[t], outs[t].at[ctx])
    work = []

    def ready(t, b):
        if b == 1:
            if t == 0:
                for layer, weight, target, bounce in zip(jobs, weights, weights_out, bounces):
                    work.append(share_param(place, wire, weight.at[layer], target, bounce))
            swapped[t].wait_recv()
            if t == 1:
                swapped.append(wire.push(q_ref, q_out, place.mirror))

    def spot(t, origin, b):
        return outs[t].at[origin if b == 0 else BLOCKS - 1 - origin]

    def own(t, b):
        return ins[t] if b == 0 else spot(t, ctx, 1)

    def onward(number):
        for steps, _ in work:
            for step in steps[number : number + 1]:
                step()

    spread(
        place,
        wire,
        own,
        spot,
        ready,
        [wire.flush, functools.partial(onward, 0), functools.partial(onward, 1)],
    )
    swapped[2].wait_recv()
    for _, last in work:
        for copy in last:
            copy.wait_recv()
    wire.drain()


def gather_pair(name, number, away, own, jobs):
    layers = [layer for layer, _ in jobs]
    weights = [weight for _, weight in jobs]
    whole = jax.ShapeDtypeStruct((BLOCKS, BLOCK, HALF), BF)
    return pl.pallas_call(
        functools.partial(gather_kernel, layers),
        out_shape=(jax.ShapeDtypeStruct((BLOCK, HALF), BF), whole, whole)
        + tuple(full_shape(weight) for weight in weights),
        in_specs=[VM] * 5 + [ANY] * len(jobs),
        out_specs=(ANY,) * (3 + len(jobs)),
        scratch_shapes=[room(*weight.shape[1:]) for weight in weights] + sems(96, 8),
        compiler_params=pltpu.CompilerParams(
            collective_id=number, has_side_effects=True, vmem_limit_bytes=60 * 2**20
        ),
        name=name,
    )(*away, *own, *weights)


def scatter_kernel(count, gk_ref, gv_ref, gq_ref, hidden_ref, *refs):
    sources, refs = refs[:count], refs[count:]
    own_out, back_out, back_q, hidden_out = refs[:4]
    targets, refs = refs[4 : 4 + count], refs[4 + count :]
    far, near, mix, total, last_far, last_near, last_mix, leave, stage = refs[:9]
    place, wire = Place(), Wire(*refs[9:])
    place.greet(
        place.around() + [place.mirror, place.beside, place.along_x(1), place.along_x(3)]
    )
    ins = (gk_ref, gv_ref)

    def block_at(t, da, db, b):
        origin = place.ring(t, da, db)
        return origin if b == 0 else BLOCKS - 1 - origin

    order = [(da, t) for da in (2, 1, 3, 0) for t in (0, 1)]
    way = {0: 1, 1: -1}
    first, second, loose = {}, {}, {}
    for b in (1, 0):
        for da, t in order:
            first[t, da, b] = wire.push(
                ins[t].at[block_at(t, da, 2, b)], far.at[t, da, b], place.near(t, 1, way[b])
            )
    swapped = [wire.push(gq_ref, back_q, place.mirror)]
    for b in (1, 0):
        for da, t in order:
            loose[t, da, b] = wire.push(
                ins[t].at[block_at(t, da, -way[b], b)],
                near.at[t, da, 1, b],
                place.near(t, 1, -way[b]),
            )
    work = []
    for b in (1, 0):
        if b == 0:
            work.append(share_columns(place, wire, hidden_ref, hidden_out, stage))
            for source, target in zip(sources, targets):
                work.append(share_rows(place, wire, source, target))
        for da, t in order:
            first[t, da, b].wait_recv()
            mix[t, da, b] = (
                ins[t][block_at(t, da, way[b], b)].astype(F32) + far[t, da, b].astype(F32)
            ).astype(BF)
            second[t, da, b] = wire.push(
                mix.at[t, da, b], near.at[t, da, 0, b], place.near(t, 1, way[b])
            )

    def settle(t, da, b):
        loose[t, da, b].wait_recv()
        second[t, da, b].wait_recv()
        total[t, da, b] = (
            ins[t][block_at(t, da, 0, b)].astype(F32)
            + near[t, da, 0, b].astype(F32)
            + near[t, da, 1, b].astype(F32)
        ).astype(BF)

    third, fourth = {}, {}
    for b in (1, 0):
        for t in (0, 1):
            settle(t, 2, b)
            third[t, b] = wire.push(
                total.at[t, 2, b], last_far.at[t, b], place.near(t, 0, way[b])
            )
        for t in (0, 1):
            settle(t, 1, b)
            settle(t, 3, b)
            fourth[t, b] = [
                wire.push(
                    total.at[t, -way[b] % 4, b], last_near.at[t, 1, b], place.near(t, 0, -way[b])
                )
            ]
        for t in (0, 1):
            third[t, b].wait_recv()
            last_mix[t, b] = (
                total[t, way[b] % 4, b].astype(F32) + last_far[t, b].astype(F32)
            ).astype(BF)
            fourth[t, b].append(
                wire.push(last_mix.at[t, b], last_near.at[t, 0, b], place.near(t, 0, way[b]))
            )
        for t in (0, 1):
            settle(t, 0, b)

    def final(t, b):
        for copy in fourth[t, b]:
            copy.wait_recv()
        return (
            total[t, 0, b].astype(F32)
            + last_near[t, 0, b].astype(F32)
            + last_near[t, 1, b].astype(F32)
        )

    for t in (0, 1):
        leave[t] = final(t, 1).astype(BF)
        swapped.append(wire.push(leave.at[t], back_out.at[t], place.mirror))
    for steps, _ in work:
        for step in steps:
            step()
    for t in (0, 1):
        own_out[t] = final(t, 0)
    for _, last in work:
        for copy in last:
            copy.wait_recv()
    for copy in swapped:
        copy.wait_recv()
    wire.drain()


def rows_shape(source):
    return jax.ShapeDtypeStruct((4 * source.shape[0], source.shape[1]), BF)


def scatter_pair(name, number, grad_keys, grad_values, away, hidden, sources):
    return pl.pallas_call(
        functools.partial(scatter_kernel, len(sources)),
        out_shape=(
            jax.ShapeDtypeStruct((2, BLOCK, HALF), F32),
            jax.ShapeDtypeStruct((2, BLOCK, HALF), BF),
            jax.ShapeDtypeStruct((BLOCK, HALF), BF),
            jax.ShapeDtypeStruct((4 * BLOCK, D), BF),
        )
        + tuple(rows_shape(source) for source in sources),
        in_specs=[VM] * (4 + len(sources)),
        out_specs=(VM,) + (ANY,) * (3 + len(sources)),
        scratch_shapes=[
            room(2, 4, 2, BLOCK, HALF),
            room(2, 4, 2, 2, BLOCK, HALF),
            room(2, 4, 2, BLOCK, HALF),
            room(2, 4, 2, BLOCK, HALF),
            room(2, 2, BLOCK, HALF),
            room(2, 2, 2, BLOCK, HALF),
            room(2, 2, BLOCK, HALF),
            room(2, BLOCK, HALF),
            room(BLOCK, D),
        ]
        + sems(128, 12),
        compiler_params=pltpu.CompilerParams(
            collective_id=number, has_side_effects=True, vmem_limit_bytes=60 * 2**20
        ),
        name=name,
    )(grad_keys, grad_values, away, hidden, *sources)


def late_kernel(one_ref, two_ref, one_out, two_out, *sem):
    place, wire = Place(), Wire(*sem)
    place.greet([place.beside, place.along_x(1), place.along_x(3)])
    work = [
        share_rows(place, wire, one_ref, one_out),
        share_rows(place, wire, two_ref, two_out),
    ]
    for steps, _ in work:
        for step in steps:
            step()
    for _, last in work:
        for copy in last:
            copy.wait_recv()
    wire.drain()


def gather_late(one, two):
    return pl.pallas_call(
        late_kernel,
        out_shape=(rows_shape(one), rows_shape(two)),
        in_specs=[VM] * 2,
        out_specs=(ANY,) * 2,
        scratch_shapes=sems(16, 4),
        compiler_params=pltpu.CompilerParams(collective_id=5, has_side_effects=True),
        name="gather_late",
    )(one, two)


PIECE = 144
CUT = 80


def sum_kernel(
    one_ref, two_ref, small_one, small_two, out_ref, small_out,
    far, mix, near, total, far_two, mix_two, near_two, part, other, final, small, heard, *sem,
):
    place, wire = Place(), Wire(*sem)
    y, z, h = place.y, place.z, place.h
    turns = [
        (place.fsdp, (y + 1 - 2 * (y % 2)) * 8 + z * 2 + h),
        (place.fsdp, ((y + 2) % 4) * 8 + z * 2 + h),
        (place.fsdp, y * 8 + (z + 1 - 2 * (z % 2)) * 2 + h),
        (place.fsdp, y * 8 + ((z + 2) % 4) * 2 + h),
        place.half,
    ]
    place.greet(place.around() + [turns[1], turns[3], place.half])
    ins = (one_ref, two_ref)
    parts = {0: pl.ds(0, CUT), 1: pl.ds(CUT, PIECE - CUT)}

    def chunk(t, da, db):
        origin = place.ring(t, da, db)
        return origin // 2

    def plus(*terms):
        result = terms[0].astype(F32)
        for term in terms[1:]:
            result = result + term.astype(F32)
        return result.astype(BF)

    small[0] = small_one[...]
    small[1] = small_two[...]
    passing = wire.push(small, heard.at[0], turns[0])
    order = (2, 1, 3, 0)
    way = {2: 1, 1: 1, 3: -1, 0: -1}
    first, second, loose = {}, {}, {}
    for db in order:
        for t in (0, 1):
            first[t, db] = wire.push(
                ins[t].at[chunk(t, 2, db)], far.at[t, db], place.near(t, 0, way[db])
            )
    for db in order:
        for t in (0, 1):
            loose[t, db] = wire.push(
                ins[t].at[chunk(t, -way[db], db)], near.at[t, db, 1], place.near(t, 0, -way[db])
            )
    for db in order:
        for t in (0, 1):
            first[t, db].wait_recv()
            mix[t, db] = plus(ins[t][chunk(t, way[db], db)], far[t, db])
            second[t, db] = wire.push(mix.at[t, db], near.at[t, db, 0], place.near(t, 0, way[db]))

    def hear(step):
        wire.sent[step_numbers[-1]].wait_send()
        wire.sent[step_numbers[-1]].wait_recv()
        small[...] += heard[step]
        waited.add(step_numbers[-1])
        if step < 4:
            step_numbers.append(len(wire.sent))
            wire.push(small, heard.at[step + 1], turns[step + 1])

    step_numbers, waited = [0], set()

    def settle(t, db):
        second[t, db].wait_recv()
        loose[t, db].wait_recv()
        total[t, db] = plus(ins[t][chunk(t, 0, db)], near[t, db, 0], near[t, db, 1])

    third, fourth = {}, {}
    for t in (0, 1):
        settle(t, 2)
        third[t] = [
            wire.push(
                total.at[t, 2, parts[b]], far_two.at[t, parts[b]], place.near(t, 1, sign)
            )
            for b, sign in ((0, 1), (1, -1))
        ]
    hear(0)
    for t in (0, 1):
        fourth[t] = []
        for b, sign, db in ((0, 1, 1), (1, -1, 3)):
            settle(t, db)
            fourth[t].append(
                wire.push(
                    total.at[t, db, parts[1 - b]],
                    near_two.at[t, b, parts[1 - b]],
                    place.near(t, 1, sign),
                )
            )
    hear(1)
    for t in (0, 1):
        for b, sign, db in ((0, 1, 1), (1, -1, 3)):
            third[t][b].wait_recv()
            mix_two[t, parts[b]] = plus(total[t, db, parts[b]], far_two[t, parts[b]])
            fourth[t].append(
                wire.push(
                    mix_two.at[t, parts[b]], near_two.at[t, b, parts[b]], place.near(t, 1, sign)
                )
            )
    hear(2)
    swapped = []
    for t in (0, 1):
        settle(t, 0)
        for copy in fourth[t]:
            copy.wait_recv()
        part[t] = plus(total[t, 0], near_two[t, 0], near_two[t, 1])
        swapped.append(wire.push(part.at[t], other.at[t], place.half))
    hear(3)

    def spot(t, origin, b):
        return out_ref.at[1 - t, origin // 2, parts[b]]

    def own(t, b):
        return final.at[1 - t, parts[b]]

    def ready(t, b):
        if b == 0:
            swapped[1 - t].wait_recv()
            final[1 - t] = plus(part[1 - t], other[1 - t])
            wire.keep(final.at[1 - t], out_ref.at[1 - t, place.ctx // 2])

    spread(place, wire, own, spot, ready)
    hear(4)
    small_out[...] = small[...]
    for number, copy in enumerate(wire.sent):
        if number not in waited:
            copy.wait_send()
    for copy in wire.local:
        copy.wait()


def sum_over_ctx(one, two, small_one, small_two):
    shape = (16, PIECE, D)
    small_shape = (2,) + small_one.shape
    return pl.pallas_call(
        sum_kernel,
        out_shape=(
            jax.ShapeDtypeStruct((2,) + shape, BF),
            jax.ShapeDtypeStruct(small_shape, F32),
        ),
        in_specs=[VM] * 4,
        out_specs=(ANY, VM),
        scratch_shapes=[
            room(2, 4, PIECE, D),
            room(2, 4, PIECE, D),
            room(2, 4, 2, PIECE, D),
            room(2, 4, PIECE, D),
            room(2, PIECE, D),
            room(2, PIECE, D),
            room(2, 2, PIECE, D),
            room(2, PIECE, D),
            room(2, PIECE, D),
            room(2, PIECE, D),
            pltpu.VMEM(small_shape, F32),
            pltpu.VMEM((5,) + small_shape, F32),
        ]
        + sems(128, 4),
        compiler_params=pltpu.CompilerParams(
            collective_id=6, has_side_effects=True, vmem_limit_bytes=60 * 2**20
        ),
        name="sum_over_ctx",
    )(one.reshape(shape), two.reshape(shape), small_one, small_two)


def weight_kernel(
    fsdp_ref, one_ref, mixed_ref, two_ref, hidden_ref, joined_ref, low_ref, pre_ref, norm_ref,
    rows_ref, sums_ref, turned, turned_hidden,
):
    start = pl.multiple_of(fsdp_ref[0] * 192, 64)
    lefts = []
    for i, ref in enumerate((one_ref, mixed_ref, two_ref)):
        turned[i] = jnp.transpose(ref[...])
        lefts.append(turned[i, pl.ds(start, 192), :])
    turned_hidden[...] = jnp.transpose(hidden_ref[...])
    ones = jnp.ones((8, low_ref.shape[0]), BF)

    def panel(first, left, right, line):
        rows = left.shape[0]
        rows_ref[first : first + rows, :] = contract(left, right, ((1,), (0,))).astype(BF)
        if line is not None:
            sums_ref[line : line + 1, :] = contract(ones, right, ((1,), (0,)))[:1]

    low = low_ref[...]
    panel(1536, turned_hidden[...], low, None)
    panel(576, lefts[1], low, 0)
    for i in range(3):
        panel(i * 192, lefts[0], joined_ref[:, i * D : (i + 1) * D], 1 + i)
    for i in range(4):
        panel(768 + i * 192, lefts[2], pre_ref[:, i * D : (i + 1) * D], 4 + i)
    norms = norm_ref[0:16, :].astype(F32)
    for i in range(1, 4):
        norms = norms + norm_ref[i * 16 : (i + 1) * 16, :].astype(F32)
    sums_ref[8:16, :] = norms[:8]


def weight_grads(fsdp, one, mixed, two, hidden, joined, low, pre, norms):
    tokens = one.shape[0]
    return pl.pallas_call(
        weight_kernel,
        out_shape=(
            jax.ShapeDtypeStruct((2304, D), BF),
            jax.ShapeDtypeStruct((16, D), F32),
        ),
        in_specs=[SM] + [VM] * 8,
        out_specs=(VM, VM),
        scratch_shapes=[room(3, D, tokens), room(D, tokens)],
        compiler_params=pltpu.CompilerParams(vmem_limit_bytes=60 * 2**20),
        cost_estimate=pl.CostEstimate(
            flops=2 * 512 * 1769472, bytes_accessed=12 * 2**20, transcendentals=0
        ),
        name="weight_grads",
    )(fsdp, one, mixed, two, hidden, joined, low, pre, norms)


def pair_rows(values):
    lane = lax.broadcasted_iota(jnp.int32, values.shape, 1)
    zero = jnp.zeros_like(values)
    return jnp.concatenate(
        [jnp.where(lane < HEAD_DIM, values, zero), jnp.where(lane >= HEAD_DIM, values, zero)], 0
    )


def contract(left, right, dims):
    return lax.dot_general(left, right, (dims, ((), ())), preferred_element_type=F32)


def allowed_at(tile, block):
    key = tile * TILE + lax.broadcasted_iota(jnp.int32, (TILE, 2 * BLOCK), 0)
    query = block * BLOCK + lax.broadcasted_iota(jnp.int32, (TILE, 2 * BLOCK), 1) % BLOCK
    return key <= query


def forward_kernel(
    ctx_ref, q_own, q_away, k_ref, v_ref, mixed_own, mixed_away, turned_ref, log_ref, top, mass, acc
):
    ctx = ctx_ref[0]
    for b in (0, 1):
        block = ctx if b == 0 else BLOCKS - 1 - ctx
        rows = slice(b * BLOCK, (b + 1) * BLOCK)
        q_ref, mixed_ref = (q_own, mixed_own) if b == 0 else (q_away, mixed_away)
        queries = [
            pair_rows(q_ref[:, p * 128 : (p + 1) * 128] * jnp.asarray(0.125, BF))
            for p in range(PAIRS)
        ]

        def step(tile, masked):
            start = pl.multiple_of(tile * TILE, TILE)
            for p in range(PAIRS):
                cols = slice(p * 128, (p + 1) * 128)
                scores = contract(k_ref[pl.ds(start, TILE), cols], queries[p], ((1,), (1,)))
                if masked:
                    scores = jnp.where(allowed_at(tile, block), scores, masked_score)
                    new_top = jnp.max(scores, 0, keepdims=True)
                else:
                    old_top = top[p : p + 1, :]
                    new_top = jnp.maximum(old_top, jnp.max(scores, 0, keepdims=True))
                weights = jnp.exp(scores - new_top)
                fresh_mass = jnp.sum(weights, 0, keepdims=True)
                fresh = contract(
                    v_ref[pl.ds(start, TILE), cols], weights.astype(BF), ((0,), (0,))
                )
                if not masked:
                    fade = jnp.exp(old_top - new_top)
                    fresh_mass = fresh_mass + mass[p : p + 1, :] * fade
                    fresh = fresh + acc[p] * fade
                top[p : p + 1, :] = new_top
                mass[p : p + 1, :] = fresh_mass
                acc[p] = fresh

        step(block // 4, True)

        @pl.loop(0, block // 4)
        def _(tile):
            step(tile, False)

        for p in range(PAIRS):
            cols = slice(p * 128, (p + 1) * 128)
            done = acc[p] / mass[p : p + 1, :]
            turned = jnp.concatenate([done[:HEAD_DIM, :BLOCK], done[HEAD_DIM:, BLOCK:]], 0)
            turned_ref[cols, rows] = turned
            mixed_ref[:, cols] = jnp.transpose(turned).astype(BF)
            row = b * PAIRS + p
            log_ref[row : row + 1, :] = top[p : p + 1, :] + jnp.log(mass[p : p + 1, :])


def attend_forward(ctx, own, away, keys, values):
    return pl.pallas_call(
        forward_kernel,
        out_shape=(
            jax.ShapeDtypeStruct((BLOCK, HALF), BF),
            jax.ShapeDtypeStruct((BLOCK, HALF), BF),
            jax.ShapeDtypeStruct((HALF, 2 * BLOCK), F32),
            jax.ShapeDtypeStruct((8, 2 * BLOCK), F32),
        ),
        in_specs=[SM, VM, VM, VM, VM],
        out_specs=(VM, VM, VM, VM),
        scratch_shapes=[
            pltpu.VMEM((8, 2 * BLOCK), F32),
            pltpu.VMEM((8, 2 * BLOCK), F32),
            pltpu.VMEM((PAIRS, 128, 2 * BLOCK), F32),
        ],
        compiler_params=pltpu.CompilerParams(vmem_limit_bytes=60 * 2**20),
        cost_estimate=pl.CostEstimate(
            flops=4 * 33 * 128 * 128 * 6 * 128, bytes_accessed=8 * 2**20, transcendentals=33 * 128 * 128 * 6
        ),
        name="attend_forward",
    )(ctx, own, away, keys, values)


def backward_kernel(
    ctx_ref, q_own, q_away, k_ref, v_ref, g_own, g_away, turned_ref, log_ref,
    gq_own, gq_away, gk_ref, gv_ref, gk_acc, gv_acc, gq_acc,
):
    ctx = ctx_ref[0]
    gk_acc[...] = jnp.zeros_like(gk_acc)
    gv_acc[...] = jnp.zeros_like(gv_acc)
    for b in (0, 1):
        block = ctx if b == 0 else BLOCKS - 1 - ctx
        rows = slice(b * BLOCK, (b + 1) * BLOCK)
        queries, grads, deltas = [], [], []
        q_ref, g_ref, gq_ref = (q_own, g_own, gq_own) if b == 0 else (q_away, g_away, gq_away)
        for p in range(PAIRS):
            cols = slice(p * 128, (p + 1) * 128)
            queries.append(pair_rows(q_ref[:, cols] * jnp.asarray(0.125, BF)))
            grad = g_ref[:, cols]
            grads.append(pair_rows(grad))
            both = jnp.transpose(grad.astype(F32)) * turned_ref[cols, rows]
            deltas.append(
                jnp.concatenate(
                    [
                        jnp.sum(both[:HEAD_DIM], 0, keepdims=True),
                        jnp.sum(both[HEAD_DIM:], 0, keepdims=True),
                    ],
                    1,
                )
            )
        gq_acc[...] = jnp.zeros_like(gq_acc)

        def step(tile, masked):
            start = pl.multiple_of(tile * TILE, TILE)
            here = pl.ds(start, TILE)
            for p in range(PAIRS):
                cols = slice(p * 128, (p + 1) * 128)
                row = b * PAIRS + p
                keys = k_ref[here, cols]
                scores = contract(keys, queries[p], ((1,), (1,)))
                chances = jnp.exp(scores - log_ref[row : row + 1, :])
                if masked:
                    chances = jnp.where(allowed_at(tile, block), chances, 0.0)
                grad_chance = contract(v_ref[here, cols], grads[p], ((1,), (1,)))
                grad_score = (chances * (grad_chance - deltas[p])).astype(BF)
                gv_acc[here, cols] += contract(chances.astype(BF), grads[p], ((1,), (0,)))
                gk_acc[here, cols] += contract(grad_score, queries[p], ((1,), (0,)))
                gq_acc[p] += contract(keys, grad_score, ((0,), (0,)))

        step(block // 4, True)

        @pl.loop(0, block // 4)
        def _(tile):
            step(tile, False)

        for p in range(PAIRS):
            cols = slice(p * 128, (p + 1) * 128)
            done = gq_acc[p] * 0.125
            turned = jnp.concatenate([done[:HEAD_DIM, :BLOCK], done[HEAD_DIM:, BLOCK:]], 0)
            gq_ref[:, cols] = jnp.transpose(turned).astype(gq_ref.dtype)
    gk_ref[...] = gk_acc[...].astype(BF)
    gv_ref[...] = gv_acc[...].astype(BF)


def attend_backward(ctx, own, away, keys, values, grad_own, grad_away, turned, log_total):
    whole = jax.ShapeDtypeStruct((BLOCKS * BLOCK, HALF), BF)
    return pl.pallas_call(
        backward_kernel,
        out_shape=(
            jax.ShapeDtypeStruct((BLOCK, HALF), F32),
            jax.ShapeDtypeStruct((BLOCK, HALF), BF),
            whole,
            whole,
        ),
        in_specs=[SM] + [VM] * 8,
        out_specs=(VM,) * 4,
        scratch_shapes=[
            pltpu.VMEM((BLOCKS * BLOCK, HALF), F32),
            pltpu.VMEM((BLOCKS * BLOCK, HALF), F32),
            pltpu.VMEM((PAIRS, 128, 2 * BLOCK), F32),
        ],
        compiler_params=pltpu.CompilerParams(vmem_limit_bytes=60 * 2**20),
        cost_estimate=pl.CostEstimate(
            flops=10 * 33 * 128 * 128 * 6 * 128, bytes_accessed=16 * 2**20, transcendentals=33 * 128 * 128 * 6
        ),
        name="attend_backward",
    )(ctx, own, away, keys, values, grad_own, grad_away, turned, log_total)


GAIN_ONE, BIAS_ONE, GAIN_TWO, BIAS_TWO, BIAS_OUT, BIAS_DOWN, BIAS_QKV, BIAS_UP = (
    0, 1, 2, 3, 4, 5, 6, 9,
)


def norm_parts(values):
    centre = jnp.mean(values, -1, keepdims=True)
    shifted = values - centre
    spread = jnp.mean(shifted * shifted, -1, keepdims=True)
    scale = lax.rsqrt(spread + epsilon)
    return shifted * scale, scale


def norm_input_grad(grad_norm, gain, unit, scale):
    e = grad_norm * gain
    return scale * (
        e - jnp.mean(e, -1, keepdims=True) - unit * jnp.mean(e * unit, -1, keepdims=True)
    )


def turn_tables(first_row, row_count):
    shape = (row_count, 128)
    feature = lax.broadcasted_iota(jnp.int32, shape, 1) % HEAD_DIM
    position = first_row + lax.broadcasted_iota(jnp.int32, shape, 0)
    half_rot = ROTARY // 2
    exponent = (feature % half_rot).astype(F32) * (2.0 / ROTARY)
    angle = position.astype(F32) * jnp.power(10000.0, -exponent)
    cosine, sine = jnp.cos(angle), jnp.sin(angle)
    keep = jnp.where(feature < ROTARY, cosine, 1.0)
    low = jnp.where(feature < half_rot, -sine, 0.0)
    high = jnp.where((feature >= half_rot) & (feature < ROTARY), sine, 0.0)
    return keep, low, high


def rotate(values, table_ref):
    shift = ROTARY // 2
    return (
        values * table_ref[0]
        + pltpu.roll(values, 128 - shift, 1) * table_ref[1]
        + pltpu.roll(values, shift, 1) * table_ref[2]
    )


def rotate_back(values, table_ref):
    shift = ROTARY // 2
    return (
        values * table_ref[0]
        + pltpu.roll(values * table_ref[1], shift, 1)
        + pltpu.roll(values * table_ref[2], 128 - shift, 1)
    )


def phi_parts(values):
    cumulative = 0.5 * (1.0 + lax.erf(values * (2.0**-0.5)))
    density = jnp.exp(-0.5 * values * values) * (0.5 / jnp.pi) ** 0.5
    return cumulative, density


def line(vec_ref, row):
    return vec_ref[row : row + 1, :]


def put_halves(upper_ref, low, high, mine_ref, theirs_ref):
    upper = upper_ref[0] == 1

    @pl.when(upper)
    def _():
        mine_ref[...] = high
        theirs_ref[...] = low

    @pl.when(jnp.logical_not(upper))
    def _():
        mine_ref[...] = low
        theirs_ref[...] = high


def put_joined(upper_ref, mine, theirs, out_ref, first):
    upper = upper_ref[0] == 1
    low, high = slice(first, first + HALF), slice(first + HALF, first + D)

    @pl.when(upper)
    def _():
        out_ref[:, low] = theirs
        out_ref[:, high] = mine

    @pl.when(jnp.logical_not(upper))
    def _():
        out_ref[:, low] = mine
        out_ref[:, high] = theirs


def enter(upper_ref, stream, vec_ref, weight_ref, table_ref, one_ref, two_ref, *parts):
    unit, _ = norm_parts(stream)
    one = (unit * line(vec_ref, GAIN_ONE) + line(vec_ref, BIAS_ONE)).astype(BF)
    one_ref[...] = one
    two_ref[...] = (unit * line(vec_ref, GAIN_TWO) + line(vec_ref, BIAS_TWO)).astype(BF)
    for i in range(3):
        joined = contract(one, weight_ref[:, i * D : (i + 1) * D], ((1,), (0,)))
        joined = joined + line(vec_ref, BIAS_QKV + i)
        groups = [joined[:, g * 128 : (g + 1) * 128] for g in range(6)]
        if i < 2:
            groups = [rotate(group, table_ref) for group in groups]
        groups = [group.astype(BF) for group in groups]
        put_halves(
            upper_ref,
            jnp.concatenate(groups[:3], 1),
            jnp.concatenate(groups[3:], 1),
            parts[2 * i],
            parts[2 * i + 1],
        )


def enter_kernel(upper_ref, tokens_ref, vec_ref, weight_ref, keep, low, high, *outs):
    table_ref = (keep[...], low[...], high[...])
    enter(upper_ref, tokens_ref[...].astype(F32), vec_ref, weight_ref, table_ref, *outs)


def leave(upper_ref, stream_ref, own_ref, away_ref, weight_ref, mlp_ref, vec_ref, mixed_ref):
    put_joined(upper_ref, own_ref[...], away_ref[...], mixed_ref, 0)
    return (
        stream_ref[...].astype(F32)
        + contract(mixed_ref[...], weight_ref[...], ((1,), (0,)))
        + line(vec_ref, BIAS_OUT)
        + mlp_ref[...]
        + line(vec_ref, BIAS_DOWN)
    )


def pass_kernel(
    upper_ref, stream_ref, own_ref, away_ref, out_ref, mlp_ref, vec_ref,
    next_vec_ref, weight_ref, keep, low, high, mixed_ref, next_ref, *outs,
):
    table_ref = (keep[...], low[...], high[...])
    stream = leave(upper_ref, stream_ref, own_ref, away_ref, out_ref, mlp_ref, vec_ref, mixed_ref)
    next_ref[...] = stream
    enter(upper_ref, stream, next_vec_ref, weight_ref, table_ref, *outs)


def last_kernel(
    upper_ref, stream_ref, own_ref, away_ref, out_ref, mlp_ref, vec_ref, mixed_ref, next_ref
):
    next_ref[...] = leave(
        upper_ref, stream_ref, own_ref, away_ref, out_ref, mlp_ref, vec_ref, mixed_ref
    ).astype(BF)


def mlp_kernel(two_ref, up_ref, down_ref, vec_ref, pre_ref, hidden_ref, mlp_ref):
    two = two_ref[...]
    for i in range(FF // D):
        cols = slice(i * D, (i + 1) * D)
        pre = contract(two, up_ref[:, cols], ((1,), (0,))) + line(vec_ref, BIAS_UP + i)
        pre_ref[:, cols] = pre
        hidden = (pre * phi_parts(pre)[0]).astype(BF)
        hidden_ref[:, cols] = hidden
        fresh = contract(hidden, down_ref[cols, :], ((1,), (0,)))
        mlp_ref[...] = fresh if i == 0 else mlp_ref[...] + fresh


def back(upper_ref, gradient, weight_ref, low_ref, mine_ref, theirs_ref):
    low = gradient.astype(BF)
    low_ref[...] = low
    mixed = contract(low, weight_ref[...], ((1,), (1,))).astype(BF)
    put_halves(upper_ref, mixed[:, :HALF], mixed[:, HALF:], mine_ref, theirs_ref)


def back_kernel(upper_ref, cotangent_ref, weight_ref, *outs):
    back(upper_ref, cotangent_ref[...].astype(F32), weight_ref, *outs)


def mlp_back_kernel(low_ref, pre_ref, up_ref, down_ref, grad_pre_ref, norm_ref):
    low = low_ref[...]
    for i in range(FF // D):
        cols = slice(i * D, (i + 1) * D)
        pre = pre_ref[:, cols]
        cumulative, density = phi_parts(pre)
        hidden = contract(low, down_ref[cols, :], ((1,), (1,)))
        grad_pre = (hidden * (cumulative + pre * density)).astype(BF)
        grad_pre_ref[:, cols] = grad_pre
        fresh = contract(grad_pre, up_ref[:, cols], ((1,), (1,)))
        norm_ref[...] = fresh if i == 0 else norm_ref[...] + fresh


def join_kernel(
    more, upper_ref, own_ref, back_ref, own_q, back_q, keep, low, high, weight_ref, stream_ref,
    vec_ref, two_ref, gradient_ref, *refs,
):
    table_ref = (keep[...], low[...], high[...])
    next_weight, refs = (refs[:1], refs[1:]) if more else ((), refs)
    joined_ref, sums_ref, next_ref, *outs = refs

    def turned(values):
        groups = [rotate_back(values[:, g * 128 : (g + 1) * 128], table_ref) for g in range(3)]
        return jnp.concatenate(groups, 1).astype(BF)

    put_joined(upper_ref, turned(own_q[...]), turned(back_q[...].astype(F32)), joined_ref, 0)
    put_joined(upper_ref, turned(own_ref[0]), turned(back_ref[0].astype(F32)), joined_ref, D)
    put_joined(upper_ref, own_ref[1].astype(BF), back_ref[1], joined_ref, 2 * D)
    one = contract(joined_ref[...], weight_ref[...], ((1,), (1,)))
    two = two_ref[...]
    unit, scale = norm_parts(stream_ref[...].astype(F32))
    sums = [jnp.sum(values, 0, keepdims=True) for values in (one * unit, one, two * unit, two)]
    sums_ref[...] = jnp.concatenate(sums + [jnp.zeros((12, D), F32)], 0).astype(BF)
    gradient = (
        gradient_ref[...].astype(F32)
        + norm_input_grad(one, line(vec_ref, GAIN_ONE), unit, scale)
        + norm_input_grad(two, line(vec_ref, GAIN_TWO), unit, scale)
    )
    next_ref[...] = gradient
    if more:
        back(upper_ref, gradient, next_weight[0], *outs)


def unpack_kernel(rows_ref, qkv_ref, out_ref, up_ref, down_ref):
    for i in range(3):
        qkv_ref[0, :, i * D : (i + 1) * D] = rows_ref[0, i * 192 : (i + 1) * 192, :].astype(F32)
    out_ref[0] = rows_ref[0, 576:768, :].astype(F32)
    for i in range(4):
        up_ref[0, :, i * D : (i + 1) * D] = rows_ref[
            0, 768 + i * 192 : 960 + i * 192, :
        ].astype(F32)
    down_ref[0] = rows_ref[0, 1536:, :].astype(F32)


def unpack(rows):
    shapes = [(192, 3 * D), (192, D), (192, FF), (D, D)]
    return pl.pallas_call(
        unpack_kernel,
        grid=(LAYERS,),
        out_shape=tuple(jax.ShapeDtypeStruct((LAYERS,) + shape, F32) for shape in shapes),
        in_specs=[pl.BlockSpec((1, 2304, D), lambda i: (i, 0, 0))],
        out_specs=tuple(pl.BlockSpec((1,) + shape, lambda i: (i, 0, 0)) for shape in shapes),
        compiler_params=pltpu.CompilerParams(vmem_limit_bytes=60 * 2**20),
        name="unpack",
    )(rows)


def dense(name, kernel, specs, outs, args, flops):
    shapes = tuple(
        jax.ShapeDtypeStruct((BLOCK, size) if isinstance(size, int) else size, kind)
        for size, kind in outs
    )
    return pl.pallas_call(
        kernel,
        out_shape=shapes,
        in_specs=specs,
        out_specs=(VM,) * len(shapes),
        compiler_params=pltpu.CompilerParams(vmem_limit_bytes=60 * 2**20),
        cost_estimate=pl.CostEstimate(
            flops=2 * BLOCK * flops, bytes_accessed=2 * flops, transcendentals=0
        ),
        name=name,
    )(*args)


def vector_kernel(table_ref, *out_refs):
    for layer_index, out_ref in enumerate(out_refs):
        at = slice(layer_index, layer_index + 1)
        for row in range(6):
            pieces = [table_ref[f, at, row * 192 : (row + 1) * 192] for f in range(4)]
            out_ref[row : row + 1, :] = jnp.concatenate(pieces, 1)
        joined = jnp.concatenate([table_ref[f, at, 1152:1728] for f in range(4)], 1)
        for i in range(3):
            out_ref[BIAS_QKV + i : BIAS_QKV + i + 1, :] = joined[:, i * D : (i + 1) * D]
        for f in range(4):
            out_ref[BIAS_UP + f : BIAS_UP + f + 1, :] = table_ref[f, at, 1728:2496]
        out_ref[13:, :] = jnp.zeros((3, D), F32)


def order_vectors(table):
    return pl.pallas_call(
        vector_kernel,
        out_shape=(jax.ShapeDtypeStruct((16, D), F32),) * LAYERS,
        in_specs=[VM],
        out_specs=(VM,) * LAYERS,
        name="order_vectors",
    )(table)


ENTER_OUTS = ((D, BF),) * 2 + ((HALF, BF),) * 6


def shards(
    tokens,
    cotangent,
    ln1_gain,
    ln1_bias,
    ln2_gain,
    ln2_bias,
    qkv_weight,
    qkv_bias,
    out_weight,
    out_bias,
    up_weight,
    up_bias,
    down_weight,
    down_bias,
):
    row_count = tokens.shape[1]
    fsdp = lax.axis_index("fsdp")
    ctx = lax.axis_index("ctx")
    ctx_word = ctx.astype(jnp.int32).reshape(1)
    upper = (ctx % 2).astype(jnp.int32).reshape(1)
    tables = turn_tables(ctx * row_count, row_count)

    vectors = (ln1_gain, ln1_bias, ln2_gain, ln2_bias, out_bias, down_bias, qkv_bias, up_bias)
    packed = jnp.concatenate(vectors, 1).astype(F32)
    packed = jnp.pad(packed, ((0, 8 - LAYERS), (0, 2560 - packed.shape[1])))
    first_weight, table = gather_first(qkv_weight, packed)
    vecs = order_vectors(table)
    qkv_full = [first_weight, None]
    gathered = [None] * LAYERS
    stream = tokens[0]
    entered = dense(
        "enter",
        enter_kernel,
        [SM] + [VM] * 6,
        ENTER_OUTS,
        (upper, stream, vecs[0], first_weight, *tables),
        D * 3 * D,
    )
    saved = []
    for layer_index in range(LAYERS):
        norm_one, norm_two, q_own, q_away, k_own, k_away, v_own, v_away = entered
        jobs = [(layer_index, out_weight), (layer_index, up_weight), (layer_index, down_weight)]
        if layer_index + 1 < LAYERS:
            jobs.append((layer_index + 1, qkv_weight))
        q_other, keys, values, w_out, w_up, w_down, *more = gather_pair(
            "gather_pair_%d" % layer_index,
            1 + layer_index,
            (q_away, k_away, v_away),
            (k_own, v_own),
            jobs,
        )
        if more:
            qkv_full[layer_index + 1] = more[0]
        gathered[layer_index] = (qkv_full[layer_index], w_out, w_up, w_down)
        keys = keys.reshape(BLOCKS * BLOCK, HALF)
        values = values.reshape(BLOCKS * BLOCK, HALF)
        mixed_own, mixed_away, turned, log_total = attend_forward(
            ctx_word, q_own, q_other, keys, values
        )
        mixed_back = mirrored(mixed_away)
        hidden_pre, hidden_low, mlp_branch = dense(
            "mlp",
            mlp_kernel,
            [VM] * 4,
            ((FF, F32), (FF, BF), (D, F32)),
            (norm_two, w_up, w_down, vecs[layer_index]),
            2 * D * FF,
        )
        before = stream
        common = (upper, stream, mixed_own, mixed_back, w_out, mlp_branch, vecs[layer_index])
        if more:
            mixed_low, stream, *entered = dense(
                "pass_on",
                pass_kernel,
                [SM] + [VM] * 11,
                ((D, BF), (D, F32)) + ENTER_OUTS,
                common + (vecs[layer_index + 1], more[0], *tables),
                D * 4 * D,
            )
        else:
            mixed_low, output = dense(
                "last", last_kernel, [SM] + [VM] * 6, ((D, BF), (D, BF)), common, D * D
            )
        lefts = (norm_one, mixed_low, norm_two)
        saved.append(
            (before, q_own, q_other, keys, values, turned, log_total, hidden_pre, hidden_low, lefts)
        )

    gradient = cotangent[0]
    waiting, early_rows, late_rows = (), [None] * 2, [None] * 2
    grad_low, grad_own, grad_away = dense(
        "back",
        back_kernel,
        [SM, VM, VM],
        ((D, BF), (HALF, BF), (HALF, BF)),
        (upper, gradient, gathered[LAYERS - 1][1]),
        D * D,
    )
    for layer_index in range(LAYERS - 1, -1, -1):
        w_qkv, w_out, w_up, w_down = gathered[layer_index]
        before, q_own, q_other, keys, values, turned, log_total, hidden_pre, hidden_low, lefts = (
            saved[layer_index]
        )
        grad_back = mirrored(grad_away)
        grad_pre, grad_norm_two = dense(
            "mlp_back",
            mlp_back_kernel,
            [VM] * 4,
            ((FF, BF), (D, F32)),
            (grad_low, hidden_pre, w_up, w_down),
            2 * D * FF,
        )
        gq_own, gq_away, grad_keys, grad_values = attend_backward(
            ctx_word, q_own, q_other, keys, values, grad_own, grad_back, turned, log_total
        )
        whole = (BLOCKS, BLOCK, HALF)
        own_pair, back_pair, back_query, *gathered_rows = scatter_pair(
            "scatter_pair_%d" % layer_index,
            3 + layer_index,
            grad_keys.reshape(whole),
            grad_values.reshape(whole),
            gq_away,
            hidden_low,
            lefts + (grad_low, grad_pre) + waiting,
        )
        early_rows[layer_index] = gathered_rows[:6]
        if waiting:
            late_rows[layer_index + 1] = gathered_rows[6:]
        going_on = layer_index > 0
        grad_joined, norm_sums, gradient, *outs = dense(
            "join_%d" % layer_index,
            functools.partial(join_kernel, going_on),
            [SM] + [VM] * (13 if going_on else 12),
            ((3 * D, BF), ((16, D), BF), (D, F32))
            + (((D, BF), (HALF, BF), (HALF, BF)) if going_on else ()),
            (
                upper,
                own_pair,
                back_pair,
                gq_own,
                back_query,
                *tables,
                w_qkv,
                before,
                vecs[layer_index],
                grad_norm_two,
                gradient,
            )
            + ((gathered[layer_index - 1][1],) if going_on else ()),
            D * 3 * D,
        )
        waiting = (grad_joined, norm_sums)
        if going_on:
            grad_low, grad_own, grad_away = outs
    late_rows[0] = gather_late(*waiting)
    fsdp_word = fsdp.astype(jnp.int32).reshape(1)
    packs, lines = [], []
    for layer_index in range(LAYERS):
        hidden, one, mixed, two, low, pre = early_rows[layer_index]
        joined, norms = late_rows[layer_index]
        rows, sums = weight_grads(fsdp_word, one, mixed, two, hidden, joined, low, pre, norms)
        packs.append(rows)
        lines.append(sums)
    summed, small = sum_over_ctx(*packs, *lines)

    def own_part(vectors, width):
        return lax.dynamic_slice_in_dim(vectors, fsdp * width, width, vectors.ndim - 1)

    bias_sum = own_part(small[:, 0], 192)
    joined_sum = own_part(small[:, 1:4].reshape(LAYERS, 3 * D), 576)
    up_sum = own_part(small[:, 4:8].reshape(LAYERS, 4 * D), D)
    norm_sums = own_part(small[:, 8:12], 192)
    qkv_grad, out_grad, up_grad, down_grad = unpack(summed.reshape(LAYERS, 2304, D))
    return (
        output[None],
        gradient[None],
        norm_sums[:, 0],
        norm_sums[:, 1],
        norm_sums[:, 2],
        norm_sums[:, 3],
        qkv_grad,
        joined_sum,
        out_grad,
        bias_sum,
        up_grad,
        up_sum,
        down_grad,
        bias_sum,
    )


def solution(mesh):
    matrix, vector = P(None, "fsdp", None), P(None, "fsdp")
    rows = P("fsdp", "ctx", None)
    params = (
        vector,
        vector,
        vector,
        vector,
        matrix,
        vector,
        matrix,
        vector,
        matrix,
        vector,
        matrix,
        vector,
    )
    return jax.shard_map(
        shards,
        mesh=mesh,
        in_specs=(rows, rows) + params,
        out_specs=(rows, rows) + params,
        check_vma=False,
    )
```

```python
import functools

import jax
import jax.numpy as jnp
from jax import lax
from jax.experimental import pallas as pl
from jax.experimental.pallas import tpu as pltpu
from jax.sharding import PartitionSpec as P

D = 768
HEADS = 12
HEAD_DIM = 64
FF = 3072
ROTARY = 16
LAYERS = 2
HALF = 384
BLOCK = 128
BLOCKS = 32
TILE = 512
PAIRS = 3

epsilon = 1e-05
masked_score = -1e30
MESH = pl.DeviceIdType.MESH
BF = jnp.bfloat16
F32 = jnp.float32


def mirrored(values):
    pairs = [(f * 32 + c, f * 32 + 31 - c) for f in range(4) for c in range(32)]
    return lax.ppermute(values, ("fsdp", "ctx"), pairs)


class Place:
    def __init__(self):
        self.fsdp = lax.axis_index("fsdp")
        self.ctx = lax.axis_index("ctx")
        self.y, self.z, self.h = self.ctx // 8, (self.ctx // 2) % 4, self.ctx % 2
        self.x_lo, self.core = self.fsdp // 2, self.fsdp % 2
        self.beside = (self.fsdp + 1 - 2 * self.core, self.ctx)
        self.mirror = (self.fsdp, BLOCKS - 1 - self.ctx)
        self.half = (self.fsdp, self.ctx + 1 - 2 * self.h)

    def along_x(self, step):
        x = (2 * self.h + self.x_lo + step) % 4
        return (2 * (x % 2) + self.core, self.y * 8 + self.z * 2 + x // 2)

    def ctx_at(self, dy, dz):
        return ((self.y + dy) % 4) * 8 + ((self.z + dz) % 4) * 2 + self.h

    def ring(self, t, da, db):
        return self.ctx_at(da, db) if t == 0 else self.ctx_at(db, da)

    def near(self, t, axis, sign):
        steps = (sign, 0) if axis == 0 else (0, sign)
        return (self.fsdp, self.ring(t, *steps))

    def around(self):
        return [self.near(0, axis, sign) for axis in (0, 1) for sign in (1, -1)]

    def greet(self, partners):
        barrier = pltpu.get_barrier_semaphore()
        for partner in partners:
            pl.semaphore_signal(barrier, inc=1, device_id=partner, device_id_type=MESH)
        pl.semaphore_wait(barrier, len(partners))


class Wire:
    def __init__(self, send_sem, recv_sem, local_sem=None):
        self.send_sem, self.recv_sem, self.local_sem = send_sem, recv_sem, local_sem
        self.sent, self.local, self.bounced = [], [], []

    def push(self, source, target, partner):
        number = len(self.sent)
        copy = pltpu.make_async_remote_copy(
            src_ref=source,
            dst_ref=target,
            send_sem=self.send_sem.at[number],
            recv_sem=self.recv_sem.at[number],
            device_id=partner,
            device_id_type=MESH,
        )
        copy.start()
        self.sent.append(copy)
        return copy

    def keep(self, source, target, bounce=None):
        if bounce is None:
            copy = pltpu.make_async_copy(source, target, self.local_sem.at[len(self.local)])
        else:
            copy = pltpu.make_async_copy(source, bounce, self.local_sem.at[len(self.local)])
            self.bounced.append((len(self.local), bounce, target))
        copy.start()
        self.local.append(copy)

    def flush(self):
        for number, bounce, target in self.bounced:
            self.local[number].wait()
            copy = pltpu.make_async_copy(bounce, target, self.local_sem.at[number])
            copy.start()
            self.local[number] = copy
        self.bounced = []

    def drain(self):
        for copy in self.sent:
            copy.wait_send()
        for copy in self.local:
            copy.wait()


def share_param(place, wire, source, target, bounce):
    rows = source.shape[0]
    cut = rows // 2
    mine, far = place.fsdp * rows, ((place.fsdp + 2) % 4) * rows
    parts = [(0, cut, 1), (cut, cut, 3)]
    across = [
        wire.push(
            source.at[pl.ds(start, count)],
            target.at[pl.ds(mine + start, count)],
            place.along_x(step),
        )
        for start, count, step in parts
    ]
    beside = wire.push(source, target.at[pl.ds(mine, rows)], place.beside)
    wire.keep(source, target.at[pl.ds(mine, rows)], bounce)
    last = [beside]

    def onward(copy, start, count):
        copy.wait_recv()
        spot = target.at[pl.ds(far + start, count)]
        last.append(wire.push(spot, spot, place.beside))

    steps = [
        functools.partial(onward, copy, start, count)
        for copy, (start, count, _) in zip(across, parts)
    ]
    return steps, last


def share_rows(place, wire, source, target):
    rows = source.shape[0]
    cut = rows // 2
    parts = [(0, cut, 1), (cut, cut, 3)] if rows % 32 == 0 else [(0, rows, 1)]
    across = [
        wire.push(
            source.at[pl.ds(start, count)],
            target.at[pl.ds(2 * rows + start, count)],
            place.along_x(step),
        )
        for start, count, step in parts
    ]
    last = [wire.push(source, target.at[pl.ds(rows, rows)], place.beside)]
    wire.keep(source, target.at[pl.ds(0, rows)])

    def onward(copy, start, count):
        copy.wait_recv()
        last.append(
            wire.push(
                target.at[pl.ds(2 * rows + start, count)],
                target.at[pl.ds(3 * rows + start, count)],
                place.beside,
            )
        )

    steps = [
        functools.partial(onward, copy, start, count)
        for copy, (start, count, _) in zip(across, parts)
    ]
    return steps, last


def share_columns(place, wire, source, target, stage):
    rows = source.shape[0]
    cut = rows // 2
    fsdp, core = place.fsdp, place.core
    parts = [(0, cut, 1), (cut, cut, 3)]

    def panel(start, count, shard):
        return source.at[pl.ds(start, count), pl.ds(pl.multiple_of(shard * D, D), D)]

    passing, last = [], []
    for start, count, step in parts:
        passing.append(
            wire.push(
                panel(start, count, 3 - fsdp),
                stage.at[pl.ds(start, count)],
                place.along_x(step),
            )
        )
    for start, count, step in parts:
        last.append(
            wire.push(
                panel(start, count, (fsdp + 2) % 4),
                target.at[pl.ds(2 * rows + start, count)],
                place.along_x(step),
            )
        )
    last.append(
        wire.push(
            panel(0, rows, fsdp + 1 - 2 * core), target.at[pl.ds(rows, rows)], place.beside
        )
    )
    wire.keep(panel(0, rows, fsdp), target.at[pl.ds(0, rows)])

    def onward(copy, start, count):
        copy.wait_recv()
        last.append(
            wire.push(
                stage.at[pl.ds(start, count)],
                target.at[pl.ds(3 * rows + start, count)],
                place.beside,
            )
        )

    steps = [
        functools.partial(onward, copy, start, count)
        for copy, (start, count, _) in zip(passing, parts)
    ]
    return steps, last


def spread(place, wire, own, spot, ready, between=()):
    between = list(between)
    arrivals = {}

    def push(t, da, db, b, axis, sign):
        target = spot(t, place.ring(t, da, db), b)
        source = own(t, b) if da == 0 and db == 0 else target
        sa, sb = (sign, 0) if axis == 0 else (0, sign)
        arrivals[t, (da - sa) % 4, (db - sb) % 4, b] = wire.push(
            source, target, place.near(t, axis, sign)
        )

    def landed(t, da, db):
        for b in (0, 1):
            arrivals[t, da, db, b].wait_recv()

    def pause():
        if between:
            between.pop(0)()

    for b in (0, 1):
        for t in (0, 1):
            ready(t, b)
            for axis in (0, 1):
                for sign in (1, -1):
                    push(t, 0, 0, b, axis, sign)
    for da, keep, onward in ((1, 0, -1), (3, 1, 1)):
        for t in (0, 1):
            landed(t, da, 0)
            push(t, da, 0, keep, 0, onward)
            for sign in (1, -1):
                for b in (0, 1):
                    push(t, da, 0, b, 1, sign)
    for db, keep, onward in ((1, 0, -1), (3, 1, 1)):
        for t in (0, 1):
            landed(t, 0, db)
            push(t, 0, db, keep, 1, onward)
    for t in (0, 1):
        landed(t, 2, 0)
        for sign in (1, -1):
            for b in (0, 1):
                push(t, 2, 0, b, 1, sign)
    pause()
    for da in (1, 3, 2):
        for db, keep, onward in ((1, 0, -1), (3, 1, 1)):
            for t in (0, 1):
                landed(t, da, db)
                push(t, da, db, keep, 1, onward)
    while between:
        pause()
    for da in (0, 1, 3, 2):
        for t in (0, 1):
            landed(t, da, 2)


ANY = pl.BlockSpec(memory_space=pl.ANY)
VM = pl.BlockSpec(memory_space=pltpu.VMEM)
SM = pl.BlockSpec(memory_space=pltpu.SMEM)


def room(*shape):
    return pltpu.VMEM(shape, BF)


def sems(count, local):
    return [
        pltpu.SemaphoreType.DMA((count,)),
        pltpu.SemaphoreType.DMA((count,)),
        pltpu.SemaphoreType.DMA((local,)),
    ]


def full_shape(shard):
    return jax.ShapeDtypeStruct((4 * shard.shape[-2], shard.shape[-1]), BF)


def first_kernel(weight_ref, vector_ref, weight_out, vector_out, bounce, *sem):
    place, wire = Place(), Wire(*sem)
    place.greet([place.beside, place.along_x(1), place.along_x(3)])
    far = vector_out.at[(place.fsdp + 2) % 4]
    across = wire.push(vector_ref, vector_out.at[place.fsdp], place.along_x(1))
    last = [wire.push(vector_ref, vector_out.at[place.fsdp], place.beside)]
    wire.keep(vector_ref, vector_out.at[place.fsdp])
    steps, ends = share_param(place, wire, weight_ref.at[0], weight_out, bounce)
    wire.flush()
    across.wait_recv()
    last.append(wire.push(far, far, place.beside))
    for step in steps:
        step()
    for copy in last + ends:
        copy.wait_recv()
    wire.drain()


def gather_first(weight, vectors):
    return pl.pallas_call(
        first_kernel,
        out_shape=(full_shape(weight), jax.ShapeDtypeStruct((4,) + vectors.shape, F32)),
        in_specs=[ANY, VM],
        out_specs=(ANY, ANY),
        scratch_shapes=[room(*weight.shape[1:])] + sems(16, 4),
        compiler_params=pltpu.CompilerParams(
            collective_id=0, has_side_effects=True, vmem_limit_bytes=60 * 2**20
        ),
        name="gather_first",
    )(weight, vectors)


def gather_kernel(jobs, q_ref, k_ref, v_ref, k_own, v_own, *refs):
    count = len(jobs)
    weights, refs = refs[:count], refs[count:]
    q_out, k_out, v_out = refs[:3]
    weights_out, refs = refs[3 : 3 + count], refs[3 + count :]
    bounces, refs = refs[:count], refs[count:]
    place, wire = Place(), Wire(*refs)
    place.greet(
        place.around() + [place.mirror, place.beside, place.along_x(1), place.along_x(3)]
    )
    ins, outs = (k_own, v_own), (k_out, v_out)
    ctx = place.ctx
    swapped = [
        wire.push(source, out.at[ctx], place.mirror) for source, out in zip((k_ref, v_ref), outs)
    ]
    for t in (0, 1):
        wire.keep(ins[t], outs[t].at[ctx])
    work = []

    def ready(t, b):
        if b == 1:
            if t == 0:
                for layer, weight, target, bounce in zip(jobs, weights, weights_out, bounces):
                    work.append(share_param(place, wire, weight.at[layer], target, bounce))
            swapped[t].wait_recv()
            if t == 1:
                swapped.append(wire.push(q_ref, q_out, place.mirror))

    def spot(t, origin, b):
        return outs[t].at[origin if b == 0 else BLOCKS - 1 - origin]

    def own(t, b):
        return ins[t] if b == 0 else spot(t, ctx, 1)

    def onward(number):
        for steps, _ in work:
            for step in steps[number : number + 1]:
                step()

    spread(
        place,
        wire,
        own,
        spot,
        ready,
        [wire.flush, functools.partial(onward, 0), functools.partial(onward, 1)],
    )
    swapped[2].wait_recv()
    for _, last in work:
        for copy in last:
            copy.wait_recv()
    wire.drain()


def gather_pair(name, number, away, own, jobs):
    layers = [layer for layer, _ in jobs]
    weights = [weight for _, weight in jobs]
    whole = jax.ShapeDtypeStruct((BLOCKS, BLOCK, HALF), BF)
    return pl.pallas_call(
        functools.partial(gather_kernel, layers),
        out_shape=(jax.ShapeDtypeStruct((BLOCK, HALF), BF), whole, whole)
        + tuple(full_shape(weight) for weight in weights),
        in_specs=[VM] * 5 + [ANY] * len(jobs),
        out_specs=(ANY,) * (3 + len(jobs)),
        scratch_shapes=[room(*weight.shape[1:]) for weight in weights] + sems(96, 8),
        compiler_params=pltpu.CompilerParams(
            collective_id=number, has_side_effects=True, vmem_limit_bytes=60 * 2**20
        ),
        name=name,
    )(*away, *own, *weights)


def scatter_kernel(count, gk_ref, gv_ref, gq_ref, hidden_ref, *refs):
    sources, refs = refs[:count], refs[count:]
    own_out, back_out, back_q, hidden_out = refs[:4]
    targets, refs = refs[4 : 4 + count], refs[4 + count :]
    far, near, mix, total, last_far, last_near, last_mix, leave, stage = refs[:9]
    place, wire = Place(), Wire(*refs[9:])
    place.greet(
        place.around() + [place.mirror, place.beside, place.along_x(1), place.along_x(3)]
    )
    ins = (gk_ref, gv_ref)

    def block_at(t, da, db, b):
        origin = place.ring(t, da, db)
        return origin if b == 0 else BLOCKS - 1 - origin

    order = [(da, t) for da in (2, 1, 3, 0) for t in (0, 1)]
    way = {0: 1, 1: -1}
    first, second, loose = {}, {}, {}
    for b in (1, 0):
        for da, t in order:
            first[t, da, b] = wire.push(
                ins[t].at[block_at(t, da, 2, b)], far.at[t, da, b], place.near(t, 1, way[b])
            )
    swapped = [wire.push(gq_ref, back_q, place.mirror)]
    for b in (1, 0):
        for da, t in order:
            loose[t, da, b] = wire.push(
                ins[t].at[block_at(t, da, -way[b], b)],
                near.at[t, da, 1, b],
                place.near(t, 1, -way[b]),
            )
    work = []
    for b in (1, 0):
        if b == 0:
            work.append(share_columns(place, wire, hidden_ref, hidden_out, stage))
            for source, target in zip(sources, targets):
                work.append(share_rows(place, wire, source, target))
        for da, t in order:
            first[t, da, b].wait_recv()
            mix[t, da, b] = (
                ins[t][block_at(t, da, way[b], b)].astype(F32) + far[t, da, b].astype(F32)
            ).astype(BF)
            second[t, da, b] = wire.push(
                mix.at[t, da, b], near.at[t, da, 0, b], place.near(t, 1, way[b])
            )

    def settle(t, da, b):
        loose[t, da, b].wait_recv()
        second[t, da, b].wait_recv()
        total[t, da, b] = (
            ins[t][block_at(t, da, 0, b)].astype(F32)
            + near[t, da, 0, b].astype(F32)
            + near[t, da, 1, b].astype(F32)
        ).astype(BF)

    third, fourth = {}, {}
    for b in (1, 0):
        for t in (0, 1):
            settle(t, 2, b)
            third[t, b] = wire.push(
                total.at[t, 2, b], last_far.at[t, b], place.near(t, 0, way[b])
            )
        for t in (0, 1):
            settle(t, 1, b)
            settle(t, 3, b)
            fourth[t, b] = [
                wire.push(
                    total.at[t, -way[b] % 4, b], last_near.at[t, 1, b], place.near(t, 0, -way[b])
                )
            ]
        for t in (0, 1):
            third[t, b].wait_recv()
            last_mix[t, b] = (
                total[t, way[b] % 4, b].astype(F32) + last_far[t, b].astype(F32)
            ).astype(BF)
            fourth[t, b].append(
                wire.push(last_mix.at[t, b], last_near.at[t, 0, b], place.near(t, 0, way[b]))
            )
        for t in (0, 1):
            settle(t, 0, b)

    def final(t, b):
        for copy in fourth[t, b]:
            copy.wait_recv()
        return (
            total[t, 0, b].astype(F32)
            + last_near[t, 0, b].astype(F32)
            + last_near[t, 1, b].astype(F32)
        )

    for t in (0, 1):
        leave[t] = final(t, 1).astype(BF)
        swapped.append(wire.push(leave.at[t], back_out.at[t], place.mirror))
    for steps, _ in work:
        for step in steps:
            step()
    for t in (0, 1):
        own_out[t] = final(t, 0)
    for _, last in work:
        for copy in last:
            copy.wait_recv()
    for copy in swapped:
        copy.wait_recv()
    wire.drain()


def rows_shape(source):
    return jax.ShapeDtypeStruct((4 * source.shape[0], source.shape[1]), BF)


def scatter_pair(name, number, grad_keys, grad_values, away, hidden, sources):
    return pl.pallas_call(
        functools.partial(scatter_kernel, len(sources)),
        out_shape=(
            jax.ShapeDtypeStruct((2, BLOCK, HALF), F32),
            jax.ShapeDtypeStruct((2, BLOCK, HALF), BF),
            jax.ShapeDtypeStruct((BLOCK, HALF), BF),
            jax.ShapeDtypeStruct((4 * BLOCK, D), BF),
        )
        + tuple(rows_shape(source) for source in sources),
        in_specs=[VM] * (4 + len(sources)),
        out_specs=(VM,) + (ANY,) * (3 + len(sources)),
        scratch_shapes=[
            room(2, 4, 2, BLOCK, HALF),
            room(2, 4, 2, 2, BLOCK, HALF),
            room(2, 4, 2, BLOCK, HALF),
            room(2, 4, 2, BLOCK, HALF),
            room(2, 2, BLOCK, HALF),
            room(2, 2, 2, BLOCK, HALF),
            room(2, 2, BLOCK, HALF),
            room(2, BLOCK, HALF),
            room(BLOCK, D),
        ]
        + sems(128, 12),
        compiler_params=pltpu.CompilerParams(
            collective_id=number, has_side_effects=True, vmem_limit_bytes=60 * 2**20
        ),
        name=name,
    )(grad_keys, grad_values, away, hidden, *sources)


def late_kernel(one_ref, two_ref, one_out, two_out, *sem):
    place, wire = Place(), Wire(*sem)
    place.greet([place.beside, place.along_x(1), place.along_x(3)])
    work = [
        share_rows(place, wire, one_ref, one_out),
        share_rows(place, wire, two_ref, two_out),
    ]
    for steps, _ in work:
        for step in steps:
            step()
    for _, last in work:
        for copy in last:
            copy.wait_recv()
    wire.drain()


def gather_late(one, two):
    return pl.pallas_call(
        late_kernel,
        out_shape=(rows_shape(one), rows_shape(two)),
        in_specs=[VM] * 2,
        out_specs=(ANY,) * 2,
        scratch_shapes=sems(16, 4),
        compiler_params=pltpu.CompilerParams(collective_id=5, has_side_effects=True),
        name="gather_late",
    )(one, two)


PIECE = 96
CUT = 48
PACK = 32 * PIECE


def sum_kernel(
    rows_ref, small_ref, out_ref, small_out,
    far, mix, near, total, far_two, mix_two, near_two, part, other, final, small, heard, *sem,
):
    place, wire = Place(), Wire(*sem)
    y, z, h = place.y, place.z, place.h
    turns = [
        (place.fsdp, (y + 1 - 2 * (y % 2)) * 8 + z * 2 + h),
        (place.fsdp, ((y + 2) % 4) * 8 + z * 2 + h),
        (place.fsdp, y * 8 + (z + 1 - 2 * (z % 2)) * 2 + h),
        (place.fsdp, y * 8 + ((z + 2) % 4) * 2 + h),
        place.half,
    ]
    place.greet(place.around() + [turns[1], turns[3], place.half])
    ins = (rows_ref.at[0], rows_ref.at[1])
    parts = {0: pl.ds(0, CUT), 1: pl.ds(CUT, PIECE - CUT)}

    def chunk(t, da, db):
        origin = place.ring(t, da, db)
        return origin // 2

    def plus(*terms):
        result = terms[0].astype(F32)
        for term in terms[1:]:
            result = result + term.astype(F32)
        return result.astype(BF)

    small[...] = small_ref[...]
    passing = wire.push(small, heard.at[0], turns[0])
    order = (2, 1, 3, 0)
    way = {2: 1, 1: 1, 3: -1, 0: -1}
    first, second, loose = {}, {}, {}
    for db in order:
        for t in (0, 1):
            first[t, db] = wire.push(
                ins[t].at[chunk(t, 2, db)], far.at[t, db], place.near(t, 0, way[db])
            )
    for db in order:
        for t in (0, 1):
            loose[t, db] = wire.push(
                ins[t].at[chunk(t, -way[db], db)], near.at[t, db, 1], place.near(t, 0, -way[db])
            )
    for db in order:
        for t in (0, 1):
            first[t, db].wait_recv()
            mix[t, db] = plus(ins[t][chunk(t, way[db], db)], far[t, db])
            second[t, db] = wire.push(mix.at[t, db], near.at[t, db, 0], place.near(t, 0, way[db]))

    def hear(step):
        wire.sent[step_numbers[-1]].wait_send()
        wire.sent[step_numbers[-1]].wait_recv()
        small[...] += heard[step]
        waited.add(step_numbers[-1])
        if step < 4:
            step_numbers.append(len(wire.sent))
            wire.push(small, heard.at[step + 1], turns[step + 1])

    step_numbers, waited = [0], set()

    def settle(t, db):
        second[t, db].wait_recv()
        loose[t, db].wait_recv()
        total[t, db] = plus(ins[t][chunk(t, 0, db)], near[t, db, 0], near[t, db, 1])

    third, fourth = {}, {}
    for t in (0, 1):
        settle(t, 2)
        third[t] = [
            wire.push(
                total.at[t, 2, parts[b]], far_two.at[t, parts[b]], place.near(t, 1, sign)
            )
            for b, sign in ((0, 1), (1, -1))
        ]
    hear(0)
    for t in (0, 1):
        fourth[t] = []
        for b, sign, db in ((0, 1, 1), (1, -1, 3)):
            settle(t, db)
            fourth[t].append(
                wire.push(
                    total.at[t, db, parts[1 - b]],
                    near_two.at[t, b, parts[1 - b]],
                    place.near(t, 1, sign),
                )
            )
    hear(1)
    for t in (0, 1):
        for b, sign, db in ((0, 1, 1), (1, -1, 3)):
            third[t][b].wait_recv()
            mix_two[t, parts[b]] = plus(total[t, db, parts[b]], far_two[t, parts[b]])
            fourth[t].append(
                wire.push(
                    mix_two.at[t, parts[b]], near_two.at[t, b, parts[b]], place.near(t, 1, sign)
                )
            )
    hear(2)
    swapped = []
    for t in (0, 1):
        settle(t, 0)
        for copy in fourth[t]:
            copy.wait_recv()
        part[t] = plus(total[t, 0], near_two[t, 0], near_two[t, 1])
        swapped.append(wire.push(part.at[t], other.at[t], place.half))
    hear(3)

    def spot(t, origin, b):
        return out_ref.at[1 - t, origin // 2, parts[b]]

    def own(t, b):
        return final.at[1 - t, parts[b]]

    def ready(t, b):
        if b == 0:
            swapped[1 - t].wait_recv()
            final[1 - t] = plus(part[1 - t], other[1 - t])
            wire.keep(final.at[1 - t], out_ref.at[1 - t, place.ctx // 2])

    spread(place, wire, own, spot, ready)
    hear(4)
    small_out[...] = small[...]
    for number, copy in enumerate(wire.sent):
        if number not in waited:
            copy.wait_send()
    for copy in wire.local:
        copy.wait()


def sum_over_ctx(rows, small):
    shape = (2, 16, PIECE, D)
    small_shape = small.shape
    return pl.pallas_call(
        sum_kernel,
        out_shape=(
            jax.ShapeDtypeStruct(shape, BF),
            jax.ShapeDtypeStruct(small_shape, F32),
        ),
        in_specs=[VM] * 2,
        out_specs=(ANY, VM),
        scratch_shapes=[
            room(2, 4, PIECE, D),
            room(2, 4, PIECE, D),
            room(2, 4, 2, PIECE, D),
            room(2, 4, PIECE, D),
            room(2, PIECE, D),
            room(2, PIECE, D),
            room(2, 2, PIECE, D),
            room(2, PIECE, D),
            room(2, PIECE, D),
            room(2, PIECE, D),
            pltpu.VMEM(small_shape, F32),
            pltpu.VMEM((5,) + small_shape, F32),
        ]
        + sems(128, 4),
        compiler_params=pltpu.CompilerParams(
            collective_id=6, has_side_effects=True, vmem_limit_bytes=60 * 2**20
        ),
        name="sum_over_ctx",
    )(rows.reshape(shape), small)


def fetch(sources, buffers, sem):
    copies = []
    for number, (source, buffer) in enumerate(zip(sources, buffers)):
        copy = pltpu.make_async_copy(source, buffer, sem.at[number])
        copy.start()
        copies.append(copy)

    def take(number):
        copies[number].wait()
        return buffers[number]

    return take


def own_columns(fsdp_ref, values, turned):
    turned[...] = jnp.transpose(values)
    return turned[pl.ds(pl.multiple_of(fsdp_ref[0] * 192, 64), 192), :]


def column_sums(right):
    return contract(jnp.ones((8, right.shape[0]), BF), right, ((1,), (0,)))[:1]


def panel(rows_ref, first, left, right):
    rows_ref[first : first + left.shape[0], :] = contract(left, right, ((1,), (0,))).astype(BF)


def early_panels(fsdp_ref, take, rows_ref, turned, put):
    low = take(0)[...]
    left = own_columns(fsdp_ref, take(1)[...], turned)
    panel(rows_ref, 0, left, low)
    put(0, column_sums(low))
    turned[...] = jnp.transpose(take(2)[...])
    panel(rows_ref, 960, turned[...], low)
    left = own_columns(fsdp_ref, take(3)[...], turned)
    pre = take(4)
    for i in range(4):
        right = pre[:, i * D : (i + 1) * D]
        panel(rows_ref, 192 + i * 192, left, right)
        put(1 + i, column_sums(right))


def late_panels(fsdp_ref, one, joined, rows_ref, first, turned, put):
    left = own_columns(fsdp_ref, one, turned)
    for i in range(3):
        right = joined[:, i * D : (i + 1) * D]
        panel(rows_ref, first + i * 192, left, right)
        put(i, column_sums(right))


def early_kernel(fsdp_ref, *refs):
    sources, (rows_ref, sums_ref), buffers = refs[:5], refs[5:7], refs[7:12]
    turned, sem = refs[12:]
    take = fetch(sources, buffers, sem)
    sums_ref[...] = jnp.zeros_like(sums_ref)

    def put(i, row):
        sums_ref[i : i + 1, :] = row

    early_panels(fsdp_ref, take, rows_ref, turned, put)


def rooms(arrays):
    return [pltpu.VMEM(array.shape, array.dtype) for array in arrays]


def early_grads(fsdp, low, mixed, hidden, two, pre):
    arrays = (low, mixed, hidden, two, pre)
    return pl.pallas_call(
        early_kernel,
        out_shape=(jax.ShapeDtypeStruct((1728, D), BF), jax.ShapeDtypeStruct((8, D), F32)),
        in_specs=[SM] + [ANY] * 5,
        out_specs=(VM, VM),
        scratch_shapes=rooms(arrays) + [room(D, low.shape[0]), pltpu.SemaphoreType.DMA((5,))],
        compiler_params=pltpu.CompilerParams(vmem_limit_bytes=60 * 2**20),
        cost_estimate=pl.CostEstimate(
            flops=2 * 512 * 1327104, bytes_accessed=9 * 2**20, transcendentals=0
        ),
        name="early_grads",
    )(fsdp, *arrays)


def last_grads_kernel(fsdp_ref, norm_one, norm_two, sums_in, *refs):
    sources, (rows_ref, sums_ref), buffers = refs[:9], refs[9:11], refs[11:20]
    turned, sem = refs[20:]
    take = fetch(sources, buffers, sem)
    sums_ref[...] = jnp.zeros_like(sums_ref)

    def put_early(i, row):
        at = 0 if i == 0 else 3 + i
        sums_ref[0, at : at + 1, :] = row

    early_panels(fsdp_ref, take, rows_ref, turned, put_early)
    for layer_index in range(LAYERS):

        def put_late(i, row):
            sums_ref[layer_index, 1 + i : 2 + i, :] = row

        one, joined = take(5 + 2 * layer_index)[...], take(6 + 2 * layer_index)
        late_panels(
            fsdp_ref, one, joined, rows_ref, 1728 + 576 * layer_index, turned, put_late
        )
        norm_ref = (norm_one, norm_two)[layer_index]
        norms = norm_ref[0:16, :].astype(F32)
        for i in range(1, 4):
            norms = norms + norm_ref[i * 16 : (i + 1) * 16, :].astype(F32)
        sums_ref[layer_index, 8:16, :] = norms[:8]
    rows_ref[2880:, :] = jnp.zeros((PACK - 2880, D), BF)
    sums_ref[1, 0:1, :] = sums_in[0:1, :]
    sums_ref[1, 4:8, :] = sums_in[1:5, :]


def last_grads(fsdp, norm_one, norm_two, sums, arrays):
    return pl.pallas_call(
        last_grads_kernel,
        out_shape=(
            jax.ShapeDtypeStruct((PACK, D), BF),
            jax.ShapeDtypeStruct((LAYERS, 16, D), F32),
        ),
        in_specs=[SM, VM, VM, VM] + [ANY] * 9,
        out_specs=(VM, VM),
        scratch_shapes=rooms(arrays)
        + [room(D, arrays[0].shape[0]), pltpu.SemaphoreType.DMA((9,))],
        compiler_params=pltpu.CompilerParams(vmem_limit_bytes=60 * 2**20),
        cost_estimate=pl.CostEstimate(
            flops=2 * 512 * 2211840, bytes_accessed=16 * 2**20, transcendentals=0
        ),
        name="last_grads",
    )(fsdp, norm_one, norm_two, sums, *arrays)


def pair_rows(values):
    lane = lax.broadcasted_iota(jnp.int32, values.shape, 1)
    zero = jnp.zeros_like(values)
    return jnp.concatenate(
        [jnp.where(lane < HEAD_DIM, values, zero), jnp.where(lane >= HEAD_DIM, values, zero)], 0
    )


def contract(left, right, dims):
    return lax.dot_general(left, right, (dims, ((), ())), preferred_element_type=F32)


def allowed_at(tile, block):
    key = tile * TILE + lax.broadcasted_iota(jnp.int32, (TILE, 2 * BLOCK), 0)
    query = block * BLOCK + lax.broadcasted_iota(jnp.int32, (TILE, 2 * BLOCK), 1) % BLOCK
    return key <= query


def forward_kernel(
    ctx_ref, q_own, q_away, k_ref, v_ref, mixed_own, mixed_away, turned_ref, log_ref, top, mass, acc
):
    ctx = ctx_ref[0]
    for b in (0, 1):
        block = ctx if b == 0 else BLOCKS - 1 - ctx
        rows = slice(b * BLOCK, (b + 1) * BLOCK)
        q_ref, mixed_ref = (q_own, mixed_own) if b == 0 else (q_away, mixed_away)
        queries = [
            pair_rows(q_ref[:, p * 128 : (p + 1) * 128] * jnp.asarray(0.125, BF))
            for p in range(PAIRS)
        ]

        def step(tile, masked):
            start = pl.multiple_of(tile * TILE, TILE)
            for p in range(PAIRS):
                cols = slice(p * 128, (p + 1) * 128)
                scores = contract(k_ref[pl.ds(start, TILE), cols], queries[p], ((1,), (1,)))
                if masked:
                    scores = jnp.where(allowed_at(tile, block), scores, masked_score)
                    new_top = jnp.max(scores, 0, keepdims=True)
                else:
                    old_top = top[p : p + 1, :]
                    new_top = jnp.maximum(old_top, jnp.max(scores, 0, keepdims=True))
                weights = jnp.exp(scores - new_top)
                fresh_mass = jnp.sum(weights, 0, keepdims=True)
                fresh = contract(
                    v_ref[pl.ds(start, TILE), cols], weights.astype(BF), ((0,), (0,))
                )
                if not masked:
                    fade = jnp.exp(old_top - new_top)
                    fresh_mass = fresh_mass + mass[p : p + 1, :] * fade
                    fresh = fresh + acc[p] * fade
                top[p : p + 1, :] = new_top
                mass[p : p + 1, :] = fresh_mass
                acc[p] = fresh

        step(block // 4, True)

        @pl.loop(0, block // 4)
        def _(tile):
            step(tile, False)

        for p in range(PAIRS):
            cols = slice(p * 128, (p + 1) * 128)
            done = acc[p] / mass[p : p + 1, :]
            turned = jnp.concatenate([done[:HEAD_DIM, :BLOCK], done[HEAD_DIM:, BLOCK:]], 0)
            turned_ref[cols, rows] = turned
            mixed_ref[:, cols] = jnp.transpose(turned).astype(BF)
            row = b * PAIRS + p
            log_ref[row : row + 1, :] = top[p : p + 1, :] + jnp.log(mass[p : p + 1, :])


def attend_forward(ctx, own, away, keys, values):
    return pl.pallas_call(
        forward_kernel,
        out_shape=(
            jax.ShapeDtypeStruct((BLOCK, HALF), BF),
            jax.ShapeDtypeStruct((BLOCK, HALF), BF),
            jax.ShapeDtypeStruct((HALF, 2 * BLOCK), F32),
            jax.ShapeDtypeStruct((8, 2 * BLOCK), F32),
        ),
        in_specs=[SM, VM, VM, VM, VM],
        out_specs=(VM, VM, VM, VM),
        scratch_shapes=[
            pltpu.VMEM((8, 2 * BLOCK), F32),
            pltpu.VMEM((8, 2 * BLOCK), F32),
            pltpu.VMEM((PAIRS, 128, 2 * BLOCK), F32),
        ],
        compiler_params=pltpu.CompilerParams(vmem_limit_bytes=60 * 2**20),
        cost_estimate=pl.CostEstimate(
            flops=4 * 33 * 128 * 128 * 6 * 128, bytes_accessed=8 * 2**20, transcendentals=33 * 128 * 128 * 6
        ),
        name="attend_forward",
    )(ctx, own, away, keys, values)


def backward_kernel(
    ctx_ref, q_own, q_away, k_ref, v_ref, g_own, g_away, turned_ref, log_ref,
    gq_own, gq_away, gk_ref, gv_ref, gk_acc, gv_acc, gq_acc,
):
    ctx = ctx_ref[0]
    gk_acc[...] = jnp.zeros_like(gk_acc)
    gv_acc[...] = jnp.zeros_like(gv_acc)
    for b in (0, 1):
        block = ctx if b == 0 else BLOCKS - 1 - ctx
        rows = slice(b * BLOCK, (b + 1) * BLOCK)
        queries, grads, deltas = [], [], []
        q_ref, g_ref, gq_ref = (q_own, g_own, gq_own) if b == 0 else (q_away, g_away, gq_away)
        for p in range(PAIRS):
            cols = slice(p * 128, (p + 1) * 128)
            queries.append(pair_rows(q_ref[:, cols] * jnp.asarray(0.125, BF)))
            grad = g_ref[:, cols]
            grads.append(pair_rows(grad))
            both = jnp.transpose(grad.astype(F32)) * turned_ref[cols, rows]
            deltas.append(
                jnp.concatenate(
                    [
                        jnp.sum(both[:HEAD_DIM], 0, keepdims=True),
                        jnp.sum(both[HEAD_DIM:], 0, keepdims=True),
                    ],
                    1,
                )
            )
        gq_acc[...] = jnp.zeros_like(gq_acc)

        def step(tile, masked):
            start = pl.multiple_of(tile * TILE, TILE)
            here = pl.ds(start, TILE)
            for p in range(PAIRS):
                cols = slice(p * 128, (p + 1) * 128)
                row = b * PAIRS + p
                keys = k_ref[here, cols]
                scores = contract(keys, queries[p], ((1,), (1,)))
                chances = jnp.exp(scores - log_ref[row : row + 1, :])
                if masked:
                    chances = jnp.where(allowed_at(tile, block), chances, 0.0)
                grad_chance = contract(v_ref[here, cols], grads[p], ((1,), (1,)))
                grad_score = (chances * (grad_chance - deltas[p])).astype(BF)
                gv_acc[here, cols] += contract(chances.astype(BF), grads[p], ((1,), (0,)))
                gk_acc[here, cols] += contract(grad_score, queries[p], ((1,), (0,)))
                gq_acc[p] += contract(keys, grad_score, ((0,), (0,)))

        step(block // 4, True)

        @pl.loop(0, block // 4)
        def _(tile):
            step(tile, False)

        for p in range(PAIRS):
            cols = slice(p * 128, (p + 1) * 128)
            done = gq_acc[p] * 0.125
            turned = jnp.concatenate([done[:HEAD_DIM, :BLOCK], done[HEAD_DIM:, BLOCK:]], 0)
            gq_ref[:, cols] = jnp.transpose(turned).astype(gq_ref.dtype)
    gk_ref[...] = gk_acc[...].astype(BF)
    gv_ref[...] = gv_acc[...].astype(BF)


def attend_backward(ctx, own, away, keys, values, grad_own, grad_away, turned, log_total):
    whole = jax.ShapeDtypeStruct((BLOCKS * BLOCK, HALF), BF)
    return pl.pallas_call(
        backward_kernel,
        out_shape=(
            jax.ShapeDtypeStruct((BLOCK, HALF), F32),
            jax.ShapeDtypeStruct((BLOCK, HALF), BF),
            whole,
            whole,
        ),
        in_specs=[SM] + [VM] * 8,
        out_specs=(VM,) * 4,
        scratch_shapes=[
            pltpu.VMEM((BLOCKS * BLOCK, HALF), F32),
            pltpu.VMEM((BLOCKS * BLOCK, HALF), F32),
            pltpu.VMEM((PAIRS, 128, 2 * BLOCK), F32),
        ],
        compiler_params=pltpu.CompilerParams(vmem_limit_bytes=60 * 2**20),
        cost_estimate=pl.CostEstimate(
            flops=10 * 33 * 128 * 128 * 6 * 128, bytes_accessed=16 * 2**20, transcendentals=33 * 128 * 128 * 6
        ),
        name="attend_backward",
    )(ctx, own, away, keys, values, grad_own, grad_away, turned, log_total)


GAIN_ONE, BIAS_ONE, GAIN_TWO, BIAS_TWO, BIAS_OUT, BIAS_DOWN, BIAS_QKV, BIAS_UP = (
    0, 1, 2, 3, 4, 5, 6, 9,
)


def norm_parts(values):
    centre = jnp.mean(values, -1, keepdims=True)
    shifted = values - centre
    spread = jnp.mean(shifted * shifted, -1, keepdims=True)
    scale = lax.rsqrt(spread + epsilon)
    return shifted * scale, scale


def norm_input_grad(grad_norm, gain, unit, scale):
    e = grad_norm * gain
    return scale * (
        e - jnp.mean(e, -1, keepdims=True) - unit * jnp.mean(e * unit, -1, keepdims=True)
    )


def turn_tables(first_row, row_count):
    shape = (row_count, 128)
    feature = lax.broadcasted_iota(jnp.int32, shape, 1) % HEAD_DIM
    position = first_row + lax.broadcasted_iota(jnp.int32, shape, 0)
    half_rot = ROTARY // 2
    exponent = (feature % half_rot).astype(F32) * (2.0 / ROTARY)
    angle = position.astype(F32) * jnp.power(10000.0, -exponent)
    cosine, sine = jnp.cos(angle), jnp.sin(angle)
    keep = jnp.where(feature < ROTARY, cosine, 1.0)
    low = jnp.where(feature < half_rot, -sine, 0.0)
    high = jnp.where((feature >= half_rot) & (feature < ROTARY), sine, 0.0)
    return keep, low, high


def rotate(values, table_ref):
    shift = ROTARY // 2
    return (
        values * table_ref[0]
        + pltpu.roll(values, 128 - shift, 1) * table_ref[1]
        + pltpu.roll(values, shift, 1) * table_ref[2]
    )


def rotate_back(values, table_ref):
    shift = ROTARY // 2
    return (
        values * table_ref[0]
        + pltpu.roll(values * table_ref[1], shift, 1)
        + pltpu.roll(values * table_ref[2], 128 - shift, 1)
    )


def phi_parts(values):
    cumulative = 0.5 * (1.0 + lax.erf(values * (2.0**-0.5)))
    density = jnp.exp(-0.5 * values * values) * (0.5 / jnp.pi) ** 0.5
    return cumulative, density


def line(vec_ref, row):
    return vec_ref[row : row + 1, :]


def put_halves(upper_ref, low, high, mine_ref, theirs_ref):
    upper = upper_ref[0] == 1

    @pl.when(upper)
    def _():
        mine_ref[...] = high
        theirs_ref[...] = low

    @pl.when(jnp.logical_not(upper))
    def _():
        mine_ref[...] = low
        theirs_ref[...] = high


def put_joined(upper_ref, mine, theirs, out_ref, first):
    upper = upper_ref[0] == 1
    low, high = slice(first, first + HALF), slice(first + HALF, first + D)

    @pl.when(upper)
    def _():
        out_ref[:, low] = theirs
        out_ref[:, high] = mine

    @pl.when(jnp.logical_not(upper))
    def _():
        out_ref[:, low] = mine
        out_ref[:, high] = theirs


def enter(upper_ref, stream, vec_ref, weight_ref, table_ref, one_ref, two_ref, *parts):
    unit, _ = norm_parts(stream)
    one = (unit * line(vec_ref, GAIN_ONE) + line(vec_ref, BIAS_ONE)).astype(BF)
    one_ref[...] = one
    two_ref[...] = (unit * line(vec_ref, GAIN_TWO) + line(vec_ref, BIAS_TWO)).astype(BF)
    for i in range(3):
        joined = contract(one, weight_ref[:, i * D : (i + 1) * D], ((1,), (0,)))
        joined = joined + line(vec_ref, BIAS_QKV + i)
        groups = [joined[:, g * 128 : (g + 1) * 128] for g in range(6)]
        if i < 2:
            groups = [rotate(group, table_ref) for group in groups]
        groups = [group.astype(BF) for group in groups]
        put_halves(
            upper_ref,
            jnp.concatenate(groups[:3], 1),
            jnp.concatenate(groups[3:], 1),
            parts[2 * i],
            parts[2 * i + 1],
        )


def enter_kernel(upper_ref, tokens_ref, vec_ref, weight_ref, keep, low, high, *outs):
    table_ref = (keep[...], low[...], high[...])
    enter(upper_ref, tokens_ref[...].astype(F32), vec_ref, weight_ref, table_ref, *outs)


def leave(upper_ref, stream_ref, own_ref, away_ref, weight_ref, mlp_ref, vec_ref, mixed_ref):
    put_joined(upper_ref, own_ref[...], away_ref[...], mixed_ref, 0)
    return (
        stream_ref[...].astype(F32)
        + contract(mixed_ref[...], weight_ref[...], ((1,), (0,)))
        + line(vec_ref, BIAS_OUT)
        + mlp_ref[...]
        + line(vec_ref, BIAS_DOWN)
    )


def pass_kernel(
    upper_ref, stream_ref, own_ref, away_ref, out_ref, mlp_ref, vec_ref,
    next_vec_ref, weight_ref, keep, low, high, mixed_ref, next_ref, *outs,
):
    table_ref = (keep[...], low[...], high[...])
    stream = leave(upper_ref, stream_ref, own_ref, away_ref, out_ref, mlp_ref, vec_ref, mixed_ref)
    next_ref[...] = stream
    enter(upper_ref, stream, next_vec_ref, weight_ref, table_ref, *outs)


def last_kernel(
    upper_ref, stream_ref, own_ref, away_ref, out_ref, mlp_ref, vec_ref, mixed_ref, next_ref
):
    next_ref[...] = leave(
        upper_ref, stream_ref, own_ref, away_ref, out_ref, mlp_ref, vec_ref, mixed_ref
    ).astype(BF)


def fetch_panels(up_ref, down_ref, up_buffer, down_buffer, sem):
    sources, buffers = [], []
    for i in range(FF // D):
        cols = slice(i * D, (i + 1) * D)
        sources += [up_ref.at[:, cols], down_ref.at[cols, :]]
        buffers += [up_buffer.at[i], down_buffer.at[cols, :]]
    return fetch(sources, buffers, sem)


def mlp_kernel(
    two_ref, vec_ref, up_ref, down_ref, pre_ref, hidden_ref, mlp_ref, up_buffer, down_buffer, sem
):
    take = fetch_panels(up_ref, down_ref, up_buffer, down_buffer, sem)
    two = two_ref[...]
    for i in range(FF // D):
        cols = slice(i * D, (i + 1) * D)
        pre = contract(two, take(2 * i)[...], ((1,), (0,))) + line(vec_ref, BIAS_UP + i)
        pre_ref[:, cols] = pre
        hidden = (pre * phi_parts(pre)[0]).astype(BF)
        hidden_ref[:, cols] = hidden
        fresh = contract(hidden, take(2 * i + 1)[...], ((1,), (0,)))
        mlp_ref[...] = fresh if i == 0 else mlp_ref[...] + fresh


def back(upper_ref, gradient, weight_ref, low_ref, mine_ref, theirs_ref):
    low = gradient.astype(BF)
    low_ref[...] = low
    mixed = contract(low, weight_ref[...], ((1,), (1,))).astype(BF)
    put_halves(upper_ref, mixed[:, :HALF], mixed[:, HALF:], mine_ref, theirs_ref)


def back_kernel(upper_ref, cotangent_ref, weight_ref, *outs):
    back(upper_ref, cotangent_ref[...].astype(F32), weight_ref, *outs)


def mlp_back_kernel(
    low_ref, pre_ref, up_ref, down_ref, grad_pre_ref, norm_ref, up_buffer, down_buffer, sem
):
    take = fetch_panels(up_ref, down_ref, up_buffer, down_buffer, sem)
    low = low_ref[...]
    for i in range(FF // D):
        cols = slice(i * D, (i + 1) * D)
        pre = pre_ref[:, cols]
        cumulative, density = phi_parts(pre)
        hidden = contract(low, take(2 * i + 1)[...], ((1,), (1,)))
        grad_pre = (hidden * (cumulative + pre * density)).astype(BF)
        grad_pre_ref[:, cols] = grad_pre
        fresh = contract(grad_pre, take(2 * i)[...], ((1,), (1,)))
        norm_ref[...] = fresh if i == 0 else norm_ref[...] + fresh


PANEL_ROOMS = (room(FF // D, D, D), room(FF, D), pltpu.SemaphoreType.DMA((2 * FF // D,)))


def join_kernel(
    more, upper_ref, own_ref, back_ref, own_q, back_q, keep, low, high, weight_ref, stream_ref,
    vec_ref, two_ref, gradient_ref, *refs,
):
    table_ref = (keep[...], low[...], high[...])
    next_weight, refs = (refs[:1], refs[1:]) if more else ((), refs)
    joined_ref, sums_ref, next_ref, *outs = refs

    def turned(values):
        groups = [rotate_back(values[:, g * 128 : (g + 1) * 128], table_ref) for g in range(3)]
        return jnp.concatenate(groups, 1).astype(BF)

    put_joined(upper_ref, turned(own_q[...]), turned(back_q[...].astype(F32)), joined_ref, 0)
    put_joined(upper_ref, turned(own_ref[0]), turned(back_ref[0].astype(F32)), joined_ref, D)
    put_joined(upper_ref, own_ref[1].astype(BF), back_ref[1], joined_ref, 2 * D)
    one = contract(joined_ref[...], weight_ref[...], ((1,), (1,)))
    two = two_ref[...]
    unit, scale = norm_parts(stream_ref[...].astype(F32))
    sums = [jnp.sum(values, 0, keepdims=True) for values in (one * unit, one, two * unit, two)]
    sums_ref[...] = jnp.concatenate(sums + [jnp.zeros((12, D), F32)], 0).astype(BF)
    gradient = (
        gradient_ref[...].astype(F32)
        + norm_input_grad(one, line(vec_ref, GAIN_ONE), unit, scale)
        + norm_input_grad(two, line(vec_ref, GAIN_TWO), unit, scale)
    )
    next_ref[...] = gradient
    if more:
        back(upper_ref, gradient, next_weight[0], *outs)


def unpack_kernel(early_ref, rows_ref, qkv_ref, out_ref, up_ref, down_ref):
    layer_index = pl.program_id(0)

    def put(source, late):
        for i in range(3):
            qkv_ref[0, :, i * D : (i + 1) * D] = rows_ref[
                late + i * 192 : late + (i + 1) * 192, :
            ].astype(F32)
        out_ref[0] = source[:192, :].astype(F32)
        for i in range(4):
            up_ref[0, :, i * D : (i + 1) * D] = source[
                192 + i * 192 : 384 + i * 192, :
            ].astype(F32)
        down_ref[0] = source[960:1728, :].astype(F32)

    @pl.when(layer_index == 0)
    def _():
        put(rows_ref, 1728)

    @pl.when(layer_index == 1)
    def _():
        put(early_ref, 2304)


def unpack(early, rows):
    shapes = [(192, 3 * D), (192, D), (192, FF), (D, D)]
    return pl.pallas_call(
        unpack_kernel,
        grid=(LAYERS,),
        out_shape=tuple(jax.ShapeDtypeStruct((LAYERS,) + shape, F32) for shape in shapes),
        in_specs=[
            pl.BlockSpec((1728, D), lambda i: (0, 0)),
            pl.BlockSpec((PACK, D), lambda i: (0, 0)),
        ],
        out_specs=tuple(pl.BlockSpec((1,) + shape, lambda i: (i, 0, 0)) for shape in shapes),
        compiler_params=pltpu.CompilerParams(vmem_limit_bytes=60 * 2**20),
        name="unpack",
    )(early, rows)


def dense(name, kernel, specs, outs, args, flops, scratch=()):
    shapes = tuple(
        jax.ShapeDtypeStruct((BLOCK, size) if isinstance(size, int) else size, kind)
        for size, kind in outs
    )
    return pl.pallas_call(
        kernel,
        out_shape=shapes,
        in_specs=specs,
        out_specs=(VM,) * len(shapes),
        scratch_shapes=list(scratch),
        compiler_params=pltpu.CompilerParams(vmem_limit_bytes=60 * 2**20),
        cost_estimate=pl.CostEstimate(
            flops=2 * BLOCK * flops, bytes_accessed=2 * flops, transcendentals=0
        ),
        name=name,
    )(*args)


def vector_kernel(table_ref, *out_refs):
    for layer_index, out_ref in enumerate(out_refs):
        at = slice(layer_index, layer_index + 1)
        for row in range(6):
            pieces = [table_ref[f, at, row * 192 : (row + 1) * 192] for f in range(4)]
            out_ref[row : row + 1, :] = jnp.concatenate(pieces, 1)
        joined = jnp.concatenate([table_ref[f, at, 1152:1728] for f in range(4)], 1)
        for i in range(3):
            out_ref[BIAS_QKV + i : BIAS_QKV + i + 1, :] = joined[:, i * D : (i + 1) * D]
        for f in range(4):
            out_ref[BIAS_UP + f : BIAS_UP + f + 1, :] = table_ref[f, at, 1728:2496]
        out_ref[13:, :] = jnp.zeros((3, D), F32)


def order_vectors(table):
    return pl.pallas_call(
        vector_kernel,
        out_shape=(jax.ShapeDtypeStruct((16, D), F32),) * LAYERS,
        in_specs=[VM],
        out_specs=(VM,) * LAYERS,
        name="order_vectors",
    )(table)


ENTER_OUTS = ((D, BF),) * 2 + ((HALF, BF),) * 6


def shards(
    tokens,
    cotangent,
    ln1_gain,
    ln1_bias,
    ln2_gain,
    ln2_bias,
    qkv_weight,
    qkv_bias,
    out_weight,
    out_bias,
    up_weight,
    up_bias,
    down_weight,
    down_bias,
):
    row_count = tokens.shape[1]
    fsdp = lax.axis_index("fsdp")
    ctx = lax.axis_index("ctx")
    ctx_word = ctx.astype(jnp.int32).reshape(1)
    upper = (ctx % 2).astype(jnp.int32).reshape(1)
    fsdp_word = fsdp.astype(jnp.int32).reshape(1)
    tables = turn_tables(ctx * row_count, row_count)

    vectors = (ln1_gain, ln1_bias, ln2_gain, ln2_bias, out_bias, down_bias, qkv_bias, up_bias)
    packed = jnp.concatenate(vectors, 1).astype(F32)
    packed = jnp.pad(packed, ((0, 8 - LAYERS), (0, 2560 - packed.shape[1])))
    first_weight, table = gather_first(qkv_weight, packed)
    vecs = order_vectors(table)
    qkv_full = [first_weight] + [
        lax.all_gather(qkv_weight[layer_index], "fsdp", axis=0, tiled=True)
        for layer_index in range(1, LAYERS)
    ]
    gathered = [None] * LAYERS
    stream = tokens[0]
    entered = dense(
        "enter",
        enter_kernel,
        [SM] + [VM] * 6,
        ENTER_OUTS,
        (upper, stream, vecs[0], first_weight, *tables),
        D * 3 * D,
    )
    saved = []
    for layer_index in range(LAYERS):
        norm_one, norm_two, q_own, q_away, k_own, k_away, v_own, v_away = entered
        jobs = [(layer_index, out_weight), (layer_index, up_weight), (layer_index, down_weight)]
        q_other, keys, values, w_out, w_up, w_down = gather_pair(
            "gather_pair_%d" % layer_index,
            1 + layer_index,
            (q_away, k_away, v_away),
            (k_own, v_own),
            jobs,
        )
        gathered[layer_index] = (qkv_full[layer_index], w_out, w_up, w_down)
        keys = keys.reshape(BLOCKS * BLOCK, HALF)
        values = values.reshape(BLOCKS * BLOCK, HALF)
        mixed_own, mixed_away, turned, log_total = attend_forward(
            ctx_word, q_own, q_other, keys, values
        )
        mixed_back = mirrored(mixed_away)
        hidden_pre, hidden_low, mlp_branch = dense(
            "mlp",
            mlp_kernel,
            [VM, VM, ANY, ANY],
            ((FF, F32), (FF, BF), (D, F32)),
            (norm_two, vecs[layer_index], w_up, w_down),
            2 * D * FF,
            PANEL_ROOMS,
        )
        before = stream
        common = (upper, stream, mixed_own, mixed_back, w_out, mlp_branch, vecs[layer_index])
        if layer_index + 1 < LAYERS:
            mixed_low, stream, *entered = dense(
                "pass_on",
                pass_kernel,
                [SM] + [VM] * 11,
                ((D, BF), (D, F32)) + ENTER_OUTS,
                common + (vecs[layer_index + 1], qkv_full[layer_index + 1], *tables),
                D * 4 * D,
            )
        else:
            mixed_low, output = dense(
                "last", last_kernel, [SM] + [VM] * 6, ((D, BF), (D, BF)), common, D * D
            )
        lefts = (norm_one, mixed_low, norm_two)
        saved.append(
            (before, q_own, q_other, keys, values, turned, log_total, hidden_pre, hidden_low, lefts)
        )

    gradient = cotangent[0]
    waiting, early_rows, late_rows = (), [None] * 2, [None] * 2
    grad_low, grad_own, grad_away = dense(
        "back",
        back_kernel,
        [SM, VM, VM],
        ((D, BF), (HALF, BF), (HALF, BF)),
        (upper, gradient, gathered[LAYERS - 1][1]),
        D * D,
    )
    for layer_index in range(LAYERS - 1, -1, -1):
        w_qkv, w_out, w_up, w_down = gathered[layer_index]
        before, q_own, q_other, keys, values, turned, log_total, hidden_pre, hidden_low, lefts = (
            saved[layer_index]
        )
        grad_back = mirrored(grad_away)
        grad_pre, grad_norm_two = dense(
            "mlp_back",
            mlp_back_kernel,
            [VM, VM, ANY, ANY],
            ((FF, BF), (D, F32)),
            (grad_low, hidden_pre, w_up, w_down),
            2 * D * FF,
            PANEL_ROOMS,
        )
        gq_own, gq_away, grad_keys, grad_values = attend_backward(
            ctx_word, q_own, q_other, keys, values, grad_own, grad_back, turned, log_total
        )
        whole = (BLOCKS, BLOCK, HALF)
        own_pair, back_pair, back_query, *gathered_rows = scatter_pair(
            "scatter_pair_%d" % layer_index,
            3 + layer_index,
            grad_keys.reshape(whole),
            grad_values.reshape(whole),
            gq_away,
            hidden_low,
            lefts + (grad_low, grad_pre) + waiting,
        )
        early_rows[layer_index] = gathered_rows[:6]
        if layer_index > 0:
            hidden, _, mixed, two, low, pre = early_rows[layer_index]
            early_pack, early_sums = early_grads(fsdp_word, low, mixed, hidden, two, pre)
            early_total = lax.psum(early_pack, "ctx")
        if waiting:
            late_rows[layer_index + 1] = gathered_rows[6:]
        going_on = layer_index > 0
        grad_joined, norm_sums, gradient, *outs = dense(
            "join_%d" % layer_index,
            functools.partial(join_kernel, going_on),
            [SM] + [VM] * (13 if going_on else 12),
            ((3 * D, BF), ((16, D), BF), (D, F32))
            + (((D, BF), (HALF, BF), (HALF, BF)) if going_on else ()),
            (
                upper,
                own_pair,
                back_pair,
                gq_own,
                back_query,
                *tables,
                w_qkv,
                before,
                vecs[layer_index],
                grad_norm_two,
                gradient,
            )
            + ((gathered[layer_index - 1][1],) if going_on else ()),
            D * 3 * D,
        )
        waiting = (grad_joined, norm_sums)
        if going_on:
            grad_low, grad_own, grad_away = outs
    late_rows[0] = gather_late(*waiting)
    hidden, one, mixed, two, low, pre = early_rows[0]
    (joined, norms), (joined_one, norms_one) = late_rows
    pack, sums = last_grads(
        fsdp_word,
        norms,
        norms_one,
        early_sums,
        (low, mixed, hidden, two, pre, one, joined, early_rows[1][1], joined_one),
    )
    summed, small = sum_over_ctx(pack, sums)

    def own_part(vectors, width):
        return lax.dynamic_slice_in_dim(vectors, fsdp * width, width, vectors.ndim - 1)

    bias_sum = own_part(small[:, 0], 192)
    joined_sum = own_part(small[:, 1:4].reshape(LAYERS, 3 * D), 576)
    up_sum = own_part(small[:, 4:8].reshape(LAYERS, 4 * D), D)
    norm_sums = own_part(small[:, 8:12], 192)
    qkv_grad, out_grad, up_grad, down_grad = unpack(early_total, summed.reshape(PACK, D))
    return (
        output[None],
        gradient[None],
        norm_sums[:, 0],
        norm_sums[:, 1],
        norm_sums[:, 2],
        norm_sums[:, 3],
        qkv_grad,
        joined_sum,
        out_grad,
        bias_sum,
        up_grad,
        up_sum,
        down_grad,
        bias_sum,
    )


def solution(mesh):
    matrix, vector = P(None, "fsdp", None), P(None, "fsdp")
    rows = P("fsdp", "ctx", None)
    params = (
        vector,
        vector,
        vector,
        vector,
        matrix,
        vector,
        matrix,
        vector,
        matrix,
        vector,
        matrix,
        vector,
    )
    return jax.shard_map(
        shards,
        mesh=mesh,
        in_specs=(rows, rows) + params,
        out_specs=(rows, rows) + params,
        check_vma=False,
    )
```

```python
import functools

import jax
import jax.numpy as jnp
from jax import lax
from jax.experimental import pallas as pl
from jax.experimental.pallas import tpu as pltpu
from jax.sharding import PartitionSpec as P

D = 768
HEADS = 12
HEAD_DIM = 64
FF = 3072
ROTARY = 16
LAYERS = 2
HALF = 384
BLOCK = 128
BLOCKS = 32
TILE = 512
PAIRS = 3

epsilon = 1e-05
masked_score = -1e30
MESH = pl.DeviceIdType.MESH
BF = jnp.bfloat16
F32 = jnp.float32


def mirrored(values):
    pairs = [(f * 32 + c, f * 32 + 31 - c) for f in range(4) for c in range(32)]
    return lax.ppermute(values, ("fsdp", "ctx"), pairs)


class Place:
    def __init__(self):
        self.fsdp = lax.axis_index("fsdp")
        self.ctx = lax.axis_index("ctx")
        self.y, self.z, self.h = self.ctx // 8, (self.ctx // 2) % 4, self.ctx % 2
        self.x_lo, self.core = self.fsdp // 2, self.fsdp % 2
        self.beside = (self.fsdp + 1 - 2 * self.core, self.ctx)
        self.mirror = (self.fsdp, BLOCKS - 1 - self.ctx)
        self.half = (self.fsdp, self.ctx + 1 - 2 * self.h)

    def along_x(self, step):
        x = (2 * self.h + self.x_lo + step) % 4
        return (2 * (x % 2) + self.core, self.y * 8 + self.z * 2 + x // 2)

    def ctx_at(self, dy, dz):
        return ((self.y + dy) % 4) * 8 + ((self.z + dz) % 4) * 2 + self.h

    def ring(self, t, da, db):
        return self.ctx_at(da, db) if t == 0 else self.ctx_at(db, da)

    def near(self, t, axis, sign):
        steps = (sign, 0) if axis == 0 else (0, sign)
        return (self.fsdp, self.ring(t, *steps))

    def around(self):
        return [self.near(0, axis, sign) for axis in (0, 1) for sign in (1, -1)]

    def greet(self, partners):
        barrier = pltpu.get_barrier_semaphore()
        for partner in partners:
            pl.semaphore_signal(barrier, inc=1, device_id=partner, device_id_type=MESH)
        pl.semaphore_wait(barrier, len(partners))


class Wire:
    def __init__(self, send_sem, recv_sem, local_sem=None):
        self.send_sem, self.recv_sem, self.local_sem = send_sem, recv_sem, local_sem
        self.sent, self.local, self.bounced = [], [], []

    def push(self, source, target, partner):
        number = len(self.sent)
        copy = pltpu.make_async_remote_copy(
            src_ref=source,
            dst_ref=target,
            send_sem=self.send_sem.at[number],
            recv_sem=self.recv_sem.at[number],
            device_id=partner,
            device_id_type=MESH,
        )
        copy.start()
        self.sent.append(copy)
        return copy

    def keep(self, source, target, bounce=None):
        if bounce is None:
            copy = pltpu.make_async_copy(source, target, self.local_sem.at[len(self.local)])
        else:
            copy = pltpu.make_async_copy(source, bounce, self.local_sem.at[len(self.local)])
            self.bounced.append((len(self.local), bounce, target))
        copy.start()
        self.local.append(copy)

    def flush(self):
        for number, bounce, target in self.bounced:
            self.local[number].wait()
            copy = pltpu.make_async_copy(bounce, target, self.local_sem.at[number])
            copy.start()
            self.local[number] = copy
        self.bounced = []

    def drain(self):
        for copy in self.sent:
            copy.wait_send()
        for copy in self.local:
            copy.wait()


def share_param(place, wire, source, target, bounce):
    rows = source.shape[0]
    cut = rows // 2
    mine, far = place.fsdp * rows, ((place.fsdp + 2) % 4) * rows
    parts = [(0, cut, 1), (cut, cut, 3)]
    across = [
        wire.push(
            source.at[pl.ds(start, count)],
            target.at[pl.ds(mine + start, count)],
            place.along_x(step),
        )
        for start, count, step in parts
    ]
    beside = wire.push(source, target.at[pl.ds(mine, rows)], place.beside)
    wire.keep(source, target.at[pl.ds(mine, rows)], bounce)
    last = [beside]

    def onward(copy, start, count):
        copy.wait_recv()
        spot = target.at[pl.ds(far + start, count)]
        last.append(wire.push(spot, spot, place.beside))

    steps = [
        functools.partial(onward, copy, start, count)
        for copy, (start, count, _) in zip(across, parts)
    ]
    return steps, last


def share_rows(place, wire, source, target):
    rows = source.shape[0]
    cut = rows // 2
    parts = [(0, cut, 1), (cut, cut, 3)] if rows % 32 == 0 else [(0, rows, 1)]
    across = [
        wire.push(
            source.at[pl.ds(start, count)],
            target.at[pl.ds(2 * rows + start, count)],
            place.along_x(step),
        )
        for start, count, step in parts
    ]
    last = [wire.push(source, target.at[pl.ds(rows, rows)], place.beside)]
    wire.keep(source, target.at[pl.ds(0, rows)])

    def onward(copy, start, count):
        copy.wait_recv()
        last.append(
            wire.push(
                target.at[pl.ds(2 * rows + start, count)],
                target.at[pl.ds(3 * rows + start, count)],
                place.beside,
            )
        )

    steps = [
        functools.partial(onward, copy, start, count)
        for copy, (start, count, _) in zip(across, parts)
    ]
    return steps, last


def share_columns(place, wire, source, target, stage):
    rows = source.shape[0]
    cut = rows // 2
    fsdp, core = place.fsdp, place.core
    parts = [(0, cut, 1), (cut, cut, 3)]

    def panel(start, count, shard):
        return source.at[pl.ds(start, count), pl.ds(pl.multiple_of(shard * D, D), D)]

    passing, last = [], []
    for start, count, step in parts:
        passing.append(
            wire.push(
                panel(start, count, 3 - fsdp),
                stage.at[pl.ds(start, count)],
                place.along_x(step),
            )
        )
    for start, count, step in parts:
        last.append(
            wire.push(
                panel(start, count, (fsdp + 2) % 4),
                target.at[pl.ds(2 * rows + start, count)],
                place.along_x(step),
            )
        )
    last.append(
        wire.push(
            panel(0, rows, fsdp + 1 - 2 * core), target.at[pl.ds(rows, rows)], place.beside
        )
    )
    wire.keep(panel(0, rows, fsdp), target.at[pl.ds(0, rows)])

    def onward(copy, start, count):
        copy.wait_recv()
        last.append(
            wire.push(
                stage.at[pl.ds(start, count)],
                target.at[pl.ds(3 * rows + start, count)],
                place.beside,
            )
        )

    steps = [
        functools.partial(onward, copy, start, count)
        for copy, (start, count, _) in zip(passing, parts)
    ]
    return steps, last


def spread(place, wire, own, spot, ready, between=()):
    between = list(between)
    arrivals = {}

    def push(t, da, db, b, axis, sign):
        target = spot(t, place.ring(t, da, db), b)
        source = own(t, b) if da == 0 and db == 0 else target
        sa, sb = (sign, 0) if axis == 0 else (0, sign)
        arrivals[t, (da - sa) % 4, (db - sb) % 4, b] = wire.push(
            source, target, place.near(t, axis, sign)
        )

    def landed(t, da, db):
        for b in (0, 1):
            arrivals[t, da, db, b].wait_recv()

    def pause():
        if between:
            between.pop(0)()

    for b in (0, 1):
        for t in (0, 1):
            ready(t, b)
            for axis in (0, 1):
                for sign in (1, -1):
                    push(t, 0, 0, b, axis, sign)
    for da, keep, onward in ((1, 0, -1), (3, 1, 1)):
        for t in (0, 1):
            landed(t, da, 0)
            push(t, da, 0, keep, 0, onward)
            for sign in (1, -1):
                for b in (0, 1):
                    push(t, da, 0, b, 1, sign)
    for db, keep, onward in ((1, 0, -1), (3, 1, 1)):
        for t in (0, 1):
            landed(t, 0, db)
            push(t, 0, db, keep, 1, onward)
    for t in (0, 1):
        landed(t, 2, 0)
        for sign in (1, -1):
            for b in (0, 1):
                push(t, 2, 0, b, 1, sign)
    pause()
    for da in (1, 3, 2):
        for db, keep, onward in ((1, 0, -1), (3, 1, 1)):
            for t in (0, 1):
                landed(t, da, db)
                push(t, da, db, keep, 1, onward)
    while between:
        pause()
    for da in (0, 1, 3, 2):
        for t in (0, 1):
            landed(t, da, 2)


ANY = pl.BlockSpec(memory_space=pl.ANY)
VM = pl.BlockSpec(memory_space=pltpu.VMEM)
SM = pl.BlockSpec(memory_space=pltpu.SMEM)


def room(*shape):
    return pltpu.VMEM(shape, BF)


def sems(count, local):
    return [
        pltpu.SemaphoreType.DMA((count,)),
        pltpu.SemaphoreType.DMA((count,)),
        pltpu.SemaphoreType.DMA((local,)),
    ]


def full_shape(shard):
    return jax.ShapeDtypeStruct((4 * shard.shape[-2], shard.shape[-1]), BF)


def first_kernel(weight_ref, vector_ref, weight_out, vector_out, bounce, *sem):
    place, wire = Place(), Wire(*sem)
    place.greet([place.beside, place.along_x(1), place.along_x(3)])
    far = vector_out.at[(place.fsdp + 2) % 4]
    across = wire.push(vector_ref, vector_out.at[place.fsdp], place.along_x(1))
    last = [wire.push(vector_ref, vector_out.at[place.fsdp], place.beside)]
    wire.keep(vector_ref, vector_out.at[place.fsdp])
    steps, ends = share_param(place, wire, weight_ref.at[0], weight_out, bounce)
    wire.flush()
    across.wait_recv()
    last.append(wire.push(far, far, place.beside))
    for step in steps:
        step()
    for copy in last + ends:
        copy.wait_recv()
    wire.drain()


def gather_first(weight, vectors):
    return pl.pallas_call(
        first_kernel,
        out_shape=(full_shape(weight), jax.ShapeDtypeStruct((4,) + vectors.shape, F32)),
        in_specs=[ANY, VM],
        out_specs=(ANY, ANY),
        scratch_shapes=[room(*weight.shape[1:])] + sems(16, 4),
        compiler_params=pltpu.CompilerParams(
            collective_id=0, has_side_effects=True, vmem_limit_bytes=60 * 2**20
        ),
        name="gather_first",
    )(weight, vectors)


def gather_kernel(jobs, q_ref, k_ref, v_ref, k_own, v_own, *refs):
    count = len(jobs)
    weights, refs = refs[:count], refs[count:]
    q_out, k_out, v_out = refs[:3]
    weights_out, refs = refs[3 : 3 + count], refs[3 + count :]
    bounces, refs = refs[:count], refs[count:]
    place, wire = Place(), Wire(*refs)
    place.greet(
        place.around() + [place.mirror, place.beside, place.along_x(1), place.along_x(3)]
    )
    ins, outs = (k_own, v_own), (k_out, v_out)
    ctx = place.ctx
    swapped = [
        wire.push(source, out.at[ctx], place.mirror) for source, out in zip((k_ref, v_ref), outs)
    ]
    for t in (0, 1):
        wire.keep(ins[t], outs[t].at[ctx])
    work = []

    def ready(t, b):
        if b == 1:
            if t == 0:
                for layer, weight, target, bounce in zip(jobs, weights, weights_out, bounces):
                    work.append(share_param(place, wire, weight.at[layer], target, bounce))
            swapped[t].wait_recv()
            if t == 1:
                swapped.append(wire.push(q_ref, q_out, place.mirror))

    def spot(t, origin, b):
        return outs[t].at[origin if b == 0 else BLOCKS - 1 - origin]

    def own(t, b):
        return ins[t] if b == 0 else spot(t, ctx, 1)

    def onward(number):
        for steps, _ in work:
            for step in steps[number : number + 1]:
                step()

    spread(
        place,
        wire,
        own,
        spot,
        ready,
        [wire.flush, functools.partial(onward, 0), functools.partial(onward, 1)],
    )
    swapped[2].wait_recv()
    for _, last in work:
        for copy in last:
            copy.wait_recv()
    wire.drain()


def gather_pair(name, number, away, own, jobs):
    layers = [layer for layer, _ in jobs]
    weights = [weight for _, weight in jobs]
    whole = jax.ShapeDtypeStruct((BLOCKS, BLOCK, HALF), BF)
    return pl.pallas_call(
        functools.partial(gather_kernel, layers),
        out_shape=(jax.ShapeDtypeStruct((BLOCK, HALF), BF), whole, whole)
        + tuple(full_shape(weight) for weight in weights),
        in_specs=[VM] * 5 + [ANY] * len(jobs),
        out_specs=(ANY,) * (3 + len(jobs)),
        scratch_shapes=[room(*weight.shape[1:]) for weight in weights] + sems(96, 8),
        compiler_params=pltpu.CompilerParams(
            collective_id=number, has_side_effects=True, vmem_limit_bytes=60 * 2**20
        ),
        name=name,
    )(*away, *own, *weights)


def scatter_kernel(count, gk_ref, gv_ref, gq_ref, hidden_ref, pre_ref, up_ref, down_ref, *refs):
    sources, refs = refs[:count], refs[count:]
    own_out, norm_out, back_out, back_q, hidden_out, grad_pre_out = refs[:6]
    targets, refs = refs[6 : 6 + count], refs[6 + count :]
    far, near, mix, total, last_far, last_near, last_mix, leave, stage = refs[:9]
    up_buffer, down_buffer, grad_pre, load_sem = refs[9:13]
    place, wire = Place(), Wire(*refs[13:])
    loads = []
    for i in range(FF // D):
        cols = slice(i * D, (i + 1) * D)
        for source, buffer in (
            (down_ref.at[cols, :], down_buffer.at[cols, :]),
            (up_ref.at[:, cols], up_buffer.at[i]),
        ):
            load = pltpu.make_async_copy(source, buffer, load_sem.at[len(loads)])
            load.start()
            loads.append(load)
    place.greet(
        place.around() + [place.mirror, place.beside, place.along_x(1), place.along_x(3)]
    )
    ins = (gk_ref, gv_ref)

    def block_at(t, da, db, b):
        origin = place.ring(t, da, db)
        return origin if b == 0 else BLOCKS - 1 - origin

    order = [(da, t) for da in (2, 1, 3, 0) for t in (0, 1)]
    way = {0: 1, 1: -1}
    first, second, loose = {}, {}, {}
    for b in (1, 0):
        for da, t in order:
            first[t, da, b] = wire.push(
                ins[t].at[block_at(t, da, 2, b)], far.at[t, da, b], place.near(t, 1, way[b])
            )
    swapped = [wire.push(gq_ref, back_q, place.mirror)]
    for b in (1, 0):
        for da, t in order:
            loose[t, da, b] = wire.push(
                ins[t].at[block_at(t, da, -way[b], b)],
                near.at[t, da, 1, b],
                place.near(t, 1, -way[b]),
            )
    work = [share_columns(place, wire, hidden_ref, hidden_out, stage)]
    for source, target in zip(sources, targets):
        work.append(share_rows(place, wire, source, target))
    for b in (1, 0):
        if b == 0:
            mlp_back(sources[3][...], pre_ref, loads, up_buffer, down_buffer, grad_pre, norm_out)
            work.append(share_rows(place, wire, grad_pre, grad_pre_out))
        for da, t in order:
            first[t, da, b].wait_recv()
            mix[t, da, b] = (
                ins[t][block_at(t, da, way[b], b)].astype(F32) + far[t, da, b].astype(F32)
            ).astype(BF)
            second[t, da, b] = wire.push(
                mix.at[t, da, b], near.at[t, da, 0, b], place.near(t, 1, way[b])
            )

    def settle(t, da, b):
        loose[t, da, b].wait_recv()
        second[t, da, b].wait_recv()
        total[t, da, b] = (
            ins[t][block_at(t, da, 0, b)].astype(F32)
            + near[t, da, 0, b].astype(F32)
            + near[t, da, 1, b].astype(F32)
        ).astype(BF)

    third, fourth = {}, {}
    for b in (1, 0):
        for t in (0, 1):
            settle(t, 2, b)
            third[t, b] = wire.push(
                total.at[t, 2, b], last_far.at[t, b], place.near(t, 0, way[b])
            )
        for t in (0, 1):
            settle(t, 1, b)
            settle(t, 3, b)
            fourth[t, b] = [
                wire.push(
                    total.at[t, -way[b] % 4, b], last_near.at[t, 1, b], place.near(t, 0, -way[b])
                )
            ]
        for t in (0, 1):
            third[t, b].wait_recv()
            last_mix[t, b] = (
                total[t, way[b] % 4, b].astype(F32) + last_far[t, b].astype(F32)
            ).astype(BF)
            fourth[t, b].append(
                wire.push(last_mix.at[t, b], last_near.at[t, 0, b], place.near(t, 0, way[b]))
            )
        for t in (0, 1):
            settle(t, 0, b)

    def final(t, b):
        for copy in fourth[t, b]:
            copy.wait_recv()
        return (
            total[t, 0, b].astype(F32)
            + last_near[t, 0, b].astype(F32)
            + last_near[t, 1, b].astype(F32)
        )

    for t in (0, 1):
        leave[t] = final(t, 1).astype(BF)
        swapped.append(wire.push(leave.at[t], back_out.at[t], place.mirror))
    for steps, _ in work:
        for step in steps:
            step()
    for t in (0, 1):
        own_out[t] = final(t, 0)
    for _, last in work:
        for copy in last:
            copy.wait_recv()
    for copy in swapped:
        copy.wait_recv()
    wire.drain()


def rows_shape(source):
    return jax.ShapeDtypeStruct((4 * source.shape[0], source.shape[1]), BF)


def mlp_back(low, pre_ref, loads, up_buffer, down_buffer, grad_pre_ref, norm_ref):
    for i in range(FF // D):
        cols = slice(i * D, (i + 1) * D)
        pre = pre_ref[:, cols]
        cumulative, density = phi_parts(pre)
        loads[2 * i].wait()
        hidden = contract(low, down_buffer[cols, :], ((1,), (1,)))
        grad_pre = (hidden * (cumulative + pre * density)).astype(BF)
        grad_pre_ref[:, cols] = grad_pre
        loads[2 * i + 1].wait()
        fresh = contract(grad_pre, up_buffer[i], ((1,), (1,)))
        norm_ref[...] = fresh if i == 0 else norm_ref[...] + fresh


def scatter_pair(name, number, grad_keys, grad_values, away, hidden, pre, up, down, sources):
    return pl.pallas_call(
        functools.partial(scatter_kernel, len(sources)),
        out_shape=(
            jax.ShapeDtypeStruct((2, BLOCK, HALF), F32),
            jax.ShapeDtypeStruct((BLOCK, D), F32),
            jax.ShapeDtypeStruct((2, BLOCK, HALF), BF),
            jax.ShapeDtypeStruct((BLOCK, HALF), BF),
            jax.ShapeDtypeStruct((4 * BLOCK, D), BF),
            jax.ShapeDtypeStruct((4 * BLOCK, FF), BF),
        )
        + tuple(rows_shape(source) for source in sources),
        in_specs=[VM] * 5 + [ANY] * 2 + [VM] * len(sources),
        out_specs=(VM, VM) + (ANY,) * (4 + len(sources)),
        scratch_shapes=[
            room(2, 4, 2, BLOCK, HALF),
            room(2, 4, 2, 2, BLOCK, HALF),
            room(2, 4, 2, BLOCK, HALF),
            room(2, 4, 2, BLOCK, HALF),
            room(2, 2, BLOCK, HALF),
            room(2, 2, 2, BLOCK, HALF),
            room(2, 2, BLOCK, HALF),
            room(2, BLOCK, HALF),
            room(BLOCK, D),
            room(FF // D, D, D),
            room(FF, D),
            room(BLOCK, FF),
            pltpu.SemaphoreType.DMA((2 * FF // D,)),
        ]
        + sems(128, 12),
        compiler_params=pltpu.CompilerParams(
            collective_id=number, has_side_effects=True, vmem_limit_bytes=60 * 2**20
        ),
        name=name,
    )(grad_keys, grad_values, away, hidden, pre, up, down, *sources)


def late_kernel(one_ref, two_ref, one_out, two_out, *sem):
    place, wire = Place(), Wire(*sem)
    place.greet([place.beside, place.along_x(1), place.along_x(3)])
    work = [
        share_rows(place, wire, one_ref, one_out),
        share_rows(place, wire, two_ref, two_out),
    ]
    for steps, _ in work:
        for step in steps:
            step()
    for _, last in work:
        for copy in last:
            copy.wait_recv()
    wire.drain()


def gather_late(one, two):
    return pl.pallas_call(
        late_kernel,
        out_shape=(rows_shape(one), rows_shape(two)),
        in_specs=[VM] * 2,
        out_specs=(ANY,) * 2,
        scratch_shapes=sems(16, 4),
        compiler_params=pltpu.CompilerParams(collective_id=5, has_side_effects=True),
        name="gather_late",
    )(one, two)


PIECE = 144
CUT = 80


def sum_kernel(
    one_ref, two_ref, small_one, small_two, out_ref, small_out,
    far, mix, near, total, far_two, mix_two, near_two, part, other, final, small, heard, *sem,
):
    place, wire = Place(), Wire(*sem)
    y, z, h = place.y, place.z, place.h
    turns = [
        (place.fsdp, (y + 1 - 2 * (y % 2)) * 8 + z * 2 + h),
        (place.fsdp, ((y + 2) % 4) * 8 + z * 2 + h),
        (place.fsdp, y * 8 + (z + 1 - 2 * (z % 2)) * 2 + h),
        (place.fsdp, y * 8 + ((z + 2) % 4) * 2 + h),
        place.half,
    ]
    place.greet(place.around() + [turns[1], turns[3], place.half])
    ins = (one_ref, two_ref)
    parts = {0: pl.ds(0, CUT), 1: pl.ds(CUT, PIECE - CUT)}

    def chunk(t, da, db):
        origin = place.ring(t, da, db)
        return origin // 2

    def plus(*terms):
        result = terms[0].astype(F32)
        for term in terms[1:]:
            result = result + term.astype(F32)
        return result.astype(BF)

    small[0] = small_one[...]
    small[1] = small_two[...]
    passing = wire.push(small, heard.at[0], turns[0])
    order = (2, 1, 3, 0)
    way = {2: 1, 1: 1, 3: -1, 0: -1}
    first, second, loose = {}, {}, {}
    for db in order:
        for t in (0, 1):
            first[t, db] = wire.push(
                ins[t].at[chunk(t, 2, db)], far.at[t, db], place.near(t, 0, way[db])
            )
    for db in order:
        for t in (0, 1):
            loose[t, db] = wire.push(
                ins[t].at[chunk(t, -way[db], db)], near.at[t, db, 1], place.near(t, 0, -way[db])
            )
    for db in order:
        for t in (0, 1):
            first[t, db].wait_recv()
            mix[t, db] = plus(ins[t][chunk(t, way[db], db)], far[t, db])
            second[t, db] = wire.push(mix.at[t, db], near.at[t, db, 0], place.near(t, 0, way[db]))

    def hear(step):
        wire.sent[step_numbers[-1]].wait_send()
        wire.sent[step_numbers[-1]].wait_recv()
        small[...] += heard[step]
        waited.add(step_numbers[-1])
        if step < 4:
            step_numbers.append(len(wire.sent))
            wire.push(small, heard.at[step + 1], turns[step + 1])

    step_numbers, waited = [0], set()

    def settle(t, db):
        second[t, db].wait_recv()
        loose[t, db].wait_recv()
        total[t, db] = plus(ins[t][chunk(t, 0, db)], near[t, db, 0], near[t, db, 1])

    third, fourth = {}, {}
    for t in (0, 1):
        settle(t, 2)
        third[t] = [
            wire.push(
                total.at[t, 2, parts[b]], far_two.at[t, parts[b]], place.near(t, 1, sign)
            )
            for b, sign in ((0, 1), (1, -1))
        ]
    hear(0)
    for t in (0, 1):
        fourth[t] = []
        for b, sign, db in ((0, 1, 1), (1, -1, 3)):
            settle(t, db)
            fourth[t].append(
                wire.push(
                    total.at[t, db, parts[1 - b]],
                    near_two.at[t, b, parts[1 - b]],
                    place.near(t, 1, sign),
                )
            )
    hear(1)
    for t in (0, 1):
        for b, sign, db in ((0, 1, 1), (1, -1, 3)):
            third[t][b].wait_recv()
            mix_two[t, parts[b]] = plus(total[t, db, parts[b]], far_two[t, parts[b]])
            fourth[t].append(
                wire.push(
                    mix_two.at[t, parts[b]], near_two.at[t, b, parts[b]], place.near(t, 1, sign)
                )
            )
    hear(2)
    swapped = []
    for t in (0, 1):
        settle(t, 0)
        for copy in fourth[t]:
            copy.wait_recv()
        part[t] = plus(total[t, 0], near_two[t, 0], near_two[t, 1])
        swapped.append(wire.push(part.at[t], other.at[t], place.half))
    hear(3)

    def spot(t, origin, b):
        return out_ref.at[1 - t, origin // 2, parts[b]]

    def own(t, b):
        return final.at[1 - t, parts[b]]

    def ready(t, b):
        if b == 0:
            swapped[1 - t].wait_recv()
            final[1 - t] = plus(part[1 - t], other[1 - t])
            wire.keep(final.at[1 - t], out_ref.at[1 - t, place.ctx // 2])

    spread(place, wire, own, spot, ready)
    hear(4)
    small_out[...] = small[...]
    for number, copy in enumerate(wire.sent):
        if number not in waited:
            copy.wait_send()
    for copy in wire.local:
        copy.wait()


def sum_over_ctx(one, two, small_one, small_two):
    shape = (16, PIECE, D)
    small_shape = (2,) + small_one.shape
    return pl.pallas_call(
        sum_kernel,
        out_shape=(
            jax.ShapeDtypeStruct((2,) + shape, BF),
            jax.ShapeDtypeStruct(small_shape, F32),
        ),
        in_specs=[VM] * 4,
        out_specs=(ANY, VM),
        scratch_shapes=[
            room(2, 4, PIECE, D),
            room(2, 4, PIECE, D),
            room(2, 4, 2, PIECE, D),
            room(2, 4, PIECE, D),
            room(2, PIECE, D),
            room(2, PIECE, D),
            room(2, 2, PIECE, D),
            room(2, PIECE, D),
            room(2, PIECE, D),
            room(2, PIECE, D),
            pltpu.VMEM(small_shape, F32),
            pltpu.VMEM((5,) + small_shape, F32),
        ]
        + sems(128, 4),
        compiler_params=pltpu.CompilerParams(
            collective_id=6, has_side_effects=True, vmem_limit_bytes=60 * 2**20
        ),
        name="sum_over_ctx",
    )(one.reshape(shape), two.reshape(shape), small_one, small_two)


def weight_kernel(
    fsdp_ref, one_ref, mixed_ref, two_ref, hidden_ref, joined_ref, low_ref, pre_ref, norm_ref,
    rows_ref, sums_ref, turned, turned_hidden,
):
    start = pl.multiple_of(fsdp_ref[0] * 192, 64)
    lefts = []
    for i, ref in enumerate((one_ref, mixed_ref, two_ref)):
        turned[i] = jnp.transpose(ref[...])
        lefts.append(turned[i, pl.ds(start, 192), :])
    turned_hidden[...] = jnp.transpose(hidden_ref[...])
    ones = jnp.ones((8, low_ref.shape[0]), BF)

    def panel(first, left, right, line):
        rows = left.shape[0]
        rows_ref[first : first + rows, :] = contract(left, right, ((1,), (0,))).astype(BF)
        if line is not None:
            sums_ref[line : line + 1, :] = contract(ones, right, ((1,), (0,)))[:1]

    low = low_ref[...]
    panel(1536, turned_hidden[...], low, None)
    panel(576, lefts[1], low, 0)
    for i in range(3):
        panel(i * 192, lefts[0], joined_ref[:, i * D : (i + 1) * D], 1 + i)
    for i in range(4):
        panel(768 + i * 192, lefts[2], pre_ref[:, i * D : (i + 1) * D], 4 + i)
    norms = norm_ref[0:16, :].astype(F32)
    for i in range(1, 4):
        norms = norms + norm_ref[i * 16 : (i + 1) * 16, :].astype(F32)
    sums_ref[8:16, :] = norms[:8]


def weight_grads(fsdp, one, mixed, two, hidden, joined, low, pre, norms):
    tokens = one.shape[0]
    return pl.pallas_call(
        weight_kernel,
        out_shape=(
            jax.ShapeDtypeStruct((2304, D), BF),
            jax.ShapeDtypeStruct((16, D), F32),
        ),
        in_specs=[SM] + [VM] * 8,
        out_specs=(VM, VM),
        scratch_shapes=[room(3, D, tokens), room(D, tokens)],
        compiler_params=pltpu.CompilerParams(vmem_limit_bytes=60 * 2**20),
        cost_estimate=pl.CostEstimate(
            flops=2 * 512 * 1769472, bytes_accessed=12 * 2**20, transcendentals=0
        ),
        name="weight_grads",
    )(fsdp, one, mixed, two, hidden, joined, low, pre, norms)


def pair_rows(values):
    lane = lax.broadcasted_iota(jnp.int32, values.shape, 1)
    zero = jnp.zeros_like(values)
    return jnp.concatenate(
        [jnp.where(lane < HEAD_DIM, values, zero), jnp.where(lane >= HEAD_DIM, values, zero)], 0
    )


def contract(left, right, dims):
    return lax.dot_general(left, right, (dims, ((), ())), preferred_element_type=F32)


def allowed_at(tile, block):
    key = tile * TILE + lax.broadcasted_iota(jnp.int32, (TILE, 2 * BLOCK), 0)
    query = block * BLOCK + lax.broadcasted_iota(jnp.int32, (TILE, 2 * BLOCK), 1) % BLOCK
    return key <= query


def low_block(ctx):
    return jnp.minimum(ctx, BLOCKS - 1 - ctx)


def by_height(ctx, own, away, two):
    @pl.when(ctx < BLOCKS // 2)
    def _():
        two[0] = own[...]
        two[1] = away[...]

    @pl.when(ctx >= BLOCKS // 2)
    def _():
        two[0] = away[...]
        two[1] = own[...]


def from_height(ctx, two, own, away):
    @pl.when(ctx < BLOCKS // 2)
    def _():
        own[...] = two[0].astype(own.dtype)
        away[...] = two[1].astype(away.dtype)

    @pl.when(ctx >= BLOCKS // 2)
    def _():
        own[...] = two[1].astype(own.dtype)
        away[...] = two[0].astype(away.dtype)


TILES = BLOCKS * BLOCK // TILE


def load_tiles(pairs, sem):
    loads = []
    for tile in range(TILES):
        rows = pl.ds(tile * TILE, TILE)
        for source, buffer in pairs:
            load = pltpu.make_async_copy(source.at[rows], buffer.at[rows], sem.at[len(loads)])
            load.start()
            loads.append(load)
    return loads


def wait_tiles(loads, b):
    half = len(loads) // 2
    for load in loads[b * half : (b + 1) * half]:
        load.wait()


def forward_kernel(
    ctx_ref, q_own, q_away, k_in, v_in, mixed_own, mixed_away, turned_ref, log_ref,
    top, mass, acc, k_ref, v_ref, q_two, mixed_two, sem,
):
    ctx = ctx_ref[0]
    loads = load_tiles(((k_in, k_ref), (v_in, v_ref)), sem)
    by_height(ctx, q_own, q_away, q_two)
    for b in (0, 1):
        block = low_block(ctx) if b == 0 else BLOCKS - 1 - low_block(ctx)
        wait_tiles(loads, b)
        rows = slice(b * BLOCK, (b + 1) * BLOCK)
        q_ref, mixed_ref = q_two.at[b], mixed_two.at[b]
        queries = [
            pair_rows(q_ref[:, p * 128 : (p + 1) * 128] * jnp.asarray(0.125, BF))
            for p in range(PAIRS)
        ]

        def step(tile, masked):
            start = pl.multiple_of(tile * TILE, TILE)
            for p in range(PAIRS):
                cols = slice(p * 128, (p + 1) * 128)
                scores = contract(k_ref[pl.ds(start, TILE), cols], queries[p], ((1,), (1,)))
                if masked:
                    scores = jnp.where(allowed_at(tile, block), scores, masked_score)
                    new_top = jnp.max(scores, 0, keepdims=True)
                else:
                    old_top = top[p : p + 1, :]
                    new_top = jnp.maximum(old_top, jnp.max(scores, 0, keepdims=True))
                weights = jnp.exp(scores - new_top)
                fresh_mass = jnp.sum(weights, 0, keepdims=True)
                fresh = contract(
                    v_ref[pl.ds(start, TILE), cols], weights.astype(BF), ((0,), (0,))
                )
                if not masked:
                    fade = jnp.exp(old_top - new_top)
                    fresh_mass = fresh_mass + mass[p : p + 1, :] * fade
                    fresh = fresh + acc[p] * fade
                top[p : p + 1, :] = new_top
                mass[p : p + 1, :] = fresh_mass
                acc[p] = fresh

        step(block // 4, True)

        @pl.loop(0, block // 4)
        def _(tile):
            step(tile, False)

        for p in range(PAIRS):
            cols = slice(p * 128, (p + 1) * 128)
            done = acc[p] / mass[p : p + 1, :]
            turned = jnp.concatenate([done[:HEAD_DIM, :BLOCK], done[HEAD_DIM:, BLOCK:]], 0)
            turned_ref[cols, rows] = turned
            mixed_ref[:, cols] = jnp.transpose(turned).astype(BF)
            row = b * PAIRS + p
            log_ref[row : row + 1, :] = top[p : p + 1, :] + jnp.log(mass[p : p + 1, :])
    from_height(ctx, mixed_two, mixed_own, mixed_away)


def attend_forward(ctx, own, away, keys, values):
    return pl.pallas_call(
        forward_kernel,
        out_shape=(
            jax.ShapeDtypeStruct((BLOCK, HALF), BF),
            jax.ShapeDtypeStruct((BLOCK, HALF), BF),
            jax.ShapeDtypeStruct((HALF, 2 * BLOCK), F32),
            jax.ShapeDtypeStruct((8, 2 * BLOCK), F32),
        ),
        in_specs=[SM, VM, VM, ANY, ANY],
        out_specs=(VM, VM, VM, VM),
        scratch_shapes=[
            pltpu.VMEM((8, 2 * BLOCK), F32),
            pltpu.VMEM((8, 2 * BLOCK), F32),
            pltpu.VMEM((PAIRS, 128, 2 * BLOCK), F32),
            room(BLOCKS * BLOCK, HALF),
            room(BLOCKS * BLOCK, HALF),
            room(2, BLOCK, HALF),
            room(2, BLOCK, HALF),
            pltpu.SemaphoreType.DMA((2 * TILES,)),
        ],
        compiler_params=pltpu.CompilerParams(vmem_limit_bytes=60 * 2**20),
        cost_estimate=pl.CostEstimate(
            flops=4 * 33 * 128 * 128 * 6 * 128, bytes_accessed=8 * 2**20, transcendentals=33 * 128 * 128 * 6
        ),
        name="attend_forward",
    )(ctx, own, away, keys, values)


def backward_kernel(
    ctx_ref, q_own, q_away, k_in, v_in, g_own, g_away, turned_ref, log_ref,
    gq_own, gq_away, gk_ref, gv_ref,
    gk_acc, gv_acc, gq_acc, k_ref, v_ref, q_two, g_two, gq_two, sem,
):
    ctx = ctx_ref[0]
    loads = load_tiles(((k_in, k_ref), (v_in, v_ref)), sem)
    by_height(ctx, q_own, q_away, q_two)
    by_height(ctx, g_own, g_away, g_two)
    gk_acc[...] = jnp.zeros_like(gk_acc)
    gv_acc[...] = jnp.zeros_like(gv_acc)
    for b in (0, 1):
        block = low_block(ctx) if b == 0 else BLOCKS - 1 - low_block(ctx)
        wait_tiles(loads, b)
        rows = slice(b * BLOCK, (b + 1) * BLOCK)
        queries, grads, deltas = [], [], []
        q_ref, g_ref, gq_ref = q_two.at[b], g_two.at[b], gq_two.at[b]
        for p in range(PAIRS):
            cols = slice(p * 128, (p + 1) * 128)
            queries.append(pair_rows(q_ref[:, cols] * jnp.asarray(0.125, BF)))
            grad = g_ref[:, cols]
            grads.append(pair_rows(grad))
            both = jnp.transpose(grad.astype(F32)) * turned_ref[cols, rows]
            deltas.append(
                jnp.concatenate(
                    [
                        jnp.sum(both[:HEAD_DIM], 0, keepdims=True),
                        jnp.sum(both[HEAD_DIM:], 0, keepdims=True),
                    ],
                    1,
                )
            )
        gq_acc[...] = jnp.zeros_like(gq_acc)

        def step(tile, masked):
            start = pl.multiple_of(tile * TILE, TILE)
            here = pl.ds(start, TILE)
            for p in range(PAIRS):
                cols = slice(p * 128, (p + 1) * 128)
                row = b * PAIRS + p
                keys = k_ref[here, cols]
                scores = contract(keys, queries[p], ((1,), (1,)))
                chances = jnp.exp(scores - log_ref[row : row + 1, :])
                if masked:
                    chances = jnp.where(allowed_at(tile, block), chances, 0.0)
                grad_chance = contract(v_ref[here, cols], grads[p], ((1,), (1,)))
                grad_score = (chances * (grad_chance - deltas[p])).astype(BF)
                gv_acc[here, cols] += contract(chances.astype(BF), grads[p], ((1,), (0,)))
                gk_acc[here, cols] += contract(grad_score, queries[p], ((1,), (0,)))
                gq_acc[p] += contract(keys, grad_score, ((0,), (0,)))

        step(block // 4, True)

        @pl.loop(0, block // 4)
        def _(tile):
            step(tile, False)

        for p in range(PAIRS):
            cols = slice(p * 128, (p + 1) * 128)
            done = gq_acc[p] * 0.125
            turned = jnp.concatenate([done[:HEAD_DIM, :BLOCK], done[HEAD_DIM:, BLOCK:]], 0)
            gq_ref[:, cols] = jnp.transpose(turned).astype(gq_ref.dtype)
    from_height(ctx, gq_two, gq_own, gq_away)
    gk_ref[...] = gk_acc[...].astype(BF)
    gv_ref[...] = gv_acc[...].astype(BF)


def attend_backward(ctx, own, away, keys, values, grad_own, grad_away, turned, log_total):
    whole = jax.ShapeDtypeStruct((BLOCKS * BLOCK, HALF), BF)
    return pl.pallas_call(
        backward_kernel,
        out_shape=(
            jax.ShapeDtypeStruct((BLOCK, HALF), F32),
            jax.ShapeDtypeStruct((BLOCK, HALF), BF),
            whole,
            whole,
        ),
        in_specs=[SM, VM, VM, ANY, ANY] + [VM] * 4,
        out_specs=(VM,) * 4,
        scratch_shapes=[
            pltpu.VMEM((BLOCKS * BLOCK, HALF), F32),
            pltpu.VMEM((BLOCKS * BLOCK, HALF), F32),
            pltpu.VMEM((PAIRS, 128, 2 * BLOCK), F32),
            room(BLOCKS * BLOCK, HALF),
            room(BLOCKS * BLOCK, HALF),
            room(2, BLOCK, HALF),
            room(2, BLOCK, HALF),
            pltpu.VMEM((2, BLOCK, HALF), F32),
            pltpu.SemaphoreType.DMA((2 * TILES,)),
        ],
        compiler_params=pltpu.CompilerParams(vmem_limit_bytes=60 * 2**20),
        cost_estimate=pl.CostEstimate(
            flops=10 * 33 * 128 * 128 * 6 * 128, bytes_accessed=16 * 2**20, transcendentals=33 * 128 * 128 * 6
        ),
        name="attend_backward",
    )(ctx, own, away, keys, values, grad_own, grad_away, turned, log_total)


GAIN_ONE, BIAS_ONE, GAIN_TWO, BIAS_TWO, BIAS_OUT, BIAS_DOWN, BIAS_QKV, BIAS_UP = (
    0, 1, 2, 3, 4, 5, 6, 9,
)


def norm_parts(values):
    centre = jnp.mean(values, -1, keepdims=True)
    shifted = values - centre
    spread = jnp.mean(shifted * shifted, -1, keepdims=True)
    scale = lax.rsqrt(spread + epsilon)
    return shifted * scale, scale


def norm_input_grad(grad_norm, gain, unit, scale):
    e = grad_norm * gain
    return scale * (
        e - jnp.mean(e, -1, keepdims=True) - unit * jnp.mean(e * unit, -1, keepdims=True)
    )


def turn_tables(first_row, row_count):
    shape = (row_count, 128)
    feature = lax.broadcasted_iota(jnp.int32, shape, 1) % HEAD_DIM
    position = first_row + lax.broadcasted_iota(jnp.int32, shape, 0)
    half_rot = ROTARY // 2
    exponent = (feature % half_rot).astype(F32) * (2.0 / ROTARY)
    angle = position.astype(F32) * jnp.power(10000.0, -exponent)
    cosine, sine = jnp.cos(angle), jnp.sin(angle)
    keep = jnp.where(feature < ROTARY, cosine, 1.0)
    low = jnp.where(feature < half_rot, -sine, 0.0)
    high = jnp.where((feature >= half_rot) & (feature < ROTARY), sine, 0.0)
    return keep, low, high


def rotate(values, table_ref):
    shift = ROTARY // 2
    return (
        values * table_ref[0]
        + pltpu.roll(values, 128 - shift, 1) * table_ref[1]
        + pltpu.roll(values, shift, 1) * table_ref[2]
    )


def rotate_back(values, table_ref):
    shift = ROTARY // 2
    return (
        values * table_ref[0]
        + pltpu.roll(values * table_ref[1], shift, 1)
        + pltpu.roll(values * table_ref[2], 128 - shift, 1)
    )


def phi_parts(values):
    cumulative = 0.5 * (1.0 + lax.erf(values * (2.0**-0.5)))
    density = jnp.exp(-0.5 * values * values) * (0.5 / jnp.pi) ** 0.5
    return cumulative, density


def line(vec_ref, row):
    return vec_ref[row : row + 1, :]


def put_halves(upper_ref, low, high, mine_ref, theirs_ref):
    upper = upper_ref[0] == 1

    @pl.when(upper)
    def _():
        mine_ref[...] = high
        theirs_ref[...] = low

    @pl.when(jnp.logical_not(upper))
    def _():
        mine_ref[...] = low
        theirs_ref[...] = high


def put_joined(upper_ref, mine, theirs, out_ref, first):
    upper = upper_ref[0] == 1
    low, high = slice(first, first + HALF), slice(first + HALF, first + D)

    @pl.when(upper)
    def _():
        out_ref[:, low] = theirs
        out_ref[:, high] = mine

    @pl.when(jnp.logical_not(upper))
    def _():
        out_ref[:, low] = mine
        out_ref[:, high] = theirs


def enter(upper_ref, stream, vec_ref, weight_ref, table_ref, one_ref, two_ref, *parts):
    unit, _ = norm_parts(stream)
    one = (unit * line(vec_ref, GAIN_ONE) + line(vec_ref, BIAS_ONE)).astype(BF)
    one_ref[...] = one
    two_ref[...] = (unit * line(vec_ref, GAIN_TWO) + line(vec_ref, BIAS_TWO)).astype(BF)
    for i in range(3):
        joined = contract(one, weight_ref[:, i * D : (i + 1) * D], ((1,), (0,)))
        joined = joined + line(vec_ref, BIAS_QKV + i)
        groups = [joined[:, g * 128 : (g + 1) * 128] for g in range(6)]
        if i < 2:
            groups = [rotate(group, table_ref) for group in groups]
        groups = [group.astype(BF) for group in groups]
        put_halves(
            upper_ref,
            jnp.concatenate(groups[:3], 1),
            jnp.concatenate(groups[3:], 1),
            parts[2 * i],
            parts[2 * i + 1],
        )


def enter_kernel(upper_ref, tokens_ref, vec_ref, weight_ref, keep, low, high, *outs):
    table_ref = (keep[...], low[...], high[...])
    enter(upper_ref, tokens_ref[...].astype(F32), vec_ref, weight_ref, table_ref, *outs)


def leave(upper_ref, stream_ref, own_ref, away_ref, weight_ref, mlp_ref, vec_ref, mixed_ref):
    put_joined(upper_ref, own_ref[...], away_ref[...], mixed_ref, 0)
    return (
        stream_ref[...].astype(F32)
        + contract(mixed_ref[...], weight_ref[...], ((1,), (0,)))
        + line(vec_ref, BIAS_OUT)
        + mlp_ref[...]
        + line(vec_ref, BIAS_DOWN)
    )


def pass_kernel(
    upper_ref, stream_ref, own_ref, away_ref, out_ref, mlp_ref, vec_ref,
    next_vec_ref, weight_ref, keep, low, high, mixed_ref, next_ref, *outs,
):
    table_ref = (keep[...], low[...], high[...])
    stream = leave(upper_ref, stream_ref, own_ref, away_ref, out_ref, mlp_ref, vec_ref, mixed_ref)
    next_ref[...] = stream
    enter(upper_ref, stream, next_vec_ref, weight_ref, table_ref, *outs)


def last_kernel(
    upper_ref, stream_ref, own_ref, away_ref, out_ref, mlp_ref, vec_ref, mixed_ref, next_ref
):
    next_ref[...] = leave(
        upper_ref, stream_ref, own_ref, away_ref, out_ref, mlp_ref, vec_ref, mixed_ref
    ).astype(BF)


def mlp_kernel(two_ref, up_ref, down_ref, vec_ref, pre_ref, hidden_ref, mlp_ref):
    two = two_ref[...]
    for i in range(FF // D):
        cols = slice(i * D, (i + 1) * D)
        pre = contract(two, up_ref[:, cols], ((1,), (0,))) + line(vec_ref, BIAS_UP + i)
        pre_ref[:, cols] = pre
        hidden = (pre * phi_parts(pre)[0]).astype(BF)
        hidden_ref[:, cols] = hidden
        fresh = contract(hidden, down_ref[cols, :], ((1,), (0,)))
        mlp_ref[...] = fresh if i == 0 else mlp_ref[...] + fresh


def back(upper_ref, gradient, weight_ref, low_ref, mine_ref, theirs_ref):
    low = gradient.astype(BF)
    low_ref[...] = low
    mixed = contract(low, weight_ref[...], ((1,), (1,))).astype(BF)
    put_halves(upper_ref, mixed[:, :HALF], mixed[:, HALF:], mine_ref, theirs_ref)


def back_kernel(upper_ref, cotangent_ref, weight_ref, *outs):
    back(upper_ref, cotangent_ref[...].astype(F32), weight_ref, *outs)


def join_kernel(
    more, upper_ref, own_ref, back_ref, own_q, back_q, keep, low, high, weight_ref, stream_ref,
    vec_ref, two_ref, gradient_ref, *refs,
):
    table_ref = (keep[...], low[...], high[...])
    next_weight, refs = (refs[:1], refs[1:]) if more else ((), refs)
    joined_ref, sums_ref, next_ref, *outs = refs

    def turned(values):
        groups = [rotate_back(values[:, g * 128 : (g + 1) * 128], table_ref) for g in range(3)]
        return jnp.concatenate(groups, 1).astype(BF)

    put_joined(upper_ref, turned(own_q[...]), turned(back_q[...].astype(F32)), joined_ref, 0)
    put_joined(upper_ref, turned(own_ref[0]), turned(back_ref[0].astype(F32)), joined_ref, D)
    put_joined(upper_ref, own_ref[1].astype(BF), back_ref[1], joined_ref, 2 * D)
    one = contract(joined_ref[...], weight_ref[...], ((1,), (1,)))
    two = two_ref[...]
    unit, scale = norm_parts(stream_ref[...].astype(F32))
    sums = [jnp.sum(values, 0, keepdims=True) for values in (one * unit, one, two * unit, two)]
    sums_ref[...] = jnp.concatenate(sums + [jnp.zeros((12, D), F32)], 0).astype(BF)
    gradient = (
        gradient_ref[...].astype(F32)
        + norm_input_grad(one, line(vec_ref, GAIN_ONE), unit, scale)
        + norm_input_grad(two, line(vec_ref, GAIN_TWO), unit, scale)
    )
    next_ref[...] = gradient
    if more:
        back(upper_ref, gradient, next_weight[0], *outs)


def unpack_kernel(rows_ref, qkv_ref, out_ref, up_ref, down_ref):
    for i in range(3):
        qkv_ref[0, :, i * D : (i + 1) * D] = rows_ref[0, i * 192 : (i + 1) * 192, :].astype(F32)
    out_ref[0] = rows_ref[0, 576:768, :].astype(F32)
    for i in range(4):
        up_ref[0, :, i * D : (i + 1) * D] = rows_ref[
            0, 768 + i * 192 : 960 + i * 192, :
        ].astype(F32)
    down_ref[0] = rows_ref[0, 1536:, :].astype(F32)


def unpack(rows):
    shapes = [(192, 3 * D), (192, D), (192, FF), (D, D)]
    return pl.pallas_call(
        unpack_kernel,
        grid=(LAYERS,),
        out_shape=tuple(jax.ShapeDtypeStruct((LAYERS,) + shape, F32) for shape in shapes),
        in_specs=[pl.BlockSpec((1, 2304, D), lambda i: (i, 0, 0))],
        out_specs=tuple(pl.BlockSpec((1,) + shape, lambda i: (i, 0, 0)) for shape in shapes),
        compiler_params=pltpu.CompilerParams(vmem_limit_bytes=60 * 2**20),
        name="unpack",
    )(rows)


def dense(name, kernel, specs, outs, args, flops):
    shapes = tuple(
        jax.ShapeDtypeStruct((BLOCK, size) if isinstance(size, int) else size, kind)
        for size, kind in outs
    )
    return pl.pallas_call(
        kernel,
        out_shape=shapes,
        in_specs=specs,
        out_specs=(VM,) * len(shapes),
        compiler_params=pltpu.CompilerParams(vmem_limit_bytes=60 * 2**20),
        cost_estimate=pl.CostEstimate(
            flops=2 * BLOCK * flops, bytes_accessed=2 * flops, transcendentals=0
        ),
        name=name,
    )(*args)


def vector_kernel(table_ref, *out_refs):
    for layer_index, out_ref in enumerate(out_refs):
        at = slice(layer_index, layer_index + 1)
        for row in range(6):
            pieces = [table_ref[f, at, row * 192 : (row + 1) * 192] for f in range(4)]
            out_ref[row : row + 1, :] = jnp.concatenate(pieces, 1)
        joined = jnp.concatenate([table_ref[f, at, 1152:1728] for f in range(4)], 1)
        for i in range(3):
            out_ref[BIAS_QKV + i : BIAS_QKV + i + 1, :] = joined[:, i * D : (i + 1) * D]
        for f in range(4):
            out_ref[BIAS_UP + f : BIAS_UP + f + 1, :] = table_ref[f, at, 1728:2496]
        out_ref[13:, :] = jnp.zeros((3, D), F32)


def order_vectors(table):
    return pl.pallas_call(
        vector_kernel,
        out_shape=(jax.ShapeDtypeStruct((16, D), F32),) * LAYERS,
        in_specs=[VM],
        out_specs=(VM,) * LAYERS,
        name="order_vectors",
    )(table)


ENTER_OUTS = ((D, BF),) * 2 + ((HALF, BF),) * 6


def shards(
    tokens,
    cotangent,
    ln1_gain,
    ln1_bias,
    ln2_gain,
    ln2_bias,
    qkv_weight,
    qkv_bias,
    out_weight,
    out_bias,
    up_weight,
    up_bias,
    down_weight,
    down_bias,
):
    row_count = tokens.shape[1]
    fsdp = lax.axis_index("fsdp")
    ctx = lax.axis_index("ctx")
    ctx_word = ctx.astype(jnp.int32).reshape(1)
    upper = (ctx % 2).astype(jnp.int32).reshape(1)
    tables = turn_tables(ctx * row_count, row_count)

    vectors = (ln1_gain, ln1_bias, ln2_gain, ln2_bias, out_bias, down_bias, qkv_bias, up_bias)
    packed = jnp.concatenate(vectors, 1).astype(F32)
    packed = jnp.pad(packed, ((0, 8 - LAYERS), (0, 2560 - packed.shape[1])))
    first_weight, table = gather_first(qkv_weight, packed)
    vecs = order_vectors(table)
    qkv_full = [first_weight, None]
    gathered = [None] * LAYERS
    stream = tokens[0]
    entered = dense(
        "enter",
        enter_kernel,
        [SM] + [VM] * 6,
        ENTER_OUTS,
        (upper, stream, vecs[0], first_weight, *tables),
        D * 3 * D,
    )
    saved = []
    for layer_index in range(LAYERS):
        norm_one, norm_two, q_own, q_away, k_own, k_away, v_own, v_away = entered
        jobs = [(layer_index, out_weight), (layer_index, up_weight), (layer_index, down_weight)]
        if layer_index + 1 < LAYERS:
            jobs.append((layer_index + 1, qkv_weight))
        q_other, keys, values, w_out, w_up, w_down, *more = gather_pair(
            "gather_pair_%d" % layer_index,
            1 + layer_index,
            (q_away, k_away, v_away),
            (k_own, v_own),
            jobs,
        )
        if more:
            qkv_full[layer_index + 1] = more[0]
        gathered[layer_index] = (qkv_full[layer_index], w_out, w_up, w_down)
        keys = keys.reshape(BLOCKS * BLOCK, HALF)
        values = values.reshape(BLOCKS * BLOCK, HALF)
        mixed_own, mixed_away, turned, log_total = attend_forward(
            ctx_word, q_own, q_other, keys, values
        )
        mixed_back = mirrored(mixed_away)
        hidden_pre, hidden_low, mlp_branch = dense(
            "mlp",
            mlp_kernel,
            [VM] * 4,
            ((FF, F32), (FF, BF), (D, F32)),
            (norm_two, w_up, w_down, vecs[layer_index]),
            2 * D * FF,
        )
        before = stream
        common = (upper, stream, mixed_own, mixed_back, w_out, mlp_branch, vecs[layer_index])
        if more:
            mixed_low, stream, *entered = dense(
                "pass_on",
                pass_kernel,
                [SM] + [VM] * 11,
                ((D, BF), (D, F32)) + ENTER_OUTS,
                common + (vecs[layer_index + 1], more[0], *tables),
                D * 4 * D,
            )
        else:
            mixed_low, output = dense(
                "last", last_kernel, [SM] + [VM] * 6, ((D, BF), (D, BF)), common, D * D
            )
        lefts = (norm_one, mixed_low, norm_two)
        saved.append(
            (before, q_own, q_other, keys, values, turned, log_total, hidden_pre, hidden_low, lefts)
        )

    gradient = cotangent[0]
    waiting, early_rows, late_rows = (), [None] * 2, [None] * 2
    grad_low, grad_own, grad_away = dense(
        "back",
        back_kernel,
        [SM, VM, VM],
        ((D, BF), (HALF, BF), (HALF, BF)),
        (upper, gradient, gathered[LAYERS - 1][1]),
        D * D,
    )
    for layer_index in range(LAYERS - 1, -1, -1):
        w_qkv, w_out, w_up, w_down = gathered[layer_index]
        before, q_own, q_other, keys, values, turned, log_total, hidden_pre, hidden_low, lefts = (
            saved[layer_index]
        )
        grad_back = mirrored(grad_away)
        gq_own, gq_away, grad_keys, grad_values = attend_backward(
            ctx_word, q_own, q_other, keys, values, grad_own, grad_back, turned, log_total
        )
        whole = (BLOCKS, BLOCK, HALF)
        own_pair, grad_norm_two, back_pair, back_query, hidden, pre, *gathered_rows = scatter_pair(
            "scatter_pair_%d" % layer_index,
            3 + layer_index,
            grad_keys.reshape(whole),
            grad_values.reshape(whole),
            gq_away,
            hidden_low,
            hidden_pre,
            w_up,
            w_down,
            lefts + (grad_low,) + waiting,
        )
        early_rows[layer_index] = (hidden, *gathered_rows[:4], pre)
        if waiting:
            late_rows[layer_index + 1] = gathered_rows[4:]
        going_on = layer_index > 0
        grad_joined, norm_sums, gradient, *outs = dense(
            "join_%d" % layer_index,
            functools.partial(join_kernel, going_on),
            [SM] + [VM] * (13 if going_on else 12),
            ((3 * D, BF), ((16, D), BF), (D, F32))
            + (((D, BF), (HALF, BF), (HALF, BF)) if going_on else ()),
            (
                upper,
                own_pair,
                back_pair,
                gq_own,
                back_query,
                *tables,
                w_qkv,
                before,
                vecs[layer_index],
                grad_norm_two,
                gradient,
            )
            + ((gathered[layer_index - 1][1],) if going_on else ()),
            D * 3 * D,
        )
        waiting = (grad_joined, norm_sums)
        if going_on:
            grad_low, grad_own, grad_away = outs
    late_rows[0] = gather_late(*waiting)
    fsdp_word = fsdp.astype(jnp.int32).reshape(1)
    packs, lines = [], []
    for layer_index in range(LAYERS):
        hidden, one, mixed, two, low, pre = early_rows[layer_index]
        joined, norms = late_rows[layer_index]
        rows, sums = weight_grads(fsdp_word, one, mixed, two, hidden, joined, low, pre, norms)
        packs.append(rows)
        lines.append(sums)
    summed, small = sum_over_ctx(*packs, *lines)

    def own_part(vectors, width):
        return lax.dynamic_slice_in_dim(vectors, fsdp * width, width, vectors.ndim - 1)

    bias_sum = own_part(small[:, 0], 192)
    joined_sum = own_part(small[:, 1:4].reshape(LAYERS, 3 * D), 576)
    up_sum = own_part(small[:, 4:8].reshape(LAYERS, 4 * D), D)
    norm_sums = own_part(small[:, 8:12], 192)
    qkv_grad, out_grad, up_grad, down_grad = unpack(summed.reshape(LAYERS, 2304, D))
    return (
        output[None],
        gradient[None],
        norm_sums[:, 0],
        norm_sums[:, 1],
        norm_sums[:, 2],
        norm_sums[:, 3],
        qkv_grad,
        joined_sum,
        out_grad,
        bias_sum,
        up_grad,
        up_sum,
        down_grad,
        bias_sum,
    )


def solution(mesh):
    matrix, vector = P(None, "fsdp", None), P(None, "fsdp")
    rows = P("fsdp", "ctx", None)
    params = (
        vector,
        vector,
        vector,
        vector,
        matrix,
        vector,
        matrix,
        vector,
        matrix,
        vector,
        matrix,
        vector,
    )
    return jax.shard_map(
        shards,
        mesh=mesh,
        in_specs=(rows, rows) + params,
        out_specs=(rows, rows) + params,
        check_vma=False,
    )
```

```python
import functools

import jax
import jax.numpy as jnp
from jax import lax
from jax.experimental import pallas as pl
from jax.experimental.pallas import tpu as pltpu
from jax.sharding import PartitionSpec as P

D = 768
HEADS = 12
HEAD_DIM = 64
FF = 3072
ROTARY = 16
LAYERS = 2
HALF = 384
BLOCK = 128
BLOCKS = 32
TILE = 512
PAIRS = 3

epsilon = 1e-05
masked_score = -1e30
MESH = pl.DeviceIdType.MESH
BF = jnp.bfloat16
F32 = jnp.float32


def mirrored(values):
    pairs = [(f * 32 + c, f * 32 + 31 - c) for f in range(4) for c in range(32)]
    return lax.ppermute(values, ("fsdp", "ctx"), pairs)


class Place:
    def __init__(self):
        self.fsdp = lax.axis_index("fsdp")
        self.ctx = lax.axis_index("ctx")
        self.y, self.z, self.h = self.ctx // 8, (self.ctx // 2) % 4, self.ctx % 2
        self.x_lo, self.core = self.fsdp // 2, self.fsdp % 2
        self.beside = (self.fsdp + 1 - 2 * self.core, self.ctx)
        self.mirror = (self.fsdp, BLOCKS - 1 - self.ctx)
        self.half = (self.fsdp, self.ctx + 1 - 2 * self.h)

    def along_x(self, step):
        x = (2 * self.h + self.x_lo + step) % 4
        return (2 * (x % 2) + self.core, self.y * 8 + self.z * 2 + x // 2)

    def ctx_at(self, dy, dz):
        return ((self.y + dy) % 4) * 8 + ((self.z + dz) % 4) * 2 + self.h

    def ring(self, t, da, db):
        return self.ctx_at(da, db) if t == 0 else self.ctx_at(db, da)

    def near(self, t, axis, sign):
        steps = (sign, 0) if axis == 0 else (0, sign)
        return (self.fsdp, self.ring(t, *steps))

    def around(self):
        return [self.near(0, axis, sign) for axis in (0, 1) for sign in (1, -1)]

    def greet(self, partners):
        barrier = pltpu.get_barrier_semaphore()
        for partner in partners:
            pl.semaphore_signal(barrier, inc=1, device_id=partner, device_id_type=MESH)
        pl.semaphore_wait(barrier, len(partners))


class Wire:
    def __init__(self, send_sem, recv_sem, local_sem=None):
        self.send_sem, self.recv_sem, self.local_sem = send_sem, recv_sem, local_sem
        self.sent, self.local, self.bounced = [], [], []

    def push(self, source, target, partner):
        number = len(self.sent)
        copy = pltpu.make_async_remote_copy(
            src_ref=source,
            dst_ref=target,
            send_sem=self.send_sem.at[number],
            recv_sem=self.recv_sem.at[number],
            device_id=partner,
            device_id_type=MESH,
        )
        copy.start()
        self.sent.append(copy)
        return copy

    def keep(self, source, target, bounce=None):
        if bounce is None:
            copy = pltpu.make_async_copy(source, target, self.local_sem.at[len(self.local)])
        else:
            copy = pltpu.make_async_copy(source, bounce, self.local_sem.at[len(self.local)])
            self.bounced.append((len(self.local), bounce, target))
        copy.start()
        self.local.append(copy)

    def flush(self):
        for number, bounce, target in self.bounced:
            self.local[number].wait()
            copy = pltpu.make_async_copy(bounce, target, self.local_sem.at[number])
            copy.start()
            self.local[number] = copy
        self.bounced = []

    def drain(self):
        for copy in self.sent:
            copy.wait_send()
        for copy in self.local:
            copy.wait()


def share_param(place, wire, source, target, bounce):
    rows = source.shape[0]
    cut = rows // 2
    mine, far = place.fsdp * rows, ((place.fsdp + 2) % 4) * rows
    parts = [(0, cut, 1), (cut, cut, 3)]
    across = [
        wire.push(
            source.at[pl.ds(start, count)],
            target.at[pl.ds(mine + start, count)],
            place.along_x(step),
        )
        for start, count, step in parts
    ]
    beside = wire.push(source, target.at[pl.ds(mine, rows)], place.beside)
    wire.keep(source, target.at[pl.ds(mine, rows)], bounce)
    last = [beside]

    def onward(copy, start, count):
        copy.wait_recv()
        spot = target.at[pl.ds(far + start, count)]
        last.append(wire.push(spot, spot, place.beside))

    steps = [
        functools.partial(onward, copy, start, count)
        for copy, (start, count, _) in zip(across, parts)
    ]
    return steps, last


def share_rows(place, wire, source, target):
    rows = source.shape[0]
    cut = rows // 2
    parts = [(0, cut, 1), (cut, cut, 3)] if rows % 32 == 0 else [(0, rows, 1)]
    across = [
        wire.push(
            source.at[pl.ds(start, count)],
            target.at[pl.ds(2 * rows + start, count)],
            place.along_x(step),
        )
        for start, count, step in parts
    ]
    last = [wire.push(source, target.at[pl.ds(rows, rows)], place.beside)]
    wire.keep(source, target.at[pl.ds(0, rows)])

    def onward(copy, start, count):
        copy.wait_recv()
        last.append(
            wire.push(
                target.at[pl.ds(2 * rows + start, count)],
                target.at[pl.ds(3 * rows + start, count)],
                place.beside,
            )
        )

    steps = [
        functools.partial(onward, copy, start, count)
        for copy, (start, count, _) in zip(across, parts)
    ]
    return steps, last


def share_columns(place, wire, source, target, stage):
    rows = source.shape[0]
    cut = rows // 2
    fsdp, core = place.fsdp, place.core
    parts = [(0, cut, 1), (cut, cut, 3)]

    def panel(start, count, shard):
        return source.at[pl.ds(start, count), pl.ds(pl.multiple_of(shard * D, D), D)]

    passing, last = [], []
    for start, count, step in parts:
        passing.append(
            wire.push(
                panel(start, count, 3 - fsdp),
                stage.at[pl.ds(start, count)],
                place.along_x(step),
            )
        )
    for start, count, step in parts:
        last.append(
            wire.push(
                panel(start, count, (fsdp + 2) % 4),
                target.at[pl.ds(2 * rows + start, count)],
                place.along_x(step),
            )
        )
    last.append(
        wire.push(
            panel(0, rows, fsdp + 1 - 2 * core), target.at[pl.ds(rows, rows)], place.beside
        )
    )
    wire.keep(panel(0, rows, fsdp), target.at[pl.ds(0, rows)])

    def onward(copy, start, count):
        copy.wait_recv()
        last.append(
            wire.push(
                stage.at[pl.ds(start, count)],
                target.at[pl.ds(3 * rows + start, count)],
                place.beside,
            )
        )

    steps = [
        functools.partial(onward, copy, start, count)
        for copy, (start, count, _) in zip(passing, parts)
    ]
    return steps, last


def spread(place, wire, own, spot, ready, between=()):
    between = list(between)
    arrivals = {}

    def push(t, da, db, b, axis, sign):
        target = spot(t, place.ring(t, da, db), b)
        source = own(t, b) if da == 0 and db == 0 else target
        sa, sb = (sign, 0) if axis == 0 else (0, sign)
        arrivals[t, (da - sa) % 4, (db - sb) % 4, b] = wire.push(
            source, target, place.near(t, axis, sign)
        )

    def landed(t, da, db):
        for b in (0, 1):
            arrivals[t, da, db, b].wait_recv()

    def pause():
        if between:
            between.pop(0)()

    for b in (0, 1):
        for t in (0, 1):
            ready(t, b)
            for axis in (0, 1):
                for sign in (1, -1):
                    push(t, 0, 0, b, axis, sign)
    for da, keep, onward in ((1, 0, -1), (3, 1, 1)):
        for t in (0, 1):
            landed(t, da, 0)
            push(t, da, 0, keep, 0, onward)
            for sign in (1, -1):
                for b in (0, 1):
                    push(t, da, 0, b, 1, sign)
    for db, keep, onward in ((1, 0, -1), (3, 1, 1)):
        for t in (0, 1):
            landed(t, 0, db)
            push(t, 0, db, keep, 1, onward)
    for t in (0, 1):
        landed(t, 2, 0)
        for sign in (1, -1):
            for b in (0, 1):
                push(t, 2, 0, b, 1, sign)
    pause()
    for da in (1, 3, 2):
        for db, keep, onward in ((1, 0, -1), (3, 1, 1)):
            for t in (0, 1):
                landed(t, da, db)
                push(t, da, db, keep, 1, onward)
    while between:
        pause()
    for da in (0, 1, 3, 2):
        for t in (0, 1):
            landed(t, da, 2)


ANY = pl.BlockSpec(memory_space=pl.ANY)
VM = pl.BlockSpec(memory_space=pltpu.VMEM)
SM = pl.BlockSpec(memory_space=pltpu.SMEM)


def room(*shape):
    return pltpu.VMEM(shape, BF)


def sems(count, local):
    return [
        pltpu.SemaphoreType.DMA((count,)),
        pltpu.SemaphoreType.DMA((count,)),
        pltpu.SemaphoreType.DMA((local,)),
    ]


def full_shape(shard):
    return jax.ShapeDtypeStruct((4 * shard.shape[-2], shard.shape[-1]), BF)


def first_kernel(weight_ref, vector_ref, weight_out, vector_out, bounce, *sem):
    place, wire = Place(), Wire(*sem)
    place.greet([place.beside, place.along_x(1), place.along_x(3)])
    far = vector_out.at[(place.fsdp + 2) % 4]
    across = wire.push(vector_ref, vector_out.at[place.fsdp], place.along_x(1))
    last = [wire.push(vector_ref, vector_out.at[place.fsdp], place.beside)]
    wire.keep(vector_ref, vector_out.at[place.fsdp])
    steps, ends = share_param(place, wire, weight_ref.at[0], weight_out, bounce)
    wire.flush()
    across.wait_recv()
    last.append(wire.push(far, far, place.beside))
    for step in steps:
        step()
    for copy in last + ends:
        copy.wait_recv()
    wire.drain()


def gather_first(weight, vectors):
    return pl.pallas_call(
        first_kernel,
        out_shape=(full_shape(weight), jax.ShapeDtypeStruct((4,) + vectors.shape, F32)),
        in_specs=[ANY, VM],
        out_specs=(ANY, ANY),
        scratch_shapes=[room(*weight.shape[1:])] + sems(16, 4),
        compiler_params=pltpu.CompilerParams(
            collective_id=0, has_side_effects=True, vmem_limit_bytes=60 * 2**20
        ),
        name="gather_first",
    )(weight, vectors)


def gather_kernel(jobs, q_ref, k_ref, v_ref, k_own, v_own, *refs):
    count = len(jobs)
    weights, refs = refs[:count], refs[count:]
    q_out, k_out, v_out = refs[:3]
    weights_out, refs = refs[3 : 3 + count], refs[3 + count :]
    bounces, refs = refs[:count], refs[count:]
    place, wire = Place(), Wire(*refs)
    place.greet(
        place.around() + [place.mirror, place.beside, place.along_x(1), place.along_x(3)]
    )
    ins, outs = (k_own, v_own), (k_out, v_out)
    ctx = place.ctx
    swapped = [
        wire.push(source, out.at[ctx], place.mirror) for source, out in zip((k_ref, v_ref), outs)
    ]
    for t in (0, 1):
        wire.keep(ins[t], outs[t].at[ctx])
    work = []

    def ready(t, b):
        if b == 1:
            if t == 0:
                for layer, weight, target, bounce in zip(jobs, weights, weights_out, bounces):
                    work.append(share_param(place, wire, weight.at[layer], target, bounce))
            swapped[t].wait_recv()
            if t == 1:
                swapped.append(wire.push(q_ref, q_out, place.mirror))

    def spot(t, origin, b):
        return outs[t].at[origin if b == 0 else BLOCKS - 1 - origin]

    def own(t, b):
        return ins[t] if b == 0 else spot(t, ctx, 1)

    def onward(number):
        for steps, _ in work:
            for step in steps[number : number + 1]:
                step()

    spread(
        place,
        wire,
        own,
        spot,
        ready,
        [wire.flush, functools.partial(onward, 0), functools.partial(onward, 1)],
    )
    swapped[2].wait_recv()
    for _, last in work:
        for copy in last:
            copy.wait_recv()
    wire.drain()


def gather_pair(name, number, away, own, jobs):
    layers = [layer for layer, _ in jobs]
    weights = [weight for _, weight in jobs]
    whole = jax.ShapeDtypeStruct((BLOCKS, BLOCK, HALF), BF)
    return pl.pallas_call(
        functools.partial(gather_kernel, layers),
        out_shape=(jax.ShapeDtypeStruct((BLOCK, HALF), BF), whole, whole)
        + tuple(full_shape(weight) for weight in weights),
        in_specs=[VM] * 5 + [ANY] * len(jobs),
        out_specs=(ANY,) * (3 + len(jobs)),
        scratch_shapes=[room(*weight.shape[1:]) for weight in weights] + sems(96, 8),
        compiler_params=pltpu.CompilerParams(
            collective_id=number, has_side_effects=True, vmem_limit_bytes=60 * 2**20
        ),
        name=name,
    )(*away, *own, *weights)


def scatter_kernel(count, gk_ref, gv_ref, gq_ref, hidden_ref, pre_ref, up_ref, down_ref, *refs):
    sources, refs = refs[:count], refs[count:]
    own_out, norm_out, back_out, back_q, hidden_out, grad_pre_out = refs[:6]
    targets, refs = refs[6 : 6 + count], refs[6 + count :]
    far, near, mix, total, last_far, last_near, last_mix, leave, stage = refs[:9]
    up_buffer, down_buffer, grad_pre, load_sem = refs[9:13]
    place, wire = Place(), Wire(*refs[13:])
    loads = []
    for i in range(FF // D):
        cols = slice(i * D, (i + 1) * D)
        for source, buffer in (
            (down_ref.at[cols, :], down_buffer.at[cols, :]),
            (up_ref.at[:, cols], up_buffer.at[i]),
        ):
            load = pltpu.make_async_copy(source, buffer, load_sem.at[len(loads)])
            load.start()
            loads.append(load)
    place.greet(
        place.around() + [place.mirror, place.beside, place.along_x(1), place.along_x(3)]
    )
    ins = (gk_ref, gv_ref)

    def block_at(t, da, db, b):
        origin = place.ring(t, da, db)
        return origin if b == 0 else BLOCKS - 1 - origin

    order = [(da, t) for da in (2, 1, 3, 0) for t in (0, 1)]
    way = {0: 1, 1: -1}
    first, second, loose = {}, {}, {}
    for b in (1, 0):
        for da, t in order:
            first[t, da, b] = wire.push(
                ins[t].at[block_at(t, da, 2, b)], far.at[t, da, b], place.near(t, 1, way[b])
            )
    swapped = [wire.push(gq_ref, back_q, place.mirror)]
    for b in (1, 0):
        for da, t in order:
            loose[t, da, b] = wire.push(
                ins[t].at[block_at(t, da, -way[b], b)],
                near.at[t, da, 1, b],
                place.near(t, 1, -way[b]),
            )
    work = [share_columns(place, wire, hidden_ref, hidden_out, stage)]
    for source, target in zip(sources, targets):
        work.append(share_rows(place, wire, source, target))
    for b in (1, 0):
        if b == 0:
            mlp_back(sources[3][...], pre_ref, loads, up_buffer, down_buffer, grad_pre, norm_out)
            work.append(share_rows(place, wire, grad_pre, grad_pre_out))
        for da, t in order:
            first[t, da, b].wait_recv()
            mix[t, da, b] = (
                ins[t][block_at(t, da, way[b], b)].astype(F32) + far[t, da, b].astype(F32)
            ).astype(BF)
            second[t, da, b] = wire.push(
                mix.at[t, da, b], near.at[t, da, 0, b], place.near(t, 1, way[b])
            )

    def settle(t, da, b):
        loose[t, da, b].wait_recv()
        second[t, da, b].wait_recv()
        total[t, da, b] = (
            ins[t][block_at(t, da, 0, b)].astype(F32)
            + near[t, da, 0, b].astype(F32)
            + near[t, da, 1, b].astype(F32)
        ).astype(BF)

    third, fourth = {}, {}
    for b in (1, 0):
        for t in (0, 1):
            settle(t, 2, b)
            third[t, b] = wire.push(
                total.at[t, 2, b], last_far.at[t, b], place.near(t, 0, way[b])
            )
        for t in (0, 1):
            settle(t, 1, b)
            settle(t, 3, b)
            fourth[t, b] = [
                wire.push(
                    total.at[t, -way[b] % 4, b], last_near.at[t, 1, b], place.near(t, 0, -way[b])
                )
            ]
        for t in (0, 1):
            third[t, b].wait_recv()
            last_mix[t, b] = (
                total[t, way[b] % 4, b].astype(F32) + last_far[t, b].astype(F32)
            ).astype(BF)
            fourth[t, b].append(
                wire.push(last_mix.at[t, b], last_near.at[t, 0, b], place.near(t, 0, way[b]))
            )
        for t in (0, 1):
            settle(t, 0, b)

    def final(t, b):
        for copy in fourth[t, b]:
            copy.wait_recv()
        return (
            total[t, 0, b].astype(F32)
            + last_near[t, 0, b].astype(F32)
            + last_near[t, 1, b].astype(F32)
        )

    for t in (0, 1):
        leave[t] = final(t, 1).astype(BF)
        swapped.append(wire.push(leave.at[t], back_out.at[t], place.mirror))
    for steps, _ in work:
        for step in steps:
            step()
    for t in (0, 1):
        own_out[t] = final(t, 0)
    for _, last in work:
        for copy in last:
            copy.wait_recv()
    for copy in swapped:
        copy.wait_recv()
    wire.drain()


def rows_shape(source):
    return jax.ShapeDtypeStruct((4 * source.shape[0], source.shape[1]), BF)


def mlp_back(low, pre_ref, loads, up_buffer, down_buffer, grad_pre_ref, norm_ref):
    for i in range(FF // D):
        cols = slice(i * D, (i + 1) * D)
        pre = pre_ref[:, cols]
        cumulative, density = phi_parts(pre)
        loads[2 * i].wait()
        hidden = contract(low, down_buffer[cols, :], ((1,), (1,)))
        grad_pre = (hidden * (cumulative + pre * density)).astype(BF)
        grad_pre_ref[:, cols] = grad_pre
        loads[2 * i + 1].wait()
        fresh = contract(grad_pre, up_buffer[i], ((1,), (1,)))
        norm_ref[...] = fresh if i == 0 else norm_ref[...] + fresh


def scatter_pair(name, number, grad_keys, grad_values, away, hidden, pre, up, down, sources):
    return pl.pallas_call(
        functools.partial(scatter_kernel, len(sources)),
        out_shape=(
            jax.ShapeDtypeStruct((2, BLOCK, HALF), F32),
            jax.ShapeDtypeStruct((BLOCK, D), F32),
            jax.ShapeDtypeStruct((2, BLOCK, HALF), BF),
            jax.ShapeDtypeStruct((BLOCK, HALF), BF),
            jax.ShapeDtypeStruct((4 * BLOCK, D), BF),
            jax.ShapeDtypeStruct((4 * BLOCK, FF), BF),
        )
        + tuple(rows_shape(source) for source in sources),
        in_specs=[VM] * 5 + [ANY] * 2 + [VM] * len(sources),
        out_specs=(VM, VM) + (ANY,) * (4 + len(sources)),
        scratch_shapes=[
            room(2, 4, 2, BLOCK, HALF),
            room(2, 4, 2, 2, BLOCK, HALF),
            room(2, 4, 2, BLOCK, HALF),
            room(2, 4, 2, BLOCK, HALF),
            room(2, 2, BLOCK, HALF),
            room(2, 2, 2, BLOCK, HALF),
            room(2, 2, BLOCK, HALF),
            room(2, BLOCK, HALF),
            room(BLOCK, D),
            room(FF // D, D, D),
            room(FF, D),
            room(BLOCK, FF),
            pltpu.SemaphoreType.DMA((2 * FF // D,)),
        ]
        + sems(128, 12),
        compiler_params=pltpu.CompilerParams(
            collective_id=number, has_side_effects=True, vmem_limit_bytes=60 * 2**20
        ),
        name=name,
    )(grad_keys, grad_values, away, hidden, pre, up, down, *sources)


PIECE = 144
CUT = 80


LOADS = 13


def sum_kernel(joined_ref, norm_ref, norm_one, *refs):
    sources, (out_ref, small_out), refs = refs[:LOADS], refs[LOADS : LOADS + 2], refs[LOADS + 2 :]
    buffers, refs = refs[:LOADS], refs[LOADS:]
    rows, joined_land, norm_land, turned, load_sem = refs[:5]
    far, mix, near, total, far_two, mix_two, near_two, part, other, final, small, heard = refs[5:17]
    place, wire = Place(), Wire(*refs[17:])
    loads = []
    for source, buffer in zip(sources, buffers):
        load = pltpu.make_async_copy(source, buffer, load_sem.at[len(loads)])
        load.start()
        loads.append(load)
    y, z, h = place.y, place.z, place.h
    turns = [
        (place.fsdp, (y + 1 - 2 * (y % 2)) * 8 + z * 2 + h),
        (place.fsdp, ((y + 2) % 4) * 8 + z * 2 + h),
        (place.fsdp, y * 8 + (z + 1 - 2 * (z % 2)) * 2 + h),
        (place.fsdp, y * 8 + ((z + 2) % 4) * 2 + h),
        place.half,
    ]
    place.greet(
        place.around()
        + [turns[1], turns[3], place.half, place.beside, place.along_x(1), place.along_x(3)]
    )
    parts = {0: pl.ds(0, CUT), 1: pl.ds(CUT, PIECE - CUT)}

    def chunk(t, da, db):
        start = pl.multiple_of(place.ring(t, da, db) // 2 * PIECE, 16)
        return rows.at[t, pl.ds(start, PIECE)]

    def plus(*terms):
        result = terms[0].astype(F32)
        for term in terms[1:]:
            result = result + term.astype(F32)
        return result.astype(BF)

    order = (2, 1, 3, 0)
    way = {2: 1, 1: 1, 3: -1, 0: -1}
    first, second, loose = {}, {}, {}

    def take(number):
        loads[number].wait()
        return buffers[number]

    def panel(t, start, left, right):
        rows[t, start : start + left.shape[0], :] = contract(left, right, ((1,), (0,))).astype(BF)

    def note(t, row, right):
        ones = jnp.ones((8, right.shape[0]), BF)
        small[1 - t, row : row + 1, :] = contract(ones, right, ((1,), (0,)))[:1]

    def own_rows(values):
        turned[...] = jnp.transpose(values)
        return turned[pl.ds(pl.multiple_of(place.fsdp * 192, 64), 192), :]

    def early_grads(t, at):
        low = take(at)[...]
        panel(t, 576, own_rows(take(at + 1)[...]), low)
        note(t, 0, low)
        turned[...] = jnp.transpose(take(at + 2)[...])
        panel(t, 1536, turned[...], low)
        left, pre = own_rows(take(at + 3)[...]), take(at + 4)
        for i in range(4):
            right = pre[:, i * D : (i + 1) * D]
            panel(t, 768 + i * 192, left, right)
            note(t, 4 + i, right)

    def late_grads(t, one, joined, norms):
        left = own_rows(one[...])
        for i in range(3):
            right = joined[:, i * D : (i + 1) * D]
            panel(t, i * 192, left, right)
            note(t, 1 + i, right)
        sums = norms[0:16, :].astype(F32)
        for i in range(1, 4):
            sums = sums + norms[i * 16 : (i + 1) * 16, :].astype(F32)
        small[1 - t, 8:16, :] = sums[:8]

    def set_out(t):
        for db in order:
            first[t, db] = wire.push(chunk(t, 2, db), far.at[t, db], place.near(t, 0, way[db]))
        for db in order:
            loose[t, db] = wire.push(
                chunk(t, -way[db], db), near.at[t, db, 1], place.near(t, 0, -way[db])
            )

    work = [
        share_rows(place, wire, joined_ref, joined_land),
        share_rows(place, wire, norm_ref, norm_land),
    ]
    early_grads(0, 0)
    late_grads(0, take(5), take(6), norm_one)
    set_out(0)
    for steps, _ in work:
        for step in steps:
            step()
    early_grads(1, 7)
    for _, last in work:
        for copy in last:
            copy.wait_recv()
    for copy in wire.local:
        copy.wait()
    settled = len(wire.local)
    late_grads(1, take(12), joined_land, norm_land)
    set_out(1)
    step_numbers, waited = [len(wire.sent)], set()
    wire.push(small, heard.at[0], turns[0])
    for db in order:
        for t in (0, 1):
            first[t, db].wait_recv()
            mix[t, db] = plus(chunk(t, way[db], db)[...], far[t, db])
            second[t, db] = wire.push(mix.at[t, db], near.at[t, db, 0], place.near(t, 0, way[db]))

    def hear(step):
        wire.sent[step_numbers[-1]].wait_send()
        wire.sent[step_numbers[-1]].wait_recv()
        small[...] += heard[step]
        waited.add(step_numbers[-1])
        if step < 4:
            step_numbers.append(len(wire.sent))
            wire.push(small, heard.at[step + 1], turns[step + 1])

    def settle(t, db):
        second[t, db].wait_recv()
        loose[t, db].wait_recv()
        total[t, db] = plus(chunk(t, 0, db)[...], near[t, db, 0], near[t, db, 1])

    third, fourth = {}, {}
    for t in (0, 1):
        settle(t, 2)
        third[t] = [
            wire.push(
                total.at[t, 2, parts[b]], far_two.at[t, parts[b]], place.near(t, 1, sign)
            )
            for b, sign in ((0, 1), (1, -1))
        ]
    hear(0)
    for t in (0, 1):
        fourth[t] = []
        for b, sign, db in ((0, 1, 1), (1, -1, 3)):
            settle(t, db)
            fourth[t].append(
                wire.push(
                    total.at[t, db, parts[1 - b]],
                    near_two.at[t, b, parts[1 - b]],
                    place.near(t, 1, sign),
                )
            )
    hear(1)
    for t in (0, 1):
        for b, sign, db in ((0, 1, 1), (1, -1, 3)):
            third[t][b].wait_recv()
            mix_two[t, parts[b]] = plus(total[t, db, parts[b]], far_two[t, parts[b]])
            fourth[t].append(
                wire.push(
                    mix_two.at[t, parts[b]], near_two.at[t, b, parts[b]], place.near(t, 1, sign)
                )
            )
    hear(2)
    swapped = []
    for t in (0, 1):
        settle(t, 0)
        for copy in fourth[t]:
            copy.wait_recv()
        part[t] = plus(total[t, 0], near_two[t, 0], near_two[t, 1])
        swapped.append(wire.push(part.at[t], other.at[t], place.half))
    hear(3)

    def spot(t, origin, b):
        return out_ref.at[1 - t, origin // 2, parts[b]]

    def own(t, b):
        return final.at[1 - t, parts[b]]

    def ready(t, b):
        if b == 0:
            swapped[1 - t].wait_recv()
            final[1 - t] = plus(part[1 - t], other[1 - t])
            wire.keep(final.at[1 - t], out_ref.at[1 - t, place.ctx // 2])

    spread(place, wire, own, spot, ready)
    hear(4)
    small_out[...] = small[...]
    for number, copy in enumerate(wire.sent):
        if number not in waited:
            copy.wait_send()
    for copy in wire.local[settled:]:
        copy.wait()


def sum_over_ctx(joined, norms, norms_one, arrays):
    shape = (16, PIECE, D)
    small_shape = (LAYERS, 16, D)
    tokens = 4 * BLOCK
    return pl.pallas_call(
        sum_kernel,
        out_shape=(
            jax.ShapeDtypeStruct((2,) + shape, BF),
            jax.ShapeDtypeStruct(small_shape, F32),
        ),
        in_specs=[VM] * 3 + [ANY] * LOADS,
        out_specs=(ANY, VM),
        scratch_shapes=[room(*array.shape) for array in arrays]
        + [
            room(2, 16 * PIECE, D),
            room(tokens, 3 * D),
            room(64, D),
            room(D, tokens),
            pltpu.SemaphoreType.DMA((LOADS,)),
            room(2, 4, PIECE, D),
            room(2, 4, PIECE, D),
            room(2, 4, 2, PIECE, D),
            room(2, 4, PIECE, D),
            room(2, PIECE, D),
            room(2, PIECE, D),
            room(2, 2, PIECE, D),
            room(2, PIECE, D),
            room(2, PIECE, D),
            room(2, PIECE, D),
            pltpu.VMEM(small_shape, F32),
            pltpu.VMEM((5,) + small_shape, F32),
        ]
        + sems(128, 4),
        compiler_params=pltpu.CompilerParams(
            collective_id=6, has_side_effects=True, vmem_limit_bytes=60 * 2**20
        ),
        name="sum_over_ctx",
    )(joined, norms, norms_one, *arrays)


def pair_rows(values):
    lane = lax.broadcasted_iota(jnp.int32, values.shape, 1)
    zero = jnp.zeros_like(values)
    return jnp.concatenate(
        [jnp.where(lane < HEAD_DIM, values, zero), jnp.where(lane >= HEAD_DIM, values, zero)], 0
    )


def contract(left, right, dims):
    return lax.dot_general(left, right, (dims, ((), ())), preferred_element_type=F32)


def allowed_at(tile, block):
    key = tile * TILE + lax.broadcasted_iota(jnp.int32, (TILE, 2 * BLOCK), 0)
    query = block * BLOCK + lax.broadcasted_iota(jnp.int32, (TILE, 2 * BLOCK), 1) % BLOCK
    return key <= query


def low_block(ctx):
    return jnp.minimum(ctx, BLOCKS - 1 - ctx)


def by_height(ctx, own, away, two):
    @pl.when(ctx < BLOCKS // 2)
    def _():
        two[0] = own[...]
        two[1] = away[...]

    @pl.when(ctx >= BLOCKS // 2)
    def _():
        two[0] = away[...]
        two[1] = own[...]


def from_height(ctx, two, own, away):
    @pl.when(ctx < BLOCKS // 2)
    def _():
        own[...] = two[0].astype(own.dtype)
        away[...] = two[1].astype(away.dtype)

    @pl.when(ctx >= BLOCKS // 2)
    def _():
        own[...] = two[1].astype(own.dtype)
        away[...] = two[0].astype(away.dtype)


TILES = BLOCKS * BLOCK // TILE


def load_tiles(pairs, sem):
    loads = []
    for tile in range(TILES):
        rows = pl.ds(tile * TILE, TILE)
        for source, buffer in pairs:
            load = pltpu.make_async_copy(source.at[rows], buffer.at[rows], sem.at[len(loads)])
            load.start()
            loads.append(load)
    return loads


def wait_tiles(loads, b):
    half = len(loads) // 2
    for load in loads[b * half : (b + 1) * half]:
        load.wait()


def forward_kernel(
    ctx_ref, q_own, q_away, k_in, v_in, mixed_own, mixed_away, turned_ref, log_ref,
    top, mass, acc, k_ref, v_ref, q_two, mixed_two, sem,
):
    ctx = ctx_ref[0]
    loads = load_tiles(((k_in, k_ref), (v_in, v_ref)), sem)
    by_height(ctx, q_own, q_away, q_two)
    for b in (0, 1):
        block = low_block(ctx) if b == 0 else BLOCKS - 1 - low_block(ctx)
        wait_tiles(loads, b)
        rows = slice(b * BLOCK, (b + 1) * BLOCK)
        q_ref, mixed_ref = q_two.at[b], mixed_two.at[b]
        queries = [
            pair_rows(q_ref[:, p * 128 : (p + 1) * 128] * jnp.asarray(0.125, BF))
            for p in range(PAIRS)
        ]

        def step(tile, masked):
            start = pl.multiple_of(tile * TILE, TILE)
            for p in range(PAIRS):
                cols = slice(p * 128, (p + 1) * 128)
                scores = contract(k_ref[pl.ds(start, TILE), cols], queries[p], ((1,), (1,)))
                if masked:
                    scores = jnp.where(allowed_at(tile, block), scores, masked_score)
                    new_top = jnp.max(scores, 0, keepdims=True)
                else:
                    old_top = top[p : p + 1, :]
                    new_top = jnp.maximum(old_top, jnp.max(scores, 0, keepdims=True))
                weights = jnp.exp(scores - new_top)
                fresh_mass = jnp.sum(weights, 0, keepdims=True)
                fresh = contract(
                    v_ref[pl.ds(start, TILE), cols], weights.astype(BF), ((0,), (0,))
                )
                if not masked:
                    fade = jnp.exp(old_top - new_top)
                    fresh_mass = fresh_mass + mass[p : p + 1, :] * fade
                    fresh = fresh + acc[p] * fade
                top[p : p + 1, :] = new_top
                mass[p : p + 1, :] = fresh_mass
                acc[p] = fresh

        step(block // 4, True)

        @pl.loop(0, block // 4)
        def _(tile):
            step(tile, False)

        for p in range(PAIRS):
            cols = slice(p * 128, (p + 1) * 128)
            done = acc[p] / mass[p : p + 1, :]
            turned = jnp.concatenate([done[:HEAD_DIM, :BLOCK], done[HEAD_DIM:, BLOCK:]], 0)
            turned_ref[cols, rows] = turned
            mixed_ref[:, cols] = jnp.transpose(turned).astype(BF)
            row = b * PAIRS + p
            log_ref[row : row + 1, :] = top[p : p + 1, :] + jnp.log(mass[p : p + 1, :])
    from_height(ctx, mixed_two, mixed_own, mixed_away)


def attend_forward(ctx, own, away, keys, values):
    return pl.pallas_call(
        forward_kernel,
        out_shape=(
            jax.ShapeDtypeStruct((BLOCK, HALF), BF),
            jax.ShapeDtypeStruct((BLOCK, HALF), BF),
            jax.ShapeDtypeStruct((HALF, 2 * BLOCK), F32),
            jax.ShapeDtypeStruct((8, 2 * BLOCK), F32),
        ),
        in_specs=[SM, VM, VM, ANY, ANY],
        out_specs=(VM, VM, VM, VM),
        scratch_shapes=[
            pltpu.VMEM((8, 2 * BLOCK), F32),
            pltpu.VMEM((8, 2 * BLOCK), F32),
            pltpu.VMEM((PAIRS, 128, 2 * BLOCK), F32),
            room(BLOCKS * BLOCK, HALF),
            room(BLOCKS * BLOCK, HALF),
            room(2, BLOCK, HALF),
            room(2, BLOCK, HALF),
            pltpu.SemaphoreType.DMA((2 * TILES,)),
        ],
        compiler_params=pltpu.CompilerParams(vmem_limit_bytes=60 * 2**20),
        cost_estimate=pl.CostEstimate(
            flops=4 * 33 * 128 * 128 * 6 * 128, bytes_accessed=8 * 2**20, transcendentals=33 * 128 * 128 * 6
        ),
        name="attend_forward",
    )(ctx, own, away, keys, values)


def backward_kernel(
    ctx_ref, q_own, q_away, k_in, v_in, g_own, g_away, turned_ref, log_ref,
    gq_own, gq_away, gk_ref, gv_ref,
    gk_acc, gv_acc, gq_acc, k_ref, v_ref, q_two, g_two, gq_two, sem,
):
    ctx = ctx_ref[0]
    loads = load_tiles(((k_in, k_ref), (v_in, v_ref)), sem)
    by_height(ctx, q_own, q_away, q_two)
    by_height(ctx, g_own, g_away, g_two)
    gk_acc[...] = jnp.zeros_like(gk_acc)
    gv_acc[...] = jnp.zeros_like(gv_acc)
    for b in (0, 1):
        block = low_block(ctx) if b == 0 else BLOCKS - 1 - low_block(ctx)
        wait_tiles(loads, b)
        rows = slice(b * BLOCK, (b + 1) * BLOCK)
        queries, grads, deltas = [], [], []
        q_ref, g_ref, gq_ref = q_two.at[b], g_two.at[b], gq_two.at[b]
        for p in range(PAIRS):
            cols = slice(p * 128, (p + 1) * 128)
            queries.append(pair_rows(q_ref[:, cols] * jnp.asarray(0.125, BF)))
            grad = g_ref[:, cols]
            grads.append(pair_rows(grad))
            both = jnp.transpose(grad.astype(F32)) * turned_ref[cols, rows]
            deltas.append(
                jnp.concatenate(
                    [
                        jnp.sum(both[:HEAD_DIM], 0, keepdims=True),
                        jnp.sum(both[HEAD_DIM:], 0, keepdims=True),
                    ],
                    1,
                )
            )
        gq_acc[...] = jnp.zeros_like(gq_acc)

        def step(tile, masked):
            start = pl.multiple_of(tile * TILE, TILE)
            here = pl.ds(start, TILE)
            for p in range(PAIRS):
                cols = slice(p * 128, (p + 1) * 128)
                row = b * PAIRS + p
                keys = k_ref[here, cols]
                scores = contract(keys, queries[p], ((1,), (1,)))
                chances = jnp.exp(scores - log_ref[row : row + 1, :])
                if masked:
                    chances = jnp.where(allowed_at(tile, block), chances, 0.0)
                grad_chance = contract(v_ref[here, cols], grads[p], ((1,), (1,)))
                grad_score = (chances * (grad_chance - deltas[p])).astype(BF)
                gv_acc[here, cols] += contract(chances.astype(BF), grads[p], ((1,), (0,)))
                gk_acc[here, cols] += contract(grad_score, queries[p], ((1,), (0,)))
                gq_acc[p] += contract(keys, grad_score, ((0,), (0,)))

        step(block // 4, True)

        @pl.loop(0, block // 4)
        def _(tile):
            step(tile, False)

        for p in range(PAIRS):
            cols = slice(p * 128, (p + 1) * 128)
            done = gq_acc[p] * 0.125
            turned = jnp.concatenate([done[:HEAD_DIM, :BLOCK], done[HEAD_DIM:, BLOCK:]], 0)
            gq_ref[:, cols] = jnp.transpose(turned).astype(gq_ref.dtype)
    from_height(ctx, gq_two, gq_own, gq_away)
    gk_ref[...] = gk_acc[...].astype(BF)
    gv_ref[...] = gv_acc[...].astype(BF)


def attend_backward(ctx, own, away, keys, values, grad_own, grad_away, turned, log_total):
    whole = jax.ShapeDtypeStruct((BLOCKS * BLOCK, HALF), BF)
    return pl.pallas_call(
        backward_kernel,
        out_shape=(
            jax.ShapeDtypeStruct((BLOCK, HALF), F32),
            jax.ShapeDtypeStruct((BLOCK, HALF), BF),
            whole,
            whole,
        ),
        in_specs=[SM, VM, VM, ANY, ANY] + [VM] * 4,
        out_specs=(VM,) * 4,
        scratch_shapes=[
            pltpu.VMEM((BLOCKS * BLOCK, HALF), F32),
            pltpu.VMEM((BLOCKS * BLOCK, HALF), F32),
            pltpu.VMEM((PAIRS, 128, 2 * BLOCK), F32),
            room(BLOCKS * BLOCK, HALF),
            room(BLOCKS * BLOCK, HALF),
            room(2, BLOCK, HALF),
            room(2, BLOCK, HALF),
            pltpu.VMEM((2, BLOCK, HALF), F32),
            pltpu.SemaphoreType.DMA((2 * TILES,)),
        ],
        compiler_params=pltpu.CompilerParams(vmem_limit_bytes=60 * 2**20),
        cost_estimate=pl.CostEstimate(
            flops=10 * 33 * 128 * 128 * 6 * 128, bytes_accessed=16 * 2**20, transcendentals=33 * 128 * 128 * 6
        ),
        name="attend_backward",
    )(ctx, own, away, keys, values, grad_own, grad_away, turned, log_total)


GAIN_ONE, BIAS_ONE, GAIN_TWO, BIAS_TWO, BIAS_OUT, BIAS_DOWN, BIAS_QKV, BIAS_UP = (
    0, 1, 2, 3, 4, 5, 6, 9,
)


def norm_parts(values):
    centre = jnp.mean(values, -1, keepdims=True)
    shifted = values - centre
    spread = jnp.mean(shifted * shifted, -1, keepdims=True)
    scale = lax.rsqrt(spread + epsilon)
    return shifted * scale, scale


def norm_input_grad(grad_norm, gain, unit, scale):
    e = grad_norm * gain
    return scale * (
        e - jnp.mean(e, -1, keepdims=True) - unit * jnp.mean(e * unit, -1, keepdims=True)
    )


def turn_tables(first_row, row_count):
    shape = (row_count, 128)
    feature = lax.broadcasted_iota(jnp.int32, shape, 1) % HEAD_DIM
    position = first_row + lax.broadcasted_iota(jnp.int32, shape, 0)
    half_rot = ROTARY // 2
    exponent = (feature % half_rot).astype(F32) * (2.0 / ROTARY)
    angle = position.astype(F32) * jnp.power(10000.0, -exponent)
    cosine, sine = jnp.cos(angle), jnp.sin(angle)
    keep = jnp.where(feature < ROTARY, cosine, 1.0)
    low = jnp.where(feature < half_rot, -sine, 0.0)
    high = jnp.where((feature >= half_rot) & (feature < ROTARY), sine, 0.0)
    return keep, low, high


def rotate(values, table_ref):
    shift = ROTARY // 2
    return (
        values * table_ref[0]
        + pltpu.roll(values, 128 - shift, 1) * table_ref[1]
        + pltpu.roll(values, shift, 1) * table_ref[2]
    )


def rotate_back(values, table_ref):
    shift = ROTARY // 2
    return (
        values * table_ref[0]
        + pltpu.roll(values * table_ref[1], shift, 1)
        + pltpu.roll(values * table_ref[2], 128 - shift, 1)
    )


def phi_parts(values):
    cumulative = 0.5 * (1.0 + lax.erf(values * (2.0**-0.5)))
    density = jnp.exp(-0.5 * values * values) * (0.5 / jnp.pi) ** 0.5
    return cumulative, density


def line(vec_ref, row):
    return vec_ref[row : row + 1, :]


def put_halves(upper_ref, low, high, mine_ref, theirs_ref):
    upper = upper_ref[0] == 1

    @pl.when(upper)
    def _():
        mine_ref[...] = high
        theirs_ref[...] = low

    @pl.when(jnp.logical_not(upper))
    def _():
        mine_ref[...] = low
        theirs_ref[...] = high


def put_joined(upper_ref, mine, theirs, out_ref, first):
    upper = upper_ref[0] == 1
    low, high = slice(first, first + HALF), slice(first + HALF, first + D)

    @pl.when(upper)
    def _():
        out_ref[:, low] = theirs
        out_ref[:, high] = mine

    @pl.when(jnp.logical_not(upper))
    def _():
        out_ref[:, low] = mine
        out_ref[:, high] = theirs


def enter(upper_ref, stream, vec_ref, weight_ref, table_ref, one_ref, two_ref, *parts):
    unit, _ = norm_parts(stream)
    one = (unit * line(vec_ref, GAIN_ONE) + line(vec_ref, BIAS_ONE)).astype(BF)
    one_ref[...] = one
    two_ref[...] = (unit * line(vec_ref, GAIN_TWO) + line(vec_ref, BIAS_TWO)).astype(BF)
    for i in range(3):
        joined = contract(one, weight_ref[:, i * D : (i + 1) * D], ((1,), (0,)))
        joined = joined + line(vec_ref, BIAS_QKV + i)
        groups = [joined[:, g * 128 : (g + 1) * 128] for g in range(6)]
        if i < 2:
            groups = [rotate(group, table_ref) for group in groups]
        groups = [group.astype(BF) for group in groups]
        put_halves(
            upper_ref,
            jnp.concatenate(groups[:3], 1),
            jnp.concatenate(groups[3:], 1),
            parts[2 * i],
            parts[2 * i + 1],
        )


def enter_kernel(upper_ref, tokens_ref, vec_ref, weight_ref, keep, low, high, *outs):
    table_ref = (keep[...], low[...], high[...])
    enter(upper_ref, tokens_ref[...].astype(F32), vec_ref, weight_ref, table_ref, *outs)


def leave(upper_ref, stream_ref, own_ref, away_ref, weight_ref, mlp_ref, vec_ref, mixed_ref):
    put_joined(upper_ref, own_ref[...], away_ref[...], mixed_ref, 0)
    return (
        stream_ref[...].astype(F32)
        + contract(mixed_ref[...], weight_ref[...], ((1,), (0,)))
        + line(vec_ref, BIAS_OUT)
        + mlp_ref[...]
        + line(vec_ref, BIAS_DOWN)
    )


def pass_kernel(
    upper_ref, stream_ref, own_ref, away_ref, out_ref, mlp_ref, vec_ref,
    next_vec_ref, weight_ref, keep, low, high, mixed_ref, next_ref, *outs,
):
    table_ref = (keep[...], low[...], high[...])
    stream = leave(upper_ref, stream_ref, own_ref, away_ref, out_ref, mlp_ref, vec_ref, mixed_ref)
    next_ref[...] = stream
    enter(upper_ref, stream, next_vec_ref, weight_ref, table_ref, *outs)


def last_kernel(
    upper_ref, stream_ref, own_ref, away_ref, out_ref, mlp_ref, vec_ref, mixed_ref, next_ref
):
    next_ref[...] = leave(
        upper_ref, stream_ref, own_ref, away_ref, out_ref, mlp_ref, vec_ref, mixed_ref
    ).astype(BF)


def mlp_kernel(two_ref, up_ref, down_ref, vec_ref, pre_ref, hidden_ref, mlp_ref):
    two = two_ref[...]
    for i in range(FF // D):
        cols = slice(i * D, (i + 1) * D)
        pre = contract(two, up_ref[:, cols], ((1,), (0,))) + line(vec_ref, BIAS_UP + i)
        pre_ref[:, cols] = pre
        hidden = (pre * phi_parts(pre)[0]).astype(BF)
        hidden_ref[:, cols] = hidden
        fresh = contract(hidden, down_ref[cols, :], ((1,), (0,)))
        mlp_ref[...] = fresh if i == 0 else mlp_ref[...] + fresh


def back(upper_ref, gradient, weight_ref, low_ref, mine_ref, theirs_ref):
    low = gradient.astype(BF)
    low_ref[...] = low
    mixed = contract(low, weight_ref[...], ((1,), (1,))).astype(BF)
    put_halves(upper_ref, mixed[:, :HALF], mixed[:, HALF:], mine_ref, theirs_ref)


def back_kernel(upper_ref, cotangent_ref, weight_ref, *outs):
    back(upper_ref, cotangent_ref[...].astype(F32), weight_ref, *outs)


def join_kernel(
    more, upper_ref, own_ref, back_ref, own_q, back_q, keep, low, high, weight_ref, stream_ref,
    vec_ref, two_ref, gradient_ref, *refs,
):
    table_ref = (keep[...], low[...], high[...])
    next_weight, refs = (refs[:1], refs[1:]) if more else ((), refs)
    joined_ref, sums_ref, next_ref, *outs = refs

    def turned(values):
        groups = [rotate_back(values[:, g * 128 : (g + 1) * 128], table_ref) for g in range(3)]
        return jnp.concatenate(groups, 1).astype(BF)

    put_joined(upper_ref, turned(own_q[...]), turned(back_q[...].astype(F32)), joined_ref, 0)
    put_joined(upper_ref, turned(own_ref[0]), turned(back_ref[0].astype(F32)), joined_ref, D)
    put_joined(upper_ref, own_ref[1].astype(BF), back_ref[1], joined_ref, 2 * D)
    one = contract(joined_ref[...], weight_ref[...], ((1,), (1,)))
    two = two_ref[...]
    unit, scale = norm_parts(stream_ref[...].astype(F32))
    sums = [jnp.sum(values, 0, keepdims=True) for values in (one * unit, one, two * unit, two)]
    sums_ref[...] = jnp.concatenate(sums + [jnp.zeros((12, D), F32)], 0).astype(BF)
    gradient = (
        gradient_ref[...].astype(F32)
        + norm_input_grad(one, line(vec_ref, GAIN_ONE), unit, scale)
        + norm_input_grad(two, line(vec_ref, GAIN_TWO), unit, scale)
    )
    next_ref[...] = gradient
    if more:
        back(upper_ref, gradient, next_weight[0], *outs)


def unpack_kernel(rows_ref, qkv_ref, out_ref, up_ref, down_ref):
    for i in range(3):
        qkv_ref[0, :, i * D : (i + 1) * D] = rows_ref[0, i * 192 : (i + 1) * 192, :].astype(F32)
    out_ref[0] = rows_ref[0, 576:768, :].astype(F32)
    for i in range(4):
        up_ref[0, :, i * D : (i + 1) * D] = rows_ref[
            0, 768 + i * 192 : 960 + i * 192, :
        ].astype(F32)
    down_ref[0] = rows_ref[0, 1536:, :].astype(F32)


def unpack(rows):
    shapes = [(192, 3 * D), (192, D), (192, FF), (D, D)]
    return pl.pallas_call(
        unpack_kernel,
        grid=(LAYERS,),
        out_shape=tuple(jax.ShapeDtypeStruct((LAYERS,) + shape, F32) for shape in shapes),
        in_specs=[pl.BlockSpec((1, 2304, D), lambda i: (LAYERS - 1 - i, 0, 0))],
        out_specs=tuple(pl.BlockSpec((1,) + shape, lambda i: (i, 0, 0)) for shape in shapes),
        compiler_params=pltpu.CompilerParams(vmem_limit_bytes=60 * 2**20),
        name="unpack",
    )(rows)


def dense(name, kernel, specs, outs, args, flops):
    shapes = tuple(
        jax.ShapeDtypeStruct((BLOCK, size) if isinstance(size, int) else size, kind)
        for size, kind in outs
    )
    return pl.pallas_call(
        kernel,
        out_shape=shapes,
        in_specs=specs,
        out_specs=(VM,) * len(shapes),
        compiler_params=pltpu.CompilerParams(vmem_limit_bytes=60 * 2**20),
        cost_estimate=pl.CostEstimate(
            flops=2 * BLOCK * flops, bytes_accessed=2 * flops, transcendentals=0
        ),
        name=name,
    )(*args)


def vector_kernel(table_ref, *out_refs):
    for layer_index, out_ref in enumerate(out_refs):
        at = slice(layer_index, layer_index + 1)
        for row in range(6):
            pieces = [table_ref[f, at, row * 192 : (row + 1) * 192] for f in range(4)]
            out_ref[row : row + 1, :] = jnp.concatenate(pieces, 1)
        joined = jnp.concatenate([table_ref[f, at, 1152:1728] for f in range(4)], 1)
        for i in range(3):
            out_ref[BIAS_QKV + i : BIAS_QKV + i + 1, :] = joined[:, i * D : (i + 1) * D]
        for f in range(4):
            out_ref[BIAS_UP + f : BIAS_UP + f + 1, :] = table_ref[f, at, 1728:2496]
        out_ref[13:, :] = jnp.zeros((3, D), F32)


def order_vectors(table):
    return pl.pallas_call(
        vector_kernel,
        out_shape=(jax.ShapeDtypeStruct((16, D), F32),) * LAYERS,
        in_specs=[VM],
        out_specs=(VM,) * LAYERS,
        name="order_vectors",
    )(table)


ENTER_OUTS = ((D, BF),) * 2 + ((HALF, BF),) * 6


def shards(
    tokens,
    cotangent,
    ln1_gain,
    ln1_bias,
    ln2_gain,
    ln2_bias,
    qkv_weight,
    qkv_bias,
    out_weight,
    out_bias,
    up_weight,
    up_bias,
    down_weight,
    down_bias,
):
    row_count = tokens.shape[1]
    fsdp = lax.axis_index("fsdp")
    ctx = lax.axis_index("ctx")
    ctx_word = ctx.astype(jnp.int32).reshape(1)
    upper = (ctx % 2).astype(jnp.int32).reshape(1)
    tables = turn_tables(ctx * row_count, row_count)

    vectors = (ln1_gain, ln1_bias, ln2_gain, ln2_bias, out_bias, down_bias, qkv_bias, up_bias)
    packed = jnp.concatenate(vectors, 1).astype(F32)
    packed = jnp.pad(packed, ((0, 8 - LAYERS), (0, 2560 - packed.shape[1])))
    first_weight, table = gather_first(qkv_weight, packed)
    vecs = order_vectors(table)
    qkv_full = [first_weight, None]
    gathered = [None] * LAYERS
    stream = tokens[0]
    entered = dense(
        "enter",
        enter_kernel,
        [SM] + [VM] * 6,
        ENTER_OUTS,
        (upper, stream, vecs[0], first_weight, *tables),
        D * 3 * D,
    )
    saved = []
    for layer_index in range(LAYERS):
        norm_one, norm_two, q_own, q_away, k_own, k_away, v_own, v_away = entered
        jobs = [(layer_index, out_weight), (layer_index, up_weight), (layer_index, down_weight)]
        if layer_index + 1 < LAYERS:
            jobs.append((layer_index + 1, qkv_weight))
        q_other, keys, values, w_out, w_up, w_down, *more = gather_pair(
            "gather_pair_%d" % layer_index,
            1 + layer_index,
            (q_away, k_away, v_away),
            (k_own, v_own),
            jobs,
        )
        if more:
            qkv_full[layer_index + 1] = more[0]
        gathered[layer_index] = (qkv_full[layer_index], w_out, w_up, w_down)
        keys = keys.reshape(BLOCKS * BLOCK, HALF)
        values = values.reshape(BLOCKS * BLOCK, HALF)
        mixed_own, mixed_away, turned, log_total = attend_forward(
            ctx_word, q_own, q_other, keys, values
        )
        mixed_back = mirrored(mixed_away)
        hidden_pre, hidden_low, mlp_branch = dense(
            "mlp",
            mlp_kernel,
            [VM] * 4,
            ((FF, F32), (FF, BF), (D, F32)),
            (norm_two, w_up, w_down, vecs[layer_index]),
            2 * D * FF,
        )
        before = stream
        common = (upper, stream, mixed_own, mixed_back, w_out, mlp_branch, vecs[layer_index])
        if more:
            mixed_low, stream, *entered = dense(
                "pass_on",
                pass_kernel,
                [SM] + [VM] * 11,
                ((D, BF), (D, F32)) + ENTER_OUTS,
                common + (vecs[layer_index + 1], more[0], *tables),
                D * 4 * D,
            )
        else:
            mixed_low, output = dense(
                "last", last_kernel, [SM] + [VM] * 6, ((D, BF), (D, BF)), common, D * D
            )
        lefts = (norm_one, mixed_low, norm_two)
        saved.append(
            (before, q_own, q_other, keys, values, turned, log_total, hidden_pre, hidden_low, lefts)
        )

    gradient = cotangent[0]
    waiting, early_rows, late_rows = (), [None] * 2, [None] * 2
    grad_low, grad_own, grad_away = dense(
        "back",
        back_kernel,
        [SM, VM, VM],
        ((D, BF), (HALF, BF), (HALF, BF)),
        (upper, gradient, gathered[LAYERS - 1][1]),
        D * D,
    )
    for layer_index in range(LAYERS - 1, -1, -1):
        w_qkv, w_out, w_up, w_down = gathered[layer_index]
        before, q_own, q_other, keys, values, turned, log_total, hidden_pre, hidden_low, lefts = (
            saved[layer_index]
        )
        grad_back = mirrored(grad_away)
        gq_own, gq_away, grad_keys, grad_values = attend_backward(
            ctx_word, q_own, q_other, keys, values, grad_own, grad_back, turned, log_total
        )
        whole = (BLOCKS, BLOCK, HALF)
        own_pair, grad_norm_two, back_pair, back_query, hidden, pre, *gathered_rows = scatter_pair(
            "scatter_pair_%d" % layer_index,
            3 + layer_index,
            grad_keys.reshape(whole),
            grad_values.reshape(whole),
            gq_away,
            hidden_low,
            hidden_pre,
            w_up,
            w_down,
            lefts + (grad_low,) + waiting,
        )
        early_rows[layer_index] = (hidden, *gathered_rows[:4], pre)
        if waiting:
            late_rows[layer_index + 1] = gathered_rows[4:]
        going_on = layer_index > 0
        grad_joined, norm_sums, gradient, *outs = dense(
            "join_%d" % layer_index,
            functools.partial(join_kernel, going_on),
            [SM] + [VM] * (13 if going_on else 12),
            ((3 * D, BF), ((16, D), BF), (D, F32))
            + (((D, BF), (HALF, BF), (HALF, BF)) if going_on else ()),
            (
                upper,
                own_pair,
                back_pair,
                gq_own,
                back_query,
                *tables,
                w_qkv,
                before,
                vecs[layer_index],
                grad_norm_two,
                gradient,
            )
            + ((gathered[layer_index - 1][1],) if going_on else ()),
            D * 3 * D,
        )
        waiting = (grad_joined, norm_sums)
        if going_on:
            grad_low, grad_own, grad_away = outs
    arrays = []
    for layer_index in (1, 0):
        hidden, one, mixed, two, low, pre = early_rows[layer_index]
        arrays += [low, mixed, hidden, two, pre, one]
        if layer_index == 1:
            joined_one, norms_one = late_rows[1]
            arrays.append(joined_one)
    summed, small = sum_over_ctx(*waiting, norms_one, arrays)

    def own_part(vectors, width):
        return lax.dynamic_slice_in_dim(vectors, fsdp * width, width, vectors.ndim - 1)

    bias_sum = own_part(small[:, 0], 192)
    joined_sum = own_part(small[:, 1:4].reshape(LAYERS, 3 * D), 576)
    up_sum = own_part(small[:, 4:8].reshape(LAYERS, 4 * D), D)
    norm_sums = own_part(small[:, 8:12], 192)
    qkv_grad, out_grad, up_grad, down_grad = unpack(summed.reshape(LAYERS, 2304, D))
    return (
        output[None],
        gradient[None],
        norm_sums[:, 0],
        norm_sums[:, 1],
        norm_sums[:, 2],
        norm_sums[:, 3],
        qkv_grad,
        joined_sum,
        out_grad,
        bias_sum,
        up_grad,
        up_sum,
        down_grad,
        bias_sum,
    )


def solution(mesh):
    matrix, vector = P(None, "fsdp", None), P(None, "fsdp")
    rows = P("fsdp", "ctx", None)
    params = (
        vector,
        vector,
        vector,
        vector,
        matrix,
        vector,
        matrix,
        vector,
        matrix,
        vector,
        matrix,
        vector,
    )
    return jax.shard_map(
        shards,
        mesh=mesh,
        in_specs=(rows, rows) + params,
        out_specs=(rows, rows) + params,
        check_vma=False,
    )
```

```python
import functools

import jax
import jax.numpy as jnp
from jax import lax
from jax.experimental import pallas as pl
from jax.experimental.pallas import tpu as pltpu
from jax.sharding import PartitionSpec as P

D = 768
HEADS = 12
HEAD_DIM = 64
FF = 3072
ROTARY = 16
LAYERS = 2
HALF = 384
BLOCK = 128
BLOCKS = 32
TILE = 512
PAIRS = 3

epsilon = 1e-05
masked_score = -1e30
MESH = pl.DeviceIdType.MESH
BF = jnp.bfloat16
F32 = jnp.float32


def mirrored(values):
    pairs = [(f * 32 + c, f * 32 + 31 - c) for f in range(4) for c in range(32)]
    return lax.ppermute(values, ("fsdp", "ctx"), pairs)


class Place:
    def __init__(self):
        self.fsdp = lax.axis_index("fsdp")
        self.ctx = lax.axis_index("ctx")
        self.y, self.z, self.h = self.ctx // 8, (self.ctx // 2) % 4, self.ctx % 2
        self.x_lo, self.core = self.fsdp // 2, self.fsdp % 2
        self.beside = (self.fsdp + 1 - 2 * self.core, self.ctx)
        self.mirror = (self.fsdp, BLOCKS - 1 - self.ctx)
        self.half = (self.fsdp, self.ctx + 1 - 2 * self.h)

    def along_x(self, step):
        x = (2 * self.h + self.x_lo + step) % 4
        return (2 * (x % 2) + self.core, self.y * 8 + self.z * 2 + x // 2)

    def ctx_at(self, dy, dz):
        return ((self.y + dy) % 4) * 8 + ((self.z + dz) % 4) * 2 + self.h

    def ring(self, t, da, db):
        return self.ctx_at(da, db) if t == 0 else self.ctx_at(db, da)

    def near(self, t, axis, sign):
        steps = (sign, 0) if axis == 0 else (0, sign)
        return (self.fsdp, self.ring(t, *steps))

    def around(self):
        return [self.near(0, axis, sign) for axis in (0, 1) for sign in (1, -1)]

    def greet(self, partners):
        barrier = pltpu.get_barrier_semaphore()
        for partner in partners:
            pl.semaphore_signal(barrier, inc=1, device_id=partner, device_id_type=MESH)
        pl.semaphore_wait(barrier, len(partners))


class Wire:
    def __init__(self, send_sem, recv_sem, local_sem=None):
        self.send_sem, self.recv_sem, self.local_sem = send_sem, recv_sem, local_sem
        self.sent, self.local, self.bounced = [], [], []

    def push(self, source, target, partner):
        number = len(self.sent)
        copy = pltpu.make_async_remote_copy(
            src_ref=source,
            dst_ref=target,
            send_sem=self.send_sem.at[number],
            recv_sem=self.recv_sem.at[number],
            device_id=partner,
            device_id_type=MESH,
        )
        copy.start()
        self.sent.append(copy)
        return copy

    def keep(self, source, target, bounce=None):
        if bounce is None:
            copy = pltpu.make_async_copy(source, target, self.local_sem.at[len(self.local)])
        else:
            copy = pltpu.make_async_copy(source, bounce, self.local_sem.at[len(self.local)])
            self.bounced.append((len(self.local), bounce, target))
        copy.start()
        self.local.append(copy)

    def flush(self):
        for number, bounce, target in self.bounced:
            self.local[number].wait()
            copy = pltpu.make_async_copy(bounce, target, self.local_sem.at[number])
            copy.start()
            self.local[number] = copy
        self.bounced = []

    def drain(self):
        for copy in self.sent:
            copy.wait_send()
        for copy in self.local:
            copy.wait()


def share_param(place, wire, source, target, bounce):
    rows = source.shape[0]
    cut = rows // 2
    mine, far = place.fsdp * rows, ((place.fsdp + 2) % 4) * rows
    parts = [(0, cut, 1), (cut, cut, 3)]
    across = [
        wire.push(
            source.at[pl.ds(start, count)],
            target.at[pl.ds(mine + start, count)],
            place.along_x(step),
        )
        for start, count, step in parts
    ]
    beside = wire.push(source, target.at[pl.ds(mine, rows)], place.beside)
    wire.keep(source, target.at[pl.ds(mine, rows)], bounce)
    last = [beside]

    def onward(copy, start, count):
        copy.wait_recv()
        spot = target.at[pl.ds(far + start, count)]
        last.append(wire.push(spot, spot, place.beside))

    steps = [
        functools.partial(onward, copy, start, count)
        for copy, (start, count, _) in zip(across, parts)
    ]
    return steps, last


def share_rows(place, wire, source, target):
    rows = source.shape[0]
    cut = rows // 2
    parts = [(0, cut, 1), (cut, cut, 3)] if rows % 32 == 0 else [(0, rows, 1)]
    across = [
        wire.push(
            source.at[pl.ds(start, count)],
            target.at[pl.ds(2 * rows + start, count)],
            place.along_x(step),
        )
        for start, count, step in parts
    ]
    last = [wire.push(source, target.at[pl.ds(rows, rows)], place.beside)]
    wire.keep(source, target.at[pl.ds(0, rows)])

    def onward(copy, start, count):
        copy.wait_recv()
        last.append(
            wire.push(
                target.at[pl.ds(2 * rows + start, count)],
                target.at[pl.ds(3 * rows + start, count)],
                place.beside,
            )
        )

    steps = [
        functools.partial(onward, copy, start, count)
        for copy, (start, count, _) in zip(across, parts)
    ]
    return steps, last


def share_columns(place, wire, source, target, stage):
    rows = source.shape[0]
    cut = rows // 2
    fsdp, core = place.fsdp, place.core
    parts = [(0, cut, 1), (cut, cut, 3)]

    def panel(start, count, shard):
        return source.at[pl.ds(start, count), pl.ds(pl.multiple_of(shard * D, D), D)]

    passing, last = [], []
    for start, count, step in parts:
        passing.append(
            wire.push(
                panel(start, count, 3 - fsdp),
                stage.at[pl.ds(start, count)],
                place.along_x(step),
            )
        )
    for start, count, step in parts:
        last.append(
            wire.push(
                panel(start, count, (fsdp + 2) % 4),
                target.at[pl.ds(2 * rows + start, count)],
                place.along_x(step),
            )
        )
    last.append(
        wire.push(
            panel(0, rows, fsdp + 1 - 2 * core), target.at[pl.ds(rows, rows)], place.beside
        )
    )
    wire.keep(panel(0, rows, fsdp), target.at[pl.ds(0, rows)])

    def onward(copy, start, count):
        copy.wait_recv()
        last.append(
            wire.push(
                stage.at[pl.ds(start, count)],
                target.at[pl.ds(3 * rows + start, count)],
                place.beside,
            )
        )

    steps = [
        functools.partial(onward, copy, start, count)
        for copy, (start, count, _) in zip(passing, parts)
    ]
    return steps, last


def spread(place, wire, own, spot, ready, between=()):
    between = list(between)
    arrivals = {}

    def push(t, da, db, b, axis, sign):
        target = spot(t, place.ring(t, da, db), b)
        source = own(t, b) if da == 0 and db == 0 else target
        sa, sb = (sign, 0) if axis == 0 else (0, sign)
        arrivals[t, (da - sa) % 4, (db - sb) % 4, b] = wire.push(
            source, target, place.near(t, axis, sign)
        )

    def landed(t, da, db):
        for b in (0, 1):
            arrivals[t, da, db, b].wait_recv()

    def pause():
        if between:
            between.pop(0)()

    for b in (0, 1):
        for t in (0, 1):
            ready(t, b)
            for axis in (0, 1):
                for sign in (1, -1):
                    push(t, 0, 0, b, axis, sign)
    for da, keep, onward in ((1, 0, -1), (3, 1, 1)):
        for t in (0, 1):
            landed(t, da, 0)
            push(t, da, 0, keep, 0, onward)
            for sign in (1, -1):
                for b in (0, 1):
                    push(t, da, 0, b, 1, sign)
    for db, keep, onward in ((1, 0, -1), (3, 1, 1)):
        for t in (0, 1):
            landed(t, 0, db)
            push(t, 0, db, keep, 1, onward)
    for t in (0, 1):
        landed(t, 2, 0)
        for sign in (1, -1):
            for b in (0, 1):
                push(t, 2, 0, b, 1, sign)
    pause()
    for da in (1, 3, 2):
        for db, keep, onward in ((1, 0, -1), (3, 1, 1)):
            for t in (0, 1):
                landed(t, da, db)
                push(t, da, db, keep, 1, onward)
    while between:
        pause()
    for da in (0, 1, 3, 2):
        for t in (0, 1):
            landed(t, da, 2)


ANY = pl.BlockSpec(memory_space=pl.ANY)
VM = pl.BlockSpec(memory_space=pltpu.VMEM)
SM = pl.BlockSpec(memory_space=pltpu.SMEM)


def room(*shape):
    return pltpu.VMEM(shape, BF)


def sems(count, local):
    return [
        pltpu.SemaphoreType.DMA((count,)),
        pltpu.SemaphoreType.DMA((count,)),
        pltpu.SemaphoreType.DMA((local,)),
    ]


def full_shape(shard):
    return jax.ShapeDtypeStruct((4 * shard.shape[-2], shard.shape[-1]), BF)


def first_kernel(weight_ref, vector_ref, weight_out, vector_out, bounce, *sem):
    place, wire = Place(), Wire(*sem)
    place.greet([place.beside, place.along_x(1), place.along_x(3)])
    far = vector_out.at[(place.fsdp + 2) % 4]
    across = wire.push(vector_ref, vector_out.at[place.fsdp], place.along_x(1))
    last = [wire.push(vector_ref, vector_out.at[place.fsdp], place.beside)]
    wire.keep(vector_ref, vector_out.at[place.fsdp])
    steps, ends = share_param(place, wire, weight_ref.at[0], weight_out, bounce)
    wire.flush()
    across.wait_recv()
    last.append(wire.push(far, far, place.beside))
    for step in steps:
        step()
    for copy in last + ends:
        copy.wait_recv()
    wire.drain()


def gather_first(weight, vectors):
    return pl.pallas_call(
        first_kernel,
        out_shape=(full_shape(weight), jax.ShapeDtypeStruct((4,) + vectors.shape, F32)),
        in_specs=[ANY, VM],
        out_specs=(ANY, ANY),
        scratch_shapes=[room(*weight.shape[1:])] + sems(16, 4),
        compiler_params=pltpu.CompilerParams(
            collective_id=0, has_side_effects=True, vmem_limit_bytes=60 * 2**20
        ),
        name="gather_first",
    )(weight, vectors)


def gather_kernel(jobs, q_ref, k_ref, v_ref, k_own, v_own, *refs):
    count = len(jobs)
    weights, refs = refs[:count], refs[count:]
    q_out, k_out, v_out = refs[:3]
    weights_out, refs = refs[3 : 3 + count], refs[3 + count :]
    bounces, refs = refs[:count], refs[count:]
    place, wire = Place(), Wire(*refs)
    place.greet(
        place.around() + [place.mirror, place.beside, place.along_x(1), place.along_x(3)]
    )
    ins, outs = (k_own, v_own), (k_out, v_out)
    ctx = place.ctx
    swapped = [
        wire.push(source, out.at[ctx], place.mirror) for source, out in zip((k_ref, v_ref), outs)
    ]
    for t in (0, 1):
        wire.keep(ins[t], outs[t].at[ctx])
    work = []

    def ready(t, b):
        if b == 1:
            if t == 0:
                for layer, weight, target, bounce in zip(jobs, weights, weights_out, bounces):
                    work.append(share_param(place, wire, weight.at[layer], target, bounce))
            swapped[t].wait_recv()
            if t == 1:
                swapped.append(wire.push(q_ref, q_out, place.mirror))

    def spot(t, origin, b):
        return outs[t].at[origin if b == 0 else BLOCKS - 1 - origin]

    def own(t, b):
        return ins[t] if b == 0 else spot(t, ctx, 1)

    def onward(number):
        for steps, _ in work:
            for step in steps[number : number + 1]:
                step()

    spread(
        place,
        wire,
        own,
        spot,
        ready,
        [wire.flush, functools.partial(onward, 0), functools.partial(onward, 1)],
    )
    swapped[2].wait_recv()
    for _, last in work:
        for copy in last:
            copy.wait_recv()
    wire.drain()


def gather_pair(name, number, away, own, jobs):
    layers = [layer for layer, _ in jobs]
    weights = [weight for _, weight in jobs]
    whole = jax.ShapeDtypeStruct((BLOCKS, BLOCK, HALF), BF)
    return pl.pallas_call(
        functools.partial(gather_kernel, layers),
        out_shape=(jax.ShapeDtypeStruct((BLOCK, HALF), BF), whole, whole)
        + tuple(full_shape(weight) for weight in weights),
        in_specs=[VM] * 5 + [ANY] * len(jobs),
        out_specs=(ANY,) * (3 + len(jobs)),
        scratch_shapes=[room(*weight.shape[1:]) for weight in weights] + sems(96, 8),
        compiler_params=pltpu.CompilerParams(
            collective_id=number, has_side_effects=True, vmem_limit_bytes=60 * 2**20
        ),
        name=name,
    )(*away, *own, *weights)


def scatter_kernel(
    count, forward, gk_ref, gv_ref, gq_ref, hidden_ref, pre_ref, up_ref, down_ref, *refs
):
    sources, refs = refs[:count], refs[count:]
    own_out, norm_out, back_out, back_q, hidden_out, grad_pre_out = refs[:6]
    targets, refs = refs[6 : 6 + count], refs[6 + count :]
    if forward:
        vec_ref, two_ref = hidden_ref, pre_ref
        (mlp_out, hidden_ref, pre_ref), refs = (refs[0], *refs[-2:]), refs[1:-2]
    far, near, mix, total, last_far, last_near, last_mix, leave, stage = refs[:9]
    up_buffer, down_buffer, grad_pre, load_sem = refs[9:13]
    place, wire = Place(), Wire(*refs[13:])
    loads = []
    for i in range(FF // D):
        cols = slice(i * D, (i + 1) * D)
        for source, buffer in (
            (down_ref.at[cols, :], down_buffer.at[cols, :]),
            (up_ref.at[:, cols], up_buffer.at[i]),
        ):
            load = pltpu.make_async_copy(source, buffer, load_sem.at[len(loads)])
            load.start()
            loads.append(load)
    loaded = set()

    def ready(number):
        if number not in loaded:
            loads[number].wait()
            loaded.add(number)

    place.greet(
        place.around() + [place.mirror, place.beside, place.along_x(1), place.along_x(3)]
    )
    ins = (gk_ref, gv_ref)

    def block_at(t, da, db, b):
        origin = place.ring(t, da, db)
        return origin if b == 0 else BLOCKS - 1 - origin

    order = [(da, t) for da in (2, 1, 3, 0) for t in (0, 1)]
    way = {0: 1, 1: -1}
    first, second, loose = {}, {}, {}
    for b in (1, 0):
        for da, t in order:
            first[t, da, b] = wire.push(
                ins[t].at[block_at(t, da, 2, b)], far.at[t, da, b], place.near(t, 1, way[b])
            )
    swapped = [wire.push(gq_ref, back_q, place.mirror)]
    for b in (1, 0):
        for da, t in order:
            loose[t, da, b] = wire.push(
                ins[t].at[block_at(t, da, -way[b], b)],
                near.at[t, da, 1, b],
                place.near(t, 1, -way[b]),
            )
    work = [] if forward else [share_columns(place, wire, hidden_ref, hidden_out, stage)]
    for source, target in zip(sources, targets):
        work.append(share_rows(place, wire, source, target))
    for b in (1, 0):
        if b == 0:
            if forward:
                two = two_ref[...]
                for i in range(FF // D):
                    cols = slice(i * D, (i + 1) * D)
                    ready(2 * i + 1)
                    pre = contract(two, up_buffer[i], ((1,), (0,))) + line(vec_ref, BIAS_UP + i)
                    pre_ref[:, cols] = pre
                    hidden = (pre * phi_parts(pre)[0]).astype(BF)
                    hidden_ref[:, cols] = hidden
                    ready(2 * i)
                    fresh = contract(hidden, down_buffer[cols, :], ((1,), (0,)))
                    mlp_out[...] = fresh if i == 0 else mlp_out[...] + fresh
                work.append(share_columns(place, wire, hidden_ref, hidden_out, stage))
            mlp_back(sources[3][...], pre_ref, ready, up_buffer, down_buffer, grad_pre, norm_out)
            work.append(share_rows(place, wire, grad_pre, grad_pre_out))
        for da, t in order:
            first[t, da, b].wait_recv()
            mix[t, da, b] = (
                ins[t][block_at(t, da, way[b], b)].astype(F32) + far[t, da, b].astype(F32)
            ).astype(BF)
            second[t, da, b] = wire.push(
                mix.at[t, da, b], near.at[t, da, 0, b], place.near(t, 1, way[b])
            )

    def settle(t, da, b):
        loose[t, da, b].wait_recv()
        second[t, da, b].wait_recv()
        total[t, da, b] = (
            ins[t][block_at(t, da, 0, b)].astype(F32)
            + near[t, da, 0, b].astype(F32)
            + near[t, da, 1, b].astype(F32)
        ).astype(BF)

    third, fourth = {}, {}
    for b in (1, 0):
        for t in (0, 1):
            settle(t, 2, b)
            third[t, b] = wire.push(
                total.at[t, 2, b], last_far.at[t, b], place.near(t, 0, way[b])
            )
        for t in (0, 1):
            settle(t, 1, b)
            settle(t, 3, b)
            fourth[t, b] = [
                wire.push(
                    total.at[t, -way[b] % 4, b], last_near.at[t, 1, b], place.near(t, 0, -way[b])
                )
            ]
        for t in (0, 1):
            third[t, b].wait_recv()
            last_mix[t, b] = (
                total[t, way[b] % 4, b].astype(F32) + last_far[t, b].astype(F32)
            ).astype(BF)
            fourth[t, b].append(
                wire.push(last_mix.at[t, b], last_near.at[t, 0, b], place.near(t, 0, way[b]))
            )
        for t in (0, 1):
            settle(t, 0, b)

    def final(t, b):
        for copy in fourth[t, b]:
            copy.wait_recv()
        return (
            total[t, 0, b].astype(F32)
            + last_near[t, 0, b].astype(F32)
            + last_near[t, 1, b].astype(F32)
        )

    for t in (0, 1):
        leave[t] = final(t, 1).astype(BF)
        swapped.append(wire.push(leave.at[t], back_out.at[t], place.mirror))
    for steps, _ in work:
        for step in steps:
            step()
    for t in (0, 1):
        own_out[t] = final(t, 0)
    for _, last in work:
        for copy in last:
            copy.wait_recv()
    for copy in swapped:
        copy.wait_recv()
    wire.drain()


def rows_shape(source):
    return jax.ShapeDtypeStruct((4 * source.shape[0], source.shape[1]), BF)


def mlp_back(low, pre_ref, ready, up_buffer, down_buffer, grad_pre_ref, norm_ref):
    for i in range(FF // D):
        cols = slice(i * D, (i + 1) * D)
        pre = pre_ref[:, cols]
        cumulative, density = phi_parts(pre)
        ready(2 * i)
        hidden = contract(low, down_buffer[cols, :], ((1,), (1,)))
        grad_pre = (hidden * (cumulative + pre * density)).astype(BF)
        grad_pre_ref[:, cols] = grad_pre
        ready(2 * i + 1)
        fresh = contract(grad_pre, up_buffer[i], ((1,), (1,)))
        norm_ref[...] = fresh if i == 0 else norm_ref[...] + fresh


def scatter_pair(
    name, number, forward, grad_keys, grad_values, away, hidden, pre, up, down, sources
):
    return pl.pallas_call(
        functools.partial(scatter_kernel, len(sources), forward),
        out_shape=(
            jax.ShapeDtypeStruct((2, BLOCK, HALF), F32),
            jax.ShapeDtypeStruct((BLOCK, D), F32),
            jax.ShapeDtypeStruct((2, BLOCK, HALF), BF),
            jax.ShapeDtypeStruct((BLOCK, HALF), BF),
            jax.ShapeDtypeStruct((4 * BLOCK, D), BF),
            jax.ShapeDtypeStruct((4 * BLOCK, FF), BF),
        )
        + tuple(rows_shape(source) for source in sources)
        + ((jax.ShapeDtypeStruct((BLOCK, D), F32),) if forward else ()),
        in_specs=[VM] * 5 + [ANY] * 2 + [VM] * len(sources),
        out_specs=(VM, VM) + (ANY,) * (4 + len(sources)) + ((VM,) if forward else ()),
        scratch_shapes=[
            room(2, 4, 2, BLOCK, HALF),
            room(2, 4, 2, 2, BLOCK, HALF),
            room(2, 4, 2, BLOCK, HALF),
            room(2, 4, 2, BLOCK, HALF),
            room(2, 2, BLOCK, HALF),
            room(2, 2, 2, BLOCK, HALF),
            room(2, 2, BLOCK, HALF),
            room(2, BLOCK, HALF),
            room(BLOCK, D),
            room(FF // D, D, D),
            room(FF, D),
            room(BLOCK, FF),
            pltpu.SemaphoreType.DMA((2 * FF // D,)),
        ]
        + sems(128, 12)
        + ([room(BLOCK, FF), pltpu.VMEM((BLOCK, FF), F32)] if forward else []),
        compiler_params=pltpu.CompilerParams(
            collective_id=number, has_side_effects=True, vmem_limit_bytes=60 * 2**20
        ),
        name=name,
    )(grad_keys, grad_values, away, hidden, pre, up, down, *sources)


PIECE = 144
CUT = 80


LOADS = 13


def sum_kernel(joined_ref, norm_ref, norm_one, *refs):
    sources, (out_ref, small_out), refs = refs[:LOADS], refs[LOADS : LOADS + 2], refs[LOADS + 2 :]
    buffers, refs = refs[:LOADS], refs[LOADS:]
    rows, joined_land, norm_land, turned, load_sem = refs[:5]
    far, mix, near, total, far_two, mix_two, near_two, part, other, final, small, heard = refs[5:17]
    place, wire = Place(), Wire(*refs[17:])
    loads = []
    for source, buffer in zip(sources, buffers):
        load = pltpu.make_async_copy(source, buffer, load_sem.at[len(loads)])
        load.start()
        loads.append(load)
    y, z, h = place.y, place.z, place.h
    turns = [
        (place.fsdp, (y + 1 - 2 * (y % 2)) * 8 + z * 2 + h),
        (place.fsdp, ((y + 2) % 4) * 8 + z * 2 + h),
        (place.fsdp, y * 8 + (z + 1 - 2 * (z % 2)) * 2 + h),
        (place.fsdp, y * 8 + ((z + 2) % 4) * 2 + h),
        place.half,
    ]
    place.greet(
        place.around()
        + [turns[1], turns[3], place.half, place.beside, place.along_x(1), place.along_x(3)]
    )
    parts = {0: pl.ds(0, CUT), 1: pl.ds(CUT, PIECE - CUT)}

    def chunk(t, da, db):
        start = pl.multiple_of(place.ring(t, da, db) // 2 * PIECE, 16)
        return rows.at[t, pl.ds(start, PIECE)]

    def plus(*terms):
        result = terms[0].astype(F32)
        for term in terms[1:]:
            result = result + term.astype(F32)
        return result.astype(BF)

    order = (2, 1, 3, 0)
    way = {2: 1, 1: 1, 3: -1, 0: -1}
    first, second, loose = {}, {}, {}

    def take(number):
        loads[number].wait()
        return buffers[number]

    def panel(t, start, left, right):
        rows[t, start : start + left.shape[0], :] = contract(left, right, ((1,), (0,))).astype(BF)

    def note(t, row, right):
        ones = jnp.ones((8, right.shape[0]), BF)
        small[1 - t, row : row + 1, :] = contract(ones, right, ((1,), (0,)))[:1]

    def own_rows(values):
        turned[...] = jnp.transpose(values)
        return turned[pl.ds(pl.multiple_of(place.fsdp * 192, 64), 192), :]

    def early_grads(t, at):
        low = take(at)[...]
        panel(t, 576, own_rows(take(at + 1)[...]), low)
        note(t, 0, low)
        turned[...] = jnp.transpose(take(at + 2)[...])
        panel(t, 1536, turned[...], low)
        left, pre = own_rows(take(at + 3)[...]), take(at + 4)
        for i in range(4):
            right = pre[:, i * D : (i + 1) * D]
            panel(t, 768 + i * 192, left, right)
            note(t, 4 + i, right)

    def late_grads(t, one, joined, norms):
        left = own_rows(one[...])
        for i in range(3):
            right = joined[:, i * D : (i + 1) * D]
            panel(t, i * 192, left, right)
            note(t, 1 + i, right)
        sums = norms[0:16, :].astype(F32)
        for i in range(1, 4):
            sums = sums + norms[i * 16 : (i + 1) * 16, :].astype(F32)
        small[1 - t, 8:16, :] = sums[:8]

    def set_out(t):
        for db in order:
            first[t, db] = wire.push(chunk(t, 2, db), far.at[t, db], place.near(t, 0, way[db]))
        for db in order:
            loose[t, db] = wire.push(
                chunk(t, -way[db], db), near.at[t, db, 1], place.near(t, 0, -way[db])
            )

    work = [
        share_rows(place, wire, joined_ref, joined_land),
        share_rows(place, wire, norm_ref, norm_land),
    ]
    early_grads(0, 0)
    late_grads(0, take(5), take(6), norm_one)
    set_out(0)
    for steps, _ in work:
        for step in steps:
            step()
    early_grads(1, 7)
    for _, last in work:
        for copy in last:
            copy.wait_recv()
    for copy in wire.local:
        copy.wait()
    settled = len(wire.local)
    late_grads(1, take(12), joined_land, norm_land)
    set_out(1)
    step_numbers, waited = [len(wire.sent)], set()
    wire.push(small, heard.at[0], turns[0])
    for db in order:
        for t in (0, 1):
            first[t, db].wait_recv()
            mix[t, db] = plus(chunk(t, way[db], db)[...], far[t, db])
            second[t, db] = wire.push(mix.at[t, db], near.at[t, db, 0], place.near(t, 0, way[db]))

    def hear(step):
        wire.sent[step_numbers[-1]].wait_send()
        wire.sent[step_numbers[-1]].wait_recv()
        small[...] += heard[step]
        waited.add(step_numbers[-1])
        if step < 4:
            step_numbers.append(len(wire.sent))
            wire.push(small, heard.at[step + 1], turns[step + 1])

    def settle(t, db):
        second[t, db].wait_recv()
        loose[t, db].wait_recv()
        total[t, db] = plus(chunk(t, 0, db)[...], near[t, db, 0], near[t, db, 1])

    third, fourth = {}, {}
    for t in (0, 1):
        settle(t, 2)
        third[t] = [
            wire.push(
                total.at[t, 2, parts[b]], far_two.at[t, parts[b]], place.near(t, 1, sign)
            )
            for b, sign in ((0, 1), (1, -1))
        ]
    hear(0)
    for t in (0, 1):
        fourth[t] = []
        for b, sign, db in ((0, 1, 1), (1, -1, 3)):
            settle(t, db)
            fourth[t].append(
                wire.push(
                    total.at[t, db, parts[1 - b]],
                    near_two.at[t, b, parts[1 - b]],
                    place.near(t, 1, sign),
                )
            )
    hear(1)
    for t in (0, 1):
        for b, sign, db in ((0, 1, 1), (1, -1, 3)):
            third[t][b].wait_recv()
            mix_two[t, parts[b]] = plus(total[t, db, parts[b]], far_two[t, parts[b]])
            fourth[t].append(
                wire.push(
                    mix_two.at[t, parts[b]], near_two.at[t, b, parts[b]], place.near(t, 1, sign)
                )
            )
    hear(2)
    swapped = []
    for t in (0, 1):
        settle(t, 0)
        for copy in fourth[t]:
            copy.wait_recv()
        part[t] = plus(total[t, 0], near_two[t, 0], near_two[t, 1])
        swapped.append(wire.push(part.at[t], other.at[t], place.half))
    hear(3)

    def spot(t, origin, b):
        return out_ref.at[1 - t, origin // 2, parts[b]]

    def own(t, b):
        return final.at[1 - t, parts[b]]

    def ready(t, b):
        if b == 0:
            swapped[1 - t].wait_recv()
            final[1 - t] = plus(part[1 - t], other[1 - t])
            wire.keep(final.at[1 - t], out_ref.at[1 - t, place.ctx // 2])

    spread(place, wire, own, spot, ready)
    hear(4)
    small_out[...] = small[...]
    for number, copy in enumerate(wire.sent):
        if number not in waited:
            copy.wait_send()
    for copy in wire.local[settled:]:
        copy.wait()


def sum_over_ctx(joined, norms, norms_one, arrays):
    shape = (16, PIECE, D)
    small_shape = (LAYERS, 16, D)
    tokens = 4 * BLOCK
    return pl.pallas_call(
        sum_kernel,
        out_shape=(
            jax.ShapeDtypeStruct((2,) + shape, BF),
            jax.ShapeDtypeStruct(small_shape, F32),
        ),
        in_specs=[VM] * 3 + [ANY] * LOADS,
        out_specs=(ANY, VM),
        scratch_shapes=[room(*array.shape) for array in arrays]
        + [
            room(2, 16 * PIECE, D),
            room(tokens, 3 * D),
            room(64, D),
            room(D, tokens),
            pltpu.SemaphoreType.DMA((LOADS,)),
            room(2, 4, PIECE, D),
            room(2, 4, PIECE, D),
            room(2, 4, 2, PIECE, D),
            room(2, 4, PIECE, D),
            room(2, PIECE, D),
            room(2, PIECE, D),
            room(2, 2, PIECE, D),
            room(2, PIECE, D),
            room(2, PIECE, D),
            room(2, PIECE, D),
            pltpu.VMEM(small_shape, F32),
            pltpu.VMEM((5,) + small_shape, F32),
        ]
        + sems(128, 4),
        compiler_params=pltpu.CompilerParams(
            collective_id=6, has_side_effects=True, vmem_limit_bytes=60 * 2**20
        ),
        name="sum_over_ctx",
    )(joined, norms, norms_one, *arrays)


def pair_rows(values):
    lane = lax.broadcasted_iota(jnp.int32, values.shape, 1)
    zero = jnp.zeros_like(values)
    return jnp.concatenate(
        [jnp.where(lane < HEAD_DIM, values, zero), jnp.where(lane >= HEAD_DIM, values, zero)], 0
    )


def contract(left, right, dims):
    return lax.dot_general(left, right, (dims, ((), ())), preferred_element_type=F32)


def allowed_at(tile, block):
    key = tile * TILE + lax.broadcasted_iota(jnp.int32, (TILE, 2 * BLOCK), 0)
    query = block * BLOCK + lax.broadcasted_iota(jnp.int32, (TILE, 2 * BLOCK), 1) % BLOCK
    return key <= query


def low_block(ctx):
    return jnp.minimum(ctx, BLOCKS - 1 - ctx)


def by_height(ctx, own, away, two):
    @pl.when(ctx < BLOCKS // 2)
    def _():
        two[0] = own[...]
        two[1] = away[...]

    @pl.when(ctx >= BLOCKS // 2)
    def _():
        two[0] = away[...]
        two[1] = own[...]


def from_height(ctx, two, own, away):
    @pl.when(ctx < BLOCKS // 2)
    def _():
        own[...] = two[0].astype(own.dtype)
        away[...] = two[1].astype(away.dtype)

    @pl.when(ctx >= BLOCKS // 2)
    def _():
        own[...] = two[1].astype(own.dtype)
        away[...] = two[0].astype(away.dtype)


TILES = BLOCKS * BLOCK // TILE


def load_tiles(pairs, sem):
    loads = []
    for tile in range(TILES):
        rows = pl.ds(tile * TILE, TILE)
        for source, buffer in pairs:
            load = pltpu.make_async_copy(source.at[rows], buffer.at[rows], sem.at[len(loads)])
            load.start()
            loads.append(load)
    return loads


def wait_tiles(loads, b):
    half = len(loads) // 2
    for load in loads[b * half : (b + 1) * half]:
        load.wait()


def forward_kernel(
    ctx_ref, q_own, q_away, k_in, v_in, mixed_own, mixed_away, turned_ref, log_ref,
    top, mass, acc, k_ref, v_ref, q_two, mixed_two, sem,
):
    ctx = ctx_ref[0]
    loads = load_tiles(((k_in, k_ref), (v_in, v_ref)), sem)
    by_height(ctx, q_own, q_away, q_two)
    for b in (0, 1):
        block = low_block(ctx) if b == 0 else BLOCKS - 1 - low_block(ctx)
        wait_tiles(loads, b)
        rows = slice(b * BLOCK, (b + 1) * BLOCK)
        q_ref, mixed_ref = q_two.at[b], mixed_two.at[b]
        queries = [
            pair_rows(q_ref[:, p * 128 : (p + 1) * 128] * jnp.asarray(0.125, BF))
            for p in range(PAIRS)
        ]

        def step(tile, masked):
            start = pl.multiple_of(tile * TILE, TILE)
            for p in range(PAIRS):
                cols = slice(p * 128, (p + 1) * 128)
                scores = contract(k_ref[pl.ds(start, TILE), cols], queries[p], ((1,), (1,)))
                if masked:
                    scores = jnp.where(allowed_at(tile, block), scores, masked_score)
                    new_top = jnp.max(scores, 0, keepdims=True)
                else:
                    old_top = top[p : p + 1, :]
                    new_top = jnp.maximum(old_top, jnp.max(scores, 0, keepdims=True))
                weights = jnp.exp(scores - new_top)
                fresh_mass = jnp.sum(weights, 0, keepdims=True)
                fresh = contract(
                    v_ref[pl.ds(start, TILE), cols], weights.astype(BF), ((0,), (0,))
                )
                if not masked:
                    fade = jnp.exp(old_top - new_top)
                    fresh_mass = fresh_mass + mass[p : p + 1, :] * fade
                    fresh = fresh + acc[p] * fade
                top[p : p + 1, :] = new_top
                mass[p : p + 1, :] = fresh_mass
                acc[p] = fresh

        step(block // 4, True)

        @pl.loop(0, block // 4)
        def _(tile):
            step(tile, False)

        for p in range(PAIRS):
            cols = slice(p * 128, (p + 1) * 128)
            done = acc[p] / mass[p : p + 1, :]
            turned = jnp.concatenate([done[:HEAD_DIM, :BLOCK], done[HEAD_DIM:, BLOCK:]], 0)
            turned_ref[cols, rows] = turned
            mixed_ref[:, cols] = jnp.transpose(turned).astype(BF)
            row = b * PAIRS + p
            log_ref[row : row + 1, :] = top[p : p + 1, :] + jnp.log(mass[p : p + 1, :])
    from_height(ctx, mixed_two, mixed_own, mixed_away)


def attend_forward(ctx, own, away, keys, values):
    return pl.pallas_call(
        forward_kernel,
        out_shape=(
            jax.ShapeDtypeStruct((BLOCK, HALF), BF),
            jax.ShapeDtypeStruct((BLOCK, HALF), BF),
            jax.ShapeDtypeStruct((HALF, 2 * BLOCK), F32),
            jax.ShapeDtypeStruct((8, 2 * BLOCK), F32),
        ),
        in_specs=[SM, VM, VM, ANY, ANY],
        out_specs=(VM, VM, VM, VM),
        scratch_shapes=[
            pltpu.VMEM((8, 2 * BLOCK), F32),
            pltpu.VMEM((8, 2 * BLOCK), F32),
            pltpu.VMEM((PAIRS, 128, 2 * BLOCK), F32),
            room(BLOCKS * BLOCK, HALF),
            room(BLOCKS * BLOCK, HALF),
            room(2, BLOCK, HALF),
            room(2, BLOCK, HALF),
            pltpu.SemaphoreType.DMA((2 * TILES,)),
        ],
        compiler_params=pltpu.CompilerParams(vmem_limit_bytes=60 * 2**20),
        cost_estimate=pl.CostEstimate(
            flops=4 * 33 * 128 * 128 * 6 * 128, bytes_accessed=8 * 2**20, transcendentals=33 * 128 * 128 * 6
        ),
        name="attend_forward",
    )(ctx, own, away, keys, values)


def backward_kernel(
    ctx_ref, q_own, q_away, k_in, v_in, g_own, g_away, turned_ref, log_ref,
    gq_own, gq_away, gk_ref, gv_ref,
    gk_acc, gv_acc, gq_acc, k_ref, v_ref, q_two, g_two, gq_two, sem,
):
    ctx = ctx_ref[0]
    loads = load_tiles(((k_in, k_ref), (v_in, v_ref)), sem)
    by_height(ctx, q_own, q_away, q_two)
    by_height(ctx, g_own, g_away, g_two)
    gk_acc[...] = jnp.zeros_like(gk_acc)
    gv_acc[...] = jnp.zeros_like(gv_acc)
    for b in (0, 1):
        block = low_block(ctx) if b == 0 else BLOCKS - 1 - low_block(ctx)
        wait_tiles(loads, b)
        rows = slice(b * BLOCK, (b + 1) * BLOCK)
        queries, grads, deltas = [], [], []
        q_ref, g_ref, gq_ref = q_two.at[b], g_two.at[b], gq_two.at[b]
        for p in range(PAIRS):
            cols = slice(p * 128, (p + 1) * 128)
            queries.append(pair_rows(q_ref[:, cols] * jnp.asarray(0.125, BF)))
            grad = g_ref[:, cols]
            grads.append(pair_rows(grad))
            both = jnp.transpose(grad.astype(F32)) * turned_ref[cols, rows]
            deltas.append(
                jnp.concatenate(
                    [
                        jnp.sum(both[:HEAD_DIM], 0, keepdims=True),
                        jnp.sum(both[HEAD_DIM:], 0, keepdims=True),
                    ],
                    1,
                )
            )
        gq_acc[...] = jnp.zeros_like(gq_acc)

        def step(tile, masked):
            start = pl.multiple_of(tile * TILE, TILE)
            here = pl.ds(start, TILE)
            for p in range(PAIRS):
                cols = slice(p * 128, (p + 1) * 128)
                row = b * PAIRS + p
                keys = k_ref[here, cols]
                scores = contract(keys, queries[p], ((1,), (1,)))
                chances = jnp.exp(scores - log_ref[row : row + 1, :])
                if masked:
                    chances = jnp.where(allowed_at(tile, block), chances, 0.0)
                grad_chance = contract(v_ref[here, cols], grads[p], ((1,), (1,)))
                grad_score = (chances * (grad_chance - deltas[p])).astype(BF)
                gv_acc[here, cols] += contract(chances.astype(BF), grads[p], ((1,), (0,)))
                gk_acc[here, cols] += contract(grad_score, queries[p], ((1,), (0,)))
                gq_acc[p] += contract(keys, grad_score, ((0,), (0,)))

        step(block // 4, True)

        @pl.loop(0, block // 4)
        def _(tile):
            step(tile, False)

        for p in range(PAIRS):
            cols = slice(p * 128, (p + 1) * 128)
            done = gq_acc[p] * 0.125
            turned = jnp.concatenate([done[:HEAD_DIM, :BLOCK], done[HEAD_DIM:, BLOCK:]], 0)
            gq_ref[:, cols] = jnp.transpose(turned).astype(gq_ref.dtype)
    from_height(ctx, gq_two, gq_own, gq_away)
    gk_ref[...] = gk_acc[...].astype(BF)
    gv_ref[...] = gv_acc[...].astype(BF)


def attend_backward(ctx, own, away, keys, values, grad_own, grad_away, turned, log_total):
    whole = jax.ShapeDtypeStruct((BLOCKS * BLOCK, HALF), BF)
    return pl.pallas_call(
        backward_kernel,
        out_shape=(
            jax.ShapeDtypeStruct((BLOCK, HALF), F32),
            jax.ShapeDtypeStruct((BLOCK, HALF), BF),
            whole,
            whole,
        ),
        in_specs=[SM, VM, VM, ANY, ANY] + [VM] * 4,
        out_specs=(VM,) * 4,
        scratch_shapes=[
            pltpu.VMEM((BLOCKS * BLOCK, HALF), F32),
            pltpu.VMEM((BLOCKS * BLOCK, HALF), F32),
            pltpu.VMEM((PAIRS, 128, 2 * BLOCK), F32),
            room(BLOCKS * BLOCK, HALF),
            room(BLOCKS * BLOCK, HALF),
            room(2, BLOCK, HALF),
            room(2, BLOCK, HALF),
            pltpu.VMEM((2, BLOCK, HALF), F32),
            pltpu.SemaphoreType.DMA((2 * TILES,)),
        ],
        compiler_params=pltpu.CompilerParams(vmem_limit_bytes=60 * 2**20),
        cost_estimate=pl.CostEstimate(
            flops=10 * 33 * 128 * 128 * 6 * 128, bytes_accessed=16 * 2**20, transcendentals=33 * 128 * 128 * 6
        ),
        name="attend_backward",
    )(ctx, own, away, keys, values, grad_own, grad_away, turned, log_total)


GAIN_ONE, BIAS_ONE, GAIN_TWO, BIAS_TWO, BIAS_OUT, BIAS_DOWN, BIAS_QKV, BIAS_UP = (
    0, 1, 2, 3, 4, 5, 6, 9,
)


def norm_parts(values):
    centre = jnp.mean(values, -1, keepdims=True)
    shifted = values - centre
    spread = jnp.mean(shifted * shifted, -1, keepdims=True)
    scale = lax.rsqrt(spread + epsilon)
    return shifted * scale, scale


def norm_input_grad(grad_norm, gain, unit, scale):
    e = grad_norm * gain
    return scale * (
        e - jnp.mean(e, -1, keepdims=True) - unit * jnp.mean(e * unit, -1, keepdims=True)
    )


def turn_tables(first_row, row_count):
    shape = (row_count, 128)
    feature = lax.broadcasted_iota(jnp.int32, shape, 1) % HEAD_DIM
    position = first_row + lax.broadcasted_iota(jnp.int32, shape, 0)
    half_rot = ROTARY // 2
    exponent = (feature % half_rot).astype(F32) * (2.0 / ROTARY)
    angle = position.astype(F32) * jnp.power(10000.0, -exponent)
    cosine, sine = jnp.cos(angle), jnp.sin(angle)
    keep = jnp.where(feature < ROTARY, cosine, 1.0)
    low = jnp.where(feature < half_rot, -sine, 0.0)
    high = jnp.where((feature >= half_rot) & (feature < ROTARY), sine, 0.0)
    return keep, low, high


def rotate(values, table_ref):
    shift = ROTARY // 2
    return (
        values * table_ref[0]
        + pltpu.roll(values, 128 - shift, 1) * table_ref[1]
        + pltpu.roll(values, shift, 1) * table_ref[2]
    )


def rotate_back(values, table_ref):
    shift = ROTARY // 2
    return (
        values * table_ref[0]
        + pltpu.roll(values * table_ref[1], shift, 1)
        + pltpu.roll(values * table_ref[2], 128 - shift, 1)
    )


def phi_parts(values):
    cumulative = 0.5 * (1.0 + lax.erf(values * (2.0**-0.5)))
    density = jnp.exp(-0.5 * values * values) * (0.5 / jnp.pi) ** 0.5
    return cumulative, density


def line(vec_ref, row):
    return vec_ref[row : row + 1, :]


def put_halves(upper_ref, low, high, mine_ref, theirs_ref):
    upper = upper_ref[0] == 1

    @pl.when(upper)
    def _():
        mine_ref[...] = high
        theirs_ref[...] = low

    @pl.when(jnp.logical_not(upper))
    def _():
        mine_ref[...] = low
        theirs_ref[...] = high


def put_joined(upper_ref, mine, theirs, out_ref, first):
    upper = upper_ref[0] == 1
    low, high = slice(first, first + HALF), slice(first + HALF, first + D)

    @pl.when(upper)
    def _():
        out_ref[:, low] = theirs
        out_ref[:, high] = mine

    @pl.when(jnp.logical_not(upper))
    def _():
        out_ref[:, low] = mine
        out_ref[:, high] = theirs


def enter(upper_ref, stream, vec_ref, weight_ref, table_ref, one_ref, two_ref, *parts):
    unit, _ = norm_parts(stream)
    one = (unit * line(vec_ref, GAIN_ONE) + line(vec_ref, BIAS_ONE)).astype(BF)
    one_ref[...] = one
    two_ref[...] = (unit * line(vec_ref, GAIN_TWO) + line(vec_ref, BIAS_TWO)).astype(BF)
    for i in range(3):
        joined = contract(one, weight_ref[:, i * D : (i + 1) * D], ((1,), (0,)))
        joined = joined + line(vec_ref, BIAS_QKV + i)
        groups = [joined[:, g * 128 : (g + 1) * 128] for g in range(6)]
        if i < 2:
            groups = [rotate(group, table_ref) for group in groups]
        groups = [group.astype(BF) for group in groups]
        put_halves(
            upper_ref,
            jnp.concatenate(groups[:3], 1),
            jnp.concatenate(groups[3:], 1),
            parts[2 * i],
            parts[2 * i + 1],
        )


def enter_kernel(upper_ref, tokens_ref, vec_ref, weight_ref, keep, low, high, *outs):
    table_ref = (keep[...], low[...], high[...])
    enter(upper_ref, tokens_ref[...].astype(F32), vec_ref, weight_ref, table_ref, *outs)


def leave(upper_ref, stream_ref, own_ref, away_ref, weight_ref, mlp_ref, vec_ref, mixed_ref):
    put_joined(upper_ref, own_ref[...], away_ref[...], mixed_ref, 0)
    return (
        stream_ref[...].astype(F32)
        + contract(mixed_ref[...], weight_ref[...], ((1,), (0,)))
        + line(vec_ref, BIAS_OUT)
        + mlp_ref[...]
        + line(vec_ref, BIAS_DOWN)
    )


def pass_kernel(
    upper_ref, stream_ref, own_ref, away_ref, out_ref, mlp_ref, vec_ref,
    next_vec_ref, weight_ref, keep, low, high, mixed_ref, next_ref, *outs,
):
    table_ref = (keep[...], low[...], high[...])
    stream = leave(upper_ref, stream_ref, own_ref, away_ref, out_ref, mlp_ref, vec_ref, mixed_ref)
    next_ref[...] = stream
    enter(upper_ref, stream, next_vec_ref, weight_ref, table_ref, *outs)


def mixed_kernel(upper_ref, own_ref, away_ref, mixed_ref):
    put_joined(upper_ref, own_ref[...], away_ref[...], mixed_ref, 0)


def last_kernel(stream_ref, mixed_ref, weight_ref, mlp_ref, vec_ref, next_ref):
    next_ref[...] = (
        stream_ref[...].astype(F32)
        + contract(mixed_ref[...], weight_ref[...], ((1,), (0,)))
        + line(vec_ref, BIAS_OUT)
        + mlp_ref[...]
        + line(vec_ref, BIAS_DOWN)
    ).astype(BF)


def mlp_kernel(two_ref, up_ref, down_ref, vec_ref, pre_ref, hidden_ref, mlp_ref):
    two = two_ref[...]
    for i in range(FF // D):
        cols = slice(i * D, (i + 1) * D)
        pre = contract(two, up_ref[:, cols], ((1,), (0,))) + line(vec_ref, BIAS_UP + i)
        pre_ref[:, cols] = pre
        hidden = (pre * phi_parts(pre)[0]).astype(BF)
        hidden_ref[:, cols] = hidden
        fresh = contract(hidden, down_ref[cols, :], ((1,), (0,)))
        mlp_ref[...] = fresh if i == 0 else mlp_ref[...] + fresh


def back(upper_ref, gradient, weight_ref, low_ref, mine_ref, theirs_ref):
    low = gradient.astype(BF)
    low_ref[...] = low
    mixed = contract(low, weight_ref[...], ((1,), (1,))).astype(BF)
    put_halves(upper_ref, mixed[:, :HALF], mixed[:, HALF:], mine_ref, theirs_ref)


def back_kernel(upper_ref, cotangent_ref, weight_ref, *outs):
    back(upper_ref, cotangent_ref[...].astype(F32), weight_ref, *outs)


def join_kernel(
    more, upper_ref, own_ref, back_ref, own_q, back_q, keep, low, high, weight_ref, stream_ref,
    vec_ref, two_ref, gradient_ref, *refs,
):
    table_ref = (keep[...], low[...], high[...])
    next_weight, refs = (refs[:1], refs[1:]) if more else ((), refs)
    joined_ref, sums_ref, next_ref, *outs = refs

    def turned(values):
        groups = [rotate_back(values[:, g * 128 : (g + 1) * 128], table_ref) for g in range(3)]
        return jnp.concatenate(groups, 1).astype(BF)

    put_joined(upper_ref, turned(own_q[...]), turned(back_q[...].astype(F32)), joined_ref, 0)
    put_joined(upper_ref, turned(own_ref[0]), turned(back_ref[0].astype(F32)), joined_ref, D)
    put_joined(upper_ref, own_ref[1].astype(BF), back_ref[1], joined_ref, 2 * D)
    one = contract(joined_ref[...], weight_ref[...], ((1,), (1,)))
    two = two_ref[...]
    unit, scale = norm_parts(stream_ref[...].astype(F32))
    sums = [jnp.sum(values, 0, keepdims=True) for values in (one * unit, one, two * unit, two)]
    sums_ref[...] = jnp.concatenate(sums + [jnp.zeros((12, D), F32)], 0).astype(BF)
    gradient = (
        gradient_ref[...].astype(F32)
        + norm_input_grad(one, line(vec_ref, GAIN_ONE), unit, scale)
        + norm_input_grad(two, line(vec_ref, GAIN_TWO), unit, scale)
    )
    next_ref[...] = gradient
    if more:
        back(upper_ref, gradient, next_weight[0], *outs)


def unpack_kernel(rows_ref, qkv_ref, out_ref, up_ref, down_ref):
    for i in range(3):
        qkv_ref[0, :, i * D : (i + 1) * D] = rows_ref[0, i * 192 : (i + 1) * 192, :].astype(F32)
    out_ref[0] = rows_ref[0, 576:768, :].astype(F32)
    for i in range(4):
        up_ref[0, :, i * D : (i + 1) * D] = rows_ref[
            0, 768 + i * 192 : 960 + i * 192, :
        ].astype(F32)
    down_ref[0] = rows_ref[0, 1536:, :].astype(F32)


def unpack(rows):
    shapes = [(192, 3 * D), (192, D), (192, FF), (D, D)]
    return pl.pallas_call(
        unpack_kernel,
        grid=(LAYERS,),
        out_shape=tuple(jax.ShapeDtypeStruct((LAYERS,) + shape, F32) for shape in shapes),
        in_specs=[pl.BlockSpec((1, 2304, D), lambda i: (LAYERS - 1 - i, 0, 0))],
        out_specs=tuple(pl.BlockSpec((1,) + shape, lambda i: (i, 0, 0)) for shape in shapes),
        compiler_params=pltpu.CompilerParams(vmem_limit_bytes=60 * 2**20),
        name="unpack",
    )(rows)


def dense(name, kernel, specs, outs, args, flops):
    shapes = tuple(
        jax.ShapeDtypeStruct((BLOCK, size) if isinstance(size, int) else size, kind)
        for size, kind in outs
    )
    return pl.pallas_call(
        kernel,
        out_shape=shapes,
        in_specs=specs,
        out_specs=(VM,) * len(shapes),
        compiler_params=pltpu.CompilerParams(vmem_limit_bytes=60 * 2**20),
        cost_estimate=pl.CostEstimate(
            flops=2 * BLOCK * flops, bytes_accessed=2 * flops, transcendentals=0
        ),
        name=name,
    )(*args)


def vector_kernel(table_ref, *out_refs):
    for layer_index, out_ref in enumerate(out_refs):
        at = slice(layer_index, layer_index + 1)
        for row in range(6):
            pieces = [table_ref[f, at, row * 192 : (row + 1) * 192] for f in range(4)]
            out_ref[row : row + 1, :] = jnp.concatenate(pieces, 1)
        joined = jnp.concatenate([table_ref[f, at, 1152:1728] for f in range(4)], 1)
        for i in range(3):
            out_ref[BIAS_QKV + i : BIAS_QKV + i + 1, :] = joined[:, i * D : (i + 1) * D]
        for f in range(4):
            out_ref[BIAS_UP + f : BIAS_UP + f + 1, :] = table_ref[f, at, 1728:2496]
        out_ref[13:, :] = jnp.zeros((3, D), F32)


def order_vectors(table):
    return pl.pallas_call(
        vector_kernel,
        out_shape=(jax.ShapeDtypeStruct((16, D), F32),) * LAYERS,
        in_specs=[VM],
        out_specs=(VM,) * LAYERS,
        name="order_vectors",
    )(table)


ENTER_OUTS = ((D, BF),) * 2 + ((HALF, BF),) * 6


def shards(
    tokens,
    cotangent,
    ln1_gain,
    ln1_bias,
    ln2_gain,
    ln2_bias,
    qkv_weight,
    qkv_bias,
    out_weight,
    out_bias,
    up_weight,
    up_bias,
    down_weight,
    down_bias,
):
    row_count = tokens.shape[1]
    fsdp = lax.axis_index("fsdp")
    ctx = lax.axis_index("ctx")
    ctx_word = ctx.astype(jnp.int32).reshape(1)
    upper = (ctx % 2).astype(jnp.int32).reshape(1)
    tables = turn_tables(ctx * row_count, row_count)

    vectors = (ln1_gain, ln1_bias, ln2_gain, ln2_bias, out_bias, down_bias, qkv_bias, up_bias)
    packed = jnp.concatenate(vectors, 1).astype(F32)
    packed = jnp.pad(packed, ((0, 8 - LAYERS), (0, 2560 - packed.shape[1])))
    first_weight, table = gather_first(qkv_weight, packed)
    vecs = order_vectors(table)
    qkv_full = [first_weight, None]
    gathered = [None] * LAYERS
    stream = tokens[0]
    entered = dense(
        "enter",
        enter_kernel,
        [SM] + [VM] * 6,
        ENTER_OUTS,
        (upper, stream, vecs[0], first_weight, *tables),
        D * 3 * D,
    )
    saved = []
    for layer_index in range(LAYERS):
        norm_one, norm_two, q_own, q_away, k_own, k_away, v_own, v_away = entered
        jobs = [(layer_index, out_weight), (layer_index, up_weight), (layer_index, down_weight)]
        if layer_index + 1 < LAYERS:
            jobs.append((layer_index + 1, qkv_weight))
        q_other, keys, values, w_out, w_up, w_down, *more = gather_pair(
            "gather_pair_%d" % layer_index,
            1 + layer_index,
            (q_away, k_away, v_away),
            (k_own, v_own),
            jobs,
        )
        if more:
            qkv_full[layer_index + 1] = more[0]
        gathered[layer_index] = (qkv_full[layer_index], w_out, w_up, w_down)
        keys = keys.reshape(BLOCKS * BLOCK, HALF)
        values = values.reshape(BLOCKS * BLOCK, HALF)
        mixed_own, mixed_away, turned, log_total = attend_forward(
            ctx_word, q_own, q_other, keys, values
        )
        mixed_back = mirrored(mixed_away)
        if layer_index + 1 < LAYERS:
            hidden_pre, hidden_low, mlp_branch = dense(
                "mlp",
                mlp_kernel,
                [VM] * 4,
                ((FF, F32), (FF, BF), (D, F32)),
                (norm_two, w_up, w_down, vecs[layer_index]),
                2 * D * FF,
            )
        before = stream
        common = (upper, stream, mixed_own, mixed_back, w_out)
        if more:
            mixed_low, stream, *entered = dense(
                "pass_on",
                pass_kernel,
                [SM] + [VM] * 11,
                ((D, BF), (D, F32)) + ENTER_OUTS,
                common + (mlp_branch, vecs[layer_index], vecs[layer_index + 1], more[0], *tables),
                D * 4 * D,
            )
        else:
            hidden_low, hidden_pre = vecs[layer_index], norm_two
            (mixed_low,) = dense(
                "mixed",
                mixed_kernel,
                [SM] + [VM] * 2,
                ((D, BF),),
                (upper, mixed_own, mixed_back),
                0,
            )
        lefts = (norm_one, mixed_low, norm_two)
        saved.append(
            (before, q_own, q_other, keys, values, turned, log_total, hidden_pre, hidden_low, lefts)
        )

    gradient = cotangent[0]
    waiting, early_rows, late_rows = (), [None] * 2, [None] * 2
    grad_low, grad_own, grad_away = dense(
        "back",
        back_kernel,
        [SM, VM, VM],
        ((D, BF), (HALF, BF), (HALF, BF)),
        (upper, gradient, gathered[LAYERS - 1][1]),
        D * D,
    )
    for layer_index in range(LAYERS - 1, -1, -1):
        w_qkv, w_out, w_up, w_down = gathered[layer_index]
        before, q_own, q_other, keys, values, turned, log_total, hidden_pre, hidden_low, lefts = (
            saved[layer_index]
        )
        grad_back = mirrored(grad_away)
        gq_own, gq_away, grad_keys, grad_values = attend_backward(
            ctx_word, q_own, q_other, keys, values, grad_own, grad_back, turned, log_total
        )
        whole = (BLOCKS, BLOCK, HALF)
        own_pair, grad_norm_two, back_pair, back_query, hidden, pre, *gathered_rows = scatter_pair(
            "scatter_pair_%d" % layer_index,
            3 + layer_index,
            layer_index == LAYERS - 1,
            grad_keys.reshape(whole),
            grad_values.reshape(whole),
            gq_away,
            hidden_low,
            hidden_pre,
            w_up,
            w_down,
            lefts + (grad_low,) + waiting,
        )
        early_rows[layer_index] = (hidden, *gathered_rows[:4], pre)
        if waiting:
            late_rows[layer_index + 1] = gathered_rows[4:]
        else:
            (output,) = dense(
                "last",
                last_kernel,
                [VM] * 5,
                ((D, BF),),
                (before, lefts[1], w_out, gathered_rows[4], vecs[layer_index]),
                D * D,
            )
        going_on = layer_index > 0
        grad_joined, norm_sums, gradient, *outs = dense(
            "join_%d" % layer_index,
            functools.partial(join_kernel, going_on),
            [SM] + [VM] * (13 if going_on else 12),
            ((3 * D, BF), ((16, D), BF), (D, F32))
            + (((D, BF), (HALF, BF), (HALF, BF)) if going_on else ()),
            (
                upper,
                own_pair,
                back_pair,
                gq_own,
                back_query,
                *tables,
                w_qkv,
                before,
                vecs[layer_index],
                grad_norm_two,
                gradient,
            )
            + ((gathered[layer_index - 1][1],) if going_on else ()),
            D * 3 * D,
        )
        waiting = (grad_joined, norm_sums)
        if going_on:
            grad_low, grad_own, grad_away = outs
    arrays = []
    for layer_index in (1, 0):
        hidden, one, mixed, two, low, pre = early_rows[layer_index]
        arrays += [low, mixed, hidden, two, pre, one]
        if layer_index == 1:
            joined_one, norms_one = late_rows[1]
            arrays.append(joined_one)
    summed, small = sum_over_ctx(*waiting, norms_one, arrays)

    def own_part(vectors, width):
        return lax.dynamic_slice_in_dim(vectors, fsdp * width, width, vectors.ndim - 1)

    bias_sum = own_part(small[:, 0], 192)
    joined_sum = own_part(small[:, 1:4].reshape(LAYERS, 3 * D), 576)
    up_sum = own_part(small[:, 4:8].reshape(LAYERS, 4 * D), D)
    norm_sums = own_part(small[:, 8:12], 192)
    qkv_grad, out_grad, up_grad, down_grad = unpack(summed.reshape(LAYERS, 2304, D))
    return (
        output[None],
        gradient[None],
        norm_sums[:, 0],
        norm_sums[:, 1],
        norm_sums[:, 2],
        norm_sums[:, 3],
        qkv_grad,
        joined_sum,
        out_grad,
        bias_sum,
        up_grad,
        up_sum,
        down_grad,
        bias_sum,
    )


def solution(mesh):
    matrix, vector = P(None, "fsdp", None), P(None, "fsdp")
    rows = P("fsdp", "ctx", None)
    params = (
        vector,
        vector,
        vector,
        vector,
        matrix,
        vector,
        matrix,
        vector,
        matrix,
        vector,
        matrix,
        vector,
    )
    return jax.shard_map(
        shards,
        mesh=mesh,
        in_specs=(rows, rows) + params,
        out_specs=(rows, rows) + params,
        check_vma=False,
    )
```
